32 devices in a mesh: fsdp: 8 (over z, y), ctx: 2 (over x), tp: 2 (over core).
Axes of the slice: x: 2, y: 2, z: 4, core: 2. Of those that a mesh axis runs over, the one named last changes fastest.
Arguments:
- tokens: bfloat16 [8192, 1536], P(('fsdp', 'ctx')), may hold values from -6 to 6, as said below
- lengths: int32 [8, 3], P('fsdp'), may hold values from 1 to 768, 1024 in all within a row
- routes: int32 [8192, 4], P(('fsdp', 'ctx')), may hold values from 0 to 7, all different within a row; in each aligned block of 512 rows (0 to 511, 512 to 1023, ...) at most 384 rows name the same one
- norm_attn: bfloat16 [1536], P(('fsdp', 'ctx')), may hold values from 0.5 to 1.5
- w_query: bfloat16 [1536, 1536], P(('fsdp', 'ctx'), 'tp'), may hold values from -0.15625 to 0.15625
- w_key: bfloat16 [1536, 256], P(('fsdp', 'ctx'), 'tp'), may hold values from -0.15625 to 0.15625
- w_value: bfloat16 [1536, 256], P(('fsdp', 'ctx'), 'tp'), may hold values from -0.15625 to 0.15625
- w_out: bfloat16 [1536, 1536], P('tp', ('fsdp', 'ctx')), may hold values from -2 to 2
- norm_moe: bfloat16 [1536], P(('fsdp', 'ctx')), may hold values from 0.5 to 1.5
- w_router: bfloat16 [1536, 8], P(('fsdp', 'ctx')), may hold values from -0.15917969 to 0.15917969
- w_gate: bfloat16 [8, 1536, 768], P('fsdp', None, 'tp'), may hold values from -0.15625 to 0.15625
- w_up: bfloat16 [8, 1536, 768], P('fsdp', None, 'tp'), may hold values from -0.15625 to 0.15625
- w_down: bfloat16 [8, 768, 1536], P('fsdp', 'tp'), may hold values from -0.4375 to 0.4375
- out_grad: bfloat16 [8192, 1536], P(('fsdp', 'ctx')), may hold values from -6 to 6
- loss_grad: float32 [1], replicated, may hold values from 8192 to 65536
Outputs:
- output: bfloat16 [8192, 1536], P(('fsdp', 'ctx'))
- loss: float32 [1], replicated
- tokens_grad: float32 [8192, 1536], P(('fsdp', 'ctx'))
- norm_attn_grad: float32 [1536], P(('fsdp', 'ctx'))
- w_query_grad: float32 [1536, 1536], P(('fsdp', 'ctx'), 'tp')
- w_key_grad: float32 [1536, 256], P(('fsdp', 'ctx'), 'tp')
- w_value_grad: float32 [1536, 256], P(('fsdp', 'ctx'), 'tp')
- w_out_grad: float32 [1536, 1536], P('tp', ('fsdp', 'ctx'))
- norm_moe_grad: float32 [1536], P(('fsdp', 'ctx'))
- w_router_grad: float32 [1536, 8], P(('fsdp', 'ctx'))
- w_gate_grad: float32 [8, 1536, 768], P('fsdp', 'ctx', 'tp')
- w_up_grad: float32 [8, 1536, 768], P('fsdp', 'ctx', 'tp')
- w_down_grad: float32 [8, 768, 1536], P('fsdp', 'tp', 'ctx')
The draws below stay inside these ranges and needn't reach their ends.
Inputs may be any that keep to these rules, and one draw needn't show every extreme that they name: `tokens`: entries are of order one. `lengths`: each row sums to 1024; its longest document has exactly 768 tokens. `routes`: each row names 4 different experts. In the rows of one device (aligned blocks of 512 rows) no expert is named by more than 384 rows, a bound that some block reaches.
All inputs are finite; a program needn't handle non-finite values.
Results may differ from the reference program's by a relative error of at most 0.017.
Values may be sent and summed in bfloat16 or wider, within the bound.
A program may use at most 256 MiB of HBM per device.

```python
import math
import jax
import jax.numpy as jnp
import numpy as np
from jax import lax

D = 1536
HEADS = 12
KV_HEADS = 2
HEAD_DIM = 128
FF = 768
TOPK = 4
TOK_DEV = 512
NSEQ = 3
EXPERTS = 8
PACK = 1024
MOST_LEN = 768
TOKENS = 8192
CAP = 384
GROUPS = 8
N_FSDP = 8
N_CTX = 2
N_TP = 2


def draw_tokens(key, part):
    key = jax.random.fold_in(key, 11)
    common_key = jax.random.fold_in(key, 1)
    row_key = jax.random.fold_in(key, 2)
    common = 1.2 * jax.random.normal(common_key, (GROUPS, 1, D), jnp.float32)
    rows = 0.6 * jax.random.normal(row_key, (GROUPS, PACK, D), jnp.float32)
    values = jnp.clip(common + rows, -6.0, 6.0)
    return values.reshape(TOKENS, D).astype(jnp.bfloat16)


def block_levels(rng, extent, cuts, low, top_value):
    def one(dim, blocks):
        steps = jax.random.uniform(jax.random.fold_in(jax.random.fold_in(rng, 6), dim), (blocks,), jnp.float32, low / len(cuts), top_value / len(cuts))
        return jnp.repeat(jnp.exp(steps), extent[dim] // blocks).reshape((-1,) + (1,) * (len(extent) - dim - 1))

    loudness = one(*cuts[0])
    for cut in cuts[1:]:
        loudness = loudness * one(*cut)
    return loudness


def split_up(amount, total, limit, lean):
    weights = [(1 << 20) // math.isqrt(rank ** lean) + 1 for rank in range(2, amount + 1)]
    rest, given = total - limit - (amount - 1), [1] * (amount - 1)
    while rest > 0:
        movable = [i for i in range(amount - 1) if given[i] < limit]
        pool, left = sum([weights[i] for i in movable]), rest
        for i in movable:
            more = min(limit - given[i], max(1, left * weights[i] // pool), rest)
            given[i] = given[i] + more
            rest = rest - more
    return np.array([limit] + given)


def ragged(own_key, number_of, total, bound, skew):
    if number_of == 2:
        one = jax.random.randint(own_key, (), max(1, total - bound), min(bound, total - 1) + 1)
        return jnp.stack([one, total - one])
    sizes = jnp.asarray(split_up(number_of, total, bound, skew), jnp.int32)
    pairs = (number_of - 1) // 2
    donor, taker = sizes[1:1 + 2 * pairs:2], sizes[2:2 + 2 * pairs:2]
    room = jnp.minimum(donor - 1, bound - taker)
    passed = jax.random.randint(jax.random.fold_in(own_key, 1), (pairs,), 0, 1 << 20) % (room + 1)
    sizes = sizes.at[1:1 + 2 * pairs:2].set(donor - passed).at[2:2 + 2 * pairs:2].set(taker + passed)
    return sizes[jax.random.permutation(jax.random.fold_in(own_key, 2), number_of)]


def shared_out(rng, own, number, rows, amount, top, limit, skew):
    order = jax.random.permutation(rng, amount)
    heavy_load, usual = portions_of(amount, rows * top, limit, skew, True), portions_of(amount, rows * top, limit, skew, False)
    places = jnp.arange(amount)

    def named(sizes, rotation):
        used = int((sizes > 0).sum())
        fixed = max(1, used // 4)
        passed = fixed + (places - fixed + rotation * (used - fixed)) % max(1, amount - fixed)
        return jnp.zeros((amount,), jnp.int32).at[order[jnp.where(places < fixed, places, passed)]].set(jnp.asarray(sizes, jnp.int32))

    sizes = jnp.where(number % 4 == 0, named(heavy_load, number // 4), named(usual, number - number // 4 - 1))
    mixed = jax.random.permutation(jax.random.fold_in(own, 3), amount)
    source_of, receiver = mixed[0:amount // 2 * 2:2], mixed[1:amount // 2 * 2:2]
    margin = jnp.minimum(sizes[source_of] - 1, limit - sizes[receiver]) // 2
    margin = jnp.where((source_of == order[0]) | (receiver == order[0]) | (sizes[receiver] == 0), 0, jnp.maximum(margin, 0))
    passed = jax.random.randint(jax.random.fold_in(own, 4), (amount // 2,), 0, 1 << 20) % (margin + 1)
    sizes = sizes.at[source_of].add(-passed).at[receiver].add(passed)
    labels = jnp.searchsorted(jnp.cumsum(sizes), jnp.arange(rows * top), side="right").astype(jnp.int32)
    table = labels.reshape(top, rows).T
    table = table[jax.random.permutation(jax.random.fold_in(own, 1), rows)]
    rotation = jax.random.randint(jax.random.fold_in(own, 2), (rows, 1), 0, top)
    return jnp.take_along_axis(table, (jnp.arange(top)[None, :] + rotation) % top, axis=1)


def portions_of(amount, total, limit, skew, full):
    loads = [(1 << 20) // math.isqrt(rank ** skew) + 1 for rank in range(1, amount + 1)]
    largest = limit if full else min(limit, max(-(-total // amount), total * loads[0] // sum(loads)))
    least = 1 if total - largest >= amount - 1 else 0
    counts, surplus = [largest] + [least] * (amount - 1), total - largest - least * (amount - 1)
    while surplus > 0:
        movable = [i for i in range(1, amount) if counts[i] < largest] or [i for i in range(1, amount) if counts[i] < limit]
        mass, remaining = sum([loads[i] for i in movable]), surplus
        for i in movable:
            more = min(limit - counts[i], max(1, remaining * loads[i] // mass), surplus)
            counts[i] = counts[i] + more
            surplus = surplus - more
    return np.array(counts)


def scatter_about(rng, extent, scale, bound, cuts=(), held_as=jnp.bfloat16):
    level = block_levels(rng, extent, cuts, -0.22, 0.18) if cuts else 1.0
    array = jax.random.normal(rng, extent, jnp.float32) * scale * level
    return jnp.minimum(jnp.maximum(array, -bound), bound).astype(held_as)


def setup_inputs(seed: int = 0) -> dict:
    streams_of = jax.random.split(jax.random.key(seed), 16)
    tokens = draw_tokens(jax.random.fold_in(streams_of[15], 71), 0)
    lengths = jax.vmap(lambda own: ragged(own, NSEQ, PACK, MOST_LEN, 2))(jax.random.split(streams_of[1], GROUPS)).reshape((GROUPS, NSEQ)).astype(jnp.int32)
    routes_keys = jax.random.split(jax.random.fold_in(streams_of[2], 1), TOKENS // TOK_DEV)
    routes_turns = jax.random.permutation(jax.random.fold_in(streams_of[2], 3), TOKENS // TOK_DEV)
    routes = jax.vmap(lambda own, number: shared_out(jax.random.fold_in(streams_of[2], 2), own, number, TOK_DEV, EXPERTS, TOPK, CAP, 1))(routes_keys, routes_turns).reshape((TOKENS, TOPK))
    norm_attn = jnp.clip(1.0 + 0.1 * jax.random.normal(streams_of[3], (D,), jnp.float32), 0.5, 1.5).astype(jnp.bfloat16)
    w_query = scatter_about(streams_of[4], (D, HEADS * HEAD_DIM), D ** -0.5, 0.15625, ((0, 16), (1, 2)))
    w_key = scatter_about(streams_of[5], (D, KV_HEADS * HEAD_DIM), D ** -0.5, 0.15625, ((0, 16), (1, 2)))
    w_value = scatter_about(streams_of[6], (D, KV_HEADS * HEAD_DIM), D ** -0.5, 0.15625, ((0, 16), (1, 2)))
    w_out = scatter_about(streams_of[7], (HEADS * HEAD_DIM, D), 8 ** -0.5, 2.0, ((0, 2), (1, 16)))
    norm_moe = jnp.clip(1.0 + 0.1 * jax.random.normal(streams_of[8], (D,), jnp.float32), 0.5, 1.5).astype(jnp.bfloat16)
    w_router = scatter_about(streams_of[9], (D, EXPERTS), 0.025, 0.15917969, ((0, 16),))
    w_gate = scatter_about(streams_of[10], (EXPERTS, D, FF), D ** -0.5, 0.15625, ((0, 8), (2, 2)))
    w_up = scatter_about(streams_of[11], (EXPERTS, D, FF), D ** -0.5, 0.15625, ((0, 8), (2, 2)))
    w_down = scatter_about(streams_of[12], (EXPERTS, FF, D), (FF // 4) ** -0.5, 0.4375, ((0, 8), (1, 2)))
    out_grad = scatter_about(streams_of[13], (TOKENS, D), 1.0, 6.0, ((0, 16),))
    loss_grad = jnp.clip(jnp.exp(jax.random.uniform(streams_of[14], (1,), jnp.float32, math.log(8192.0), math.log(65536.0))), 8192.0, 65536.0)
    return {"tokens": tokens, "lengths": lengths, "routes": routes, "norm_attn": norm_attn, "w_query": w_query, "w_key": w_key, "w_value": w_value, "w_out": w_out, "norm_moe": norm_moe, "w_router": w_router, "w_gate": w_gate, "w_up": w_up, "w_down": w_down, "out_grad": out_grad, "loss_grad": loss_grad}


epsilon = 1e-06
rope_base = 10000.0
masked_score = -1e+30
highest = lax.Precision.HIGHEST

@jax.custom_vjp
def low(v):
    return lax.optimization_barrier(v.astype(jnp.bfloat16)).astype(jnp.float32)

@jax.custom_vjp
def low_back(v):
    return v

def low_keep(v):
    return (low(v), None)

def low_pass(kept, grad):
    return (grad,)

def back_keep(v):
    return (v, None)

def back_low(kept, grad):
    return (low(grad),)
low.defvjp(low_keep, low_pass)
low_back.defvjp(back_keep, back_low)

def matmul(left, right):
    return jnp.dot(left, right, precision=highest, preferred_element_type=jnp.float32)

def rms_scale(values, row_gains):
    inverse = lax.rsqrt(lax.optimization_barrier(jnp.mean(values * values, axis=-1, keepdims=True)) + epsilon)
    return values * inverse * row_gains

def rope_tables(positions):
    half_dim = HEAD_DIM // 2
    frequency = rope_base ** (-(jnp.arange(half_dim, dtype=jnp.float32) * (2.0 / HEAD_DIM)))
    angles = positions.astype(jnp.float32)[:, None] * frequency[None, :]
    return (jnp.cos(angles)[:, None, :], jnp.sin(angles)[:, None, :])

def rotate(vectors, cos_table, sin_table):
    half_dim = vectors.shape[-1] // 2
    first_half = vectors[..., :half_dim]
    second_half = vectors[..., half_dim:]
    return jnp.concatenate([first_half * cos_table - second_half * sin_table, second_half * cos_table + first_half * sin_table], axis=-1)

def pack_layout(length_row, row_count):
    doc_ends = jnp.cumsum(length_row).astype(jnp.int32)
    doc_starts = doc_ends - length_row
    row_index = jnp.arange(row_count, dtype=jnp.int32)
    doc_ids = lax.optimization_barrier(jnp.sum((row_index[:, None] >= doc_ends[None, :]).astype(jnp.int32), axis=1))
    doc_numbers = jnp.arange(length_row.shape[0], dtype=jnp.int32)
    doc_first = lax.optimization_barrier(jnp.sum(jnp.where(doc_ids[:, None] == doc_numbers[None, :], doc_starts[None, :], 0), axis=1))
    return (doc_ids, row_index - doc_first)

def attend_pack(queries, key_rows, value_rows, doc_ids):
    row_count = queries.shape[0]
    block_rows = min(512, row_count)
    group_size = HEADS // KV_HEADS
    scale_factor = HEAD_DIM ** (-0.5)
    key_index = jnp.arange(row_count, dtype=jnp.int32)

    def one_block(block_start):
        query_rows = lax.dynamic_slice_in_dim(queries, block_start, block_rows, 0)
        query_rows = query_rows.reshape(block_rows, KV_HEADS, group_size, HEAD_DIM)
        query_index = block_start + jnp.arange(block_rows, dtype=jnp.int32)
        query_docs = lax.dynamic_slice_in_dim(doc_ids, block_start, block_rows, 0)
        scores = low_back(jnp.einsum('qhgd,khd->hgqk', query_rows, key_rows, precision=highest) * scale_factor)
        allowed = (query_docs[:, None] == doc_ids[None, :]) & (key_index[None, :] <= query_index[:, None])
        scores = jnp.where(allowed, scores, masked_score)
        maxima = lax.optimization_barrier(jnp.max(scores, axis=-1, keepdims=True))
        exp_scores = jnp.exp(scores - maxima)
        weights = exp_scores / lax.optimization_barrier(jnp.sum(exp_scores, axis=-1, keepdims=True))
        attended = jnp.einsum('hgqk,khd->qhgd', low(weights), value_rows, precision=highest)
        return attended.reshape(block_rows, HEADS * HEAD_DIM)
    starts = jnp.arange(row_count // block_rows, dtype=jnp.int32) * block_rows
    blocks = lax.map(jax.checkpoint(one_block), starts)
    return blocks.reshape(row_count, HEADS * HEAD_DIM)

def expert_pack(normed, route_rows, w_gate, w_up, w_down):
    row_count = normed.shape[0]
    capacity = N_CTX * CAP
    flat_routes = route_rows.reshape(-1)
    onehot = (flat_routes[:, None] == jnp.arange(EXPERTS, dtype=jnp.int32)[None, :]).astype(jnp.int32)
    slot_rank = lax.optimization_barrier(jnp.sum(jnp.cumsum(onehot, axis=0).astype(jnp.int32) * onehot, axis=1)) - 1
    slot_owner = jnp.arange(flat_routes.shape[0], dtype=jnp.int32) // TOPK
    slot_tokens = jnp.zeros((EXPERTS, capacity), jnp.int32).at[flat_routes, slot_rank].set(slot_owner)
    half_width = FF // N_TP

    def one_expert(inputs):
        token_rows, gate_matrix, up_matrix, down_matrix = inputs
        taken_rows = normed[token_rows]
        combined = jnp.zeros((capacity, D), jnp.float32)
        for part_index in range(N_TP):
            columns = slice(part_index * half_width, (part_index + 1) * half_width)
            entry_rows = low_back(taken_rows)
            gate_pre = low_back(matmul(entry_rows, gate_matrix[:, columns]))
            up_pre = low_back(matmul(entry_rows, up_matrix[:, columns]))
            hidden = low(gate_pre * jax.nn.sigmoid(gate_pre) * up_pre)
            combined = combined + low(low_back(matmul(hidden, down_matrix[columns, :])))
        return combined
    expert_out = lax.map(jax.checkpoint(one_expert), (slot_tokens, w_gate, w_up, w_down))
    picked = expert_out[flat_routes, slot_rank]
    return picked.reshape(row_count, TOPK, D)

def pack_layer(x_pack, length_row, route_rows, params):
    gain_attn, w_query, w_key, w_value, w_out, gain_moe, w_router, w_gate, w_up, w_down = params
    row_count = x_pack.shape[0]
    doc_ids, positions = pack_layout(length_row, row_count)
    cos_table, sin_table = rope_tables(positions)
    normed = low(rms_scale(x_pack, gain_attn))
    queries = low(rotate(low_back(matmul(normed, w_query)).reshape(row_count, HEADS, HEAD_DIM), cos_table, sin_table))
    key_rows = low(rotate(low_back(matmul(normed, w_key)).reshape(row_count, KV_HEADS, HEAD_DIM), cos_table, sin_table))
    value_rows = low(low_back(matmul(normed, w_value))).reshape(row_count, KV_HEADS, HEAD_DIM)
    attended = low(low_back(attend_pack(queries, key_rows, value_rows, doc_ids)))
    middle = x_pack + low_back(matmul(attended, w_out))
    normed_moe = low(rms_scale(middle, gain_moe))
    logits = matmul(normed_moe, w_router)
    shifted = jnp.exp(logits - lax.optimization_barrier(jnp.max(logits, axis=-1, keepdims=True)))
    router_probs = shifted / lax.optimization_barrier(jnp.sum(shifted, axis=-1, keepdims=True))
    route_mask = (route_rows[:, :, None] == jnp.arange(EXPERTS, dtype=jnp.int32)[None, None, :]).astype(jnp.float32)
    chosen = lax.optimization_barrier(jnp.sum(route_mask * router_probs[:, None, :], axis=-1))
    gate_weights = chosen / lax.optimization_barrier(jnp.sum(chosen, axis=-1, keepdims=True))
    picked = expert_pack(normed_moe, route_rows, w_gate, w_up, w_down)
    result = middle + lax.optimization_barrier(jnp.sum(gate_weights[:, :, None] * picked, axis=1))
    return (result, lax.optimization_barrier(jnp.sum(router_probs, axis=0)))

def reference(tokens, lengths, routes, norm_attn, w_query, w_key, w_value, w_out, norm_moe, w_router, w_gate, w_up, w_down, out_grad, loss_grad):
    route_mask = (routes[:, :, None] == jnp.arange(EXPERTS, dtype=jnp.int32)[None, None, :]).astype(jnp.float32)
    fraction = lax.optimization_barrier(jnp.sum(route_mask, axis=(0, 1))) / (TOKENS * TOPK)

    def forward(inputs, params):

        def pack_step(carried, pieces):
            x_pack, length_row, route_rows = pieces
            result, prob_sum = pack_layer(x_pack, length_row, route_rows, params)
            return (carried, (result, prob_sum))
        final_carry, (results, prob_sums) = lax.scan(jax.checkpoint(pack_step), jnp.zeros((), jnp.float32), (inputs.reshape(N_FSDP, PACK, D), lengths, routes.reshape(N_FSDP, PACK, TOPK)))
        mean_prob = lax.optimization_barrier(jnp.sum(prob_sums, axis=0)) / TOKENS
        balance_loss = (EXPERTS * jnp.sum(fraction * mean_prob)).reshape(1)
        return (results.reshape(TOKENS, D), balance_loss)
    params = tuple((weight_arg.astype(jnp.float32) for weight_arg in (norm_attn, w_query, w_key, w_value, w_out, norm_moe, w_router, w_gate, w_up, w_down)))
    (output, balance_loss), pullback = jax.vjp(forward, tokens.astype(jnp.float32), params)
    token_grad, param_grads = pullback((out_grad.astype(jnp.float32), loss_grad))
    return (output.astype(jnp.bfloat16), balance_loss, token_grad, param_grads[0], param_grads[1], param_grads[2], param_grads[3], param_grads[4], param_grads[5], param_grads[6], param_grads[7], param_grads[8], param_grads[9])
```

```python
import functools

import jax
import jax.experimental.pallas as pl
import jax.experimental.pallas.tpu as pltpu
import jax.numpy as jnp
from jax import lax
from jax.sharding import PartitionSpec as P

HEAD_DIM = 128
SHARE = 2
epsilon = 1e-06
rope_base = 10000.0
masked_score = -1e30
highest = lax.Precision.HIGHEST
f32 = jnp.float32
bf16 = jnp.bfloat16


def rms_parts(values, row_gains):
    inverse = lax.rsqrt(jnp.mean(values * values, axis=-1, keepdims=True) + epsilon)
    scaled = values * inverse
    return (inverse, scaled, scaled * row_gains)


def rms_back(inverse, scaled, row_gains, upstream):
    scaled_grad = upstream * row_gains
    return inverse * (scaled_grad - scaled * jnp.mean(scaled_grad * scaled, axis=-1, keepdims=True))


def rope_tables(positions):
    half_dim = HEAD_DIM // 2
    frequency = rope_base ** (-(jnp.arange(half_dim, dtype=f32) * (2.0 / HEAD_DIM)))
    angles = positions.astype(f32)[:, None] * frequency[None, :]
    return (jnp.cos(angles)[:, None, :], jnp.sin(angles)[:, None, :])


def rotate(vectors, cos_table, sin_table):
    half_dim = vectors.shape[-1] // 2
    first_half = vectors[..., :half_dim]
    second_half = vectors[..., half_dim:]
    return jnp.concatenate(
        [
            first_half * cos_table - second_half * sin_table,
            second_half * cos_table + first_half * sin_table,
        ],
        axis=-1,
    )


def pack_layout(length_row, row_count):
    doc_ends = jnp.cumsum(length_row)
    doc_starts = doc_ends - length_row
    row_index = jnp.arange(row_count, dtype=jnp.int32)
    doc_ids = jnp.sum((row_index[:, None] >= doc_ends[None, :]).astype(jnp.int32), axis=1)
    doc_numbers = jnp.arange(length_row.shape[0], dtype=jnp.int32)
    doc_first = jnp.sum(
        jnp.where(doc_ids[:, None] == doc_numbers[None, :], doc_starts[None, :], 0), axis=1
    )
    return (doc_ids, row_index - doc_first, doc_first)


def key_block_data(key_number, block_rows, pack_keys, pack_values, doc_ids):
    key_start = key_number * block_rows
    key_block = lax.dynamic_slice_in_dim(pack_keys, key_start, block_rows, 0)
    value_block = lax.dynamic_slice_in_dim(pack_values, key_start, block_rows, 0)
    key_docs = lax.dynamic_slice_in_dim(doc_ids, key_start, block_rows, 0)
    key_index = key_start + jnp.arange(block_rows, dtype=jnp.int32)
    return (key_start, key_block, value_block, key_docs, key_index)


def block_scores(query_block, key_block, query_docs, query_index, key_docs, key_index):
    scale_factor = HEAD_DIM ** (-0.5)
    scores = (
        jnp.einsum("qhgd,khd->hgqk", query_block, key_block, preferred_element_type=f32)
        * scale_factor
    )
    allowed = (query_docs[:, None] == key_docs[None, :]) & (
        key_index[None, :] <= query_index[:, None]
    )
    return (scores, allowed)


def query_block_range(start_row, block_rows, doc_ids, doc_first):
    query_index = start_row + jnp.arange(block_rows, dtype=jnp.int32)
    query_docs = lax.dynamic_slice_in_dim(doc_ids, start_row, block_rows, 0)
    low_block = doc_first[start_row] // block_rows
    high_block = (start_row + block_rows - 1) // block_rows + 1
    return (query_index, query_docs, low_block, high_block)


def attention_forward(grouped, pack_keys, pack_values, doc_ids, doc_first, base_row, block_rows):
    row_count, local_kv, group_size, head_dim = grouped.shape
    query_index, query_docs, low_block, high_block = query_block_range(
        base_row, block_rows, doc_ids, doc_first
    )

    def scan_maxima(key_number, running):
        maxima, totals = running
        key_start, key_block, value_block, key_docs, key_index = key_block_data(
            key_number, block_rows, pack_keys, pack_values, doc_ids
        )
        scores, allowed = block_scores(
            grouped, key_block, query_docs, query_index, key_docs, key_index
        )
        new_max = jnp.maximum(maxima, jnp.max(jnp.where(allowed, scores, masked_score), axis=-1))
        weights = jnp.where(allowed, jnp.exp(scores - new_max[..., None]), 0.0)
        return (new_max, totals * jnp.exp(maxima - new_max) + jnp.sum(weights, axis=-1))

    start_max = jnp.full((local_kv, group_size, block_rows), masked_score, f32)
    start_total = jnp.zeros((local_kv, group_size, block_rows), f32)
    maxima, totals = lax.fori_loop(low_block, high_block, scan_maxima, (start_max, start_total))
    log_total = maxima + jnp.log(totals)

    def accumulate(key_number, summed):
        key_start, key_block, value_block, key_docs, key_index = key_block_data(
            key_number, block_rows, pack_keys, pack_values, doc_ids
        )
        scores, allowed = block_scores(
            grouped, key_block, query_docs, query_index, key_docs, key_index
        )
        block_probs = jnp.where(allowed, jnp.exp(scores - log_total[..., None]), 0.0).astype(bf16)
        return summed + jnp.einsum(
            "hgqk,khd->hgqd", block_probs, value_block, preferred_element_type=f32
        )

    summed = lax.fori_loop(
        low_block,
        high_block,
        accumulate,
        jnp.zeros((local_kv, group_size, block_rows, head_dim), f32),
    )
    outputs = summed.transpose(2, 0, 1, 3).reshape(block_rows, local_kv * group_size * head_dim)
    return (outputs, log_total)


def attention_backward(
    grouped, pack_keys, pack_values, grad_mixed, log_total, doc_ids, doc_first, base_row, block_rows
):
    row_count, local_kv, group_size, head_dim = grouped.shape
    pack_count = pack_keys.shape[0]
    scale_factor = HEAD_DIM ** (-0.5)
    grad_grouped = grad_mixed.reshape(row_count, local_kv, group_size, head_dim)
    key_acc = jnp.zeros((pack_count, local_kv, head_dim), f32)
    value_acc = jnp.zeros((pack_count, local_kv, head_dim), f32)
    query_index, query_docs, low_block, high_block = query_block_range(
        base_row, block_rows, doc_ids, doc_first
    )

    def probs_at(key_number):
        key_start, key_block, value_block, key_docs, key_index = key_block_data(
            key_number, block_rows, pack_keys, pack_values, doc_ids
        )
        scores, allowed = block_scores(
            grouped, key_block, query_docs, query_index, key_docs, key_index
        )
        block_probs = jnp.where(allowed, jnp.exp(scores - log_total[..., None]), 0.0)
        prob_grad = jnp.einsum(
            "qhgd,khd->hgqk", grad_grouped, value_block, preferred_element_type=f32
        )
        return (key_start, key_block, block_probs, prob_grad)

    def add_delta(key_number, row_delta):
        pieces = probs_at(key_number)
        return row_delta + jnp.sum(pieces[2] * pieces[3], axis=-1)

    row_delta = lax.fori_loop(
        low_block, high_block, add_delta, jnp.zeros((local_kv, group_size, block_rows), f32)
    )

    def add_grads(key_number, running):
        query_acc, key_total, value_total = running
        key_start, key_block, block_probs, prob_grad = probs_at(key_number)
        score_grad = (block_probs * (prob_grad - row_delta[..., None])).astype(bf16)
        query_acc = (
            query_acc
            + jnp.einsum("hgqk,khd->qhgd", score_grad, key_block, preferred_element_type=f32)
            * scale_factor
        )
        key_piece = (
            jnp.einsum("hgqk,qhgd->khd", score_grad, grouped, preferred_element_type=f32)
            * scale_factor
        )
        value_piece = jnp.einsum(
            "hgqk,qhgd->khd", block_probs.astype(bf16), grad_grouped, preferred_element_type=f32
        )
        key_total = lax.dynamic_update_slice_in_dim(
            key_total,
            lax.dynamic_slice_in_dim(key_total, key_start, block_rows, 0) + key_piece,
            key_start,
            0,
        )
        value_total = lax.dynamic_update_slice_in_dim(
            value_total,
            lax.dynamic_slice_in_dim(value_total, key_start, block_rows, 0) + value_piece,
            key_start,
            0,
        )
        return (query_acc, key_total, value_total)

    start_query = jnp.zeros((block_rows, local_kv, group_size, head_dim), f32)
    return lax.fori_loop(low_block, high_block, add_grads, (start_query, key_acc, value_acc))


def dot(left, right, left_dim=1, right_dim=0):
    return lax.dot_general(
        left, right, (((left_dim,), (right_dim,)), ((), ())), preferred_element_type=f32
    )


def swap(array, axis, bit=1):
    return lax.ppermute(array, axis, [(i, i ^ bit) for i in range(lax.axis_size(axis))])


def bit_at(axis, bit):
    return (lax.axis_index(axis) // bit) % 2


def side_by_side(mine, theirs, place, axis=0):
    first = jnp.where(place == 0, mine, theirs)
    return jnp.concatenate([first, jnp.where(place == 0, theirs, mine)], axis=axis)


def fsdp_bits():
    size = lax.axis_size("fsdp")
    return [size >> (k + 1) for k in range(size.bit_length() - 1)]


def weight_dims():
    return [("fsdp", bit) for bit in fsdp_bits()] + [("ctx", 1)]


def weight_orders():
    high = [("fsdp", bit) for bit in fsdp_bits()[:-1]]
    low, across = ("fsdp", 1), ("ctx", 1)
    return [high + [across, low], [across, low] + high, [low] + high + [across]]


def gather_rows(block, order):
    dims = weight_dims()
    held = block.reshape((1,) * len(dims) + block.shape)
    for dim in order:
        held = side_by_side(held, swap(held, *dim), bit_at(*dim), dims.index(dim))
    return held.reshape(-1, block.shape[-1])


def reduce_rows(full, order):
    dims = weight_dims()
    rows = full.shape[0] >> len(dims)
    held = full.reshape((2,) * len(dims) + (rows, full.shape[-1]))
    for dim in reversed(order):
        place, k = bit_at(*dim), dims.index(dim)
        sent = lax.dynamic_index_in_dim(held, 1 - place, k).astype(bf16)
        held = lax.dynamic_index_in_dim(held, place, k) + swap(sent, *dim).astype(f32)
    return held.reshape(rows, full.shape[-1])


def thirds(array, pieces):
    units = array.shape[-1] // 128
    ends = [units * k // pieces * 128 for k in range(pieces + 1)]
    return [array[..., a:b] for a, b in zip(ends[:-1], ends[1:])]


def gather_weights(block, orders):
    parts = thirds(block, len(orders))
    return jnp.concatenate([gather_rows(p, o) for p, o in zip(parts, orders)], axis=1)


def reduce_weights(full, orders):
    parts = thirds(full, len(orders))
    return jnp.concatenate([reduce_rows(p, o) for p, o in zip(parts, orders)], axis=1)


def token_bits():
    return [bit for bit in fsdp_bits() if bit != SHARE]


def gather_tokens(block):
    held = {0: block}
    for bit in token_bits():
        held.update({r ^ bit: swap(b, "fsdp", bit) for r, b in held.items()})
    return held


def reduce_tokens(parts):
    held = dict(parts)
    for bit in reversed(token_bits()):
        for r in sorted(held):
            if r & bit:
                got = swap(held.pop(r).astype(bf16), "fsdp", bit)
                held[r ^ bit] = held[r ^ bit] + got.astype(f32)
    return held[0]


def sum_everywhere(small):
    small = small + swap(small, "tp")
    small = small + swap(small, "ctx")
    for bit in fsdp_bits():
        small = small + swap(small, "fsdp", bit)
    return small


def as_pair(values):
    high = lax.reduce_precision(values, 8, 7)
    return [high.astype(bf16), (values - high).astype(bf16)]


def widen(columns):
    width = sum(c.shape[1] for c in columns)
    pad = jnp.zeros((columns[0].shape[0], -width % 128), columns[0].dtype)
    return jnp.concatenate(list(columns) + [pad], axis=1)


def from_pair(columns, count):
    return columns[:, :count].astype(f32) + columns[:, count : 2 * count].astype(f32)


def own_part(array, place, axis=0):
    size = array.shape[axis] // 2
    return lax.dynamic_slice_in_dim(array, place * size, size, axis)


def across_ctx(kept, axis=0):
    place = lax.axis_index("ctx")
    sent = own_part(kept, 1 - place, axis).astype(bf16)
    return own_part(kept, place, axis) + swap(sent, "ctx").astype(f32)


def across_share(kept, axis=1):
    size = kept.shape[axis] // 2
    own = lax.slice_in_dim(kept, 0, size, axis=axis)
    sent = lax.slice_in_dim(kept, size, None, axis=axis).astype(bf16)
    return own + swap(sent, "fsdp", SHARE).astype(f32)


MESH = pl.DeviceIdType.MESH


def peer(fsdp_bit=0, ctx_bit=0, tp_bit=0):
    return (
        lax.axis_index("fsdp") ^ fsdp_bit,
        lax.axis_index("ctx") ^ ctx_bit,
        lax.axis_index("tp") ^ tp_bit,
    )


def greet(peers):
    barrier = pltpu.get_barrier_semaphore()
    for who in peers:
        pl.semaphore_signal(barrier, inc=1, device_id=who, device_id_type=MESH)
    pl.semaphore_wait(barrier, len(peers))


def send(src, dst, sems, k, who):
    copy = pltpu.make_async_remote_copy(
        src_ref=src,
        dst_ref=dst,
        send_sem=sems[0].at[k],
        recv_sem=sems[1].at[k],
        device_id=who,
        device_id_type=MESH,
    )
    copy.start()
    return copy


def dot_nn(a, b):
    return lax.dot_general(a, b, (((1,), (0,)), ((), ())), preferred_element_type=f32)


def dot_nt(a, b):
    return lax.dot_general(a, b, (((1,), (1,)), ((), ())), preferred_element_type=f32)


def aligned(index, size):
    return pl.ds(pl.multiple_of(index * size, size), size)


TILE = 256


def expert_kernel(
    far,
    near,
    experts,
    x_ref,
    g_hbm,
    wg_hbm,
    wu_hbm,
    wd_hbm,
    dx_ref,
    part_ref,
    keep_gu,
    got_gu,
    keep_d,
    got_d,
    xb,
    gb,
    wg,
    wu,
    wd,
    h0,
    hw,
    dg,
    du,
    db,
    d0,
    near_in,
    near_sum,
    far_in,
    far_out,
    keep_stage,
    send_stage,
    local_sems,
    stage_sems,
    send_sems,
    recv_sems,
    tp_send,
    tp_recv,
):
    half = x_ref.shape[0]
    quarter = half // 2
    width = wg.shape[0]
    units = wg.shape[1]
    unit_tiles = units // TILE
    sems = (send_sems, recv_sems)
    far_dev, near_dev, core_dev = peer(far), peer(near), peer(0, 0, 1)
    greet([far_dev, near_dev, core_dev])

    far_rows = [pl.ds(2 * half + k * half, quarter) for k in range(2)]
    cross_rows = [pl.ds(2 * half + k * half + quarter, quarter) for k in range(2)]
    near_rows = pl.ds(half, half)
    own_half = [pl.ds(k * quarter, quarter) for k in range(2)]
    far_copy = [send(x_ref.at[own_half[k]], xb.at[far_rows[k]], sems, k, far_dev) for k in range(2)]
    near_copy = send(x_ref, xb.at[near_rows], sems, 2, near_dev)
    loads = []
    for k, (src, dst) in enumerate([(g_hbm, gb), (wd_hbm, wd), (wg_hbm, wg), (wu_hbm, wu)]):
        loads.append(pltpu.make_async_copy(src, dst, local_sems.at[k]))
        loads[-1].start()
    xb[0:half, :] = x_ref[...]
    loads[0].wait()
    loads[1].wait()

    def back_tile(j, carry):
        h0[:, aligned(j, TILE)] = dot_nt(gb[...], wd[aligned(j, TILE), :])
        return carry

    lax.fori_loop(0, unit_tiles, back_tile, 0)
    loads[2].wait()
    loads[3].wait()

    lane = lax.broadcasted_iota(jnp.int32, (half, x_ref.shape[1] - width), 1)
    own = lax.axis_index("fsdp")
    partner = own ^ SHARE

    def task(number):
        rows = pl.ds(number * half, half)
        extra = xb[rows, width:].astype(f32)

        def gate_of(expert):
            mine = (lane == expert) | (lane == experts + expert)
            return jnp.sum(jnp.where(mine, extra, 0.0), axis=1, keepdims=True)

        gates = jnp.concatenate([gate_of(own), gate_of(partner)], axis=1)

        def unit_tile(j, dots):
            cols = aligned(j, TILE)
            is_own = j < unit_tiles // 2
            gate = jnp.where(is_own, gates[:, :1], gates[:, 1:])
            x = xb[rows, :width]
            gate_pre = dot_nn(x, wg[:, cols])
            up_pre = dot_nn(x, wu[:, cols])
            back = h0[rows, cols]
            sig = 1.0 / (1.0 + jnp.exp(-gate_pre))
            silu = gate_pre * sig
            hidden = silu * up_pre
            hw[rows, cols] = (hidden * gate).astype(bf16)
            hidden_grad = back * gate
            dg[rows, cols] = (hidden_grad * up_pre * (sig * (1.0 + gate_pre * (1.0 - sig)))).astype(bf16)
            du[rows, cols] = (hidden_grad * silu).astype(bf16)
            one = jnp.sum(hidden * back, axis=1, keepdims=True)
            return (
                dots[0] + jnp.where(is_own, one, 0.0),
                dots[1] + jnp.where(is_own, 0.0, one),
            )

        zero = jnp.zeros((half, 1), f32)
        dots = lax.fori_loop(0, unit_tiles, unit_tile, (zero, zero))

        def put(cols, value):
            if number == 0:
                d0[:, cols] = value
            else:
                db[rows, cols] = value.astype(bf16)

        def in_tile(n, carry):
            cols = aligned(n, 2 * TILE)
            value = dot_nt(dg[rows, :], wg[cols, :]) + dot_nt(du[rows, :], wu[cols, :])
            put(cols, value)
            return carry

        lax.fori_loop(0, width // (2 * TILE), in_tile, 0)
        columns = jnp.zeros_like(extra)
        for expert, value in ((own, dots[0]), (partner, dots[1])):
            high = value.astype(bf16).astype(f32)
            columns = jnp.where(lane == expert, high, columns)
            columns = jnp.where(lane == experts + expert, value - high, columns)
        put(slice(width, None), columns)

    def forward(k):
        return send(xb.at[far_rows[k]], xb.at[cross_rows[k]], sems, 3 + k, near_dev)

    def cross_back(k):
        return send(db.at[cross_rows[k]], near_in.at[own_half[k]], sems, 5 + k, near_dev)

    def far_back(k):
        crossed[k].wait_recv()
        total = db[far_rows[k], :].astype(f32) + near_in[own_half[k], :].astype(f32)
        far_out[own_half[k], :] = total.astype(bf16)
        return send(far_out.at[own_half[k]], far_in.at[own_half[k]], sems, 7 + k, far_dev)

    def part_tile(j, carry):
        cols = aligned(j, 2 * TILE)
        part_ref[:, cols] = dot_nn(hw[...], wd[:, cols]).astype(bf16)
        return carry

    task(0)
    far_copy[0].wait_recv()
    forwards = [forward(0)]
    near_copy.wait_recv()
    task(1)
    forwards[0].wait_recv()
    task(2)
    crossed = [cross_back(0)]
    far_copy[1].wait_recv()
    forwards.append(forward(1))
    backs = [far_back(0)]
    forwards[1].wait_recv()
    task(3)
    crossed.append(cross_back(1))
    near_back = send(db.at[near_rows], near_sum, sems, 9, near_dev)
    lax.fori_loop(0, width // (2 * TILE), part_tile, 0)
    backs.append(far_back(1))

    piece = units // 4
    tiles = width // TILE

    def stage_copies(slot, number, rows, size, keep, got):
        return (
            pltpu.make_async_copy(
                keep_stage.at[slot, pl.ds(0, size)], keep.at[rows], stage_sems.at[slot]
            ),
            pltpu.make_async_remote_copy(
                src_ref=send_stage.at[slot, pl.ds(0, size)],
                dst_ref=got.at[rows],
                send_sem=tp_send.at[slot],
                recv_sem=tp_recv.at[number],
                device_id=core_dev,
                device_id_type=MESH,
            ),
        )

    def wait_stage(slot, size, keep, got):
        local, remote = stage_copies(slot, 0, pl.ds(0, size), size, keep, got)
        local.wait()
        remote.wait_send()

    def gate_up_tile(i, carry):
        rows = aligned(i, TILE)
        slot = lax.rem(i, 2)

        @pl.when(i >= 2)
        def _():
            wait_stage(slot, TILE, keep_gu, got_gu)

        flipped = xb[:, rows].T
        for k, source in enumerate((dg, du)):
            for p in range(4):
                value = dot_nn(flipped, source[:, p * piece : (p + 1) * piece]).astype(bf16)
                at = (2 * k + p // 2) * piece
                stage = keep_stage if p % 2 == 0 else send_stage
                stage[slot, :, at : at + piece] = value
        for copy in stage_copies(slot, i, rows, TILE, keep_gu, got_gu):
            copy.start()
        return carry

    lax.fori_loop(0, tiles, gate_up_tile, 0)
    wait_stage(0, TILE, keep_gu, got_gu)
    wait_stage(1, TILE, keep_gu, got_gu)
    down_rows = 2 * piece // 6

    def down_tile(i, carry):
        which, within = i // 3, lax.rem(i, 3)
        rows = aligned(i, down_rows)
        slot = lax.rem(i, 2)

        @pl.when(i >= 2)
        def _():
            wait_stage(slot, down_rows, keep_d, got_d)

        start = which * 2 * piece + within * down_rows
        for stage, offset in ((keep_stage, 0), (send_stage, piece)):
            cols = pl.ds(pl.multiple_of(start + offset, 128), down_rows)
            flipped = hw[:, cols].T
            for n in range(0, width, 2 * TILE):
                stage[slot, :down_rows, n : n + 2 * TILE] = dot_nn(flipped, gb[:, n : n + 2 * TILE]).astype(bf16)
        for copy in stage_copies(slot, tiles + i, rows, down_rows, keep_d, got_d):
            copy.start()
        return carry

    lax.fori_loop(0, 6, down_tile, 0)
    wait_stage(0, down_rows, keep_d, got_d)
    wait_stage(1, down_rows, keep_d, got_d)

    near_back.wait_recv()
    backs[0].wait_recv()
    backs[1].wait_recv()
    dx_ref[...] = d0[...] + near_sum[...].astype(f32) + far_in[...].astype(f32)
    for i in range(tiles):
        stage_copies(0, i, pl.ds(0, TILE), TILE, keep_gu, got_gu)[1].wait_recv()
    for i in range(6):
        stage_copies(0, tiles + i, pl.ds(0, down_rows), down_rows, keep_d, got_d)[1].wait_recv()
    for copy in far_copy + [near_copy, near_back] + forwards + crossed + backs:
        copy.wait_send()


def experts_on_chip(payload, grad_rows, gate, up, down, experts):
    half, wide = payload.shape
    rows, width = grad_rows.shape
    units = gate.shape[1]
    far, near = token_bits()
    any_spec = pl.BlockSpec(memory_space=pl.ANY)
    vmem = pl.BlockSpec(memory_space=pltpu.VMEM)
    return pl.pallas_call(
        functools.partial(expert_kernel, far, near, experts),
        name="experts",
        out_shape=(
            jax.ShapeDtypeStruct((half, wide), f32),
            jax.ShapeDtypeStruct((rows, width), bf16),
            jax.ShapeDtypeStruct((width, units), bf16),
            jax.ShapeDtypeStruct((width, units), bf16),
            jax.ShapeDtypeStruct((units // 2, width), bf16),
            jax.ShapeDtypeStruct((units // 2, width), bf16),
        ),
        in_specs=[vmem, any_spec, any_spec, any_spec, any_spec],
        out_specs=(vmem, vmem, any_spec, any_spec, any_spec, any_spec),
        scratch_shapes=[
            pltpu.VMEM((rows, wide), bf16),
            pltpu.VMEM((rows, width), bf16),
            pltpu.VMEM((width, units), bf16),
            pltpu.VMEM((width, units), bf16),
            pltpu.VMEM((units, width), bf16),
            pltpu.VMEM((rows, units), f32),
            pltpu.VMEM((rows, units), bf16),
            pltpu.VMEM((rows, units), bf16),
            pltpu.VMEM((rows, units), bf16),
            pltpu.VMEM((rows, wide), bf16),
            pltpu.VMEM((half, wide), f32),
            pltpu.VMEM((half, wide), bf16),
            pltpu.VMEM((half, wide), bf16),
            pltpu.VMEM((half, wide), bf16),
            pltpu.VMEM((half, wide), bf16),
            pltpu.VMEM((2, TILE, units), bf16),
            pltpu.VMEM((2, TILE, units), bf16),
            pltpu.SemaphoreType.DMA((4,)),
            pltpu.SemaphoreType.DMA((2,)),
            pltpu.SemaphoreType.DMA((10,)),
            pltpu.SemaphoreType.DMA((10,)),
            pltpu.SemaphoreType.DMA((2,)),
            pltpu.SemaphoreType.DMA((width // TILE + 6,)),
        ],
        compiler_params=pltpu.CompilerParams(
            collective_id=1, has_side_effects=True, vmem_limit_bytes=62 * 1024 * 1024
        ),
        cost_estimate=pl.CostEstimate(
            flops=2 * 9 * rows * width * units, bytes_accessed=60_000_000, transcendentals=rows * units
        ),
    )(payload, grad_rows, gate, up, down)


class Exchange:
    def __init__(self, send_sems, recv_sems, local_sems):
        self.sems = (send_sems, recv_sems)
        self.local_sems = local_sems
        self.all = []
        self.local = []
        self.arrived = set()

    def start(self, src, dst, who):
        self.all.append(send(src, dst, self.sems, len(self.all), who))
        return len(self.all) - 1

    def keep(self, src, dst):
        copy = pltpu.make_async_copy(src, dst, self.local_sems.at[len(self.local)])
        copy.start()
        self.local.append(copy)

    def arrive(self, number):
        if number not in self.arrived:
            self.arrived.add(number)
            self.all[number].wait_recv()

    def finish(self):
        for number in range(len(self.all)):
            self.arrive(number)
        for copy in self.all:
            copy.wait_send()
        for copy in self.local:
            copy.wait()


class RowGather:
    def __init__(self, net, block, full, part, order):
        self.net, self.full, self.order = net, full, order
        self.rows, self.first, self.size = block.shape[0], part[0], part[1]
        self.copies = {}
        self.spread((0, 0), -1, block.at[pl.ds(self.first, self.size)])

    def place(self, code):
        index = (lax.axis_index("fsdp") ^ code[0]) * 2 + (lax.axis_index("ctx") ^ code[1])
        return pl.ds(pl.multiple_of(index * self.rows + self.first, 16), self.size)

    def spread(self, code, last, src):
        for position in range(last + 1, len(self.order)):
            axis, bit = self.order[position]
            other = (code[0] ^ bit, code[1]) if axis == "fsdp" else (code[0], code[1] ^ bit)
            copy = self.net.start(src, self.full.at[self.place(code)], dim_peer((axis, bit)))
            self.copies[other] = (copy, position)

    def arrive(self, code):
        copy, position = self.copies[code]
        self.net.arrive(copy)
        self.spread(code, position, self.full.at[self.place(code)])


def dim_peer(dim):
    axis, bit = dim
    return peer(bit if axis == "fsdp" else 0, bit if axis == "ctx" else 0)


def gather_codes(far, near):
    first = [(SHARE, 0), (far, 0), (far ^ SHARE, 0)]
    rest = [(0, 1), (near, 0), (near, 1)]
    later = [(a ^ b, c) for a, _ in first for b, c in rest]
    return first, rest[:2] + later[0:2] + [rest[2]] + later[3:5] + [later[2]] + later[6:8] + [later[5], later[8]]


def gather_kernel(
    far, near, in_ref, out_ref, grad_ref, gate_ref, up_ref, down_ref,
    in_full, out_full, grads, gate_all, up_all, down_all,
    send_sems, recv_sems, local_sems,
):
    far_dev, near_dev, share_dev = peer(far), peer(near), peer(SHARE)
    ctx_dev, core_dev = peer(0, 1), peer(0, 0, 1)
    greet([far_dev, near_dev, share_dev, ctx_dev, core_dev])
    net = Exchange(send_sems, recv_sems, local_sems)
    fars = [("fsdp", far), ("fsdp", SHARE)]
    low, across = ("fsdp", near), ("ctx", 1)
    place = lax.axis_index("ctx")
    rows = in_ref.shape[0]
    parts = [((0, rows // 2), fars + [across, low]), ((rows // 2, rows // 2), fars + [low, across])]
    ins = [RowGather(net, in_ref, in_full, part, order) for part, order in parts]
    me = lax.axis_index("fsdp") * 2 + place
    own_rows = pl.ds(pl.multiple_of(me * rows, 16), rows)
    net.keep(in_ref, in_full.at[own_rows])
    net.keep(out_ref, out_full.at[own_rows])

    half = grad_ref.shape[0]
    quarter = half // 2
    own_half = [pl.ds(k * quarter, quarter) for k in range(2)]
    far_rows = [pl.ds(2 * half + k * half, quarter) for k in range(2)]
    cross_rows = [pl.ds(2 * half + k * half + quarter, quarter) for k in range(2)]
    net.keep(grad_ref, grads.at[pl.ds(0, half)])

    width, units = gate_ref.shape

    def slot(full, piece, which=None):
        if full is down_all:
            start, size = piece * units, units
        else:
            start, size = 0, width
        if which is not None:
            size //= 2
            start = pl.multiple_of(start + which * size, 16)
        if full is down_all:
            return full.at[pl.ds(start, size)]
        return full.at[pl.ds(start, size), pl.ds(piece * units, units)]

    matrices = [(gate_ref, gate_all), (up_ref, up_all), (down_ref, down_all)]
    for ref, full in matrices:
        net.keep(ref, slot(full, 0))
        net.start(ref, slot(full, 1), core_dev)
    first, rest = gather_codes(far, near)
    for code in first:
        for g in ins:
            g.arrive(code)
    outs = [RowGather(net, out_ref, out_full, part, order) for part, order in parts]
    far_copies = [net.start(grad_ref.at[own_half[k]], grads.at[far_rows[k]], far_dev) for k in range(2)]
    from_share = []
    for ref, full in matrices:
        size = ref.shape[0] // 2
        part = ref.at[pl.ds(pl.multiple_of(place * size, 16), size)]
        from_share.append(net.start(part, slot(full, 2, place), share_dev))
    for code in rest:
        for g in ins:
            g.arrive(code)
    for code in first + rest:
        for g in outs:
            g.arrive(code)
    net.start(grad_ref, grads.at[pl.ds(half, half)], near_dev)
    for k in range(2):
        net.arrive(far_copies[k])
        net.start(grads.at[far_rows[k]], grads.at[cross_rows[k]], near_dev)
    from_ctx = []
    for k, (ref, full) in enumerate(matrices):
        net.arrive(from_share[k])
        from_ctx.append(net.start(slot(full, 2, place), slot(full, 2, place), ctx_dev))
        net.start(slot(full, 2, place), slot(full, 3, place), core_dev)
    for k, (ref, full) in enumerate(matrices):
        net.arrive(from_ctx[k])
        net.start(slot(full, 2, 1 - place), slot(full, 3, 1 - place), core_dev)
    net.finish()


def gather_all(in_block, out_block, grad_half, gate, up, down):
    far, near = token_bits()
    owners = lax.axis_size("fsdp") * lax.axis_size("ctx")
    width, units = gate.shape
    any_spec = pl.BlockSpec(memory_space=pl.ANY)
    shapes = [
        (owners * in_block.shape[0], in_block.shape[1]),
        (owners * out_block.shape[0], out_block.shape[1]),
        (4 * grad_half.shape[0], width),
        (width, 4 * units),
        (width, 4 * units),
        (4 * units, width),
    ]
    return pl.pallas_call(
        functools.partial(gather_kernel, far, near),
        name="gather",
        out_shape=tuple(jax.ShapeDtypeStruct(s, bf16) for s in shapes),
        in_specs=[any_spec] * 6,
        out_specs=(any_spec,) * 6,
        scratch_shapes=[
            pltpu.SemaphoreType.DMA((80,)),
            pltpu.SemaphoreType.DMA((80,)),
            pltpu.SemaphoreType.DMA((6,)),
        ],
        compiler_params=pltpu.CompilerParams(collective_id=0, has_side_effects=True),
    )(in_block, out_block, grad_half, gate, up, down)


def rms_back_gain(inverse, scaled, row_gains, upstream):
    return jnp.sum(upstream * scaled, axis=0), rms_back(inverse, scaled, row_gains, upstream)


def to_expert(arrived, local_experts, capacity):
    sources = arrived.shape[0]
    return (
        arrived.reshape(sources, local_experts, capacity, -1)
        .transpose(1, 0, 2, 3)
        .reshape(local_experts, sources * capacity, -1)
    )


def from_expert(expert_rows, sources, capacity):
    local_experts = expert_rows.shape[0]
    return (
        expert_rows.reshape(local_experts, sources, capacity, -1)
        .transpose(1, 0, 2, 3)
        .reshape(sources, local_experts * capacity, -1)
    )


def expert_forward(expert_rows, w_gate, w_up):
    gate_pre = jnp.einsum("erd,edf->erf", expert_rows, w_gate, preferred_element_type=jnp.float32)
    up_pre = jnp.einsum("erd,edf->erf", expert_rows, w_up, preferred_element_type=jnp.float32)
    hidden = (gate_pre * jax.nn.sigmoid(gate_pre) * up_pre).astype(jnp.bfloat16)
    return (gate_pre, up_pre, hidden)


def on_any_slice(
    tokens,
    lengths,
    routes,
    norm_attn,
    w_query,
    w_key,
    w_value,
    w_out,
    norm_moe,
    w_router,
    w_gate,
    w_up,
    w_down,
    out_grad,
    loss_grad,
):
    row_count, model_width = tokens.shape
    ctx_count = lax.axis_size("ctx")
    fsdp_count = lax.axis_size("fsdp")
    ctx_place = lax.axis_index("ctx")
    top_count = routes.shape[1]
    expert_count = w_router.shape[1]
    local_experts = w_gate.shape[0]
    capacity = 3 * row_count * top_count // (2 * expert_count)
    pack_count = row_count * ctx_count
    block_rows = min(512, row_count)
    base_row = ctx_place * row_count
    gain_attn, full_query, full_key, full_value, full_out, gain_moe, full_router = (
        lax.all_gather(norm_attn, ("fsdp", "ctx"), axis=0, tiled=True),
        lax.all_gather(w_query, ("fsdp", "ctx"), axis=0, tiled=True),
        lax.all_gather(w_key, ("fsdp", "ctx"), axis=0, tiled=True),
        lax.all_gather(w_value, ("fsdp", "ctx"), axis=0, tiled=True),
        lax.all_gather(w_out, ("fsdp", "ctx"), axis=1, tiled=True),
        lax.all_gather(norm_moe, ("fsdp", "ctx"), axis=0, tiled=True),
        lax.all_gather(w_router, ("fsdp", "ctx"), axis=0, tiled=True),
    )
    doc_ids, positions, doc_first = pack_layout(lengths[0], pack_count)
    own_positions = lax.dynamic_slice_in_dim(positions, base_row, row_count, 0)
    cos_table, sin_table = rope_tables(own_positions)
    x_float = tokens.astype(jnp.float32)
    attn_gain = gain_attn.astype(jnp.float32)
    inverse_attn, scaled_attn, normed_full = rms_parts(x_float, attn_gain)
    normed_attn = normed_full.astype(jnp.bfloat16)
    local_heads = full_query.shape[1] // HEAD_DIM
    local_kv = full_key.shape[1] // HEAD_DIM
    group_size = local_heads // local_kv
    query_raw = jnp.dot(normed_attn, full_query, preferred_element_type=jnp.float32).reshape(
        row_count, local_heads, HEAD_DIM
    )
    queries = rotate(query_raw, cos_table, sin_table).astype(jnp.bfloat16)
    key_raw = jnp.dot(normed_attn, full_key, preferred_element_type=jnp.float32).reshape(
        row_count, local_kv, HEAD_DIM
    )
    key_own = rotate(key_raw, cos_table, sin_table).astype(jnp.bfloat16)
    value_own = (
        jnp.dot(normed_attn, full_value, preferred_element_type=jnp.float32)
        .astype(jnp.bfloat16)
        .reshape(row_count, local_kv, HEAD_DIM)
    )
    pack_keys, pack_values = (
        lax.all_gather(key_own, "ctx", axis=0, tiled=True),
        lax.all_gather(value_own, "ctx", axis=0, tiled=True),
    )
    grouped = queries.reshape(row_count, local_kv, group_size, HEAD_DIM)
    mixed_full, log_total = attention_forward(
        grouped, pack_keys, pack_values, doc_ids, doc_first, base_row, block_rows
    )
    attended = mixed_full.astype(jnp.bfloat16)
    out_part = jnp.dot(attended, full_out, preferred_element_type=jnp.float32)
    attn_out = lax.psum(out_part, "tp")
    middle = x_float + attn_out
    moe_gain = gain_moe.astype(jnp.float32)
    inverse_moe, scaled_moe, normed_mid = rms_parts(middle, moe_gain)
    normed_moe = normed_mid.astype(jnp.bfloat16)
    logits = jnp.dot(normed_moe, full_router, preferred_element_type=jnp.float32)
    shifted = jnp.exp(logits - jnp.max(logits, axis=-1, keepdims=True))
    router_probs = shifted / jnp.sum(shifted, axis=-1, keepdims=True)
    expert_ids = jnp.arange(expert_count, dtype=jnp.int32)
    route_mask = (routes[:, :, None] == expert_ids[None, None, :]).astype(jnp.float32)
    chosen = jnp.sum(route_mask * router_probs[:, None, :], axis=-1)
    chosen_total = jnp.sum(chosen, axis=-1, keepdims=True)
    gate_weights = chosen / chosen_total
    counts_global, probs_global = lax.psum(
        (jnp.sum(route_mask, axis=(0, 1)), jnp.sum(router_probs, axis=0)), ("fsdp", "ctx")
    )
    token_total = pack_count * fsdp_count
    fraction = counts_global / (token_total * top_count)
    balance_loss = (expert_count * jnp.sum(fraction * (probs_global / token_total))).reshape(1)
    flat_routes = routes.reshape(-1)
    flat_mask = (flat_routes[:, None] == expert_ids[None, :]).astype(jnp.int32)
    slot_rank = jnp.sum(jnp.cumsum(flat_mask, axis=0) * flat_mask, axis=1) - 1
    slot_index = flat_routes * capacity + slot_rank
    buffer_rows = expert_count * capacity
    send_rows = (
        jnp.zeros((buffer_rows, model_width), jnp.bfloat16)
        .at[slot_index]
        .set(jnp.repeat(normed_moe, top_count, axis=0))
    )
    send_rows = send_rows.reshape(fsdp_count, local_experts * capacity, model_width)
    arrived = lax.all_to_all(send_rows, "fsdp", split_axis=0, concat_axis=0, tiled=True)
    expert_rows = to_expert(arrived, local_experts, capacity)
    gate_pre, up_pre, hidden = expert_forward(expert_rows, w_gate, w_up)
    expert_out = jnp.einsum(
        "erf,efd->erd", hidden, w_down, preferred_element_type=jnp.float32
    ).astype(jnp.bfloat16)
    returned = lax.all_to_all(
        from_expert(expert_out, fsdp_count, capacity),
        "fsdp",
        split_axis=0,
        concat_axis=0,
        tiled=True,
    )
    slot_values = returned.reshape(buffer_rows, model_width)[slot_index].reshape(
        row_count, top_count, model_width
    )
    moe_part = jnp.sum(gate_weights[:, :, None] * slot_values, axis=1)
    moe_out = lax.psum(moe_part.astype(jnp.bfloat16), "tp").astype(jnp.float32)
    output = (middle + moe_out).astype(jnp.bfloat16)
    upstream = out_grad.astype(jnp.float32)
    gate_dots = jnp.sum(slot_values * upstream[:, None, :], axis=-1)
    grad_slots = (
        (gate_weights[:, :, None] * upstream[:, None, :])
        .astype(jnp.bfloat16)
        .reshape(row_count * top_count, model_width)
    )
    grad_send = jnp.zeros((buffer_rows, model_width), jnp.bfloat16).at[slot_index].set(grad_slots)
    grad_send = grad_send.reshape(fsdp_count, local_experts * capacity, model_width)
    grad_arrived = lax.all_to_all(grad_send, "fsdp", split_axis=0, concat_axis=0, tiled=True)
    kept_gate, kept_up, kept_hidden = (gate_pre, up_pre, hidden)
    grad_expert = to_expert(grad_arrived, local_experts, capacity)
    grad_hidden = jnp.einsum(
        "erd,efd->erf", grad_expert, w_down, preferred_element_type=jnp.float32
    )
    down_grad = jnp.einsum(
        "erf,erd->efd", kept_hidden, grad_expert, preferred_element_type=jnp.float32
    )
    sigmoid_gate = jax.nn.sigmoid(kept_gate)
    grad_gate = (
        grad_hidden * kept_up * sigmoid_gate * (1.0 + kept_gate * (1.0 - sigmoid_gate))
    ).astype(jnp.bfloat16)
    grad_up = (grad_hidden * kept_gate * sigmoid_gate).astype(jnp.bfloat16)
    gate_grad_w = jnp.einsum(
        "erd,erf->edf", expert_rows, grad_gate, preferred_element_type=jnp.float32
    )
    up_grad_w = jnp.einsum("erd,erf->edf", expert_rows, grad_up, preferred_element_type=jnp.float32)
    grad_rows = jnp.einsum("erf,edf->erd", grad_gate, w_gate, preferred_element_type=jnp.float32)
    grad_rows = (
        grad_rows + jnp.einsum("erf,edf->erd", grad_up, w_up, preferred_element_type=jnp.float32)
    ).astype(jnp.bfloat16)
    grad_back = lax.all_to_all(
        from_expert(grad_rows, fsdp_count, capacity),
        "fsdp",
        split_axis=0,
        concat_axis=0,
        tiled=True,
    )
    grad_slot_rows = grad_back.reshape(buffer_rows, model_width)[slot_index].reshape(
        row_count, top_count, model_width
    )
    moe_in_part = jnp.sum(grad_slot_rows.astype(jnp.float32), axis=1)
    moe_in_grad, gate_grad = lax.psum((moe_in_part, gate_dots), "tp")
    weighted = jnp.sum(gate_grad * gate_weights, axis=-1, keepdims=True)
    chosen_grad = (gate_grad - weighted) / chosen_total
    prob_grad = (
        jnp.sum(route_mask * chosen_grad[:, :, None], axis=1)
        + loss_grad[0] * expert_count * fraction / token_total
    )
    logit_grad = router_probs * (
        prob_grad - jnp.sum(prob_grad * router_probs, axis=-1, keepdims=True)
    )
    router_grad = jnp.einsum(
        "td,te->de", normed_moe.astype(jnp.float32), logit_grad, precision=highest
    )
    moe_grad = moe_in_grad + jnp.einsum(
        "te,de->td", logit_grad, full_router.astype(jnp.float32), precision=highest
    )
    gain_moe_grad, middle_norm_grad = rms_back_gain(inverse_moe, scaled_moe, moe_gain, moe_grad)
    middle_grad = upstream + middle_norm_grad
    out_in = middle_grad.astype(jnp.bfloat16)
    out_w_grad = jnp.einsum("tq,td->qd", attended, out_in, preferred_element_type=jnp.float32)
    mixed_grad = jnp.einsum(
        "td,qd->tq", out_in, full_out, preferred_element_type=jnp.float32
    ).astype(jnp.bfloat16)
    query_acc, key_grad_pack, value_grad_pack = attention_backward(
        grouped,
        pack_keys,
        pack_values,
        mixed_grad,
        log_total,
        doc_ids,
        doc_first,
        base_row,
        block_rows,
    )
    key_grad, value_grad, gate_w_out, up_w_out, down_w_out = (
        lax.psum_scatter(key_grad_pack, "ctx", scatter_dimension=0, tiled=True),
        lax.psum_scatter(value_grad_pack, "ctx", scatter_dimension=0, tiled=True),
        lax.psum_scatter(gate_grad_w, "ctx", scatter_dimension=1, tiled=True),
        lax.psum_scatter(up_grad_w, "ctx", scatter_dimension=1, tiled=True),
        lax.psum_scatter(down_grad, "ctx", scatter_dimension=2, tiled=True),
    )
    query_grad = (
        rotate(query_acc.reshape(row_count, local_heads, HEAD_DIM), cos_table, -sin_table)
        .astype(jnp.bfloat16)
        .reshape(row_count, local_heads * HEAD_DIM)
    )
    key_grad_low = (
        rotate(key_grad, cos_table, -sin_table)
        .astype(jnp.bfloat16)
        .reshape(row_count, local_kv * HEAD_DIM)
    )
    value_grad_low = value_grad.astype(jnp.bfloat16).reshape(row_count, local_kv * HEAD_DIM)
    query_w_grad = jnp.einsum(
        "td,tq->dq", normed_attn, query_grad, preferred_element_type=jnp.float32
    )
    key_w_grad = jnp.einsum(
        "td,tq->dq", normed_attn, key_grad_low, preferred_element_type=jnp.float32
    )
    value_w_grad = jnp.einsum(
        "td,tq->dq", normed_attn, value_grad_low, preferred_element_type=jnp.float32
    )
    attn_in_part = jnp.einsum(
        "tq,dq->td", query_grad, full_query, preferred_element_type=jnp.float32
    )
    attn_in_part = attn_in_part + jnp.einsum(
        "tq,dq->td", key_grad_low, full_key, preferred_element_type=jnp.float32
    )
    attn_in_part = attn_in_part + jnp.einsum(
        "tq,dq->td", value_grad_low, full_value, preferred_element_type=jnp.float32
    )
    attn_in_grad = lax.psum(attn_in_part.astype(jnp.bfloat16), "tp").astype(jnp.float32)
    gain_attn_grad, input_norm_grad = rms_back_gain(inverse_attn, scaled_attn, attn_gain, attn_in_grad)
    tokens_grad = middle_grad + input_norm_grad
    shard_grads = (
        lax.psum_scatter(gain_attn_grad, ("fsdp", "ctx"), scatter_dimension=0, tiled=True),
        lax.psum_scatter(query_w_grad, ("fsdp", "ctx"), scatter_dimension=0, tiled=True),
        lax.psum_scatter(key_w_grad, ("fsdp", "ctx"), scatter_dimension=0, tiled=True),
        lax.psum_scatter(value_w_grad, ("fsdp", "ctx"), scatter_dimension=0, tiled=True),
        lax.psum_scatter(out_w_grad, ("fsdp", "ctx"), scatter_dimension=1, tiled=True),
        lax.psum_scatter(gain_moe_grad, ("fsdp", "ctx"), scatter_dimension=0, tiled=True),
        lax.psum_scatter(router_grad, ("fsdp", "ctx"), scatter_dimension=0, tiled=True),
    )
    return (
        output,
        balance_loss,
        tokens_grad,
        shard_grads[0],
        shard_grads[1],
        shard_grads[2],
        shard_grads[3],
        shard_grads[4],
        shard_grads[5],
        shard_grads[6],
        gate_w_out,
        up_w_out,
        down_w_out,
    )


def on_device(
    tokens,
    lengths,
    routes,
    norm_attn,
    w_query,
    w_key,
    w_value,
    w_out,
    norm_moe,
    w_router,
    w_gate,
    w_up,
    w_down,
    out_grad,
    loss_grad,
):
    row_count, width = tokens.shape
    ctx_count = lax.axis_size("ctx")
    fsdp_count = lax.axis_size("fsdp")
    ctx_place = lax.axis_index("ctx")
    tp_place = lax.axis_index("tp")
    own_expert = lax.axis_index("fsdp")
    top_count = routes.shape[1]
    expert_count = w_router.shape[1]
    pack_count = row_count * ctx_count
    base_row = ctx_place * row_count
    half_rows = row_count // 2
    token_total = pack_count * fsdp_count
    if fsdp_count != 8:
        return on_any_slice(
            tokens, lengths, routes, norm_attn, w_query, w_key, w_value, w_out, norm_moe, w_router,
            w_gate, w_up, w_down, out_grad, loss_grad,
        )
    orders = weight_orders()

    extras = widen([norm_attn[:, None], norm_moe[:, None], w_router])
    extra_width = extras.shape[1]
    in_block = jnp.concatenate([extras, w_query, w_key, w_value], axis=1)
    upstream_low = own_part(out_grad, tp_place)
    in_weights, out_weights, grad_blocks, gate_all, up_all, down_all = gather_all(
        in_block, w_out.T, upstream_low, w_gate[0], w_up[0], w_down[0]
    )
    gains = in_weights[:, :2].astype(f32)
    attn_gain, moe_gain = gains[:, 0], gains[:, 1]
    full_router = in_weights[:, 2 : 2 + expert_count]
    qkv_weights = in_weights[:, extra_width:]
    query_width, kv_width = w_query.shape[1], w_key.shape[1]

    own_routes = own_part(routes, tp_place)
    expert_ids = jnp.arange(expert_count, dtype=jnp.int32)
    route_mask = jnp.sum((own_routes[:, :, None] == expert_ids).astype(f32), axis=1)
    fraction = sum_everywhere(jnp.sum(route_mask, axis=0)) / (token_total * top_count)

    doc_ids, positions, doc_first = pack_layout(lengths[0], pack_count)
    own_positions = lax.dynamic_slice_in_dim(positions, base_row, row_count, 0)
    cos_table, sin_table = rope_tables(own_positions)
    x_float = tokens.astype(f32)
    _, _, normed_full = rms_parts(x_float, attn_gain)
    normed_attn = normed_full.astype(bf16)
    local_heads = query_width // HEAD_DIM
    local_kv = kv_width // HEAD_DIM
    qkv = dot(normed_attn, qkv_weights)
    rotated = rotate(
        qkv[:, : query_width + kv_width].reshape(row_count, local_heads + local_kv, HEAD_DIM),
        cos_table,
        sin_table,
    ).astype(bf16)
    queries = rotated[:, :local_heads]
    key_own = rotated[:, local_heads:].reshape(row_count, kv_width)
    value_own = qkv[:, query_width + kv_width :].astype(bf16)
    kv_own = jnp.concatenate([key_own, value_own], axis=1)
    kv_pack = side_by_side(kv_own, swap(kv_own, "ctx"), ctx_place)
    pack_keys = kv_pack[:, :kv_width].reshape(pack_count, local_kv, HEAD_DIM)
    pack_values = kv_pack[:, kv_width:].reshape(pack_count, local_kv, HEAD_DIM)
    grouped = queries.reshape(row_count, local_kv, local_heads // local_kv, HEAD_DIM)
    mixed_full, log_total = attention_forward(
        grouped, pack_keys, pack_values, doc_ids, doc_first, base_row, row_count
    )
    attended = mixed_full.astype(bf16)
    out_part = dot(attended, out_weights, 1, 1)
    attn_out = own_part(out_part, tp_place) + swap(own_part(out_part, 1 - tp_place), "tp")

    x_half = own_part(tokens, tp_place).astype(f32)
    middle = x_half + attn_out
    inverse_moe, scaled_moe, normed_mid = rms_parts(middle, moe_gain)
    normed_moe = normed_mid.astype(bf16)
    logits = dot(normed_moe, full_router)
    shifted = jnp.exp(logits - jnp.max(logits, axis=-1, keepdims=True))
    router_probs = shifted / jnp.sum(shifted, axis=-1, keepdims=True)
    chosen = router_probs * route_mask
    chosen_total = jnp.sum(chosen, axis=-1, keepdims=True)
    gate_weights = chosen / chosen_total
    probs_global = sum_everywhere(jnp.sum(router_probs, axis=0))
    balance_loss = (expert_count * jnp.sum(fraction * (probs_global / token_total))).reshape(1)

    payload = jnp.concatenate([normed_moe, widen(as_pair(gate_weights))], axis=1)
    returned, moe_rows, keep_gu, got_gu, keep_d, got_d = experts_on_chip(
        payload, grad_blocks, gate_all, up_all, down_all, expert_count
    )
    far, near = token_bits()
    quarter = half_rows // 2
    second = 3 * half_rows
    moe_parts = {
        0: moe_rows[:half_rows].astype(f32),
        near: moe_rows[half_rows : 2 * half_rows].astype(f32),
        far: jnp.concatenate([moe_rows[2 * half_rows :][:quarter], moe_rows[second:][:quarter]]).astype(f32),
        far ^ near: jnp.concatenate([moe_rows[2 * half_rows + quarter : second], moe_rows[second + quarter :]]).astype(f32),
    }
    moe_out = reduce_tokens(moe_parts)
    out_half = (middle + moe_out).astype(bf16)
    output = side_by_side(out_half, swap(out_half, "tp"), tp_place)
    units = keep_d.shape[0] // 2

    def summed(keep, got, cols):
        return keep[:, cols].astype(f32) + got[:, cols].astype(f32)

    gate_w_out = across_share(across_ctx(summed(keep_gu, got_gu, slice(0, 2 * units))))
    up_w_out = across_ctx(across_share(summed(keep_gu, got_gu, slice(2 * units, None))))
    down_w_out = across_share(across_ctx(summed(keep_d, got_d, slice(None)), 1), 0)

    moe_in_grad = returned[:, :width]
    gate_grad = from_pair(returned[:, width:], expert_count)
    weighted = jnp.sum(gate_grad * gate_weights, axis=-1, keepdims=True)
    chosen_grad = route_mask * (gate_grad - weighted) / chosen_total
    prob_grad = chosen_grad + loss_grad[0] * expert_count * fraction / token_total
    logit_grad = router_probs * (
        prob_grad - jnp.sum(prob_grad * router_probs, axis=-1, keepdims=True)
    )
    moe_grad = moe_in_grad + lax.dot_general(
        logit_grad, full_router.astype(f32), (((1,), (1,)), ((), ())), precision=highest
    )
    router_grad = lax.dot_general(
        normed_moe.astype(f32), logit_grad, (((0,), (0,)), ((), ())), precision=highest
    )
    gain_moe_grad = jnp.sum(moe_grad * scaled_moe, axis=0)
    upstream = upstream_low.astype(f32)
    middle_grad = upstream + rms_back(inverse_moe, scaled_moe, moe_gain, moe_grad)
    out_in_half = middle_grad.astype(bf16)
    out_in = side_by_side(out_in_half, swap(out_in_half, "tp"), tp_place)
    mixed_grad = dot(out_in, out_weights).astype(bf16)
    out_w_grad = dot(out_in, attended, 0, 0)
    small_grads = widen([gain_moe_grad[:, None], router_grad])
    out_reduced = reduce_weights(jnp.concatenate([small_grads, out_w_grad], axis=1), orders)
    small_out = out_reduced[:, : 1 + expert_count]
    small_out = small_out + swap(small_out, "tp")
    w_out_grad = out_reduced[:, small_grads.shape[1] :].T

    query_acc, key_grad_pack, value_grad_pack = attention_backward(
        grouped,
        pack_keys,
        pack_values,
        mixed_grad,
        log_total,
        doc_ids,
        doc_first,
        base_row,
        row_count,
    )
    kv_grad_pack = jnp.concatenate(
        [key_grad_pack.reshape(pack_count, kv_width), value_grad_pack.reshape(pack_count, kv_width)],
        axis=1,
    )
    kv_grad = across_ctx(kv_grad_pack)
    query_grad = (
        rotate(query_acc.reshape(row_count, local_heads, HEAD_DIM), cos_table, -sin_table)
        .astype(bf16)
        .reshape(row_count, query_width)
    )
    key_grad = (
        rotate(kv_grad[:, :kv_width].reshape(row_count, local_kv, HEAD_DIM), cos_table, -sin_table)
        .astype(bf16)
        .reshape(row_count, kv_width)
    )
    qkv_grad = jnp.concatenate([query_grad, key_grad, kv_grad[:, kv_width:].astype(bf16)], axis=1)
    attn_in_part = dot(qkv_grad, qkv_weights, 1, 1)
    attn_in_grad = own_part(attn_in_part, tp_place) + swap(
        own_part(attn_in_part, 1 - tp_place).astype(bf16), "tp"
    ).astype(f32)
    inverse_attn, scaled_attn, _ = rms_parts(x_half, attn_gain)
    gain_attn_grad = jnp.sum(attn_in_grad * scaled_attn, axis=0)
    tokens_half = middle_grad + rms_back(inverse_attn, scaled_attn, attn_gain, attn_in_grad)
    tokens_grad = side_by_side(tokens_half, swap(tokens_half, "tp"), tp_place)
    qkv_w_grad = dot(normed_attn, qkv_grad, 0, 0)
    gain_column = widen([gain_attn_grad[:, None]])
    in_reduced = reduce_weights(jnp.concatenate([gain_column, qkv_w_grad], axis=1), orders)
    gain_out = in_reduced[:, :1]
    gain_out = (gain_out + swap(gain_out, "tp"))[:, 0]
    start = gain_column.shape[1]
    return (
        output,
        balance_loss,
        tokens_grad,
        gain_out,
        in_reduced[:, start : start + query_width],
        in_reduced[:, start + query_width : start + query_width + kv_width],
        in_reduced[:, start + query_width + kv_width :],
        w_out_grad,
        small_out[:, 0],
        small_out[:, 1:],
        gate_w_out[None],
        up_w_out[None],
        down_w_out[None],
    )


def solution(mesh):
    rows = P(("fsdp", "ctx"), None)
    gain = P(("fsdp", "ctx"))
    split = P(("fsdp", "ctx"), "tp")
    out_split = P("tp", ("fsdp", "ctx"))
    columns = P("fsdp", None, "tp")
    return jax.shard_map(
        on_device,
        mesh=mesh,
        in_specs=(
            rows,
            P("fsdp", None),
            rows,
            gain,
            split,
            split,
            split,
            out_split,
            gain,
            rows,
            columns,
            columns,
            P("fsdp", "tp", None),
            rows,
            P(),
        ),
        out_specs=(
            rows,
            P(),
            rows,
            gain,
            split,
            split,
            split,
            out_split,
            gain,
            rows,
            P("fsdp", "ctx", "tp"),
            P("fsdp", "ctx", "tp"),
            P("fsdp", "tp", "ctx"),
        ),
        check_vma=False,
    )
```

```python
import functools
import math

import jax
import jax.experimental.pallas as pl
import jax.experimental.pallas.tpu as pltpu
import jax.numpy as jnp
from jax import lax
from jax.sharding import PartitionSpec as P

HEAD_DIM = 128
SHARE = 2
epsilon = 1e-06
rope_base = 10000.0
masked_score = -1e30
highest = lax.Precision.HIGHEST
f32 = jnp.float32
bf16 = jnp.bfloat16


def rms_parts(values, row_gains):
    inverse = lax.rsqrt(jnp.mean(values * values, axis=-1, keepdims=True) + epsilon)
    scaled = values * inverse
    return (inverse, scaled, scaled * row_gains)


def rms_back(inverse, scaled, row_gains, upstream):
    scaled_grad = upstream * row_gains
    return inverse * (scaled_grad - scaled * jnp.mean(scaled_grad * scaled, axis=-1, keepdims=True))


def rope_tables(positions):
    half_dim = HEAD_DIM // 2
    frequency = rope_base ** (-(jnp.arange(half_dim, dtype=f32) * (2.0 / HEAD_DIM)))
    angles = positions.astype(f32)[:, None] * frequency[None, :]
    return (jnp.cos(angles)[:, None, :], jnp.sin(angles)[:, None, :])


def rotate(vectors, cos_table, sin_table):
    half_dim = vectors.shape[-1] // 2
    first_half = vectors[..., :half_dim]
    second_half = vectors[..., half_dim:]
    return jnp.concatenate(
        [
            first_half * cos_table - second_half * sin_table,
            second_half * cos_table + first_half * sin_table,
        ],
        axis=-1,
    )


def pack_layout(length_row, row_count):
    doc_ends = jnp.cumsum(length_row)
    doc_starts = doc_ends - length_row
    row_index = jnp.arange(row_count, dtype=jnp.int32)
    doc_ids = jnp.sum((row_index[:, None] >= doc_ends[None, :]).astype(jnp.int32), axis=1)
    doc_numbers = jnp.arange(length_row.shape[0], dtype=jnp.int32)
    doc_first = jnp.sum(
        jnp.where(doc_ids[:, None] == doc_numbers[None, :], doc_starts[None, :], 0), axis=1
    )
    return (doc_ids, row_index - doc_first, doc_first)


def key_block_data(key_number, block_rows, pack_keys, pack_values, doc_ids):
    key_start = key_number * block_rows
    key_block = lax.dynamic_slice_in_dim(pack_keys, key_start, block_rows, 0)
    value_block = lax.dynamic_slice_in_dim(pack_values, key_start, block_rows, 0)
    key_docs = lax.dynamic_slice_in_dim(doc_ids, key_start, block_rows, 0)
    key_index = key_start + jnp.arange(block_rows, dtype=jnp.int32)
    return (key_start, key_block, value_block, key_docs, key_index)


def block_scores(query_block, key_block, query_docs, query_index, key_docs, key_index):
    scale_factor = HEAD_DIM ** (-0.5)
    scores = (
        jnp.einsum("qhgd,khd->hgqk", query_block, key_block, preferred_element_type=f32)
        * scale_factor
    )
    allowed = (query_docs[:, None] == key_docs[None, :]) & (
        key_index[None, :] <= query_index[:, None]
    )
    return (scores, allowed)


def query_block_range(start_row, block_rows, doc_ids, doc_first):
    query_index = start_row + jnp.arange(block_rows, dtype=jnp.int32)
    query_docs = lax.dynamic_slice_in_dim(doc_ids, start_row, block_rows, 0)
    low_block = doc_first[start_row] // block_rows
    high_block = (start_row + block_rows - 1) // block_rows + 1
    return (query_index, query_docs, low_block, high_block)


def attention_forward(grouped, pack_keys, pack_values, doc_ids, doc_first, base_row, block_rows):
    row_count, local_kv, group_size, head_dim = grouped.shape
    query_index, query_docs, low_block, high_block = query_block_range(
        base_row, block_rows, doc_ids, doc_first
    )

    def scan_maxima(key_number, running):
        maxima, totals = running
        key_start, key_block, value_block, key_docs, key_index = key_block_data(
            key_number, block_rows, pack_keys, pack_values, doc_ids
        )
        scores, allowed = block_scores(
            grouped, key_block, query_docs, query_index, key_docs, key_index
        )
        new_max = jnp.maximum(maxima, jnp.max(jnp.where(allowed, scores, masked_score), axis=-1))
        weights = jnp.where(allowed, jnp.exp(scores - new_max[..., None]), 0.0)
        return (new_max, totals * jnp.exp(maxima - new_max) + jnp.sum(weights, axis=-1))

    start_max = jnp.full((local_kv, group_size, block_rows), masked_score, f32)
    start_total = jnp.zeros((local_kv, group_size, block_rows), f32)
    maxima, totals = lax.fori_loop(low_block, high_block, scan_maxima, (start_max, start_total))
    log_total = maxima + jnp.log(totals)

    def accumulate(key_number, summed):
        key_start, key_block, value_block, key_docs, key_index = key_block_data(
            key_number, block_rows, pack_keys, pack_values, doc_ids
        )
        scores, allowed = block_scores(
            grouped, key_block, query_docs, query_index, key_docs, key_index
        )
        block_probs = jnp.where(allowed, jnp.exp(scores - log_total[..., None]), 0.0).astype(bf16)
        return summed + jnp.einsum(
            "hgqk,khd->hgqd", block_probs, value_block, preferred_element_type=f32
        )

    summed = lax.fori_loop(
        low_block,
        high_block,
        accumulate,
        jnp.zeros((local_kv, group_size, block_rows, head_dim), f32),
    )
    outputs = summed.transpose(2, 0, 1, 3).reshape(block_rows, local_kv * group_size * head_dim)
    return (outputs, log_total)


def attention_backward(
    grouped, pack_keys, pack_values, grad_mixed, log_total, doc_ids, doc_first, base_row, block_rows
):
    row_count, local_kv, group_size, head_dim = grouped.shape
    pack_count = pack_keys.shape[0]
    scale_factor = HEAD_DIM ** (-0.5)
    grad_grouped = grad_mixed.reshape(row_count, local_kv, group_size, head_dim)
    key_acc = jnp.zeros((pack_count, local_kv, head_dim), f32)
    value_acc = jnp.zeros((pack_count, local_kv, head_dim), f32)
    query_index, query_docs, low_block, high_block = query_block_range(
        base_row, block_rows, doc_ids, doc_first
    )

    def probs_at(key_number):
        key_start, key_block, value_block, key_docs, key_index = key_block_data(
            key_number, block_rows, pack_keys, pack_values, doc_ids
        )
        scores, allowed = block_scores(
            grouped, key_block, query_docs, query_index, key_docs, key_index
        )
        block_probs = jnp.where(allowed, jnp.exp(scores - log_total[..., None]), 0.0)
        prob_grad = jnp.einsum(
            "qhgd,khd->hgqk", grad_grouped, value_block, preferred_element_type=f32
        )
        return (key_start, key_block, block_probs, prob_grad)

    def add_delta(key_number, row_delta):
        pieces = probs_at(key_number)
        return row_delta + jnp.sum(pieces[2] * pieces[3], axis=-1)

    row_delta = lax.fori_loop(
        low_block, high_block, add_delta, jnp.zeros((local_kv, group_size, block_rows), f32)
    )

    def add_grads(key_number, running):
        query_acc, key_total, value_total = running
        key_start, key_block, block_probs, prob_grad = probs_at(key_number)
        score_grad = (block_probs * (prob_grad - row_delta[..., None])).astype(bf16)
        query_acc = (
            query_acc
            + jnp.einsum("hgqk,khd->qhgd", score_grad, key_block, preferred_element_type=f32)
            * scale_factor
        )
        key_piece = (
            jnp.einsum("hgqk,qhgd->khd", score_grad, grouped, preferred_element_type=f32)
            * scale_factor
        )
        value_piece = jnp.einsum(
            "hgqk,qhgd->khd", block_probs.astype(bf16), grad_grouped, preferred_element_type=f32
        )
        key_total = lax.dynamic_update_slice_in_dim(
            key_total,
            lax.dynamic_slice_in_dim(key_total, key_start, block_rows, 0) + key_piece,
            key_start,
            0,
        )
        value_total = lax.dynamic_update_slice_in_dim(
            value_total,
            lax.dynamic_slice_in_dim(value_total, key_start, block_rows, 0) + value_piece,
            key_start,
            0,
        )
        return (query_acc, key_total, value_total)

    start_query = jnp.zeros((block_rows, local_kv, group_size, head_dim), f32)
    return lax.fori_loop(low_block, high_block, add_grads, (start_query, key_acc, value_acc))


def dot(left, right, left_dim=1, right_dim=0):
    return lax.dot_general(
        left, right, (((left_dim,), (right_dim,)), ((), ())), preferred_element_type=f32
    )


def swap(array, axis, bit=1):
    return lax.ppermute(array, axis, [(i, i ^ bit) for i in range(lax.axis_size(axis))])


def bit_at(axis, bit):
    return (lax.axis_index(axis) // bit) % 2


def side_by_side(mine, theirs, place, axis=0):
    first = jnp.where(place == 0, mine, theirs)
    return jnp.concatenate([first, jnp.where(place == 0, theirs, mine)], axis=axis)


def fsdp_bits():
    size = lax.axis_size("fsdp")
    return [size >> (k + 1) for k in range(size.bit_length() - 1)]


def weight_dims():
    return [("fsdp", bit) for bit in fsdp_bits()] + [("ctx", 1)]


def weight_orders():
    high = [("fsdp", bit) for bit in fsdp_bits()[:-1]]
    low, across = ("fsdp", 1), ("ctx", 1)
    return [high + [across, low], [across, low] + high, [low] + high + [across]]


def gather_rows(block, order):
    dims = weight_dims()
    held = block.reshape((1,) * len(dims) + block.shape)
    for dim in order:
        held = side_by_side(held, swap(held, *dim), bit_at(*dim), dims.index(dim))
    return held.reshape(-1, block.shape[-1])


def reduce_rows(full, order):
    dims = weight_dims()
    rows = full.shape[0] >> len(dims)
    held = full.reshape((2,) * len(dims) + (rows, full.shape[-1]))
    for dim in reversed(order):
        place, k = bit_at(*dim), dims.index(dim)
        sent = lax.dynamic_index_in_dim(held, 1 - place, k).astype(bf16)
        held = lax.dynamic_index_in_dim(held, place, k) + swap(sent, *dim).astype(f32)
    return held.reshape(rows, full.shape[-1])


def thirds(array, pieces):
    units = array.shape[-1] // 128
    ends = [units * k // pieces * 128 for k in range(pieces + 1)]
    return [array[..., a:b] for a, b in zip(ends[:-1], ends[1:])]


def gather_weights(block, orders):
    parts = thirds(block, len(orders))
    return jnp.concatenate([gather_rows(p, o) for p, o in zip(parts, orders)], axis=1)


def reduce_weights(full, orders):
    parts = thirds(full, len(orders))
    return jnp.concatenate([reduce_rows(p, o) for p, o in zip(parts, orders)], axis=1)


def token_bits():
    return [bit for bit in fsdp_bits() if bit != SHARE]


def gather_tokens(block):
    held = {0: block}
    for bit in token_bits():
        held.update({r ^ bit: swap(b, "fsdp", bit) for r, b in held.items()})
    return held


def reduce_tokens(parts):
    held = dict(parts)
    for bit in reversed(token_bits()):
        for r in sorted(held):
            if r & bit:
                got = swap(held.pop(r).astype(bf16), "fsdp", bit)
                held[r ^ bit] = held[r ^ bit] + got.astype(f32)
    return held[0]


def sum_everywhere(small):
    small = small + swap(small, "tp")
    small = small + swap(small, "ctx")
    for bit in fsdp_bits():
        small = small + swap(small, "fsdp", bit)
    return small


def as_pair(values):
    high = lax.reduce_precision(values, 8, 7)
    return [high.astype(bf16), (values - high).astype(bf16)]


def widen(columns):
    width = sum(c.shape[1] for c in columns)
    pad = jnp.zeros((columns[0].shape[0], -width % 128), columns[0].dtype)
    return jnp.concatenate(list(columns) + [pad], axis=1)


def from_pair(columns, count):
    return columns[:, :count].astype(f32) + columns[:, count : 2 * count].astype(f32)


def own_part(array, place, axis=0):
    size = array.shape[axis] // 2
    return lax.dynamic_slice_in_dim(array, place * size, size, axis)


def across_ctx(kept, axis=0):
    place = lax.axis_index("ctx")
    sent = own_part(kept, 1 - place, axis).astype(bf16)
    return own_part(kept, place, axis) + swap(sent, "ctx").astype(f32)


def across_share(kept, axis=1):
    size = kept.shape[axis] // 2
    own = lax.slice_in_dim(kept, 0, size, axis=axis)
    sent = lax.slice_in_dim(kept, size, None, axis=axis).astype(bf16)
    return own + swap(sent, "fsdp", SHARE).astype(f32)


MESH = pl.DeviceIdType.MESH


def peer(fsdp_bit=0, ctx_bit=0, tp_bit=0):
    return (
        lax.axis_index("fsdp") ^ fsdp_bit,
        lax.axis_index("ctx") ^ ctx_bit,
        lax.axis_index("tp") ^ tp_bit,
    )


def greet(peers):
    barrier = pltpu.get_barrier_semaphore()
    for who in peers:
        pl.semaphore_signal(barrier, inc=1, device_id=who, device_id_type=MESH)
    pl.semaphore_wait(barrier, len(peers))


def send(src, dst, sems, k, who):
    copy = pltpu.make_async_remote_copy(
        src_ref=src,
        dst_ref=dst,
        send_sem=sems[0].at[k],
        recv_sem=sems[1].at[k],
        device_id=who,
        device_id_type=MESH,
    )
    copy.start()
    return copy


def dot_nn(a, b):
    return lax.dot_general(a, b, (((1,), (0,)), ((), ())), preferred_element_type=f32)


def dot_nt(a, b):
    return lax.dot_general(a, b, (((1,), (1,)), ((), ())), preferred_element_type=f32)


def aligned(index, size):
    return pl.ds(pl.multiple_of(index * size, size), size)


TILE = 256


def expert_kernel(
    far,
    near,
    experts,
    x_ref,
    grad_hbm,
    gate_hbm,
    up_hbm,
    down_hbm,
    g_hbm,
    wg_hbm,
    wu_hbm,
    wd_hbm,
    dx_ref,
    part_ref,
    keep_gu,
    got_gu,
    keep_d,
    got_d,
    xb,
    gb,
    wg,
    wu,
    wd,
    h0,
    hw,
    dg,
    du,
    db,
    d0,
    near_in,
    near_sum,
    far_in,
    keep_stage,
    send_stage,
    local_sems,
    stage_sems,
    send_sems,
    recv_sems,
    tp_send,
    tp_recv,
):
    half = x_ref.shape[0]
    quarter = half // 2
    width = wg.shape[0]
    units = wg.shape[1]
    unit_tiles = units // TILE
    sems = (send_sems, recv_sems)
    far_dev, near_dev, core_dev = peer(far), peer(near), peer(0, 0, 1)
    greet([far_dev, near_dev, core_dev])

    far_rows = [pl.ds(2 * half + k * half, quarter) for k in range(2)]
    cross_rows = [pl.ds(2 * half + k * half + quarter, quarter) for k in range(2)]
    near_rows = pl.ds(half, half)
    own_half = [pl.ds(k * quarter, quarter) for k in range(2)]
    far_copy = [send(x_ref.at[own_half[k]], xb.at[far_rows[k]], sems, k, far_dev) for k in range(2)]
    near_copy = send(x_ref, xb.at[near_rows], sems, 2, near_dev)
    own_units = gate_hbm.shape[1]
    core_rows = pl.ds(pl.multiple_of(lax.axis_index("tp") * half, 16), half)
    got_rows, got_units = pl.ds(half, 3 * half), pl.ds(own_units, 3 * own_units)
    first_units = pl.ds(0, own_units)
    pairs = [
        (grad_hbm.at[core_rows], gb.at[pl.ds(0, half)]),
        (g_hbm.at[got_rows], gb.at[got_rows]),
        (down_hbm, wd.at[first_units]),
        (wd_hbm.at[got_units], wd.at[got_units]),
        (gate_hbm, wg.at[:, first_units]),
        (wg_hbm.at[:, got_units], wg.at[:, got_units]),
        (up_hbm, wu.at[:, first_units]),
        (wu_hbm.at[:, got_units], wu.at[:, got_units]),
    ]
    loads = []
    for k, (src, dst) in enumerate(pairs):
        loads.append(pltpu.make_async_copy(src, dst, local_sems.at[k]))
        loads[-1].start()
    xb[0:half, :] = x_ref[...]
    for k in range(4):
        loads[k].wait()

    def back_tile(j, carry):
        h0[:, aligned(j, TILE)] = dot_nt(gb[...], wd[aligned(j, TILE), :])
        return carry

    lax.fori_loop(0, unit_tiles, back_tile, 0)
    for k in range(4, 8):
        loads[k].wait()

    lane = lax.broadcasted_iota(jnp.int32, (half, x_ref.shape[1] - width), 1)
    own = lax.axis_index("fsdp")
    partner = own ^ SHARE

    def task(number):
        rows = pl.ds(number * half, half)
        extra = xb[rows, width:].astype(f32)

        def gate_of(expert):
            mine = (lane == expert) | (lane == experts + expert)
            return jnp.sum(jnp.where(mine, extra, 0.0), axis=1, keepdims=True)

        gates = jnp.concatenate([gate_of(own), gate_of(partner)], axis=1)

        def unit_tile(j, dots):
            cols = aligned(j, TILE)
            is_own = j < unit_tiles // 2
            gate = jnp.where(is_own, gates[:, :1], gates[:, 1:])
            x = xb[rows, :width]
            gate_pre = dot_nn(x, wg[:, cols])
            up_pre = dot_nn(x, wu[:, cols])
            back = h0[rows, cols]
            sig = 1.0 / (1.0 + jnp.exp(-gate_pre))
            silu = gate_pre * sig
            hidden = silu * up_pre
            hw[rows, cols] = (hidden * gate).astype(bf16)
            hidden_grad = back * gate
            dg[rows, cols] = (hidden_grad * up_pre * (sig * (1.0 + gate_pre * (1.0 - sig)))).astype(bf16)
            du[rows, cols] = (hidden_grad * silu).astype(bf16)
            one = jnp.sum(hidden * back, axis=1, keepdims=True)
            return (
                dots[0] + jnp.where(is_own, one, 0.0),
                dots[1] + jnp.where(is_own, 0.0, one),
            )

        zero = jnp.zeros((half, 1), f32)
        dots = lax.fori_loop(0, unit_tiles, unit_tile, (zero, zero), unroll=True)

        def put(cols, value):
            if number == 0:
                d0[:, cols] = value
            else:
                db[rows, cols] = value.astype(bf16)

        def in_tile(n, carry):
            cols = aligned(n, 2 * TILE)
            value = dot_nt(dg[rows, :], wg[cols, :]) + dot_nt(du[rows, :], wu[cols, :])
            put(cols, value)
            return carry

        lax.fori_loop(0, width // (2 * TILE), in_tile, 0, unroll=True)
        columns = jnp.zeros_like(extra)
        for expert, value in ((own, dots[0]), (partner, dots[1])):
            high = value.astype(bf16).astype(f32)
            columns = jnp.where(lane == expert, high, columns)
            columns = jnp.where(lane == experts + expert, value - high, columns)
        put(slice(width, None), columns)

    def forward(k):
        return send(xb.at[far_rows[k]], xb.at[cross_rows[k]], sems, 3 + k, near_dev)

    def cross_back(k):
        return send(db.at[cross_rows[k]], near_in.at[own_half[k]], sems, 5 + k, near_dev)

    def far_back(k):
        crossed[k].wait_recv()
        total = db[far_rows[k], :].astype(f32) + near_in[own_half[k], :].astype(f32)
        db[far_rows[k], :] = total.astype(bf16)
        return send(db.at[far_rows[k]], far_in.at[own_half[k]], sems, 7 + k, far_dev)

    def part_tile(j, carry):
        cols = aligned(j, 2 * TILE)
        part_ref[:, cols] = dot_nn(hw[...], wd[:, cols]).astype(bf16)
        return carry

    task(0)
    far_copy[0].wait_recv()
    forwards = [forward(0)]
    near_copy.wait_recv()
    task(1)
    forwards[0].wait_recv()
    task(2)
    crossed = [cross_back(0)]
    far_copy[1].wait_recv()
    forwards.append(forward(1))
    backs = [far_back(0)]
    forwards[1].wait_recv()
    task(3)
    crossed.append(cross_back(1))
    near_back = send(db.at[near_rows], near_sum, sems, 9, near_dev)
    lax.fori_loop(0, width // (2 * TILE), part_tile, 0)
    backs.append(far_back(1))

    piece = units // 4
    tiles = width // TILE

    def stage_copies(slot, number, rows, size, keep, got):
        return (
            pltpu.make_async_copy(
                keep_stage.at[slot, pl.ds(0, size)], keep.at[rows], stage_sems.at[slot]
            ),
            pltpu.make_async_remote_copy(
                src_ref=send_stage.at[slot, pl.ds(0, size)],
                dst_ref=got.at[rows],
                send_sem=tp_send.at[slot],
                recv_sem=tp_recv.at[number],
                device_id=core_dev,
                device_id_type=MESH,
            ),
        )

    def wait_stage(slot, size, keep, got):
        local, remote = stage_copies(slot, 0, pl.ds(0, size), size, keep, got)
        local.wait()
        remote.wait_send()

    def gate_up_tile(i, carry):
        rows = aligned(i, TILE)
        slot = lax.rem(i, 2)

        @pl.when(i >= 2)
        def _():
            wait_stage(slot, TILE, keep_gu, got_gu)

        flipped = xb[:, rows].T
        for k, source in enumerate((dg, du)):
            for p in range(4):
                value = dot_nn(flipped, source[:, p * piece : (p + 1) * piece]).astype(bf16)
                at = (2 * k + p // 2) * piece
                stage = keep_stage if p % 2 == 0 else send_stage
                stage[slot, :, at : at + piece] = value
        for copy in stage_copies(slot, i, rows, TILE, keep_gu, got_gu):
            copy.start()
        return carry

    lax.fori_loop(0, tiles, gate_up_tile, 0)
    wait_stage(0, TILE, keep_gu, got_gu)
    wait_stage(1, TILE, keep_gu, got_gu)
    down_rows = 2 * piece // 6

    def down_tile(i, carry):
        which, within = i // 3, lax.rem(i, 3)
        rows = aligned(i, down_rows)
        slot = lax.rem(i, 2)

        @pl.when(i >= 2)
        def _():
            wait_stage(slot, down_rows, keep_d, got_d)

        start = which * 2 * piece + within * down_rows
        for stage, offset in ((keep_stage, 0), (send_stage, piece)):
            cols = pl.ds(pl.multiple_of(start + offset, 128), down_rows)
            flipped = hw[:, cols].T
            for n in range(0, width, 2 * TILE):
                stage[slot, :down_rows, n : n + 2 * TILE] = dot_nn(flipped, gb[:, n : n + 2 * TILE]).astype(bf16)
        for copy in stage_copies(slot, tiles + i, rows, down_rows, keep_d, got_d):
            copy.start()
        return carry

    lax.fori_loop(0, 6, down_tile, 0)
    wait_stage(0, down_rows, keep_d, got_d)
    wait_stage(1, down_rows, keep_d, got_d)

    near_back.wait_recv()
    backs[0].wait_recv()
    backs[1].wait_recv()
    dx_ref[...] = d0[...] + near_sum[...].astype(f32) + far_in[...].astype(f32)
    for i in range(tiles):
        stage_copies(0, i, pl.ds(0, TILE), TILE, keep_gu, got_gu)[1].wait_recv()
    for i in range(6):
        stage_copies(0, tiles + i, pl.ds(0, down_rows), down_rows, keep_d, got_d)[1].wait_recv()
    for copy in far_copy + [near_copy, near_back] + forwards + crossed + backs:
        copy.wait_send()


def experts_on_chip(payload, out_grad, own_gate, own_up, own_down, grad_rows, gate, up, down, experts):
    half, wide = payload.shape
    rows, width = grad_rows.shape
    units = gate.shape[1]
    far, near = token_bits()
    any_spec = pl.BlockSpec(memory_space=pl.ANY)
    vmem = pl.BlockSpec(memory_space=pltpu.VMEM)
    return pl.pallas_call(
        functools.partial(expert_kernel, far, near, experts),
        name="experts",
        out_shape=(
            jax.ShapeDtypeStruct((half, wide), f32),
            jax.ShapeDtypeStruct((rows, width), bf16),
            jax.ShapeDtypeStruct((width, units), bf16),
            jax.ShapeDtypeStruct((width, units), bf16),
            jax.ShapeDtypeStruct((units // 2, width), bf16),
            jax.ShapeDtypeStruct((units // 2, width), bf16),
        ),
        in_specs=[vmem] + [any_spec] * 8,
        out_specs=(vmem, vmem, any_spec, any_spec, any_spec, any_spec),
        scratch_shapes=[
            pltpu.VMEM((rows, wide), bf16),
            pltpu.VMEM((rows, width), bf16),
            pltpu.VMEM((width, units), bf16),
            pltpu.VMEM((width, units), bf16),
            pltpu.VMEM((units, width), bf16),
            pltpu.VMEM((rows, units), f32),
            pltpu.VMEM((rows, units), bf16),
            pltpu.VMEM((rows, units), bf16),
            pltpu.VMEM((rows, units), bf16),
            pltpu.VMEM((rows, wide), bf16),
            pltpu.VMEM((half, wide), f32),
            pltpu.VMEM((half, wide), bf16),
            pltpu.VMEM((half, wide), bf16),
            pltpu.VMEM((half, wide), bf16),
            pltpu.VMEM((2, TILE, units), bf16),
            pltpu.VMEM((2, TILE, units), bf16),
            pltpu.SemaphoreType.DMA((8,)),
            pltpu.SemaphoreType.DMA((2,)),
            pltpu.SemaphoreType.DMA((10,)),
            pltpu.SemaphoreType.DMA((10,)),
            pltpu.SemaphoreType.DMA((2,)),
            pltpu.SemaphoreType.DMA((width // TILE + 6,)),
        ],
        compiler_params=pltpu.CompilerParams(
            collective_id=1, has_side_effects=True, vmem_limit_bytes=62 * 1024 * 1024
        ),
        cost_estimate=pl.CostEstimate(
            flops=2 * 9 * rows * width * units, bytes_accessed=60_000_000, transcendentals=rows * units
        ),
    )(payload, out_grad, own_gate, own_up, own_down, grad_rows, gate, up, down)


class Exchange:
    def __init__(self, send_sems, recv_sems, local_sems):
        self.sems = (send_sems, recv_sems)
        self.local_sems = local_sems
        self.all = []
        self.local = []
        self.arrived = set()
        self.settled = set()
        self.gone = set()

    def start(self, src, dst, who):
        self.all.append(send(src, dst, self.sems, len(self.all), who))
        return len(self.all) - 1

    def keep(self, src, dst):
        copy = pltpu.make_async_copy(src, dst, self.local_sems.at[len(self.local)])
        copy.start()
        self.local.append(copy)

    def arrive(self, number):
        if number not in self.arrived:
            self.arrived.add(number)
            self.all[number].wait_recv()

    def settle(self, number):
        if number not in self.settled:
            self.settled.add(number)
            self.local[number].wait()

    def sent(self, number):
        if number not in self.gone:
            self.gone.add(number)
            self.all[number].wait_send()

    def finish(self):
        for number in range(len(self.all)):
            self.arrive(number)
        for number in range(len(self.all)):
            self.sent(number)
        for number in range(len(self.local)):
            self.settle(number)


class RowGather:
    def __init__(self, net, full, part, order):
        self.net, self.full, self.order = net, full, order
        self.rows, self.first, self.size = part
        self.copies = {}
        self.spread((0, 0), -1)

    def place(self, code):
        index = (lax.axis_index("fsdp") ^ code[0]) * 2 + (lax.axis_index("ctx") ^ code[1])
        return pl.ds(pl.multiple_of(index * self.rows + self.first, 16), self.size)

    def spread(self, code, last):
        block = self.full.at[self.place(code)]
        for position in range(last + 1, len(self.order)):
            axis, bit = self.order[position]
            other = (code[0] ^ bit, code[1]) if axis == "fsdp" else (code[0], code[1] ^ bit)
            self.copies[other] = (self.net.start(block, block, dim_peer((axis, bit))), position)

    def arrive(self, code):
        copy, position = self.copies[code]
        self.net.arrive(copy)
        self.spread(code, position)


def dim_peer(dim):
    axis, bit = dim
    return peer(bit if axis == "fsdp" else 0, bit if axis == "ctx" else 0)


def gather_codes(far, near):
    first = [(SHARE, 0), (far, 0), (far ^ SHARE, 0)]
    rest = [(0, 1), (near, 0), (near, 1)]
    later = [(a ^ b, c) for a, _ in first for b, c in rest]
    return first, rest[:2] + later[0:2] + [rest[2]] + later[3:5] + [later[2]] + later[6:8] + [later[5], later[8]]


def document_start(lengths_ref, number):
    start, first = 0, jnp.zeros_like(number)
    for k in range(lengths_ref.shape[1]):
        start = start + lengths_ref[0, k]
        first = jnp.where(number >= start, start, first)
    return first


def forward_kernel(
    far, near, experts, total_rows,
    lengths_ref, loss_grad_ref, routes_ref, tokens_ref, small_hbm, query_hbm, key_hbm, value_hbm, out_hbm,
    grad_hbm, gate_hbm, up_hbm, down_hbm,
    payload_ref, middle_ref, probs_ref, mask_ref, row_ref, query, kv, lse_ref, attended, cos_ref, sin_ref,
    in_out, out_out, grads, gate_all, up_all, down_all,
    in_full, out_full, normed, raw, core_sent, core_got, count_sent, count_got,
    send_sems, recv_sems, local_sems,
):
    far_dev, near_dev, share_dev = peer(far), peer(near), peer(SHARE)
    ctx_dev, core_dev = peer(0, 1), peer(0, 0, 1)
    net = Exchange(send_sems, recv_sems, local_sems)
    place, core = lax.axis_index("ctx"), lax.axis_index("tp")
    rows, width = tokens_ref.shape
    half, quarter = rows // 2, rows // 4
    block = small_hbm.shape[0]
    heads_width, kv_width = query_hbm.shape[1], key_hbm.shape[1]
    own_block = pl.ds(pl.multiple_of((lax.axis_index("fsdp") * 2 + place) * block, 16), block)
    start = 0
    for ref in (small_hbm, query_hbm, key_hbm, value_hbm):
        net.keep(ref, in_full.at[own_block, pl.ds(start, ref.shape[1])])
        start += ref.shape[1]
    net.keep(out_hbm, out_full.at[own_block])
    greet([far_dev, near_dev, share_dev, ctx_dev, core_dev])
    for k in range(5):
        net.settle(k)
    fars = [("fsdp", far), ("fsdp", SHARE)]
    low, across = ("fsdp", near), ("ctx", 1)
    part = block // 2
    ins = [
        RowGather(net, in_full, (block, 0, part), fars + [across, low]),
        RowGather(net, in_full, (block, part, part), fars + [low, across]),
    ]

    routes = routes_ref[...]
    lane = lax.broadcasted_iota(jnp.int32, (rows, 128), 1)
    named = jnp.zeros((rows, 128), f32)
    for k in range(routes.shape[1]):
        named += (routes[:, k : k + 1] == lane).astype(f32)
    count_dims = [ctx_dev, near_dev, share_dev, far_dev]
    counts = [jnp.broadcast_to(jnp.sum(named, axis=0, keepdims=True), (8, 128))]
    count_copies = []

    def count_step():
        k = len(count_copies)
        if k > 0:
            net.arrive(count_copies[-1])
            counts[0] = counts[0] + count_got[k - 1]
        if k < len(count_dims):
            count_sent[k] = counts[0]
            count_copies.append(net.start(count_sent.at[k], count_got.at[k], count_dims[k]))

    count_step()

    units = gate_hbm.shape[1]

    def slot(full, piece, which=None):
        begin, size = (piece * units, units) if full is down_all else (0, width)
        if which is not None:
            size //= 2
            begin = pl.multiple_of(begin + which * size, 16)
        if full is down_all:
            return full.at[pl.ds(begin, size)]
        return full.at[pl.ds(begin, size), pl.ds(piece * units, units)]

    matrices = [(down_hbm, down_all), (gate_hbm, gate_all), (up_hbm, up_all)]
    for ref, full in matrices:
        net.start(ref, slot(full, 1), core_dev)

    here = lax.broadcasted_iota(jnp.int32, (rows, 1), 0) + place * rows
    position = (here - document_start(lengths_ref, here)).astype(f32)
    turn_lane = lax.broadcasted_iota(jnp.int32, (1, HEAD_DIM), 1)
    turn = lax.rem(turn_lane, HEAD_DIM // 2).astype(f32) * (2.0 / HEAD_DIM)
    angles = position * jnp.exp(turn * -math.log(rope_base))
    cos_ref[...] = jnp.cos(angles)
    sin_ref[...] = jnp.where(turn_lane < HEAD_DIM // 2, -1.0, 1.0) * jnp.sin(angles)

    first, rest = gather_codes(far, near)
    for code in first:
        for g in ins:
            g.arrive(code)
    count_step()
    own_rows = pl.ds(pl.multiple_of(core * half, 16), half)
    other_rows = pl.ds(pl.multiple_of((1 - core) * half, 16), half)
    own_quarter = [pl.ds(pl.multiple_of(core * half + k * quarter, 16), quarter) for k in range(2)]
    far_rows = [pl.ds(2 * half + k * half, quarter) for k in range(2)]
    cross_rows = [pl.ds(2 * half + k * half + quarter, quarter) for k in range(2)]
    from_share = []
    for ref, full in matrices:
        size = ref.shape[0] // 2
        piece = ref.at[pl.ds(pl.multiple_of(place * size, 16), size)]
        from_share.append(net.start(piece, slot(full, 2, place), share_dev))
    far_copies = [net.start(grad_hbm.at[own_quarter[k]], grads.at[far_rows[k]], far_dev) for k in range(2)]
    for code in rest:
        for g in ins:
            g.arrive(code)
    count_step()
    outs = [
        RowGather(net, out_full, (block, 0, part), [across] + fars + [low]),
        RowGather(net, out_full, (block, part, part), fars + [low, across]),
    ]
    gains = in_full[:, :128].astype(f32).T
    attn_gain, moe_gain = gains[experts : experts + 1], gains[experts + 1 : experts + 2]
    step = quarter // 2
    for k in range(rows // quarter):
        at = slice(k * quarter, (k + 1) * quarter)
        x = tokens_ref[at, :].astype(f32)
        inverse = lax.rsqrt(jnp.mean(x * x, axis=1, keepdims=True) + epsilon)
        normed[at, :] = (x * inverse * attn_gain).astype(bf16)

    def rotated(value, at):
        return value * cos_ref[at, :] + pltpu.roll(value, HEAD_DIM // 2, 1) * sin_ref[at, :]

    mine = pl.ds(pl.multiple_of(place * rows, 16), rows)
    raw[...] = dot_nn(normed[...], in_full[:, 128:])
    kv[mine, :kv_width] = rotated(raw[:, heads_width : heads_width + kv_width], slice(None)).astype(bf16)
    kv[mine, kv_width:] = raw[:, heads_width + kv_width :].astype(bf16)
    kv_copy = net.start(kv.at[mine], kv.at[mine], ctx_dev)
    for head in range(heads_width // HEAD_DIM):
        cols = slice(head * HEAD_DIM, (head + 1) * HEAD_DIM)
        query[:, cols] = rotated(raw[:, cols], slice(None)).astype(bf16)
    for code in first:
        for g in outs:
            g.arrive(code)
    near_copy = net.start(grad_hbm.at[own_rows], grads.at[pl.ds(half, half)], near_dev)
    count_step()
    net.arrive(kv_copy)

    keys, values_flipped = kv[:, :HEAD_DIM], kv[:, HEAD_DIM:].T
    query_number = lax.broadcasted_iota(jnp.int32, (1, half), 1) + place * rows
    key_number = lax.broadcasted_iota(jnp.int32, (kv.shape[0], 1), 0)
    scale = HEAD_DIM ** (-0.5)

    def head_block(i, carry):
        head, block_index = i // 2, lax.rem(i, 2)
        cols, at = aligned(head, HEAD_DIM), aligned(block_index, half)
        number = query_number + block_index * half
        allowed = (key_number >= document_start(lengths_ref, number)) & (key_number <= number)
        scores = jnp.where(allowed, dot_nt(keys, query[at, cols]) * scale, masked_score)
        maxima = jnp.max(scores, axis=0, keepdims=True)
        weights = jnp.exp(scores - maxima)
        totals = jnp.sum(weights, axis=0, keepdims=True)
        lse_ref[pl.ds(head, 1), at] = maxima + jnp.log(totals)
        low_weights = (weights * (1.0 / totals)).astype(bf16)
        attended[at, cols] = dot_nn(values_flipped, low_weights).T.astype(bf16)
        return carry

    group = heads_width // HEAD_DIM
    third = 2 * group // 3
    lax.fori_loop(0, third, head_block, 0)
    for code in rest:
        for g in outs:
            g.arrive(code)
    count_step()
    lax.fori_loop(third, 2 * third, head_block, 0)
    for k in range(2):
        net.arrive(far_copies[k])
        net.start(grads.at[far_rows[k]], grads.at[cross_rows[k]], near_dev)
    lax.fori_loop(2 * third, 2 * group, head_block, 0)
    from_ctx = []
    for k, (ref, full) in enumerate(matrices):
        net.arrive(from_share[k])
        from_ctx.append(net.start(slot(full, 2, place), slot(full, 2, place), ctx_dev))
        net.start(slot(full, 2, place), slot(full, 3, place), core_dev)

    core_sent[...] = dot_nt(attended[other_rows, :], out_full[...])
    core_copy = net.start(core_sent, core_got, core_dev)
    middle_ref[...] = tokens_ref[own_rows, :].astype(f32) + dot_nt(attended[own_rows, :], out_full[...])
    net.arrive(core_copy)
    own_lane = lax.broadcasted_iota(jnp.int32, (step, 128), 1)
    share_row = counts[0][0:1] * (experts / (total_rows * routes.shape[1] * total_rows))
    row_number = lax.broadcasted_iota(jnp.int32, (8, 128), 0)
    row_ref[...] = jnp.where(
        row_number == 0, share_row * loss_grad_ref[0], jnp.where(row_number == 1, share_row, 0.0)
    )
    router = in_full[:, :128]
    for k in range(half // step):
        at = slice(k * step, (k + 1) * step)
        middle = middle_ref[at, :] + core_got[at, :]
        middle_ref[at, :] = middle
        inverse = lax.rsqrt(jnp.mean(middle * middle, axis=1, keepdims=True) + epsilon)
        normed_moe = (middle * inverse * moe_gain).astype(bf16)
        payload_ref[at, :width] = normed_moe
        logits = jnp.where(own_lane < experts, dot_nn(normed_moe, router), masked_score)
        shifted = jnp.exp(logits - jnp.max(logits, axis=1, keepdims=True))
        probs = shifted / jnp.sum(shifted, axis=1, keepdims=True)
        own_routes = routes_ref[pl.ds(pl.multiple_of(core * half + k * step, 16), step), :]
        mask = jnp.zeros((step, 128), f32)
        for n in range(routes.shape[1]):
            mask += (own_routes[:, n : n + 1] == own_lane).astype(f32)
        probs_ref[at, :] = probs
        mask_ref[at, :] = mask
        chosen = probs * mask
        gates = chosen / jnp.sum(chosen, axis=1, keepdims=True)
        high = gates.astype(bf16).astype(f32)
        payload_ref[at, width:] = (high + pltpu.roll(gates - high, experts, 1)).astype(bf16)
    for k, (ref, full) in enumerate(matrices):
        net.arrive(from_ctx[k])
        net.start(slot(full, 2, 1 - place), slot(full, 3, 1 - place), core_dev)
    net.keep(in_full, in_out)
    net.keep(out_full, out_out)
    net.finish()


def forward_on_chip(
    lengths, loss_grad, routes, tokens, small, w_query, w_key, w_value, out_block, out_grad, gate, up, down, experts
):
    far, near = token_bits()
    owners = lax.axis_size("fsdp") * lax.axis_size("ctx")
    rows, width = tokens.shape
    half, pack = rows // 2, rows * lax.axis_size("ctx")
    units, block = gate.shape[1], small.shape[0]
    heads_width, kv_width = w_query.shape[1], w_key.shape[1]
    in_width, out_width = small.shape[1] + heads_width + 2 * kv_width, out_block.shape[1]
    any_spec = pl.BlockSpec(memory_space=pl.ANY)
    vmem = pl.BlockSpec(memory_space=pltpu.VMEM)
    smem = pl.BlockSpec(memory_space=pltpu.SMEM)
    outs = [
        ((half, width + 128), bf16),
        ((half, width), f32),
        ((half, 128), f32),
        ((half, 128), f32),
        ((8, 128), f32),
        ((rows, heads_width), bf16),
        ((pack, 2 * kv_width), bf16),
        ((-(-heads_width // HEAD_DIM // 8) * 8, rows), f32),
        ((rows, heads_width), bf16),
        ((rows, HEAD_DIM), f32),
        ((rows, HEAD_DIM), f32),
        ((owners * block, in_width), bf16),
        ((owners * block, out_width), bf16),
        ((4 * half, width), bf16),
        ((width, 4 * units), bf16),
        ((width, 4 * units), bf16),
        ((4 * units, width), bf16),
    ]
    return pl.pallas_call(
        functools.partial(forward_kernel, far, near, experts, rows * owners),
        name="forward",
        out_shape=tuple(jax.ShapeDtypeStruct(s, d) for s, d in outs),
        in_specs=[smem, smem, vmem, vmem] + [any_spec] * 9,
        out_specs=(vmem,) * 11 + (any_spec,) * 6,
        scratch_shapes=[
            pltpu.VMEM((owners * block, in_width), bf16),
            pltpu.VMEM((owners * block, out_width), bf16),
            pltpu.VMEM((rows, width), bf16),
            pltpu.VMEM((rows, in_width - 128), f32),
            pltpu.VMEM((half, width), f32),
            pltpu.VMEM((half, width), f32),
            pltpu.VMEM((4, 8, 128), f32),
            pltpu.VMEM((4, 8, 128), f32),
            pltpu.SemaphoreType.DMA((90,)),
            pltpu.SemaphoreType.DMA((90,)),
            pltpu.SemaphoreType.DMA((8,)),
        ],
        compiler_params=pltpu.CompilerParams(
            collective_id=0, has_side_effects=True, vmem_limit_bytes=56 * 1024 * 1024
        ),
    )(lengths, loss_grad, routes, tokens, small, w_query, w_key, w_value, out_block, out_grad, gate, up, down)


class RowReduce:
    def __init__(self, net, partial, inbox, part, order):
        self.net, self.partial, self.inbox, self.order = net, partial, inbox, order
        self.rows, self.first, self.size = part
        self.copies = {}

    def place(self, mask):
        fsdp, ctx = 0, 0
        for position, (axis, bit) in enumerate(self.order):
            if mask >> position & 1:
                fsdp, ctx = (fsdp ^ bit, ctx) if axis == "fsdp" else (fsdp, ctx ^ bit)
        index = (lax.axis_index("fsdp") ^ fsdp) * 2 + (lax.axis_index("ctx") ^ ctx)
        return pl.ds(pl.multiple_of(index * self.rows + self.first, 16), self.size)

    def box(self, mask):
        return pl.ds((mask - 1) * self.size, self.size)

    def step(self, mask):
        rows, last = self.place(mask), mask.bit_length() - 1
        if last + 1 < len(self.order):
            value = self.partial[rows, :].astype(f32)
            for later in range(last + 1, len(self.order)):
                source = mask | 1 << later
                self.net.arrive(self.copies[source])
                value = value + self.inbox[self.box(source), :].astype(f32)
            if mask == 0:
                return value
            self.partial[rows, :] = value.astype(bf16)
        self.copies[mask] = self.net.start(
            self.partial.at[rows], self.inbox.at[self.box(mask)], dim_peer(self.order[last])
        )

    def level(self, last):
        for mask in reversed(range(1 << last, 2 << last)):
            self.step(mask)


def backward_kernel(
    far, near, experts, group,
    lengths_ref, row_ref, dx_ref, middle_ref, probs_ref, mask_ref, grad_hbm,
    tokens_hbm, query_hbm, kv_hbm, lse_ref, attended_hbm, cos_ref, sin_ref,
    in_hbm, out_hbm, moe_hbm, gu_hbm, down_hbm,
    output_hbm, loss_ref, tokens_grad_hbm, in_ref, out_ref, extra_ref, gate_ref, up_ref, down_ref,
    grad_ref, tokens, query, kv, attended, in_full, out_full,
    out_in, att_grad, qkv_grad, kv_grad, kv_sent, kv_got,
    in_box, out_box,
    mid_grad, back_sent, back_got, tok_stage, extra_rows, extra_sent, extra_got,
    moe_own, moe_far, moe_near, moe_cross, moe_back,
    gate_own, gate_x, gate_sent, gate_s,
    up_own, up_s, up_sent, up_x,
    down_own, down_x, down_sent, down_s,
    loss_sent, loss_got,
    send_sems, recv_sems, local_sems,
):
    far_dev, near_dev, share_dev = peer(far), peer(near), peer(SHARE)
    ctx_dev, core_dev = peer(0, 1), peer(0, 0, 1)
    greet([far_dev, near_dev, share_dev, ctx_dev, core_dev])
    net = Exchange(send_sems, recv_sems, local_sems)
    ctx_place, core = lax.axis_index("ctx"), lax.axis_index("tp")
    half, width = middle_ref.shape
    rows = 2 * half
    quarter = half // 2
    own_rows = pl.ds(pl.multiple_of(core * half, 16), half)
    other_rows = pl.ds(pl.multiple_of((1 - core) * half, 16), half)
    halves = [pl.ds(k * quarter, quarter) for k in range(2)]

    far_rows = [pl.ds(2 * half + k * half, quarter) for k in range(2)]
    cross_rows = [pl.ds(2 * half + k * half + quarter, quarter) for k in range(2)]
    crossed = [net.start(moe_hbm.at[cross_rows[k]], moe_cross.at[halves[k]], near_dev) for k in range(2)]
    units = gu_hbm.shape[1] // 4
    wide = width // 2

    def wide_half(place):
        return pl.ds(pl.multiple_of(place * wide, 128), wide)

    gate_cols, up_own_cols, up_par_cols = pl.ds(0, 2 * units), pl.ds(2 * units, units), pl.ds(3 * units, units)
    gate_first = net.start(gu_hbm.at[wide_half(1 - ctx_place), gate_cols], gate_x, ctx_dev)
    up_first = net.start(gu_hbm.at[:, up_par_cols], up_s, share_dev)
    near_first = net.start(moe_hbm.at[pl.ds(half, half)], moe_near, near_dev)
    down_first = net.start(down_hbm.at[:, wide_half(1 - ctx_place)], down_x, ctx_dev)
    pairs = [
        (in_hbm, in_full), (out_hbm, out_full), (attended_hbm, attended), (query_hbm, query),
        (kv_hbm, kv), (tokens_hbm, tokens), (moe_hbm.at[pl.ds(0, half)], moe_own),
        (moe_hbm.at[far_rows[0]], moe_far.at[halves[0]]), (moe_hbm.at[far_rows[1]], moe_far.at[halves[1]]),
        (gu_hbm.at[wide_half(ctx_place), gate_cols], gate_own), (gu_hbm.at[:, up_own_cols], up_own),
        (down_hbm.at[:, wide_half(ctx_place)], down_own), (grad_hbm.at[own_rows], grad_ref),
    ]
    for src, dst in pairs:
        net.keep(src, dst)

    def loaded(*numbers):
        for number in numbers:
            net.settle(number)

    loaded(0, 12)
    flipped_extra = in_full[:, :128].astype(f32).T
    attn_gain, moe_gain = flipped_extra[experts : experts + 1], flipped_extra[experts + 1 : experts + 2]
    lane = lax.broadcasted_iota(jnp.int32, (half, 128), 1)
    probs, mask = probs_ref[...], mask_ref[...]
    pair = dx_ref[:, width:]
    gate_grad = jnp.where(lane < experts, pair + pltpu.roll(pair, 128 - experts, 1), 0.0)
    chosen = probs * mask
    chosen_total = jnp.sum(chosen, axis=1, keepdims=True)
    weighted = jnp.sum(gate_grad * chosen, axis=1, keepdims=True) / chosen_total
    prob_grad = mask * (gate_grad - weighted) / chosen_total + row_ref[0:1, :]
    logit_grad = probs * (prob_grad - jnp.sum(prob_grad * probs, axis=1, keepdims=True))
    logit_high = logit_grad.astype(bf16)
    logit_low = (logit_grad - logit_high.astype(f32)).astype(bf16)
    router = in_full[:, :128]
    step = quarter // 2
    gain_moe = jnp.zeros((1, width), f32)
    router_grad = jnp.zeros((128, width), f32)
    for k in range(half // step):
        at = slice(k * step, (k + 1) * step)
        middle = middle_ref[at, :]
        inverse = lax.rsqrt(jnp.mean(middle * middle, axis=1, keepdims=True) + epsilon)
        scaled = middle * inverse
        normed_moe = (scaled * moe_gain).astype(bf16)
        moe_grad = dx_ref[at, :width] + dot_nt(logit_high[at], router) + dot_nt(logit_low[at], router)
        router_grad += dot(logit_high[at], normed_moe, 0, 0) + dot(logit_low[at], normed_moe, 0, 0)
        gain_moe += jnp.sum(moe_grad * scaled, axis=0, keepdims=True)
        a = moe_grad * moe_gain
        grad = grad_ref[at, :].astype(f32) + inverse * (a - scaled * jnp.mean(a * scaled, axis=1, keepdims=True))
        mid_grad[at, :] = grad
        out_in[pl.ds(pl.multiple_of(core * half + k * step, 16), step), :] = grad.astype(bf16)
    out_in_copy = net.start(out_in.at[own_rows], out_in.at[own_rows], core_dev)
    row = lax.broadcasted_iota(jnp.int32, (128, width), 0)
    extra_rows[...] = jnp.where(row == experts + 1, gain_moe, router_grad)

    loss_dims = [core_dev, ctx_dev, near_dev, share_dev, far_dev]
    loss_state = [jnp.broadcast_to(jnp.sum(probs, axis=0, keepdims=True), (8, 128))]
    loss_copies = []

    def loss_step():
        k = len(loss_copies)
        if k > 0:
            net.arrive(loss_copies[-1])
            loss_state[0] = loss_state[0] + loss_got[k - 1]
        if k < len(loss_dims):
            loss_sent[k] = loss_state[0]
            loss_copies.append(net.start(loss_sent.at[k], loss_got.at[k], loss_dims[k]))

    loss_step()

    net.arrive(out_in_copy)
    loaded(1, 2)
    att_grad[...] = dot_nn(out_in[...], out_full[...]).astype(bf16)

    def out_tile(i, carry):
        cols = aligned(i, TILE)
        out_full[cols, :] = dot_nn(out_in[:, cols].T, attended[...]).astype(bf16)
        return carry

    lax.fori_loop(0, width // TILE, out_tile, 0)
    block = in_ref.shape[0]
    low, across = ("fsdp", near), ("ctx", 1)
    fars = [("fsdp", far), ("fsdp", SHARE)]
    orders = [fars + [across, low], fars + [low, across]]
    part_size = block // 2
    sums_out = [
        RowReduce(net, out_full, out_box.at[k], (block, k * part_size, part_size), orders[k]) for k in range(2)
    ]
    for s in sums_out:
        s.level(3)
    loss_step()
    net.sent(out_in_copy)
    loaded(5)
    normed_step = half // 2
    for k in range(rows // normed_step):
        at = slice(k * normed_step, (k + 1) * normed_step)
        x = tokens[at, :].astype(f32)
        inverse = lax.rsqrt(jnp.mean(x * x, axis=1, keepdims=True) + epsilon)
        out_in[at, :] = (x * inverse * attn_gain).astype(bf16)

    loaded(3, 4)
    pack = kv.shape[0]
    kv_grad[...] = jnp.zeros_like(kv_grad)
    keys, values = kv[:, :HEAD_DIM], kv[:, HEAD_DIM:]
    keys_flipped = keys.T
    query_number = lax.broadcasted_iota(jnp.int32, (1, half), 1) + ctx_place * rows
    key_number = lax.broadcasted_iota(jnp.int32, (pack, 1), 0)
    scale = HEAD_DIM ** (-0.5)

    def head_block(i, carry):
        head, block_index = i // 2, lax.rem(i, 2)
        cols = aligned(head, HEAD_DIM)
        at = aligned(block_index, half)
        number = query_number + block_index * half
        allowed = (key_number >= document_start(lengths_ref, number)) & (key_number <= number)
        q, grad = query[at, cols], att_grad[at, cols]
        log_total = lse_ref[pl.ds(head, 1), at]
        weights = jnp.where(allowed, jnp.exp(dot_nt(keys, q) * scale - log_total), 0.0)
        weight_grad = dot_nt(values, grad)
        delta = jnp.sum(weights * weight_grad, axis=0, keepdims=True)
        score_grad = (weights * (weight_grad - delta)).astype(bf16)
        kv_grad[:, :HEAD_DIM] += dot_nn(score_grad, q) * scale
        kv_grad[:, HEAD_DIM:] += dot_nn(weights.astype(bf16), grad)
        query_grad = (dot_nn(keys_flipped, score_grad) * scale).T
        turned = query_grad * cos_ref[at, :] - pltpu.roll(query_grad, HEAD_DIM // 2, 1) * sin_ref[at, :]
        qkv_grad[at, cols] = turned.astype(bf16)
        return carry

    third = 2 * group // 3
    lax.fori_loop(0, third, head_block, 0)
    loss_step()
    loaded(6, 7, 8)
    far_sums = []
    for k in range(2):
        net.arrive(crossed[k])
        moe_far[halves[k], :] = (moe_far[halves[k], :].astype(f32) + moe_cross[halves[k], :].astype(f32)).astype(bf16)
        far_sums.append(net.start(moe_far.at[halves[k]], moe_back.at[halves[k]], far_dev))
    for s in sums_out:
        s.level(2)
    lax.fori_loop(third, 2 * third, head_block, 0)
    loss_step()
    for s in sums_out:
        s.level(1)
    lax.fori_loop(2 * third, 2 * group, head_block, 0)
    loss_step()
    ctx_rows = pl.ds(pl.multiple_of(ctx_place * rows, 16), rows)
    ctx_other = pl.ds(pl.multiple_of((1 - ctx_place) * rows, 16), rows)
    kv_sent[...] = kv_grad[ctx_other, :].astype(bf16)
    kv_copy = net.start(kv_sent, kv_got, ctx_dev)
    for s in sums_out:
        s.level(0)
    loss_step()
    loss = jnp.sum(loss_state[0][0:1] * row_ref[1:2, :], axis=1, keepdims=True)
    loss_ref[...] = jnp.broadcast_to(loss, loss_ref.shape)
    net.arrive(kv_copy)
    kv_sum = kv_grad[ctx_rows, :] + kv_got[...].astype(f32)
    key_grad = kv_sum[:, :HEAD_DIM]
    key_grad = key_grad * cos_ref[...] - pltpu.roll(key_grad, HEAD_DIM // 2, 1) * sin_ref[...]
    heads_width = group * HEAD_DIM
    qkv_grad[:, heads_width : heads_width + HEAD_DIM] = key_grad.astype(bf16)
    qkv_grad[:, heads_width + HEAD_DIM :] = kv_sum[:, HEAD_DIM:].astype(bf16)

    gain_attn = jnp.zeros((1, width), f32)

    def attn_scaled(at):
        x = tokens[at, :].astype(f32)
        inverse = lax.rsqrt(jnp.mean(x * x, axis=1, keepdims=True) + epsilon)
        return inverse, x * inverse

    for k in range(2):
        at = other_rows if k == 0 else own_rows
        part = dot_nt(qkv_grad[at, :], in_full[:, 128:])
        gain_attn += jnp.sum(part * attn_scaled(at)[1], axis=0, keepdims=True)
        if k == 0:
            back_sent[...] = part.astype(bf16)
            back_copy = net.start(back_sent, back_got, core_dev)
        else:
            tok_stage[...] = part
    def in_tile(i, carry):
        cols = aligned(i, TILE)
        in_full[cols, 128:] = dot_nn(out_in[:, cols].T, qkv_grad[...]).astype(bf16)
        return carry

    lax.fori_loop(0, width // TILE, in_tile, 0)
    extra_rows[...] = jnp.where(row == experts, gain_attn, extra_rows[...])
    in_full[:, :128] = extra_rows[...].T.astype(bf16)
    sums_in = [
        RowReduce(net, in_full, in_box.at[k], (block, k * part_size, part_size), orders[k]) for k in range(2)
    ]
    for s in sums_in:
        s.level(3)

    net.arrive(back_copy)
    for k in range(2):
        at = pl.ds(k * quarter, quarter)
        inverse, scaled = attn_scaled(pl.ds(pl.multiple_of(core * half + k * quarter, 16), quarter))
        a = (tok_stage[at, :] + back_got[at, :].astype(f32)) * attn_gain
        tok_stage[at, :] = mid_grad[at, :] + inverse * (a - scaled * jnp.mean(a * scaled, axis=1, keepdims=True))
    net.keep(tok_stage, tokens_grad_hbm.at[own_rows])
    net.start(tok_stage, tokens_grad_hbm.at[own_rows], core_dev)

    def pieces(size):
        return [slice(k * size // 4, (k + 1) * size // 4) for k in range(4)]

    loaded(9, 10, 11)
    net.arrive(gate_first)
    for at in pieces(wide):
        total = gate_own[at, :].astype(f32) + gate_x[at, :].astype(f32)
        gate_ref[at, :] = total[:, :units]
        gate_sent[at, :] = total[:, units:].astype(bf16)
    gate_last = net.start(gate_sent, gate_s, share_dev)
    for s in sums_in:
        s.level(2)
    net.arrive(up_first)
    up_sent[...] = (up_own[wide_half(1 - ctx_place), :].astype(f32) + up_s[wide_half(1 - ctx_place), :].astype(f32)).astype(bf16)
    up_last = net.start(up_sent, up_x, ctx_dev)
    up_ref[...] = up_own[wide_half(ctx_place), :].astype(f32) + up_s[wide_half(ctx_place), :].astype(f32)
    for s in sums_in:
        s.level(1)
    net.arrive(down_first)
    for at in pieces(units):
        down_ref[at, :] = down_own[at, :].astype(f32) + down_x[at, :].astype(f32)
        after = slice(at.start + units, at.stop + units)
        down_sent[at, :] = (down_own[after, :].astype(f32) + down_x[after, :].astype(f32)).astype(bf16)
    down_last = net.start(down_sent, down_s, share_dev)
    for s in sums_in:
        s.level(0)

    net.arrive(near_first)
    for k in range(2):
        net.arrive(far_sums[k])
    for k in range(2):
        at = halves[k]
        moe_out = moe_own[at, :].astype(f32) + moe_near[at, :].astype(f32) + moe_back[at, :].astype(f32)
        moe_own[at, :] = (middle_ref[at, :] + moe_out).astype(bf16)
    net.keep(moe_own, output_hbm.at[own_rows])
    net.start(moe_own, output_hbm.at[own_rows], core_dev)

    for k in range(2):
        at = slice(k * part_size, (k + 1) * part_size)
        out_ref[at, :] = sums_out[k].step(0)
        value = sums_in[k].step(0)
        extra_sent[at, :] = value[:, :128]
        in_ref[at, :] = value[:, 128:]
    extra_copy = net.start(extra_sent, extra_got, core_dev)
    net.arrive(gate_last)
    gate_ref[...] += gate_s[...].astype(f32)
    net.arrive(up_last)
    up_ref[...] += up_x[...].astype(f32)
    net.arrive(down_last)
    down_ref[...] += down_s[...].astype(f32)
    net.arrive(extra_copy)
    extra_ref[...] = extra_sent[...] + extra_got[...]
    net.finish()


def backward_on_chip(
    lengths, row, dx, middle, probs, mask, out_grad, tokens, query, kv, lse, attended, cos, sin,
    in_full, out_full, moe_rows, gate_up, down, experts,
):
    far, near = token_bits()
    owners = lax.axis_size("fsdp") * lax.axis_size("ctx")
    half, width = middle.shape
    rows, heads_width = query.shape
    pack, kv_width = kv.shape
    units = down.shape[0] // 2
    block = in_full.shape[0] // owners
    in_width, out_width = in_full.shape[1], out_full.shape[1]
    any_spec = pl.BlockSpec(memory_space=pl.ANY)
    vmem = pl.BlockSpec(memory_space=pltpu.VMEM)
    smem = pl.BlockSpec(memory_space=pltpu.SMEM)

    def low(*shape):
        return pltpu.VMEM(shape, bf16)

    def wide(*shape):
        return pltpu.VMEM(shape, f32)

    boxes = 15 * (block // 2)
    return pl.pallas_call(
        functools.partial(backward_kernel, far, near, experts, heads_width // HEAD_DIM),
        name="backward",
        out_shape=(
            jax.ShapeDtypeStruct((rows, width), bf16),
            jax.ShapeDtypeStruct((8, 128), f32),
            jax.ShapeDtypeStruct((rows, width), f32),
            jax.ShapeDtypeStruct((block, in_width - 128), f32),
            jax.ShapeDtypeStruct((block, out_width), f32),
            jax.ShapeDtypeStruct((block, 128), f32),
            jax.ShapeDtypeStruct((width // 2, units), f32),
            jax.ShapeDtypeStruct((width // 2, units), f32),
            jax.ShapeDtypeStruct((units, width // 2), f32),
        ),
        in_specs=[smem] + [vmem] * 5 + [any_spec] * 4 + [vmem, any_spec, vmem, vmem] + [any_spec] * 5,
        out_specs=(any_spec, vmem, any_spec) + (vmem,) * 6,
        scratch_shapes=[
            low(half, width), low(rows, width), low(rows, heads_width), low(pack, kv_width), low(rows, heads_width),
            low(*in_full.shape), low(*out_full.shape),
            low(rows, width), low(rows, heads_width), low(rows, in_width - 128),
            wide(pack, kv_width), low(rows, kv_width), low(rows, kv_width),
            low(2, boxes, in_width), low(2, boxes, out_width),
            wide(half, width), low(half, width), low(half, width), wide(half, width),
            wide(128, width), wide(block, 128), wide(block, 128),
            low(half, width), low(half, width), low(half, width), low(half, width), low(half, width),
            low(width // 2, 2 * units), low(width // 2, 2 * units), low(width // 2, units), low(width // 2, units),
            low(width, units), low(width, units), low(width // 2, units), low(width // 2, units),
            low(2 * units, width // 2), low(2 * units, width // 2), low(units, width // 2), low(units, width // 2),
            wide(5, 8, 128), wide(5, 8, 128),
            pltpu.SemaphoreType.DMA((90,)),
            pltpu.SemaphoreType.DMA((90,)),
            pltpu.SemaphoreType.DMA((16,)),
        ],
        compiler_params=pltpu.CompilerParams(
            collective_id=2, has_side_effects=True, vmem_limit_bytes=62 * 1024 * 1024
        ),
    )(
        lengths, row, dx, middle, probs, mask, out_grad, tokens, query, kv, lse, attended, cos, sin,
        in_full, out_full, moe_rows, gate_up, down,
    )


def rms_back_gain(inverse, scaled, row_gains, upstream):
    return jnp.sum(upstream * scaled, axis=0), rms_back(inverse, scaled, row_gains, upstream)


def to_expert(arrived, local_experts, capacity):
    sources = arrived.shape[0]
    return (
        arrived.reshape(sources, local_experts, capacity, -1)
        .transpose(1, 0, 2, 3)
        .reshape(local_experts, sources * capacity, -1)
    )


def from_expert(expert_rows, sources, capacity):
    local_experts = expert_rows.shape[0]
    return (
        expert_rows.reshape(local_experts, sources, capacity, -1)
        .transpose(1, 0, 2, 3)
        .reshape(sources, local_experts * capacity, -1)
    )


def expert_forward(expert_rows, w_gate, w_up):
    gate_pre = jnp.einsum("erd,edf->erf", expert_rows, w_gate, preferred_element_type=jnp.float32)
    up_pre = jnp.einsum("erd,edf->erf", expert_rows, w_up, preferred_element_type=jnp.float32)
    hidden = (gate_pre * jax.nn.sigmoid(gate_pre) * up_pre).astype(jnp.bfloat16)
    return (gate_pre, up_pre, hidden)


def on_any_slice(
    tokens,
    lengths,
    routes,
    norm_attn,
    w_query,
    w_key,
    w_value,
    w_out,
    norm_moe,
    w_router,
    w_gate,
    w_up,
    w_down,
    out_grad,
    loss_grad,
):
    row_count, model_width = tokens.shape
    ctx_count = lax.axis_size("ctx")
    fsdp_count = lax.axis_size("fsdp")
    ctx_place = lax.axis_index("ctx")
    top_count = routes.shape[1]
    expert_count = w_router.shape[1]
    local_experts = w_gate.shape[0]
    capacity = 3 * row_count * top_count // (2 * expert_count)
    pack_count = row_count * ctx_count
    block_rows = min(512, row_count)
    base_row = ctx_place * row_count
    gain_attn, full_query, full_key, full_value, full_out, gain_moe, full_router = (
        lax.all_gather(norm_attn, ("fsdp", "ctx"), axis=0, tiled=True),
        lax.all_gather(w_query, ("fsdp", "ctx"), axis=0, tiled=True),
        lax.all_gather(w_key, ("fsdp", "ctx"), axis=0, tiled=True),
        lax.all_gather(w_value, ("fsdp", "ctx"), axis=0, tiled=True),
        lax.all_gather(w_out, ("fsdp", "ctx"), axis=1, tiled=True),
        lax.all_gather(norm_moe, ("fsdp", "ctx"), axis=0, tiled=True),
        lax.all_gather(w_router, ("fsdp", "ctx"), axis=0, tiled=True),
    )
    doc_ids, positions, doc_first = pack_layout(lengths[0], pack_count)
    own_positions = lax.dynamic_slice_in_dim(positions, base_row, row_count, 0)
    cos_table, sin_table = rope_tables(own_positions)
    x_float = tokens.astype(jnp.float32)
    attn_gain = gain_attn.astype(jnp.float32)
    inverse_attn, scaled_attn, normed_full = rms_parts(x_float, attn_gain)
    normed_attn = normed_full.astype(jnp.bfloat16)
    local_heads = full_query.shape[1] // HEAD_DIM
    local_kv = full_key.shape[1] // HEAD_DIM
    group_size = local_heads // local_kv
    query_raw = jnp.dot(normed_attn, full_query, preferred_element_type=jnp.float32).reshape(
        row_count, local_heads, HEAD_DIM
    )
    queries = rotate(query_raw, cos_table, sin_table).astype(jnp.bfloat16)
    key_raw = jnp.dot(normed_attn, full_key, preferred_element_type=jnp.float32).reshape(
        row_count, local_kv, HEAD_DIM
    )
    key_own = rotate(key_raw, cos_table, sin_table).astype(jnp.bfloat16)
    value_own = (
        jnp.dot(normed_attn, full_value, preferred_element_type=jnp.float32)
        .astype(jnp.bfloat16)
        .reshape(row_count, local_kv, HEAD_DIM)
    )
    pack_keys, pack_values = (
        lax.all_gather(key_own, "ctx", axis=0, tiled=True),
        lax.all_gather(value_own, "ctx", axis=0, tiled=True),
    )
    grouped = queries.reshape(row_count, local_kv, group_size, HEAD_DIM)
    mixed_full, log_total = attention_forward(
        grouped, pack_keys, pack_values, doc_ids, doc_first, base_row, block_rows
    )
    attended = mixed_full.astype(jnp.bfloat16)
    out_part = jnp.dot(attended, full_out, preferred_element_type=jnp.float32)
    attn_out = lax.psum(out_part, "tp")
    middle = x_float + attn_out
    moe_gain = gain_moe.astype(jnp.float32)
    inverse_moe, scaled_moe, normed_mid = rms_parts(middle, moe_gain)
    normed_moe = normed_mid.astype(jnp.bfloat16)
    logits = jnp.dot(normed_moe, full_router, preferred_element_type=jnp.float32)
    shifted = jnp.exp(logits - jnp.max(logits, axis=-1, keepdims=True))
    router_probs = shifted / jnp.sum(shifted, axis=-1, keepdims=True)
    expert_ids = jnp.arange(expert_count, dtype=jnp.int32)
    route_mask = (routes[:, :, None] == expert_ids[None, None, :]).astype(jnp.float32)
    chosen = jnp.sum(route_mask * router_probs[:, None, :], axis=-1)
    chosen_total = jnp.sum(chosen, axis=-1, keepdims=True)
    gate_weights = chosen / chosen_total
    counts_global, probs_global = lax.psum(
        (jnp.sum(route_mask, axis=(0, 1)), jnp.sum(router_probs, axis=0)), ("fsdp", "ctx")
    )
    token_total = pack_count * fsdp_count
    fraction = counts_global / (token_total * top_count)
    balance_loss = (expert_count * jnp.sum(fraction * (probs_global / token_total))).reshape(1)
    flat_routes = routes.reshape(-1)
    flat_mask = (flat_routes[:, None] == expert_ids[None, :]).astype(jnp.int32)
    slot_rank = jnp.sum(jnp.cumsum(flat_mask, axis=0) * flat_mask, axis=1) - 1
    slot_index = flat_routes * capacity + slot_rank
    buffer_rows = expert_count * capacity
    send_rows = (
        jnp.zeros((buffer_rows, model_width), jnp.bfloat16)
        .at[slot_index]
        .set(jnp.repeat(normed_moe, top_count, axis=0))
    )
    send_rows = send_rows.reshape(fsdp_count, local_experts * capacity, model_width)
    arrived = lax.all_to_all(send_rows, "fsdp", split_axis=0, concat_axis=0, tiled=True)
    expert_rows = to_expert(arrived, local_experts, capacity)
    gate_pre, up_pre, hidden = expert_forward(expert_rows, w_gate, w_up)
    expert_out = jnp.einsum(
        "erf,efd->erd", hidden, w_down, preferred_element_type=jnp.float32
    ).astype(jnp.bfloat16)
    returned = lax.all_to_all(
        from_expert(expert_out, fsdp_count, capacity),
        "fsdp",
        split_axis=0,
        concat_axis=0,
        tiled=True,
    )
    slot_values = returned.reshape(buffer_rows, model_width)[slot_index].reshape(
        row_count, top_count, model_width
    )
    moe_part = jnp.sum(gate_weights[:, :, None] * slot_values, axis=1)
    moe_out = lax.psum(moe_part.astype(jnp.bfloat16), "tp").astype(jnp.float32)
    output = (middle + moe_out).astype(jnp.bfloat16)
    upstream = out_grad.astype(jnp.float32)
    gate_dots = jnp.sum(slot_values * upstream[:, None, :], axis=-1)
    grad_slots = (
        (gate_weights[:, :, None] * upstream[:, None, :])
        .astype(jnp.bfloat16)
        .reshape(row_count * top_count, model_width)
    )
    grad_send = jnp.zeros((buffer_rows, model_width), jnp.bfloat16).at[slot_index].set(grad_slots)
    grad_send = grad_send.reshape(fsdp_count, local_experts * capacity, model_width)
    grad_arrived = lax.all_to_all(grad_send, "fsdp", split_axis=0, concat_axis=0, tiled=True)
    kept_gate, kept_up, kept_hidden = (gate_pre, up_pre, hidden)
    grad_expert = to_expert(grad_arrived, local_experts, capacity)
    grad_hidden = jnp.einsum(
        "erd,efd->erf", grad_expert, w_down, preferred_element_type=jnp.float32
    )
    down_grad = jnp.einsum(
        "erf,erd->efd", kept_hidden, grad_expert, preferred_element_type=jnp.float32
    )
    sigmoid_gate = jax.nn.sigmoid(kept_gate)
    grad_gate = (
        grad_hidden * kept_up * sigmoid_gate * (1.0 + kept_gate * (1.0 - sigmoid_gate))
    ).astype(jnp.bfloat16)
    grad_up = (grad_hidden * kept_gate * sigmoid_gate).astype(jnp.bfloat16)
    gate_grad_w = jnp.einsum(
        "erd,erf->edf", expert_rows, grad_gate, preferred_element_type=jnp.float32
    )
    up_grad_w = jnp.einsum("erd,erf->edf", expert_rows, grad_up, preferred_element_type=jnp.float32)
    grad_rows = jnp.einsum("erf,edf->erd", grad_gate, w_gate, preferred_element_type=jnp.float32)
    grad_rows = (
        grad_rows + jnp.einsum("erf,edf->erd", grad_up, w_up, preferred_element_type=jnp.float32)
    ).astype(jnp.bfloat16)
    grad_back = lax.all_to_all(
        from_expert(grad_rows, fsdp_count, capacity),
        "fsdp",
        split_axis=0,
        concat_axis=0,
        tiled=True,
    )
    grad_slot_rows = grad_back.reshape(buffer_rows, model_width)[slot_index].reshape(
        row_count, top_count, model_width
    )
    moe_in_part = jnp.sum(grad_slot_rows.astype(jnp.float32), axis=1)
    moe_in_grad, gate_grad = lax.psum((moe_in_part, gate_dots), "tp")
    weighted = jnp.sum(gate_grad * gate_weights, axis=-1, keepdims=True)
    chosen_grad = (gate_grad - weighted) / chosen_total
    prob_grad = (
        jnp.sum(route_mask * chosen_grad[:, :, None], axis=1)
        + loss_grad[0] * expert_count * fraction / token_total
    )
    logit_grad = router_probs * (
        prob_grad - jnp.sum(prob_grad * router_probs, axis=-1, keepdims=True)
    )
    router_grad = jnp.einsum(
        "td,te->de", normed_moe.astype(jnp.float32), logit_grad, precision=highest
    )
    moe_grad = moe_in_grad + jnp.einsum(
        "te,de->td", logit_grad, full_router.astype(jnp.float32), precision=highest
    )
    gain_moe_grad, middle_norm_grad = rms_back_gain(inverse_moe, scaled_moe, moe_gain, moe_grad)
    middle_grad = upstream + middle_norm_grad
    out_in = middle_grad.astype(jnp.bfloat16)
    out_w_grad = jnp.einsum("tq,td->qd", attended, out_in, preferred_element_type=jnp.float32)
    mixed_grad = jnp.einsum(
        "td,qd->tq", out_in, full_out, preferred_element_type=jnp.float32
    ).astype(jnp.bfloat16)
    query_acc, key_grad_pack, value_grad_pack = attention_backward(
        grouped,
        pack_keys,
        pack_values,
        mixed_grad,
        log_total,
        doc_ids,
        doc_first,
        base_row,
        block_rows,
    )
    key_grad, value_grad, gate_w_out, up_w_out, down_w_out = (
        lax.psum_scatter(key_grad_pack, "ctx", scatter_dimension=0, tiled=True),
        lax.psum_scatter(value_grad_pack, "ctx", scatter_dimension=0, tiled=True),
        lax.psum_scatter(gate_grad_w, "ctx", scatter_dimension=1, tiled=True),
        lax.psum_scatter(up_grad_w, "ctx", scatter_dimension=1, tiled=True),
        lax.psum_scatter(down_grad, "ctx", scatter_dimension=2, tiled=True),
    )
    query_grad = (
        rotate(query_acc.reshape(row_count, local_heads, HEAD_DIM), cos_table, -sin_table)
        .astype(jnp.bfloat16)
        .reshape(row_count, local_heads * HEAD_DIM)
    )
    key_grad_low = (
        rotate(key_grad, cos_table, -sin_table)
        .astype(jnp.bfloat16)
        .reshape(row_count, local_kv * HEAD_DIM)
    )
    value_grad_low = value_grad.astype(jnp.bfloat16).reshape(row_count, local_kv * HEAD_DIM)
    query_w_grad = jnp.einsum(
        "td,tq->dq", normed_attn, query_grad, preferred_element_type=jnp.float32
    )
    key_w_grad = jnp.einsum(
        "td,tq->dq", normed_attn, key_grad_low, preferred_element_type=jnp.float32
    )
    value_w_grad = jnp.einsum(
        "td,tq->dq", normed_attn, value_grad_low, preferred_element_type=jnp.float32
    )
    attn_in_part = jnp.einsum(
        "tq,dq->td", query_grad, full_query, preferred_element_type=jnp.float32
    )
    attn_in_part = attn_in_part + jnp.einsum(
        "tq,dq->td", key_grad_low, full_key, preferred_element_type=jnp.float32
    )
    attn_in_part = attn_in_part + jnp.einsum(
        "tq,dq->td", value_grad_low, full_value, preferred_element_type=jnp.float32
    )
    attn_in_grad = lax.psum(attn_in_part.astype(jnp.bfloat16), "tp").astype(jnp.float32)
    gain_attn_grad, input_norm_grad = rms_back_gain(inverse_attn, scaled_attn, attn_gain, attn_in_grad)
    tokens_grad = middle_grad + input_norm_grad
    shard_grads = (
        lax.psum_scatter(gain_attn_grad, ("fsdp", "ctx"), scatter_dimension=0, tiled=True),
        lax.psum_scatter(query_w_grad, ("fsdp", "ctx"), scatter_dimension=0, tiled=True),
        lax.psum_scatter(key_w_grad, ("fsdp", "ctx"), scatter_dimension=0, tiled=True),
        lax.psum_scatter(value_w_grad, ("fsdp", "ctx"), scatter_dimension=0, tiled=True),
        lax.psum_scatter(out_w_grad, ("fsdp", "ctx"), scatter_dimension=1, tiled=True),
        lax.psum_scatter(gain_moe_grad, ("fsdp", "ctx"), scatter_dimension=0, tiled=True),
        lax.psum_scatter(router_grad, ("fsdp", "ctx"), scatter_dimension=0, tiled=True),
    )
    return (
        output,
        balance_loss,
        tokens_grad,
        shard_grads[0],
        shard_grads[1],
        shard_grads[2],
        shard_grads[3],
        shard_grads[4],
        shard_grads[5],
        shard_grads[6],
        gate_w_out,
        up_w_out,
        down_w_out,
    )


def on_device(
    tokens,
    lengths,
    routes,
    norm_attn,
    w_query,
    w_key,
    w_value,
    w_out,
    norm_moe,
    w_router,
    w_gate,
    w_up,
    w_down,
    out_grad,
    loss_grad,
):
    expert_count = w_router.shape[1]
    if lax.axis_size("fsdp") != 8:
        return on_any_slice(
            tokens, lengths, routes, norm_attn, w_query, w_key, w_value, w_out, norm_moe, w_router,
            w_gate, w_up, w_down, out_grad, loss_grad,
        )
    small = widen([w_router, norm_attn[:, None], norm_moe[:, None]])
    query_width, kv_width = w_query.shape[1], w_key.shape[1]
    (
        payload, middle, probs, mask, row, query, kv_pack, lse, attended, cos, sin,
        in_weights, out_weights, grad_rows, gate_all, up_all, down_all,
    ) = forward_on_chip(
        lengths, loss_grad, routes, tokens, small, w_query, w_key, w_value, w_out.T, out_grad,
        w_gate[0], w_up[0], w_down[0], expert_count,
    )
    returned, moe_rows, keep_gu, got_gu, keep_d, got_d = experts_on_chip(
        payload, out_grad, w_gate[0], w_up[0], w_down[0], grad_rows, gate_all, up_all, down_all, expert_count
    )
    gate_up_grad = (keep_gu.astype(f32) + got_gu.astype(f32)).astype(bf16)
    down_grad = (keep_d.astype(f32) + got_d.astype(f32)).astype(bf16)
    output, loss, tokens_grad, in_reduced, out_reduced, small, gate_w_out, up_w_out, down_w_out = backward_on_chip(
        lengths, row, returned, middle, probs, mask, out_grad, tokens, query, kv_pack, lse, attended, cos, sin,
        in_weights, out_weights, moe_rows, gate_up_grad, down_grad, expert_count,
    )
    return (
        output,
        loss[0, :1],
        tokens_grad,
        small[:, expert_count],
        in_reduced[:, :query_width],
        in_reduced[:, query_width : query_width + kv_width],
        in_reduced[:, query_width + kv_width :],
        out_reduced.T,
        small[:, expert_count + 1],
        small[:, :expert_count],
        gate_w_out[None],
        up_w_out[None],
        down_w_out[None],
    )


def solution(mesh):
    rows = P(("fsdp", "ctx"), None)
    gain = P(("fsdp", "ctx"))
    split = P(("fsdp", "ctx"), "tp")
    out_split = P("tp", ("fsdp", "ctx"))
    columns = P("fsdp", None, "tp")
    return jax.shard_map(
        on_device,
        mesh=mesh,
        in_specs=(
            rows,
            P("fsdp", None),
            rows,
            gain,
            split,
            split,
            split,
            out_split,
            gain,
            rows,
            columns,
            columns,
            P("fsdp", "tp", None),
            rows,
            P(),
        ),
        out_specs=(
            rows,
            P(),
            rows,
            gain,
            split,
            split,
            split,
            out_split,
            gain,
            rows,
            P("fsdp", "ctx", "tp"),
            P("fsdp", "ctx", "tp"),
            P("fsdp", "tp", "ctx"),
        ),
        check_vma=False,
    )
```

```python
import functools
import math

import jax
import jax.experimental.pallas as pl
import jax.experimental.pallas.tpu as pltpu
import jax.numpy as jnp
from jax import lax
from jax.sharding import PartitionSpec as P

HEAD_DIM = 128
SHARE = 2
epsilon = 1e-06
rope_base = 10000.0
masked_score = -1e30
highest = lax.Precision.HIGHEST
f32 = jnp.float32
bf16 = jnp.bfloat16


def rms_parts(values, row_gains):
    inverse = lax.rsqrt(jnp.mean(values * values, axis=-1, keepdims=True) + epsilon)
    scaled = values * inverse
    return (inverse, scaled, scaled * row_gains)


def rms_back(inverse, scaled, row_gains, upstream):
    scaled_grad = upstream * row_gains
    return inverse * (scaled_grad - scaled * jnp.mean(scaled_grad * scaled, axis=-1, keepdims=True))


def rope_tables(positions):
    half_dim = HEAD_DIM // 2
    frequency = rope_base ** (-(jnp.arange(half_dim, dtype=f32) * (2.0 / HEAD_DIM)))
    angles = positions.astype(f32)[:, None] * frequency[None, :]
    return (jnp.cos(angles)[:, None, :], jnp.sin(angles)[:, None, :])


def rotate(vectors, cos_table, sin_table):
    half_dim = vectors.shape[-1] // 2
    first_half = vectors[..., :half_dim]
    second_half = vectors[..., half_dim:]
    return jnp.concatenate(
        [
            first_half * cos_table - second_half * sin_table,
            second_half * cos_table + first_half * sin_table,
        ],
        axis=-1,
    )


def pack_layout(length_row, row_count):
    doc_ends = jnp.cumsum(length_row)
    doc_starts = doc_ends - length_row
    row_index = jnp.arange(row_count, dtype=jnp.int32)
    doc_ids = jnp.sum((row_index[:, None] >= doc_ends[None, :]).astype(jnp.int32), axis=1)
    doc_numbers = jnp.arange(length_row.shape[0], dtype=jnp.int32)
    doc_first = jnp.sum(
        jnp.where(doc_ids[:, None] == doc_numbers[None, :], doc_starts[None, :], 0), axis=1
    )
    return (doc_ids, row_index - doc_first, doc_first)


def key_block_data(key_number, block_rows, pack_keys, pack_values, doc_ids):
    key_start = key_number * block_rows
    key_block = lax.dynamic_slice_in_dim(pack_keys, key_start, block_rows, 0)
    value_block = lax.dynamic_slice_in_dim(pack_values, key_start, block_rows, 0)
    key_docs = lax.dynamic_slice_in_dim(doc_ids, key_start, block_rows, 0)
    key_index = key_start + jnp.arange(block_rows, dtype=jnp.int32)
    return (key_start, key_block, value_block, key_docs, key_index)


def block_scores(query_block, key_block, query_docs, query_index, key_docs, key_index):
    scale_factor = HEAD_DIM ** (-0.5)
    scores = (
        jnp.einsum("qhgd,khd->hgqk", query_block, key_block, preferred_element_type=f32)
        * scale_factor
    )
    allowed = (query_docs[:, None] == key_docs[None, :]) & (
        key_index[None, :] <= query_index[:, None]
    )
    return (scores, allowed)


def query_block_range(start_row, block_rows, doc_ids, doc_first):
    query_index = start_row + jnp.arange(block_rows, dtype=jnp.int32)
    query_docs = lax.dynamic_slice_in_dim(doc_ids, start_row, block_rows, 0)
    low_block = doc_first[start_row] // block_rows
    high_block = (start_row + block_rows - 1) // block_rows + 1
    return (query_index, query_docs, low_block, high_block)


def attention_forward(grouped, pack_keys, pack_values, doc_ids, doc_first, base_row, block_rows):
    row_count, local_kv, group_size, head_dim = grouped.shape
    query_index, query_docs, low_block, high_block = query_block_range(
        base_row, block_rows, doc_ids, doc_first
    )

    def scan_maxima(key_number, running):
        maxima, totals = running
        key_start, key_block, value_block, key_docs, key_index = key_block_data(
            key_number, block_rows, pack_keys, pack_values, doc_ids
        )
        scores, allowed = block_scores(
            grouped, key_block, query_docs, query_index, key_docs, key_index
        )
        new_max = jnp.maximum(maxima, jnp.max(jnp.where(allowed, scores, masked_score), axis=-1))
        weights = jnp.where(allowed, jnp.exp(scores - new_max[..., None]), 0.0)
        return (new_max, totals * jnp.exp(maxima - new_max) + jnp.sum(weights, axis=-1))

    start_max = jnp.full((local_kv, group_size, block_rows), masked_score, f32)
    start_total = jnp.zeros((local_kv, group_size, block_rows), f32)
    maxima, totals = lax.fori_loop(low_block, high_block, scan_maxima, (start_max, start_total))
    log_total = maxima + jnp.log(totals)

    def accumulate(key_number, summed):
        key_start, key_block, value_block, key_docs, key_index = key_block_data(
            key_number, block_rows, pack_keys, pack_values, doc_ids
        )
        scores, allowed = block_scores(
            grouped, key_block, query_docs, query_index, key_docs, key_index
        )
        block_probs = jnp.where(allowed, jnp.exp(scores - log_total[..., None]), 0.0).astype(bf16)
        return summed + jnp.einsum(
            "hgqk,khd->hgqd", block_probs, value_block, preferred_element_type=f32
        )

    summed = lax.fori_loop(
        low_block,
        high_block,
        accumulate,
        jnp.zeros((local_kv, group_size, block_rows, head_dim), f32),
    )
    outputs = summed.transpose(2, 0, 1, 3).reshape(block_rows, local_kv * group_size * head_dim)
    return (outputs, log_total)


def attention_backward(
    grouped, pack_keys, pack_values, grad_mixed, log_total, doc_ids, doc_first, base_row, block_rows
):
    row_count, local_kv, group_size, head_dim = grouped.shape
    pack_count = pack_keys.shape[0]
    scale_factor = HEAD_DIM ** (-0.5)
    grad_grouped = grad_mixed.reshape(row_count, local_kv, group_size, head_dim)
    key_acc = jnp.zeros((pack_count, local_kv, head_dim), f32)
    value_acc = jnp.zeros((pack_count, local_kv, head_dim), f32)
    query_index, query_docs, low_block, high_block = query_block_range(
        base_row, block_rows, doc_ids, doc_first
    )

    def probs_at(key_number):
        key_start, key_block, value_block, key_docs, key_index = key_block_data(
            key_number, block_rows, pack_keys, pack_values, doc_ids
        )
        scores, allowed = block_scores(
            grouped, key_block, query_docs, query_index, key_docs, key_index
        )
        block_probs = jnp.where(allowed, jnp.exp(scores - log_total[..., None]), 0.0)
        prob_grad = jnp.einsum(
            "qhgd,khd->hgqk", grad_grouped, value_block, preferred_element_type=f32
        )
        return (key_start, key_block, block_probs, prob_grad)

    def add_delta(key_number, row_delta):
        pieces = probs_at(key_number)
        return row_delta + jnp.sum(pieces[2] * pieces[3], axis=-1)

    row_delta = lax.fori_loop(
        low_block, high_block, add_delta, jnp.zeros((local_kv, group_size, block_rows), f32)
    )

    def add_grads(key_number, running):
        query_acc, key_total, value_total = running
        key_start, key_block, block_probs, prob_grad = probs_at(key_number)
        score_grad = (block_probs * (prob_grad - row_delta[..., None])).astype(bf16)
        query_acc = (
            query_acc
            + jnp.einsum("hgqk,khd->qhgd", score_grad, key_block, preferred_element_type=f32)
            * scale_factor
        )
        key_piece = (
            jnp.einsum("hgqk,qhgd->khd", score_grad, grouped, preferred_element_type=f32)
            * scale_factor
        )
        value_piece = jnp.einsum(
            "hgqk,qhgd->khd", block_probs.astype(bf16), grad_grouped, preferred_element_type=f32
        )
        key_total = lax.dynamic_update_slice_in_dim(
            key_total,
            lax.dynamic_slice_in_dim(key_total, key_start, block_rows, 0) + key_piece,
            key_start,
            0,
        )
        value_total = lax.dynamic_update_slice_in_dim(
            value_total,
            lax.dynamic_slice_in_dim(value_total, key_start, block_rows, 0) + value_piece,
            key_start,
            0,
        )
        return (query_acc, key_total, value_total)

    start_query = jnp.zeros((block_rows, local_kv, group_size, head_dim), f32)
    return lax.fori_loop(low_block, high_block, add_grads, (start_query, key_acc, value_acc))


def dot(left, right, left_dim=1, right_dim=0):
    return lax.dot_general(
        left, right, (((left_dim,), (right_dim,)), ((), ())), preferred_element_type=f32
    )


def swap(array, axis, bit=1):
    return lax.ppermute(array, axis, [(i, i ^ bit) for i in range(lax.axis_size(axis))])


def bit_at(axis, bit):
    return (lax.axis_index(axis) // bit) % 2


def side_by_side(mine, theirs, place, axis=0):
    first = jnp.where(place == 0, mine, theirs)
    return jnp.concatenate([first, jnp.where(place == 0, theirs, mine)], axis=axis)


def fsdp_bits():
    size = lax.axis_size("fsdp")
    return [size >> (k + 1) for k in range(size.bit_length() - 1)]


def weight_dims():
    return [("fsdp", bit) for bit in fsdp_bits()] + [("ctx", 1)]


def weight_orders():
    high = [("fsdp", bit) for bit in fsdp_bits()[:-1]]
    low, across = ("fsdp", 1), ("ctx", 1)
    return [high + [across, low], [across, low] + high, [low] + high + [across]]


def gather_rows(block, order):
    dims = weight_dims()
    held = block.reshape((1,) * len(dims) + block.shape)
    for dim in order:
        held = side_by_side(held, swap(held, *dim), bit_at(*dim), dims.index(dim))
    return held.reshape(-1, block.shape[-1])


def reduce_rows(full, order):
    dims = weight_dims()
    rows = full.shape[0] >> len(dims)
    held = full.reshape((2,) * len(dims) + (rows, full.shape[-1]))
    for dim in reversed(order):
        place, k = bit_at(*dim), dims.index(dim)
        sent = lax.dynamic_index_in_dim(held, 1 - place, k).astype(bf16)
        held = lax.dynamic_index_in_dim(held, place, k) + swap(sent, *dim).astype(f32)
    return held.reshape(rows, full.shape[-1])


def thirds(array, pieces):
    units = array.shape[-1] // 128
    ends = [units * k // pieces * 128 for k in range(pieces + 1)]
    return [array[..., a:b] for a, b in zip(ends[:-1], ends[1:])]


def gather_weights(block, orders):
    parts = thirds(block, len(orders))
    return jnp.concatenate([gather_rows(p, o) for p, o in zip(parts, orders)], axis=1)


def reduce_weights(full, orders):
    parts = thirds(full, len(orders))
    return jnp.concatenate([reduce_rows(p, o) for p, o in zip(parts, orders)], axis=1)


def token_bits():
    return [bit for bit in fsdp_bits() if bit != SHARE]


def gather_tokens(block):
    held = {0: block}
    for bit in token_bits():
        held.update({r ^ bit: swap(b, "fsdp", bit) for r, b in held.items()})
    return held


def reduce_tokens(parts):
    held = dict(parts)
    for bit in reversed(token_bits()):
        for r in sorted(held):
            if r & bit:
                got = swap(held.pop(r).astype(bf16), "fsdp", bit)
                held[r ^ bit] = held[r ^ bit] + got.astype(f32)
    return held[0]


def sum_everywhere(small):
    small = small + swap(small, "tp")
    small = small + swap(small, "ctx")
    for bit in fsdp_bits():
        small = small + swap(small, "fsdp", bit)
    return small


def as_pair(values):
    high = lax.reduce_precision(values, 8, 7)
    return [high.astype(bf16), (values - high).astype(bf16)]


def widen(columns):
    width = sum(c.shape[1] for c in columns)
    pad = jnp.zeros((columns[0].shape[0], -width % 128), columns[0].dtype)
    return jnp.concatenate(list(columns) + [pad], axis=1)


def from_pair(columns, count):
    return columns[:, :count].astype(f32) + columns[:, count : 2 * count].astype(f32)


def own_part(array, place, axis=0):
    size = array.shape[axis] // 2
    return lax.dynamic_slice_in_dim(array, place * size, size, axis)


def across_ctx(kept, axis=0):
    place = lax.axis_index("ctx")
    sent = own_part(kept, 1 - place, axis).astype(bf16)
    return own_part(kept, place, axis) + swap(sent, "ctx").astype(f32)


def across_share(kept, axis=1):
    size = kept.shape[axis] // 2
    own = lax.slice_in_dim(kept, 0, size, axis=axis)
    sent = lax.slice_in_dim(kept, size, None, axis=axis).astype(bf16)
    return own + swap(sent, "fsdp", SHARE).astype(f32)


MESH = pl.DeviceIdType.MESH


def peer(fsdp_bit=0, ctx_bit=0, tp_bit=0):
    return (
        lax.axis_index("fsdp") ^ fsdp_bit,
        lax.axis_index("ctx") ^ ctx_bit,
        lax.axis_index("tp") ^ tp_bit,
    )


def greet(peers):
    barrier = pltpu.get_barrier_semaphore()
    for who in peers:
        pl.semaphore_signal(barrier, inc=1, device_id=who, device_id_type=MESH)
    pl.semaphore_wait(barrier, len(peers))


def send(src, dst, sems, k, who):
    copy = pltpu.make_async_remote_copy(
        src_ref=src,
        dst_ref=dst,
        send_sem=sems[0].at[k],
        recv_sem=sems[1].at[k],
        device_id=who,
        device_id_type=MESH,
    )
    copy.start()
    return copy


def dot_nn(a, b):
    return lax.dot_general(a, b, (((1,), (0,)), ((), ())), preferred_element_type=f32)


def dot_nt(a, b):
    return lax.dot_general(a, b, (((1,), (1,)), ((), ())), preferred_element_type=f32)


def aligned(index, size):
    return pl.ds(pl.multiple_of(index * size, size), size)


TILE = 256
CHUNKS = 4


def token_rows(half):
    size = half // CHUNKS
    own = [pl.ds(k * size, size) for k in range(CHUNKS)]
    far = [pl.ds(2 * half + 2 * k * size, size) for k in range(CHUNKS)]
    cross = [pl.ds(2 * half + (2 * k + 1) * size, size) for k in range(CHUNKS)]
    return own, far, cross


def expert_kernel(
    far,
    near,
    experts,
    x_ref,
    grad_hbm,
    gate_hbm,
    up_hbm,
    down_hbm,
    g_hbm,
    wg_hbm,
    wu_hbm,
    wd_hbm,
    dx_ref,
    part_ref,
    sum_gu,
    sum_d,
    xb,
    gb,
    wg,
    wu,
    wd,
    h0,
    hw,
    dg,
    du,
    db,
    d0,
    near_in,
    near_sum,
    far_in,
    keep_stage,
    send_stage,
    local_sems,
    stage_sems,
    send_sems,
    recv_sems,
    tp_send,
    tp_recv,
    free_sem,
):
    half = x_ref.shape[0]
    width = wg.shape[0]
    units = wg.shape[1]
    unit_tiles = units // TILE
    sems = (send_sems, recv_sems)
    far_dev, near_dev, core_dev = peer(far), peer(near), peer(0, 0, 1)
    greet([far_dev, near_dev, core_dev])

    own_chunks, far_rows, cross_rows = token_rows(half)
    near_rows = pl.ds(half, half)
    far_copy = [
        send(x_ref.at[own_chunks[k]], xb.at[far_rows[k]], sems, k, far_dev) for k in range(CHUNKS)
    ]
    near_copy = send(x_ref, xb.at[near_rows], sems, 4 * CHUNKS, near_dev)
    own_units = gate_hbm.shape[1]
    core_rows = pl.ds(pl.multiple_of(lax.axis_index("tp") * half, 16), half)
    got_rows, got_units = pl.ds(half, 3 * half), pl.ds(own_units, 3 * own_units)
    first_units = pl.ds(0, own_units)
    pairs = [
        (grad_hbm.at[core_rows], gb.at[pl.ds(0, half)]),
        (g_hbm.at[got_rows], gb.at[got_rows]),
        (down_hbm, wd.at[first_units]),
        (wd_hbm.at[got_units], wd.at[got_units]),
        (gate_hbm, wg.at[:, first_units]),
        (wg_hbm.at[:, got_units], wg.at[:, got_units]),
        (up_hbm, wu.at[:, first_units]),
        (wu_hbm.at[:, got_units], wu.at[:, got_units]),
    ]
    loads = []
    for k, (src, dst) in enumerate(pairs):
        loads.append(pltpu.make_async_copy(src, dst, local_sems.at[k]))
        loads[-1].start()
    xb[0:half, :] = x_ref[...]
    for k in range(4):
        loads[k].wait()

    def back_tile(j, carry):
        h0[:, aligned(j, TILE)] = dot_nt(gb[...], wd[aligned(j, TILE), :])
        return carry

    lax.fori_loop(0, unit_tiles, back_tile, 0)
    for k in range(4, 8):
        loads[k].wait()

    lane = lax.broadcasted_iota(jnp.int32, (half, x_ref.shape[1] - width), 1)
    own = lax.axis_index("fsdp")
    partner = own ^ SHARE

    def task(number):
        rows = pl.ds(number * half, half)
        extra = xb[rows, width:].astype(f32)

        def gate_of(expert):
            mine = (lane == expert) | (lane == experts + expert)
            return jnp.sum(jnp.where(mine, extra, 0.0), axis=1, keepdims=True)

        gates = jnp.concatenate([gate_of(own), gate_of(partner)], axis=1)

        def unit_tile(j, dots):
            cols = aligned(j, TILE)
            is_own = j < unit_tiles // 2
            gate = jnp.where(is_own, gates[:, :1], gates[:, 1:])
            x = xb[rows, :width]
            gate_pre = dot_nn(x, wg[:, cols])
            up_pre = dot_nn(x, wu[:, cols])
            back = h0[rows, cols]
            sig = 1.0 / (1.0 + jnp.exp(-gate_pre))
            silu = gate_pre * sig
            hidden = silu * up_pre
            hw[rows, cols] = (hidden * gate).astype(bf16)
            hidden_grad = back * gate
            dg[rows, cols] = (hidden_grad * up_pre * (sig * (1.0 + gate_pre * (1.0 - sig)))).astype(bf16)
            du[rows, cols] = (hidden_grad * silu).astype(bf16)
            one = jnp.sum(hidden * back, axis=1, keepdims=True)
            return (
                dots[0] + jnp.where(is_own, one, 0.0),
                dots[1] + jnp.where(is_own, 0.0, one),
            )

        zero = jnp.zeros((half, 1), f32)
        dots = lax.fori_loop(0, unit_tiles, unit_tile, (zero, zero), unroll=True)

        def put(cols, value):
            if number == 0:
                d0[:, cols] = value
            else:
                db[rows, cols] = value.astype(bf16)

        def in_tile(n, carry):
            cols = aligned(n, 2 * TILE)
            value = dot_nt(dg[rows, :], wg[cols, :]) + dot_nt(du[rows, :], wu[cols, :])
            put(cols, value)
            return carry

        lax.fori_loop(0, width // (2 * TILE), in_tile, 0, unroll=True)
        columns = jnp.zeros_like(extra)
        for expert, value in ((own, dots[0]), (partner, dots[1])):
            high = value.astype(bf16).astype(f32)
            columns = jnp.where(lane == expert, high, columns)
            columns = jnp.where(lane == experts + expert, value - high, columns)
        put(slice(width, None), columns)

    def forward(k):
        return send(xb.at[far_rows[k]], xb.at[cross_rows[k]], sems, CHUNKS + k, near_dev)

    def cross_back(k):
        return send(db.at[cross_rows[k]], near_in.at[own_chunks[k]], sems, 2 * CHUNKS + k, near_dev)

    def far_back(k):
        crossed[k].wait_recv()
        total = db[far_rows[k], :].astype(f32) + near_in[own_chunks[k], :].astype(f32)
        db[far_rows[k], :] = total.astype(bf16)
        return send(db.at[far_rows[k]], far_in.at[own_chunks[k]], sems, 3 * CHUNKS + k, far_dev)

    def part_rows(rows):
        def part_tile(j, carry):
            cols = aligned(j, 2 * TILE)
            part_ref[rows, cols] = dot_nn(hw[rows, :], wd[:, cols]).astype(bf16)
            return carry

        lax.fori_loop(0, width // (2 * TILE), part_tile, 0)

    forwards, crossed, backs = [], [], []

    def pass_on(k):
        far_copy[k].wait_recv()
        forwards.append(forward(k))

    pass_on(0)
    task(0)
    pass_on(1)
    forwards[0].wait_recv()
    forwards[1].wait_recv()
    task(2)
    crossed += [cross_back(0), cross_back(1)]
    pass_on(2)
    near_copy.wait_recv()
    task(1)
    backs += [far_back(0), far_back(1)]
    pass_on(3)
    part_rows(pl.ds(0, 2 * half))
    forwards[2].wait_recv()
    forwards[3].wait_recv()
    task(3)
    crossed += [cross_back(2), cross_back(3)]
    near_back = send(db.at[near_rows], near_sum, sems, 4 * CHUNKS + 1, near_dev)

    pl.semaphore_signal(free_sem, inc=1, device_id=core_dev, device_id_type=MESH)
    part_rows(pl.ds(2 * half, 2 * half))
    backs.append(far_back(2))

    piece = units // 4
    tiles = width // TILE

    def to_core(slot, number, rows, size, got):
        return pltpu.make_async_remote_copy(
            src_ref=send_stage.at[slot, pl.ds(0, size)],
            dst_ref=got.at[rows],
            send_sem=tp_send.at[slot],
            recv_sem=tp_recv.at[number],
            device_id=core_dev,
            device_id_type=MESH,
        )

    def to_hbm(slot, rows, size, full):
        return pltpu.make_async_copy(
            keep_stage.at[slot, pl.ds(0, size)], full.at[rows], stage_sems.at[slot]
        )

    def gradient_loop(count, first, size, compute, got, full):
        def close(i):
            slot, rows = lax.rem(i, 2), aligned(i, size)
            to_core(slot, first + i, rows, size, got).wait_recv()
            keep = keep_stage[slot, :size, :].astype(f32) + got[rows, :].astype(f32)
            keep_stage[slot, :size, :] = keep.astype(bf16)
            to_hbm(slot, rows, size, full).start()

        def free(slot):
            to_hbm(slot, pl.ds(0, size), size, full).wait()
            to_core(slot, 0, pl.ds(0, size), size, got).wait_send()

        def one(i, carry):
            slot = lax.rem(i, 2)

            @pl.when(i >= 2)
            def _():
                free(slot)

            compute(i, slot)
            to_core(slot, first + i, aligned(i, size), size, got).start()

            @pl.when(i >= 1)
            def _():
                close(i - 1)

            return carry

        lax.fori_loop(0, count, one, 0)
        close(count - 1)
        free(0)
        free(1)

    def gate_up_tile(i, slot):
        flipped = xb[:, aligned(i, TILE)].T
        for k, source in enumerate((dg, du)):
            value = dot_nn(flipped, source[...]).astype(bf16)
            for p in range(4):
                at = (2 * k + p // 2) * piece
                stage = keep_stage if p % 2 == 0 else send_stage
                stage[slot, :TILE, at : at + piece] = value[:, p * piece : (p + 1) * piece]

    def down_tile(i, slot):
        for stage, offset in ((keep_stage, 0), (send_stage, piece)):
            cols = pl.ds(pl.multiple_of(i * 2 * piece + offset, 128), piece)
            flipped = hw[:, cols].T
            for n in range(0, width, 2 * TILE):
                stage[slot, :, n : n + 2 * TILE] = dot_nn(flipped, gb[:, n : n + 2 * TILE]).astype(bf16)

    pl.semaphore_wait(free_sem, 1)
    gradient_loop(2, tiles, piece, down_tile, wg, sum_d)
    backs.append(far_back(3))
    gradient_loop(tiles, 0, TILE, gate_up_tile, wu, sum_gu)
    near_back.wait_recv()
    for copy in backs:
        copy.wait_recv()
    dx_ref[...] = d0[...] + near_sum[...].astype(f32) + far_in[...].astype(f32)
    for copy in far_copy + [near_copy, near_back] + forwards + crossed + backs:
        copy.wait_send()


def experts_on_chip(payload, out_grad, own_gate, own_up, own_down, grad_rows, gate, up, down, experts):
    half, wide = payload.shape
    rows, width = grad_rows.shape
    units = gate.shape[1]
    far, near = token_bits()
    any_spec = pl.BlockSpec(memory_space=pl.ANY)
    vmem = pl.BlockSpec(memory_space=pltpu.VMEM)
    return pl.pallas_call(
        functools.partial(expert_kernel, far, near, experts),
        name="experts",
        out_shape=(
            jax.ShapeDtypeStruct((half, wide), f32),
            jax.ShapeDtypeStruct((rows, width), bf16),
            jax.ShapeDtypeStruct((width, units), bf16),
            jax.ShapeDtypeStruct((units // 2, width), bf16),
        ),
        in_specs=[vmem] + [any_spec] * 8,
        out_specs=(vmem, vmem, any_spec, any_spec),
        scratch_shapes=[
            pltpu.VMEM((rows, wide), bf16),
            pltpu.VMEM((rows, width), bf16),
            pltpu.VMEM((width, units), bf16),
            pltpu.VMEM((width, units), bf16),
            pltpu.VMEM((units, width), bf16),
            pltpu.VMEM((rows, units), f32),
            pltpu.VMEM((rows, units), bf16),
            pltpu.VMEM((rows, units), bf16),
            pltpu.VMEM((rows, units), bf16),
            pltpu.VMEM((rows, wide), bf16),
            pltpu.VMEM((half, wide), f32),
            pltpu.VMEM((half, wide), bf16),
            pltpu.VMEM((half, wide), bf16),
            pltpu.VMEM((half, wide), bf16),
            pltpu.VMEM((2, units // 4, width), bf16),
            pltpu.VMEM((2, units // 4, width), bf16),
            pltpu.SemaphoreType.DMA((8,)),
            pltpu.SemaphoreType.DMA((2,)),
            pltpu.SemaphoreType.DMA((4 * CHUNKS + 2,)),
            pltpu.SemaphoreType.DMA((4 * CHUNKS + 2,)),
            pltpu.SemaphoreType.DMA((2,)),
            pltpu.SemaphoreType.DMA((width // TILE + 2,)),
            pltpu.SemaphoreType.REGULAR,
        ],
        compiler_params=pltpu.CompilerParams(
            collective_id=1, has_side_effects=True, vmem_limit_bytes=62 * 1024 * 1024
        ),
        cost_estimate=pl.CostEstimate(
            flops=2 * 9 * rows * width * units, bytes_accessed=60_000_000, transcendentals=rows * units
        ),
    )(payload, out_grad, own_gate, own_up, own_down, grad_rows, gate, up, down)


class Exchange:
    def __init__(self, send_sems, recv_sems, local_sems):
        self.sems = (send_sems, recv_sems)
        self.local_sems = local_sems
        self.all = []
        self.local = []
        self.arrived = set()
        self.settled = set()
        self.gone = set()

    def start(self, src, dst, who):
        self.all.append(send(src, dst, self.sems, len(self.all), who))
        return len(self.all) - 1

    def keep(self, src, dst):
        copy = pltpu.make_async_copy(src, dst, self.local_sems.at[len(self.local)])
        copy.start()
        self.local.append(copy)

    def arrive(self, number):
        if number not in self.arrived:
            self.arrived.add(number)
            self.all[number].wait_recv()

    def settle(self, number):
        if number not in self.settled:
            self.settled.add(number)
            self.local[number].wait()

    def sent(self, number):
        if number not in self.gone:
            self.gone.add(number)
            self.all[number].wait_send()

    def finish(self):
        for number in range(len(self.all)):
            self.arrive(number)
        for number in range(len(self.all)):
            self.sent(number)
        for number in range(len(self.local)):
            self.settle(number)


class RowGather:
    def __init__(self, net, full, part, order):
        self.net, self.full, self.order = net, full, order
        self.rows, self.first, self.size = part
        self.copies = {}
        self.spread((0, 0), -1)

    def place(self, code):
        index = (lax.axis_index("fsdp") ^ code[0]) * 2 + (lax.axis_index("ctx") ^ code[1])
        return pl.ds(pl.multiple_of(index * self.rows + self.first, 16), self.size)

    def spread(self, code, last):
        block = self.full.at[self.place(code)]
        for position in range(last + 1, len(self.order)):
            axis, bit = self.order[position]
            other = (code[0] ^ bit, code[1]) if axis == "fsdp" else (code[0], code[1] ^ bit)
            self.copies[other] = (self.net.start(block, block, dim_peer((axis, bit))), position)

    def arrive(self, code):
        copy, position = self.copies[code]
        self.net.arrive(copy)
        self.spread(code, position)


def dim_peer(dim):
    axis, bit = dim
    return peer(bit if axis == "fsdp" else 0, bit if axis == "ctx" else 0)


def gather_codes(far, near):
    first = [(SHARE, 0), (far, 0), (far ^ SHARE, 0)]
    rest = [(0, 1), (near, 0), (near, 1)]
    later = [(a ^ b, c) for a, _ in first for b, c in rest]
    return first, rest[:2] + later[0:2] + [rest[2]] + later[3:5] + [later[2]] + later[6:8] + [later[5], later[8]]


def document_start(lengths_ref, number):
    start, first = 0, jnp.zeros_like(number)
    for k in range(lengths_ref.shape[1]):
        start = start + lengths_ref[0, k]
        first = jnp.where(number >= start, start, first)
    return first


def forward_kernel(
    far, near, experts, total_rows,
    lengths_ref, loss_grad_ref, routes_ref, tokens_ref, small_hbm, query_hbm, key_hbm, value_hbm, out_hbm,
    grad_hbm, gate_hbm, up_hbm, down_hbm,
    payload_ref, middle_ref, probs_ref, mask_ref, row_ref, query, kv, lse_ref, attended, cos_ref, sin_ref,
    in_out, out_out, grads, gate_all, up_all, down_all,
    in_full, out_full, normed, raw, core_sent, core_got, count_sent, count_got,
    send_sems, recv_sems, local_sems,
):
    far_dev, near_dev, share_dev = peer(far), peer(near), peer(SHARE)
    ctx_dev, core_dev = peer(0, 1), peer(0, 0, 1)
    net = Exchange(send_sems, recv_sems, local_sems)
    place, core = lax.axis_index("ctx"), lax.axis_index("tp")
    rows, width = tokens_ref.shape
    half, quarter = rows // 2, rows // 4
    block = small_hbm.shape[0]
    heads_width, kv_width = query_hbm.shape[1], key_hbm.shape[1]
    own_block = pl.ds(pl.multiple_of((lax.axis_index("fsdp") * 2 + place) * block, 16), block)
    start = 0
    for ref in (small_hbm, query_hbm, key_hbm, value_hbm):
        net.keep(ref, in_full.at[own_block, pl.ds(start, ref.shape[1])])
        start += ref.shape[1]
    net.keep(out_hbm, out_full.at[own_block])
    greet([far_dev, near_dev, share_dev, ctx_dev, core_dev])
    for k in range(5):
        net.settle(k)
    fars = [("fsdp", far), ("fsdp", SHARE)]
    low, across = ("fsdp", near), ("ctx", 1)
    part = block // 2
    ins = [
        RowGather(net, in_full, (block, 0, part), fars + [across, low]),
        RowGather(net, in_full, (block, part, part), fars + [low, across]),
    ]

    routes = routes_ref[...]
    lane = lax.broadcasted_iota(jnp.int32, (rows, 128), 1)
    named = jnp.zeros((rows, 128), f32)
    for k in range(routes.shape[1]):
        named += (routes[:, k : k + 1] == lane).astype(f32)
    count_dims = [ctx_dev, near_dev, share_dev, far_dev]
    counts = [jnp.broadcast_to(jnp.sum(named, axis=0, keepdims=True), (8, 128))]
    count_copies = []

    def count_step():
        k = len(count_copies)
        if k > 0:
            net.arrive(count_copies[-1])
            counts[0] = counts[0] + count_got[k - 1]
        if k < len(count_dims):
            count_sent[k] = counts[0]
            count_copies.append(net.start(count_sent.at[k], count_got.at[k], count_dims[k]))

    count_step()

    units = gate_hbm.shape[1]

    def slot(full, piece, which=None):
        begin, size = (piece * units, units) if full is down_all else (0, width)
        if which is not None:
            size //= 2
            begin = pl.multiple_of(begin + which * size, 16)
        if full is down_all:
            return full.at[pl.ds(begin, size)]
        return full.at[pl.ds(begin, size), pl.ds(piece * units, units)]

    matrices = [(down_hbm, down_all), (gate_hbm, gate_all), (up_hbm, up_all)]
    for ref, full in matrices:
        net.start(ref, slot(full, 1), core_dev)

    from_share, from_ctx = [], []

    def share_start(k):
        ref, full = matrices[k]
        size = ref.shape[0] // 2
        piece = ref.at[pl.ds(pl.multiple_of(place * size, 16), size)]
        from_share.append(net.start(piece, slot(full, 2, place), share_dev))

    def share_on(k):
        ref, full = matrices[k]
        net.arrive(from_share[k])
        from_ctx.append(net.start(slot(full, 2, place), slot(full, 2, place), ctx_dev))
        net.start(slot(full, 2, place), slot(full, 3, place), core_dev)

    here = lax.broadcasted_iota(jnp.int32, (rows, 1), 0) + place * rows
    position = (here - document_start(lengths_ref, here)).astype(f32)
    turn_lane = lax.broadcasted_iota(jnp.int32, (1, HEAD_DIM), 1)
    turn = lax.rem(turn_lane, HEAD_DIM // 2).astype(f32) * (2.0 / HEAD_DIM)
    angles = position * jnp.exp(turn * -math.log(rope_base))
    cos_ref[...] = jnp.cos(angles)
    sin_ref[...] = jnp.where(turn_lane < HEAD_DIM // 2, -1.0, 1.0) * jnp.sin(angles)

    first, rest = gather_codes(far, near)
    for code in first:
        for g in ins:
            g.arrive(code)
    count_step()
    own_rows = pl.ds(pl.multiple_of(core * half, 16), half)
    other_rows = pl.ds(pl.multiple_of((1 - core) * half, 16), half)
    chunk = half // CHUNKS
    own_chunks = [pl.ds(pl.multiple_of(core * half + k * chunk, 16), chunk) for k in range(CHUNKS)]
    _, far_rows, cross_rows = token_rows(half)
    share_start(0)
    far_copies = [net.start(grad_hbm.at[own_chunks[k]], grads.at[far_rows[k]], far_dev) for k in range(CHUNKS)]
    def cross_on(k):
        net.arrive(far_copies[k])
        net.start(grads.at[far_rows[k]], grads.at[cross_rows[k]], near_dev)

    for code in rest[:6]:
        for g in ins:
            g.arrive(code)
    for code in rest[6:]:
        for g in ins:
            g.arrive(code)
    count_step()
    net.arrive(from_share[0])
    share_start(1)
    outs = [
        RowGather(net, out_full, (block, 0, part), fars + [across, low]),
        RowGather(net, out_full, (block, part, part), fars + [low, across]),
    ]
    net.start(grad_hbm.at[own_rows], grads.at[pl.ds(half, half)], near_dev)
    gains = in_full[:, :128].astype(f32).T
    attn_gain, moe_gain = gains[experts : experts + 1], gains[experts + 1 : experts + 2]
    step = quarter // 2
    for k in range(rows // quarter):
        at = slice(k * quarter, (k + 1) * quarter)
        x = tokens_ref[at, :].astype(f32)
        inverse = lax.rsqrt(jnp.mean(x * x, axis=1, keepdims=True) + epsilon)
        normed[at, :] = (x * inverse * attn_gain).astype(bf16)

    def rotated(value, at):
        return value * cos_ref[at, :] + pltpu.roll(value, HEAD_DIM // 2, 1) * sin_ref[at, :]

    mine = pl.ds(pl.multiple_of(place * rows, 16), rows)
    raw[...] = dot_nn(normed[...], in_full[:, 128:])
    kv[mine, :kv_width] = rotated(raw[:, heads_width : heads_width + kv_width], slice(None)).astype(bf16)
    kv[mine, kv_width:] = raw[:, heads_width + kv_width :].astype(bf16)
    kv_copy = net.start(kv.at[mine], kv.at[mine], ctx_dev)
    for head in range(heads_width // HEAD_DIM):
        cols = slice(head * HEAD_DIM, (head + 1) * HEAD_DIM)
        query[:, cols] = rotated(raw[:, cols], slice(None)).astype(bf16)
    share_on(0)
    for code in first:
        for g in outs:
            g.arrive(code)
    count_step()
    net.arrive(kv_copy)
    net.arrive(from_share[1])
    share_start(2)
    share_on(1)
    cross_on(0)

    keys, values_flipped = kv[:, :HEAD_DIM], kv[:, HEAD_DIM:].T
    query_number = lax.broadcasted_iota(jnp.int32, (1, half), 1) + place * rows
    key_number = lax.broadcasted_iota(jnp.int32, (kv.shape[0], 1), 0)
    scale = HEAD_DIM ** (-0.5)

    def head_block(i, carry):
        head, block_index = i // 2, lax.rem(i, 2)
        cols, at = aligned(head, HEAD_DIM), aligned(block_index, half)
        number = query_number + block_index * half
        allowed = (key_number >= document_start(lengths_ref, number)) & (key_number <= number)
        scores = jnp.where(allowed, dot_nt(keys, query[at, cols]) * scale, masked_score)
        maxima = jnp.max(scores, axis=0, keepdims=True)
        weights = jnp.exp(scores - maxima)
        totals = jnp.sum(weights, axis=0, keepdims=True)
        lse_ref[pl.ds(head, 1), at] = maxima + jnp.log(totals)
        low_weights = (weights * (1.0 / totals)).astype(bf16)
        attended[at, cols] = dot_nn(values_flipped, low_weights).T.astype(bf16)
        return carry

    group = heads_width // HEAD_DIM
    third = 2 * group // 3
    lax.fori_loop(0, third, head_block, 0)
    for code in rest[:6]:
        for g in outs:
            g.arrive(code)
    cross_on(1)
    lax.fori_loop(third, 2 * third, head_block, 0)
    for code in rest[6:]:
        for g in outs:
            g.arrive(code)
    cross_on(2)
    count_step()
    lax.fori_loop(2 * third, 2 * group, head_block, 0)
    cross_on(3)

    core_sent[...] = dot_nt(attended[other_rows, :], out_full[...])
    core_copy = net.start(core_sent, core_got, core_dev)
    share_on(2)
    middle_ref[...] = tokens_ref[own_rows, :].astype(f32) + dot_nt(attended[own_rows, :], out_full[...])
    net.arrive(core_copy)
    own_lane = lax.broadcasted_iota(jnp.int32, (step, 128), 1)
    share_row = counts[0][0:1] * (experts / (total_rows * routes.shape[1] * total_rows))
    row_number = lax.broadcasted_iota(jnp.int32, (8, 128), 0)
    row_ref[...] = jnp.where(
        row_number == 0, share_row * loss_grad_ref[0], jnp.where(row_number == 1, share_row, 0.0)
    )
    router = in_full[:, :128]
    for k in range(half // step):
        at = slice(k * step, (k + 1) * step)
        middle = middle_ref[at, :] + core_got[at, :]
        middle_ref[at, :] = middle
        inverse = lax.rsqrt(jnp.mean(middle * middle, axis=1, keepdims=True) + epsilon)
        normed_moe = (middle * inverse * moe_gain).astype(bf16)
        payload_ref[at, :width] = normed_moe
        logits = jnp.where(own_lane < experts, dot_nn(normed_moe, router), masked_score)
        shifted = jnp.exp(logits - jnp.max(logits, axis=1, keepdims=True))
        probs = shifted / jnp.sum(shifted, axis=1, keepdims=True)
        own_routes = routes_ref[pl.ds(pl.multiple_of(core * half + k * step, 16), step), :]
        mask = jnp.zeros((step, 128), f32)
        for n in range(routes.shape[1]):
            mask += (own_routes[:, n : n + 1] == own_lane).astype(f32)
        probs_ref[at, :] = probs
        mask_ref[at, :] = mask
        chosen = probs * mask
        gates = chosen / jnp.sum(chosen, axis=1, keepdims=True)
        high = gates.astype(bf16).astype(f32)
        payload_ref[at, width:] = (high + pltpu.roll(gates - high, experts, 1)).astype(bf16)
    for k, (ref, full) in enumerate(matrices):
        net.arrive(from_ctx[k])
        net.start(slot(full, 2, 1 - place), slot(full, 3, 1 - place), core_dev)
    net.keep(in_full, in_out)
    net.keep(out_full, out_out)
    net.finish()


def forward_on_chip(
    lengths, loss_grad, routes, tokens, small, w_query, w_key, w_value, out_block, out_grad, gate, up, down, experts
):
    far, near = token_bits()
    owners = lax.axis_size("fsdp") * lax.axis_size("ctx")
    rows, width = tokens.shape
    half, pack = rows // 2, rows * lax.axis_size("ctx")
    units, block = gate.shape[1], small.shape[0]
    heads_width, kv_width = w_query.shape[1], w_key.shape[1]
    in_width, out_width = small.shape[1] + heads_width + 2 * kv_width, out_block.shape[1]
    any_spec = pl.BlockSpec(memory_space=pl.ANY)
    vmem = pl.BlockSpec(memory_space=pltpu.VMEM)
    smem = pl.BlockSpec(memory_space=pltpu.SMEM)
    outs = [
        ((half, width + 128), bf16),
        ((half, width), f32),
        ((half, 128), f32),
        ((half, 128), f32),
        ((8, 128), f32),
        ((rows, heads_width), bf16),
        ((pack, 2 * kv_width), bf16),
        ((-(-heads_width // HEAD_DIM // 8) * 8, rows), f32),
        ((rows, heads_width), bf16),
        ((rows, HEAD_DIM), f32),
        ((rows, HEAD_DIM), f32),
        ((owners * block, in_width), bf16),
        ((owners * block, out_width), bf16),
        ((4 * half, width), bf16),
        ((width, 4 * units), bf16),
        ((width, 4 * units), bf16),
        ((4 * units, width), bf16),
    ]
    return pl.pallas_call(
        functools.partial(forward_kernel, far, near, experts, rows * owners),
        name="forward",
        out_shape=tuple(jax.ShapeDtypeStruct(s, d) for s, d in outs),
        in_specs=[smem, smem, vmem, vmem] + [any_spec] * 9,
        out_specs=(vmem,) * 11 + (any_spec,) * 6,
        scratch_shapes=[
            pltpu.VMEM((owners * block, in_width), bf16),
            pltpu.VMEM((owners * block, out_width), bf16),
            pltpu.VMEM((rows, width), bf16),
            pltpu.VMEM((rows, in_width - 128), f32),
            pltpu.VMEM((half, width), f32),
            pltpu.VMEM((half, width), f32),
            pltpu.VMEM((4, 8, 128), f32),
            pltpu.VMEM((4, 8, 128), f32),
            pltpu.SemaphoreType.DMA((100,)),
            pltpu.SemaphoreType.DMA((100,)),
            pltpu.SemaphoreType.DMA((8,)),
        ],
        compiler_params=pltpu.CompilerParams(
            collective_id=0, has_side_effects=True, vmem_limit_bytes=56 * 1024 * 1024
        ),
    )(lengths, loss_grad, routes, tokens, small, w_query, w_key, w_value, out_block, out_grad, gate, up, down)


class RowReduce:
    def __init__(self, net, partial, inbox, part, order):
        self.net, self.partial, self.inbox, self.order = net, partial, inbox, order
        self.rows, self.first, self.size = part
        self.copies = {}

    def place(self, mask):
        fsdp, ctx = 0, 0
        for position, (axis, bit) in enumerate(self.order):
            if mask >> position & 1:
                fsdp, ctx = (fsdp ^ bit, ctx) if axis == "fsdp" else (fsdp, ctx ^ bit)
        index = (lax.axis_index("fsdp") ^ fsdp) * 2 + (lax.axis_index("ctx") ^ ctx)
        return pl.ds(pl.multiple_of(index * self.rows + self.first, 16), self.size)

    def box(self, mask):
        return pl.ds((mask - 1) * self.size, self.size)

    def step(self, mask):
        rows, last = self.place(mask), mask.bit_length() - 1
        if last + 1 < len(self.order):
            value = self.partial[rows, :].astype(f32)
            for later in range(last + 1, len(self.order)):
                source = mask | 1 << later
                self.net.arrive(self.copies[source])
                value = value + self.inbox[self.box(source), :].astype(f32)
            if mask == 0:
                return value
            self.partial[rows, :] = value.astype(bf16)
        self.copies[mask] = self.net.start(
            self.partial.at[rows], self.inbox.at[self.box(mask)], dim_peer(self.order[last])
        )

    def level(self, last):
        for mask in reversed(range(1 << last, 2 << last)):
            self.step(mask)


def backward_kernel(
    far, near, experts, group,
    lengths_ref, row_ref, dx_ref, middle_ref, probs_ref, mask_ref, grad_hbm,
    tokens_hbm, query_hbm, kv_hbm, lse_ref, attended_hbm, cos_ref, sin_ref,
    in_hbm, out_hbm, moe_hbm, gu_hbm, down_hbm,
    output_hbm, loss_ref, tokens_grad_hbm, query_out, key_out, value_out, out_ref, extra_ref, gate_ref, up_ref, down_ref,
    grad_ref, tokens, query, kv, attended, in_full, out_full,
    out_in, att_grad, qkv_grad, kv_grad, kv_sent, kv_got,
    in_box, out_box,
    mid_grad, back_sent, back_got, tok_stage, extra_rows, extra_sent, extra_got,
    moe_own, moe_far, moe_near, moe_cross, moe_back,
    gate_own, gate_x, gate_sent, gate_s,
    up_own, up_s, up_sent, up_x,
    down_own, down_x, down_sent, down_s,
    loss_sent, loss_got,
    send_sems, recv_sems, local_sems,
):
    far_dev, near_dev, share_dev = peer(far), peer(near), peer(SHARE)
    ctx_dev, core_dev = peer(0, 1), peer(0, 0, 1)
    greet([far_dev, near_dev, share_dev, ctx_dev, core_dev])
    net = Exchange(send_sems, recv_sems, local_sems)
    ctx_place, core = lax.axis_index("ctx"), lax.axis_index("tp")
    half, width = middle_ref.shape
    rows = 2 * half
    quarter = half // 2
    own_rows = pl.ds(pl.multiple_of(core * half, 16), half)
    other_rows = pl.ds(pl.multiple_of((1 - core) * half, 16), half)
    chunks, far_rows, cross_rows = token_rows(half)

    crossed = [net.start(moe_hbm.at[cross_rows[k]], moe_cross.at[chunks[k]], near_dev) for k in range(CHUNKS)]
    units = gu_hbm.shape[1] // 4
    wide = width // 2

    def wide_half(place):
        return pl.ds(pl.multiple_of(place * wide, 128), wide)

    gate_cols, up_own_cols, up_par_cols = pl.ds(0, 2 * units), pl.ds(2 * units, units), pl.ds(3 * units, units)
    gate_first = net.start(gu_hbm.at[wide_half(1 - ctx_place), gate_cols], gate_x, ctx_dev)
    up_first = net.start(gu_hbm.at[:, up_par_cols], up_s, share_dev)
    pairs = [
        (in_hbm, in_full), (out_hbm, out_full), (attended_hbm, attended), (query_hbm, query),
        (kv_hbm, kv), (tokens_hbm, tokens), (moe_hbm.at[pl.ds(0, half)], moe_own),
        (gu_hbm.at[wide_half(ctx_place), gate_cols], gate_own), (gu_hbm.at[:, up_own_cols], up_own),
        (down_hbm.at[:, wide_half(ctx_place)], down_own), (grad_hbm.at[own_rows], grad_ref),
    ] + [(moe_hbm.at[far_rows[k]], moe_far.at[chunks[k]]) for k in range(CHUNKS)]
    for src, dst in pairs:
        net.keep(src, dst)

    def loaded(*numbers):
        for number in numbers:
            net.settle(number)

    def pieces(size):
        return [slice(k * size // 4, (k + 1) * size // 4) for k in range(4)]

    loaded(0, 10)
    flipped_extra = in_full[:, :128].astype(f32).T
    attn_gain, moe_gain = flipped_extra[experts : experts + 1], flipped_extra[experts + 1 : experts + 2]
    lane = lax.broadcasted_iota(jnp.int32, (half, 128), 1)
    probs, mask = probs_ref[...], mask_ref[...]
    pair = dx_ref[:, width:]
    gate_grad = jnp.where(lane < experts, pair + pltpu.roll(pair, 128 - experts, 1), 0.0)
    chosen = probs * mask
    chosen_total = jnp.sum(chosen, axis=1, keepdims=True)
    weighted = jnp.sum(gate_grad * chosen, axis=1, keepdims=True) / chosen_total
    prob_grad = mask * (gate_grad - weighted) / chosen_total + row_ref[0:1, :]
    logit_grad = probs * (prob_grad - jnp.sum(prob_grad * probs, axis=1, keepdims=True))
    logit_high = logit_grad.astype(bf16)
    logit_low = (logit_grad - logit_high.astype(f32)).astype(bf16)
    router = in_full[:, :128]
    step = quarter // 2
    gain_moe = jnp.zeros((1, width), f32)
    router_grad = jnp.zeros((128, width), f32)
    for k in range(half // step):
        at = slice(k * step, (k + 1) * step)
        middle = middle_ref[at, :]
        inverse = lax.rsqrt(jnp.mean(middle * middle, axis=1, keepdims=True) + epsilon)
        scaled = middle * inverse
        normed_moe = (scaled * moe_gain).astype(bf16)
        moe_grad = dx_ref[at, :width] + dot_nt(logit_high[at], router) + dot_nt(logit_low[at], router)
        router_grad += dot(logit_high[at], normed_moe, 0, 0) + dot(logit_low[at], normed_moe, 0, 0)
        gain_moe += jnp.sum(moe_grad * scaled, axis=0, keepdims=True)
        a = moe_grad * moe_gain
        grad = grad_ref[at, :].astype(f32) + inverse * (a - scaled * jnp.mean(a * scaled, axis=1, keepdims=True))
        mid_grad[at, :] = grad
        out_in[pl.ds(pl.multiple_of(core * half + k * step, 16), step), :] = grad.astype(bf16)
    out_in_copy = net.start(out_in.at[own_rows], out_in.at[own_rows], core_dev)
    row = lax.broadcasted_iota(jnp.int32, (128, width), 0)
    extra_rows[...] = jnp.where(row == experts + 1, gain_moe, router_grad)

    loss_dims = [core_dev, ctx_dev, near_dev, share_dev, far_dev]
    loss_state = [jnp.broadcast_to(jnp.sum(probs, axis=0, keepdims=True), (8, 128))]
    loss_copies = []

    def loss_step():
        k = len(loss_copies)
        if k > 0:
            net.arrive(loss_copies[-1])
            loss_state[0] = loss_state[0] + loss_got[k - 1]
        if k < len(loss_dims):
            loss_sent[k] = loss_state[0]
            loss_copies.append(net.start(loss_sent.at[k], loss_got.at[k], loss_dims[k]))

    loss_step()
    loaded(6, *range(11, 11 + CHUNKS))
    far_sums = []

    def far_sum(k):
        net.arrive(crossed[k])
        at = chunks[k]
        moe_far[at, :] = (moe_far[at, :].astype(f32) + moe_cross[at, :].astype(f32)).astype(bf16)
        far_sums.append(net.start(moe_far.at[at], moe_back.at[at], far_dev))

    far_sum(0)
    net.arrive(out_in_copy)
    loaded(1, 2)
    att_grad[...] = dot_nn(out_in[...], out_full[...]).astype(bf16)

    def out_tile(i, carry):
        cols = aligned(i, TILE)
        out_full[cols, :] = dot_nn(out_in[:, cols].T, attended[...]).astype(bf16)
        return carry

    lax.fori_loop(0, width // TILE, out_tile, 0)
    block = key_out.shape[0]
    low, across = ("fsdp", near), ("ctx", 1)
    fars = [("fsdp", far), ("fsdp", SHARE)]
    orders = [fars + [across, low], fars + [low, across]]
    part_size = block // 2
    sums_out = [
        RowReduce(net, out_full, out_box.at[k], (block, k * part_size, part_size), [across] + fars + [low])
        for k in range(2)
    ]
    far_sum(1)
    for s in sums_out:
        s.level(3)
    loss_step()
    far_sum(2)
    far_sum(3)
    net.sent(out_in_copy)
    loaded(5)
    normed_step = half // 2
    for k in range(rows // normed_step):
        at = slice(k * normed_step, (k + 1) * normed_step)
        x = tokens[at, :].astype(f32)
        inverse = lax.rsqrt(jnp.mean(x * x, axis=1, keepdims=True) + epsilon)
        out_in[at, :] = (x * inverse * attn_gain).astype(bf16)

    loaded(3, 4)
    pack = kv.shape[0]
    kv_grad[...] = jnp.zeros_like(kv_grad)
    keys, values = kv[:, :HEAD_DIM], kv[:, HEAD_DIM:]
    keys_flipped = keys.T
    query_number = lax.broadcasted_iota(jnp.int32, (1, half), 1) + ctx_place * rows
    key_number = lax.broadcasted_iota(jnp.int32, (pack, 1), 0)
    scale = HEAD_DIM ** (-0.5)

    def head_block(i, carry):
        head, block_index = i // 2, lax.rem(i, 2)
        cols = aligned(head, HEAD_DIM)
        at = aligned(block_index, half)
        number = query_number + block_index * half
        allowed = (key_number >= document_start(lengths_ref, number)) & (key_number <= number)
        q, grad = query[at, cols], att_grad[at, cols]
        log_total = lse_ref[pl.ds(head, 1), at]
        weights = jnp.where(allowed, jnp.exp(dot_nt(keys, q) * scale - log_total), 0.0)
        weight_grad = dot_nt(values, grad)
        delta = jnp.sum(weights * weight_grad, axis=0, keepdims=True)
        score_grad = (weights * (weight_grad - delta)).astype(bf16)
        kv_grad[:, :HEAD_DIM] += dot_nn(score_grad, q) * scale
        kv_grad[:, HEAD_DIM:] += dot_nn(weights.astype(bf16), grad)
        query_grad = (dot_nn(keys_flipped, score_grad) * scale).T
        turned = query_grad * cos_ref[at, :] - pltpu.roll(query_grad, HEAD_DIM // 2, 1) * sin_ref[at, :]
        qkv_grad[at, cols] = turned.astype(bf16)
        return carry

    third = 2 * group // 3
    lax.fori_loop(0, third, head_block, 0)
    loss_step()
    down_first = net.start(down_hbm.at[:, wide_half(1 - ctx_place)], down_x, ctx_dev)
    lax.fori_loop(third, 2 * third, head_block, 0)
    loss_step()
    loaded(7, 8, 9)
    net.arrive(gate_first)
    for at in pieces(wide):
        total = gate_own[at, :].astype(f32) + gate_x[at, :].astype(f32)
        gate_ref[at, :] = total[:, :units]
        gate_sent[at, :] = total[:, units:].astype(bf16)
    gate_last = net.start(gate_sent, gate_s, share_dev)
    net.arrive(up_first)
    up_sent[...] = (up_own[wide_half(1 - ctx_place), :].astype(f32) + up_s[wide_half(1 - ctx_place), :].astype(f32)).astype(bf16)
    up_ref[...] = up_own[wide_half(ctx_place), :].astype(f32) + up_s[wide_half(ctx_place), :].astype(f32)
    lax.fori_loop(2 * third, 2 * group, head_block, 0)
    loss_step()
    ctx_rows = pl.ds(pl.multiple_of(ctx_place * rows, 16), rows)
    ctx_other = pl.ds(pl.multiple_of((1 - ctx_place) * rows, 16), rows)
    kv_sent[...] = kv_grad[ctx_other, :].astype(bf16)
    kv_copy = net.start(kv_sent, kv_got, ctx_dev)
    up_last = net.start(up_sent, up_x, ctx_dev)
    for mask in (7, 6, 5, 4):
        for s in sums_out:
            s.step(mask)
    near_first = net.start(moe_hbm.at[pl.ds(half, half)], moe_near, near_dev)
    loss_step()
    loss = jnp.sum(loss_state[0][0:1] * row_ref[1:2, :], axis=1, keepdims=True)
    loss_ref[...] = jnp.broadcast_to(loss, loss_ref.shape)
    net.arrive(kv_copy)
    kv_sum = kv_grad[ctx_rows, :] + kv_got[...].astype(f32)
    key_grad = kv_sum[:, :HEAD_DIM]
    key_grad = key_grad * cos_ref[...] - pltpu.roll(key_grad, HEAD_DIM // 2, 1) * sin_ref[...]
    heads_width = group * HEAD_DIM
    qkv_grad[:, heads_width : heads_width + HEAD_DIM] = key_grad.astype(bf16)
    qkv_grad[:, heads_width + HEAD_DIM :] = kv_sum[:, HEAD_DIM:].astype(bf16)

    gain_attn = jnp.zeros((1, width), f32)

    def attn_scaled(at):
        x = tokens[at, :].astype(f32)
        inverse = lax.rsqrt(jnp.mean(x * x, axis=1, keepdims=True) + epsilon)
        return inverse, x * inverse

    for k in range(2):
        at = other_rows if k == 0 else own_rows
        part = dot_nt(qkv_grad[at, :], in_full[:, 128:])
        gain_attn += jnp.sum(part * attn_scaled(at)[1], axis=0, keepdims=True)
        if k == 0:
            back_sent[...] = part.astype(bf16)
            back_copy = net.start(back_sent, back_got, core_dev)
        else:
            tok_stage[...] = part
    def in_tile(i, carry):
        cols = aligned(i, TILE)
        in_full[cols, 128:] = dot_nn(out_in[:, cols].T, qkv_grad[...]).astype(bf16)
        return carry

    lax.fori_loop(0, width // TILE, in_tile, 0)
    extra_rows[...] = jnp.where(row == experts, gain_attn, extra_rows[...])
    in_full[:, :128] = extra_rows[...].T.astype(bf16)
    sums_in = [
        RowReduce(net, in_full, in_box.at[k], (block, k * part_size, part_size), orders[k]) for k in range(2)
    ]
    for s in sums_in:
        s.level(3)
    for mask in (3, 2):
        for s in sums_out:
            s.step(mask)

    net.arrive(back_copy)
    for k in range(2):
        at = pl.ds(k * quarter, quarter)
        inverse, scaled = attn_scaled(pl.ds(pl.multiple_of(core * half + k * quarter, 16), quarter))
        a = (tok_stage[at, :] + back_got[at, :].astype(f32)) * attn_gain
        tok_stage[at, :] = mid_grad[at, :] + inverse * (a - scaled * jnp.mean(a * scaled, axis=1, keepdims=True))
    net.keep(tok_stage, tokens_grad_hbm.at[own_rows])
    net.start(tok_stage, tokens_grad_hbm.at[own_rows], core_dev)

    for mask in (7, 6, 5, 4):
        for s in sums_in:
            s.step(mask)
    for s in sums_out:
        s.step(1)
    net.arrive(down_first)
    for at in pieces(units):
        down_ref[at, :] = down_own[at, :].astype(f32) + down_x[at, :].astype(f32)
        after = slice(at.start + units, at.stop + units)
        down_sent[at, :] = (down_own[after, :].astype(f32) + down_x[after, :].astype(f32)).astype(bf16)
    down_last = net.start(down_sent, down_s, share_dev)
    for mask in (3, 2, 1):
        for s in sums_in:
            s.step(mask)

    net.arrive(near_first)
    for k in range(CHUNKS):
        net.arrive(far_sums[k])
        at = chunks[k]
        moe_out = moe_own[at, :].astype(f32) + moe_near[at, :].astype(f32) + moe_back[at, :].astype(f32)
        moe_own[at, :] = (middle_ref[at, :] + moe_out).astype(bf16)
    net.keep(moe_own, output_hbm.at[own_rows])
    net.start(moe_own, output_hbm.at[own_rows], core_dev)

    for k in range(2):
        at = slice(k * part_size, (k + 1) * part_size)
        out_ref[at, :] = sums_out[k].step(0)
        value = sums_in[k].step(0)
        extra_sent[at, :] = value[:, :128]
        query_out[at, :] = value[:, 128 : 128 + heads_width]
        key_out[at, :] = value[:, 128 + heads_width : 128 + heads_width + HEAD_DIM]
        value_out[at, :] = value[:, 128 + heads_width + HEAD_DIM :]
    extra_copy = net.start(extra_sent, extra_got, core_dev)
    net.arrive(gate_last)
    gate_ref[...] += gate_s[...].astype(f32)
    net.arrive(up_last)
    up_ref[...] += up_x[...].astype(f32)
    net.arrive(down_last)
    down_ref[...] += down_s[...].astype(f32)
    net.arrive(extra_copy)
    extra_ref[...] = extra_sent[...] + extra_got[...]
    net.finish()


def backward_on_chip(
    lengths, row, dx, middle, probs, mask, out_grad, tokens, query, kv, lse, attended, cos, sin,
    in_full, out_full, moe_rows, gate_up, down, experts,
):
    far, near = token_bits()
    owners = lax.axis_size("fsdp") * lax.axis_size("ctx")
    half, width = middle.shape
    rows, heads_width = query.shape
    pack, kv_width = kv.shape
    units = down.shape[0] // 2
    block = in_full.shape[0] // owners
    in_width, out_width = in_full.shape[1], out_full.shape[1]
    any_spec = pl.BlockSpec(memory_space=pl.ANY)
    vmem = pl.BlockSpec(memory_space=pltpu.VMEM)
    smem = pl.BlockSpec(memory_space=pltpu.SMEM)

    def low(*shape):
        return pltpu.VMEM(shape, bf16)

    def wide(*shape):
        return pltpu.VMEM(shape, f32)

    boxes = 15 * (block // 2)
    return pl.pallas_call(
        functools.partial(backward_kernel, far, near, experts, heads_width // HEAD_DIM),
        name="backward",
        out_shape=(
            jax.ShapeDtypeStruct((rows, width), bf16),
            jax.ShapeDtypeStruct((8, 128), f32),
            jax.ShapeDtypeStruct((rows, width), f32),
            jax.ShapeDtypeStruct((block, heads_width), f32),
            jax.ShapeDtypeStruct((block, HEAD_DIM), f32),
            jax.ShapeDtypeStruct((block, HEAD_DIM), f32),
            jax.ShapeDtypeStruct((block, out_width), f32),
            jax.ShapeDtypeStruct((block, 128), f32),
            jax.ShapeDtypeStruct((width // 2, units), f32),
            jax.ShapeDtypeStruct((width // 2, units), f32),
            jax.ShapeDtypeStruct((units, width // 2), f32),
        ),
        in_specs=[smem] + [vmem] * 5 + [any_spec] * 4 + [vmem, any_spec, vmem, vmem] + [any_spec] * 5,
        out_specs=(any_spec, vmem, any_spec) + (vmem,) * 8,
        scratch_shapes=[
            low(half, width), low(rows, width), low(rows, heads_width), low(pack, kv_width), low(rows, heads_width),
            low(*in_full.shape), low(*out_full.shape),
            low(rows, width), low(rows, heads_width), low(rows, in_width - 128),
            wide(pack, kv_width), low(rows, kv_width), low(rows, kv_width),
            low(2, boxes, in_width), low(2, boxes, out_width),
            wide(half, width), low(half, width), low(half, width), wide(half, width),
            wide(128, width), wide(block, 128), wide(block, 128),
            low(half, width), low(half, width), low(half, width), low(half, width), low(half, width),
            low(width // 2, 2 * units), low(width // 2, 2 * units), low(width // 2, units), low(width // 2, units),
            low(width, units), low(width, units), low(width // 2, units), low(width // 2, units),
            low(2 * units, width // 2), low(2 * units, width // 2), low(units, width // 2), low(units, width // 2),
            wide(5, 8, 128), wide(5, 8, 128),
            pltpu.SemaphoreType.DMA((100,)),
            pltpu.SemaphoreType.DMA((100,)),
            pltpu.SemaphoreType.DMA((20,)),
        ],
        compiler_params=pltpu.CompilerParams(
            collective_id=2, has_side_effects=True, vmem_limit_bytes=62 * 1024 * 1024
        ),
    )(
        lengths, row, dx, middle, probs, mask, out_grad, tokens, query, kv, lse, attended, cos, sin,
        in_full, out_full, moe_rows, gate_up, down,
    )


def rms_back_gain(inverse, scaled, row_gains, upstream):
    return jnp.sum(upstream * scaled, axis=0), rms_back(inverse, scaled, row_gains, upstream)


def to_expert(arrived, local_experts, capacity):
    sources = arrived.shape[0]
    return (
        arrived.reshape(sources, local_experts, capacity, -1)
        .transpose(1, 0, 2, 3)
        .reshape(local_experts, sources * capacity, -1)
    )


def from_expert(expert_rows, sources, capacity):
    local_experts = expert_rows.shape[0]
    return (
        expert_rows.reshape(local_experts, sources, capacity, -1)
        .transpose(1, 0, 2, 3)
        .reshape(sources, local_experts * capacity, -1)
    )


def expert_forward(expert_rows, w_gate, w_up):
    gate_pre = jnp.einsum("erd,edf->erf", expert_rows, w_gate, preferred_element_type=jnp.float32)
    up_pre = jnp.einsum("erd,edf->erf", expert_rows, w_up, preferred_element_type=jnp.float32)
    hidden = (gate_pre * jax.nn.sigmoid(gate_pre) * up_pre).astype(jnp.bfloat16)
    return (gate_pre, up_pre, hidden)


def on_any_slice(
    tokens,
    lengths,
    routes,
    norm_attn,
    w_query,
    w_key,
    w_value,
    w_out,
    norm_moe,
    w_router,
    w_gate,
    w_up,
    w_down,
    out_grad,
    loss_grad,
):
    row_count, model_width = tokens.shape
    ctx_count = lax.axis_size("ctx")
    fsdp_count = lax.axis_size("fsdp")
    ctx_place = lax.axis_index("ctx")
    top_count = routes.shape[1]
    expert_count = w_router.shape[1]
    local_experts = w_gate.shape[0]
    capacity = 3 * row_count * top_count // (2 * expert_count)
    pack_count = row_count * ctx_count
    block_rows = min(512, row_count)
    base_row = ctx_place * row_count
    gain_attn, full_query, full_key, full_value, full_out, gain_moe, full_router = (
        lax.all_gather(norm_attn, ("fsdp", "ctx"), axis=0, tiled=True),
        lax.all_gather(w_query, ("fsdp", "ctx"), axis=0, tiled=True),
        lax.all_gather(w_key, ("fsdp", "ctx"), axis=0, tiled=True),
        lax.all_gather(w_value, ("fsdp", "ctx"), axis=0, tiled=True),
        lax.all_gather(w_out, ("fsdp", "ctx"), axis=1, tiled=True),
        lax.all_gather(norm_moe, ("fsdp", "ctx"), axis=0, tiled=True),
        lax.all_gather(w_router, ("fsdp", "ctx"), axis=0, tiled=True),
    )
    doc_ids, positions, doc_first = pack_layout(lengths[0], pack_count)
    own_positions = lax.dynamic_slice_in_dim(positions, base_row, row_count, 0)
    cos_table, sin_table = rope_tables(own_positions)
    x_float = tokens.astype(jnp.float32)
    attn_gain = gain_attn.astype(jnp.float32)
    inverse_attn, scaled_attn, normed_full = rms_parts(x_float, attn_gain)
    normed_attn = normed_full.astype(jnp.bfloat16)
    local_heads = full_query.shape[1] // HEAD_DIM
    local_kv = full_key.shape[1] // HEAD_DIM
    group_size = local_heads // local_kv
    query_raw = jnp.dot(normed_attn, full_query, preferred_element_type=jnp.float32).reshape(
        row_count, local_heads, HEAD_DIM
    )
    queries = rotate(query_raw, cos_table, sin_table).astype(jnp.bfloat16)
    key_raw = jnp.dot(normed_attn, full_key, preferred_element_type=jnp.float32).reshape(
        row_count, local_kv, HEAD_DIM
    )
    key_own = rotate(key_raw, cos_table, sin_table).astype(jnp.bfloat16)
    value_own = (
        jnp.dot(normed_attn, full_value, preferred_element_type=jnp.float32)
        .astype(jnp.bfloat16)
        .reshape(row_count, local_kv, HEAD_DIM)
    )
    pack_keys, pack_values = (
        lax.all_gather(key_own, "ctx", axis=0, tiled=True),
        lax.all_gather(value_own, "ctx", axis=0, tiled=True),
    )
    grouped = queries.reshape(row_count, local_kv, group_size, HEAD_DIM)
    mixed_full, log_total = attention_forward(
        grouped, pack_keys, pack_values, doc_ids, doc_first, base_row, block_rows
    )
    attended = mixed_full.astype(jnp.bfloat16)
    out_part = jnp.dot(attended, full_out, preferred_element_type=jnp.float32)
    attn_out = lax.psum(out_part, "tp")
    middle = x_float + attn_out
    moe_gain = gain_moe.astype(jnp.float32)
    inverse_moe, scaled_moe, normed_mid = rms_parts(middle, moe_gain)
    normed_moe = normed_mid.astype(jnp.bfloat16)
    logits = jnp.dot(normed_moe, full_router, preferred_element_type=jnp.float32)
    shifted = jnp.exp(logits - jnp.max(logits, axis=-1, keepdims=True))
    router_probs = shifted / jnp.sum(shifted, axis=-1, keepdims=True)
    expert_ids = jnp.arange(expert_count, dtype=jnp.int32)
    route_mask = (routes[:, :, None] == expert_ids[None, None, :]).astype(jnp.float32)
    chosen = jnp.sum(route_mask * router_probs[:, None, :], axis=-1)
    chosen_total = jnp.sum(chosen, axis=-1, keepdims=True)
    gate_weights = chosen / chosen_total
    counts_global, probs_global = lax.psum(
        (jnp.sum(route_mask, axis=(0, 1)), jnp.sum(router_probs, axis=0)), ("fsdp", "ctx")
    )
    token_total = pack_count * fsdp_count
    fraction = counts_global / (token_total * top_count)
    balance_loss = (expert_count * jnp.sum(fraction * (probs_global / token_total))).reshape(1)
    flat_routes = routes.reshape(-1)
    flat_mask = (flat_routes[:, None] == expert_ids[None, :]).astype(jnp.int32)
    slot_rank = jnp.sum(jnp.cumsum(flat_mask, axis=0) * flat_mask, axis=1) - 1
    slot_index = flat_routes * capacity + slot_rank
    buffer_rows = expert_count * capacity
    send_rows = (
        jnp.zeros((buffer_rows, model_width), jnp.bfloat16)
        .at[slot_index]
        .set(jnp.repeat(normed_moe, top_count, axis=0))
    )
    send_rows = send_rows.reshape(fsdp_count, local_experts * capacity, model_width)
    arrived = lax.all_to_all(send_rows, "fsdp", split_axis=0, concat_axis=0, tiled=True)
    expert_rows = to_expert(arrived, local_experts, capacity)
    gate_pre, up_pre, hidden = expert_forward(expert_rows, w_gate, w_up)
    expert_out = jnp.einsum(
        "erf,efd->erd", hidden, w_down, preferred_element_type=jnp.float32
    ).astype(jnp.bfloat16)
    returned = lax.all_to_all(
        from_expert(expert_out, fsdp_count, capacity),
        "fsdp",
        split_axis=0,
        concat_axis=0,
        tiled=True,
    )
    slot_values = returned.reshape(buffer_rows, model_width)[slot_index].reshape(
        row_count, top_count, model_width
    )
    moe_part = jnp.sum(gate_weights[:, :, None] * slot_values, axis=1)
    moe_out = lax.psum(moe_part.astype(jnp.bfloat16), "tp").astype(jnp.float32)
    output = (middle + moe_out).astype(jnp.bfloat16)
    upstream = out_grad.astype(jnp.float32)
    gate_dots = jnp.sum(slot_values * upstream[:, None, :], axis=-1)
    grad_slots = (
        (gate_weights[:, :, None] * upstream[:, None, :])
        .astype(jnp.bfloat16)
        .reshape(row_count * top_count, model_width)
    )
    grad_send = jnp.zeros((buffer_rows, model_width), jnp.bfloat16).at[slot_index].set(grad_slots)
    grad_send = grad_send.reshape(fsdp_count, local_experts * capacity, model_width)
    grad_arrived = lax.all_to_all(grad_send, "fsdp", split_axis=0, concat_axis=0, tiled=True)
    kept_gate, kept_up, kept_hidden = (gate_pre, up_pre, hidden)
    grad_expert = to_expert(grad_arrived, local_experts, capacity)
    grad_hidden = jnp.einsum(
        "erd,efd->erf", grad_expert, w_down, preferred_element_type=jnp.float32
    )
    down_grad = jnp.einsum(
        "erf,erd->efd", kept_hidden, grad_expert, preferred_element_type=jnp.float32
    )
    sigmoid_gate = jax.nn.sigmoid(kept_gate)
    grad_gate = (
        grad_hidden * kept_up * sigmoid_gate * (1.0 + kept_gate * (1.0 - sigmoid_gate))
    ).astype(jnp.bfloat16)
    grad_up = (grad_hidden * kept_gate * sigmoid_gate).astype(jnp.bfloat16)
    gate_grad_w = jnp.einsum(
        "erd,erf->edf", expert_rows, grad_gate, preferred_element_type=jnp.float32
    )
    up_grad_w = jnp.einsum("erd,erf->edf", expert_rows, grad_up, preferred_element_type=jnp.float32)
    grad_rows = jnp.einsum("erf,edf->erd", grad_gate, w_gate, preferred_element_type=jnp.float32)
    grad_rows = (
        grad_rows + jnp.einsum("erf,edf->erd", grad_up, w_up, preferred_element_type=jnp.float32)
    ).astype(jnp.bfloat16)
    grad_back = lax.all_to_all(
        from_expert(grad_rows, fsdp_count, capacity),
        "fsdp",
        split_axis=0,
        concat_axis=0,
        tiled=True,
    )
    grad_slot_rows = grad_back.reshape(buffer_rows, model_width)[slot_index].reshape(
        row_count, top_count, model_width
    )
    moe_in_part = jnp.sum(grad_slot_rows.astype(jnp.float32), axis=1)
    moe_in_grad, gate_grad = lax.psum((moe_in_part, gate_dots), "tp")
    weighted = jnp.sum(gate_grad * gate_weights, axis=-1, keepdims=True)
    chosen_grad = (gate_grad - weighted) / chosen_total
    prob_grad = (
        jnp.sum(route_mask * chosen_grad[:, :, None], axis=1)
        + loss_grad[0] * expert_count * fraction / token_total
    )
    logit_grad = router_probs * (
        prob_grad - jnp.sum(prob_grad * router_probs, axis=-1, keepdims=True)
    )
    router_grad = jnp.einsum(
        "td,te->de", normed_moe.astype(jnp.float32), logit_grad, precision=highest
    )
    moe_grad = moe_in_grad + jnp.einsum(
        "te,de->td", logit_grad, full_router.astype(jnp.float32), precision=highest
    )
    gain_moe_grad, middle_norm_grad = rms_back_gain(inverse_moe, scaled_moe, moe_gain, moe_grad)
    middle_grad = upstream + middle_norm_grad
    out_in = middle_grad.astype(jnp.bfloat16)
    out_w_grad = jnp.einsum("tq,td->qd", attended, out_in, preferred_element_type=jnp.float32)
    mixed_grad = jnp.einsum(
        "td,qd->tq", out_in, full_out, preferred_element_type=jnp.float32
    ).astype(jnp.bfloat16)
    query_acc, key_grad_pack, value_grad_pack = attention_backward(
        grouped,
        pack_keys,
        pack_values,
        mixed_grad,
        log_total,
        doc_ids,
        doc_first,
        base_row,
        block_rows,
    )
    key_grad, value_grad, gate_w_out, up_w_out, down_w_out = (
        lax.psum_scatter(key_grad_pack, "ctx", scatter_dimension=0, tiled=True),
        lax.psum_scatter(value_grad_pack, "ctx", scatter_dimension=0, tiled=True),
        lax.psum_scatter(gate_grad_w, "ctx", scatter_dimension=1, tiled=True),
        lax.psum_scatter(up_grad_w, "ctx", scatter_dimension=1, tiled=True),
        lax.psum_scatter(down_grad, "ctx", scatter_dimension=2, tiled=True),
    )
    query_grad = (
        rotate(query_acc.reshape(row_count, local_heads, HEAD_DIM), cos_table, -sin_table)
        .astype(jnp.bfloat16)
        .reshape(row_count, local_heads * HEAD_DIM)
    )
    key_grad_low = (
        rotate(key_grad, cos_table, -sin_table)
        .astype(jnp.bfloat16)
        .reshape(row_count, local_kv * HEAD_DIM)
    )
    value_grad_low = value_grad.astype(jnp.bfloat16).reshape(row_count, local_kv * HEAD_DIM)
    query_w_grad = jnp.einsum(
        "td,tq->dq", normed_attn, query_grad, preferred_element_type=jnp.float32
    )
    key_w_grad = jnp.einsum(
        "td,tq->dq", normed_attn, key_grad_low, preferred_element_type=jnp.float32
    )
    value_w_grad = jnp.einsum(
        "td,tq->dq", normed_attn, value_grad_low, preferred_element_type=jnp.float32
    )
    attn_in_part = jnp.einsum(
        "tq,dq->td", query_grad, full_query, preferred_element_type=jnp.float32
    )
    attn_in_part = attn_in_part + jnp.einsum(
        "tq,dq->td", key_grad_low, full_key, preferred_element_type=jnp.float32
    )
    attn_in_part = attn_in_part + jnp.einsum(
        "tq,dq->td", value_grad_low, full_value, preferred_element_type=jnp.float32
    )
    attn_in_grad = lax.psum(attn_in_part.astype(jnp.bfloat16), "tp").astype(jnp.float32)
    gain_attn_grad, input_norm_grad = rms_back_gain(inverse_attn, scaled_attn, attn_gain, attn_in_grad)
    tokens_grad = middle_grad + input_norm_grad
    shard_grads = (
        lax.psum_scatter(gain_attn_grad, ("fsdp", "ctx"), scatter_dimension=0, tiled=True),
        lax.psum_scatter(query_w_grad, ("fsdp", "ctx"), scatter_dimension=0, tiled=True),
        lax.psum_scatter(key_w_grad, ("fsdp", "ctx"), scatter_dimension=0, tiled=True),
        lax.psum_scatter(value_w_grad, ("fsdp", "ctx"), scatter_dimension=0, tiled=True),
        lax.psum_scatter(out_w_grad, ("fsdp", "ctx"), scatter_dimension=1, tiled=True),
        lax.psum_scatter(gain_moe_grad, ("fsdp", "ctx"), scatter_dimension=0, tiled=True),
        lax.psum_scatter(router_grad, ("fsdp", "ctx"), scatter_dimension=0, tiled=True),
    )
    return (
        output,
        balance_loss,
        tokens_grad,
        shard_grads[0],
        shard_grads[1],
        shard_grads[2],
        shard_grads[3],
        shard_grads[4],
        shard_grads[5],
        shard_grads[6],
        gate_w_out,
        up_w_out,
        down_w_out,
    )


def on_device(
    tokens,
    lengths,
    routes,
    norm_attn,
    w_query,
    w_key,
    w_value,
    w_out,
    norm_moe,
    w_router,
    w_gate,
    w_up,
    w_down,
    out_grad,
    loss_grad,
):
    expert_count = w_router.shape[1]
    if lax.axis_size("fsdp") != 8:
        return on_any_slice(
            tokens, lengths, routes, norm_attn, w_query, w_key, w_value, w_out, norm_moe, w_router,
            w_gate, w_up, w_down, out_grad, loss_grad,
        )
    small = widen([w_router, norm_attn[:, None], norm_moe[:, None]])
    (
        payload, middle, probs, mask, row, query, kv_pack, lse, attended, cos, sin,
        in_weights, out_weights, grad_rows, gate_all, up_all, down_all,
    ) = forward_on_chip(
        lengths, loss_grad, routes, tokens, small, w_query, w_key, w_value, w_out.T, out_grad,
        w_gate[0], w_up[0], w_down[0], expert_count,
    )
    returned, moe_rows, gate_up_grad, down_grad = experts_on_chip(
        payload, out_grad, w_gate[0], w_up[0], w_down[0], grad_rows, gate_all, up_all, down_all, expert_count
    )
    (
        output, loss, tokens_grad, query_grad, key_grad, value_grad, out_reduced, small, gate_w_out, up_w_out, down_w_out,
    ) = backward_on_chip(
        lengths, row, returned, middle, probs, mask, out_grad, tokens, query, kv_pack, lse, attended, cos, sin,
        in_weights, out_weights, moe_rows, gate_up_grad, down_grad, expert_count,
    )
    return (
        output,
        loss[0, :1],
        tokens_grad,
        small[:, expert_count],
        query_grad,
        key_grad,
        value_grad,
        out_reduced.T,
        small[:, expert_count + 1],
        small[:, :expert_count],
        gate_w_out[None],
        up_w_out[None],
        down_w_out[None],
    )


def solution(mesh):
    rows = P(("fsdp", "ctx"), None)
    gain = P(("fsdp", "ctx"))
    split = P(("fsdp", "ctx"), "tp")
    out_split = P("tp", ("fsdp", "ctx"))
    columns = P("fsdp", None, "tp")
    return jax.shard_map(
        on_device,
        mesh=mesh,
        in_specs=(
            rows,
            P("fsdp", None),
            rows,
            gain,
            split,
            split,
            split,
            out_split,
            gain,
            rows,
            columns,
            columns,
            P("fsdp", "tp", None),
            rows,
            P(),
        ),
        out_specs=(
            rows,
            P(),
            rows,
            gain,
            split,
            split,
            split,
            out_split,
            gain,
            rows,
            P("fsdp", "ctx", "tp"),
            P("fsdp", "ctx", "tp"),
            P("fsdp", "tp", "ctx"),
        ),
        check_vma=False,
    )
```

```python
import functools
import math

import jax
import jax.experimental.pallas as pl
import jax.experimental.pallas.tpu as pltpu
import jax.numpy as jnp
from jax import lax
from jax.sharding import PartitionSpec as P

HEAD_DIM = 128
SHARE = 2
epsilon = 1e-06
rope_base = 10000.0
masked_score = -1e30
highest = lax.Precision.HIGHEST
f32 = jnp.float32
bf16 = jnp.bfloat16


def rms_parts(values, row_gains):
    inverse = lax.rsqrt(jnp.mean(values * values, axis=-1, keepdims=True) + epsilon)
    scaled = values * inverse
    return (inverse, scaled, scaled * row_gains)


def rms_back(inverse, scaled, row_gains, upstream):
    scaled_grad = upstream * row_gains
    return inverse * (scaled_grad - scaled * jnp.mean(scaled_grad * scaled, axis=-1, keepdims=True))


def rope_tables(positions):
    half_dim = HEAD_DIM // 2
    frequency = rope_base ** (-(jnp.arange(half_dim, dtype=f32) * (2.0 / HEAD_DIM)))
    angles = positions.astype(f32)[:, None] * frequency[None, :]
    return (jnp.cos(angles)[:, None, :], jnp.sin(angles)[:, None, :])


def rotate(vectors, cos_table, sin_table):
    half_dim = vectors.shape[-1] // 2
    first_half = vectors[..., :half_dim]
    second_half = vectors[..., half_dim:]
    return jnp.concatenate(
        [
            first_half * cos_table - second_half * sin_table,
            second_half * cos_table + first_half * sin_table,
        ],
        axis=-1,
    )


def pack_layout(length_row, row_count):
    doc_ends = jnp.cumsum(length_row)
    doc_starts = doc_ends - length_row
    row_index = jnp.arange(row_count, dtype=jnp.int32)
    doc_ids = jnp.sum((row_index[:, None] >= doc_ends[None, :]).astype(jnp.int32), axis=1)
    doc_numbers = jnp.arange(length_row.shape[0], dtype=jnp.int32)
    doc_first = jnp.sum(
        jnp.where(doc_ids[:, None] == doc_numbers[None, :], doc_starts[None, :], 0), axis=1
    )
    return (doc_ids, row_index - doc_first, doc_first)


def key_block_data(key_number, block_rows, pack_keys, pack_values, doc_ids):
    key_start = key_number * block_rows
    key_block = lax.dynamic_slice_in_dim(pack_keys, key_start, block_rows, 0)
    value_block = lax.dynamic_slice_in_dim(pack_values, key_start, block_rows, 0)
    key_docs = lax.dynamic_slice_in_dim(doc_ids, key_start, block_rows, 0)
    key_index = key_start + jnp.arange(block_rows, dtype=jnp.int32)
    return (key_start, key_block, value_block, key_docs, key_index)


def block_scores(query_block, key_block, query_docs, query_index, key_docs, key_index):
    scale_factor = HEAD_DIM ** (-0.5)
    scores = (
        jnp.einsum("qhgd,khd->hgqk", query_block, key_block, preferred_element_type=f32)
        * scale_factor
    )
    allowed = (query_docs[:, None] == key_docs[None, :]) & (
        key_index[None, :] <= query_index[:, None]
    )
    return (scores, allowed)


def query_block_range(start_row, block_rows, doc_ids, doc_first):
    query_index = start_row + jnp.arange(block_rows, dtype=jnp.int32)
    query_docs = lax.dynamic_slice_in_dim(doc_ids, start_row, block_rows, 0)
    low_block = doc_first[start_row] // block_rows
    high_block = (start_row + block_rows - 1) // block_rows + 1
    return (query_index, query_docs, low_block, high_block)


def attention_forward(grouped, pack_keys, pack_values, doc_ids, doc_first, base_row, block_rows):
    row_count, local_kv, group_size, head_dim = grouped.shape
    query_index, query_docs, low_block, high_block = query_block_range(
        base_row, block_rows, doc_ids, doc_first
    )

    def scan_maxima(key_number, running):
        maxima, totals = running
        key_start, key_block, value_block, key_docs, key_index = key_block_data(
            key_number, block_rows, pack_keys, pack_values, doc_ids
        )
        scores, allowed = block_scores(
            grouped, key_block, query_docs, query_index, key_docs, key_index
        )
        new_max = jnp.maximum(maxima, jnp.max(jnp.where(allowed, scores, masked_score), axis=-1))
        weights = jnp.where(allowed, jnp.exp(scores - new_max[..., None]), 0.0)
        return (new_max, totals * jnp.exp(maxima - new_max) + jnp.sum(weights, axis=-1))

    start_max = jnp.full((local_kv, group_size, block_rows), masked_score, f32)
    start_total = jnp.zeros((local_kv, group_size, block_rows), f32)
    maxima, totals = lax.fori_loop(low_block, high_block, scan_maxima, (start_max, start_total))
    log_total = maxima + jnp.log(totals)

    def accumulate(key_number, summed):
        key_start, key_block, value_block, key_docs, key_index = key_block_data(
            key_number, block_rows, pack_keys, pack_values, doc_ids
        )
        scores, allowed = block_scores(
            grouped, key_block, query_docs, query_index, key_docs, key_index
        )
        block_probs = jnp.where(allowed, jnp.exp(scores - log_total[..., None]), 0.0).astype(bf16)
        return summed + jnp.einsum(
            "hgqk,khd->hgqd", block_probs, value_block, preferred_element_type=f32
        )

    summed = lax.fori_loop(
        low_block,
        high_block,
        accumulate,
        jnp.zeros((local_kv, group_size, block_rows, head_dim), f32),
    )
    outputs = summed.transpose(2, 0, 1, 3).reshape(block_rows, local_kv * group_size * head_dim)
    return (outputs, log_total)


def attention_backward(
    grouped, pack_keys, pack_values, grad_mixed, log_total, doc_ids, doc_first, base_row, block_rows
):
    row_count, local_kv, group_size, head_dim = grouped.shape
    pack_count = pack_keys.shape[0]
    scale_factor = HEAD_DIM ** (-0.5)
    grad_grouped = grad_mixed.reshape(row_count, local_kv, group_size, head_dim)
    key_acc = jnp.zeros((pack_count, local_kv, head_dim), f32)
    value_acc = jnp.zeros((pack_count, local_kv, head_dim), f32)
    query_index, query_docs, low_block, high_block = query_block_range(
        base_row, block_rows, doc_ids, doc_first
    )

    def probs_at(key_number):
        key_start, key_block, value_block, key_docs, key_index = key_block_data(
            key_number, block_rows, pack_keys, pack_values, doc_ids
        )
        scores, allowed = block_scores(
            grouped, key_block, query_docs, query_index, key_docs, key_index
        )
        block_probs = jnp.where(allowed, jnp.exp(scores - log_total[..., None]), 0.0)
        prob_grad = jnp.einsum(
            "qhgd,khd->hgqk", grad_grouped, value_block, preferred_element_type=f32
        )
        return (key_start, key_block, block_probs, prob_grad)

    def add_delta(key_number, row_delta):
        pieces = probs_at(key_number)
        return row_delta + jnp.sum(pieces[2] * pieces[3], axis=-1)

    row_delta = lax.fori_loop(
        low_block, high_block, add_delta, jnp.zeros((local_kv, group_size, block_rows), f32)
    )

    def add_grads(key_number, running):
        query_acc, key_total, value_total = running
        key_start, key_block, block_probs, prob_grad = probs_at(key_number)
        score_grad = (block_probs * (prob_grad - row_delta[..., None])).astype(bf16)
        query_acc = (
            query_acc
            + jnp.einsum("hgqk,khd->qhgd", score_grad, key_block, preferred_element_type=f32)
            * scale_factor
        )
        key_piece = (
            jnp.einsum("hgqk,qhgd->khd", score_grad, grouped, preferred_element_type=f32)
            * scale_factor
        )
        value_piece = jnp.einsum(
            "hgqk,qhgd->khd", block_probs.astype(bf16), grad_grouped, preferred_element_type=f32
        )
        key_total = lax.dynamic_update_slice_in_dim(
            key_total,
            lax.dynamic_slice_in_dim(key_total, key_start, block_rows, 0) + key_piece,
            key_start,
            0,
        )
        value_total = lax.dynamic_update_slice_in_dim(
            value_total,
            lax.dynamic_slice_in_dim(value_total, key_start, block_rows, 0) + value_piece,
            key_start,
            0,
        )
        return (query_acc, key_total, value_total)

    start_query = jnp.zeros((block_rows, local_kv, group_size, head_dim), f32)
    return lax.fori_loop(low_block, high_block, add_grads, (start_query, key_acc, value_acc))


def dot(left, right, left_dim=1, right_dim=0):
    return lax.dot_general(
        left, right, (((left_dim,), (right_dim,)), ((), ())), preferred_element_type=f32
    )


def swap(array, axis, bit=1):
    return lax.ppermute(array, axis, [(i, i ^ bit) for i in range(lax.axis_size(axis))])


def bit_at(axis, bit):
    return (lax.axis_index(axis) // bit) % 2


def side_by_side(mine, theirs, place, axis=0):
    first = jnp.where(place == 0, mine, theirs)
    return jnp.concatenate([first, jnp.where(place == 0, theirs, mine)], axis=axis)


def fsdp_bits():
    size = lax.axis_size("fsdp")
    return [size >> (k + 1) for k in range(size.bit_length() - 1)]


def weight_dims():
    return [("fsdp", bit) for bit in fsdp_bits()] + [("ctx", 1)]


def weight_orders():
    high = [("fsdp", bit) for bit in fsdp_bits()[:-1]]
    low, across = ("fsdp", 1), ("ctx", 1)
    return [high + [across, low], [across, low] + high, [low] + high + [across]]


def gather_rows(block, order):
    dims = weight_dims()
    held = block.reshape((1,) * len(dims) + block.shape)
    for dim in order:
        held = side_by_side(held, swap(held, *dim), bit_at(*dim), dims.index(dim))
    return held.reshape(-1, block.shape[-1])


def reduce_rows(full, order):
    dims = weight_dims()
    rows = full.shape[0] >> len(dims)
    held = full.reshape((2,) * len(dims) + (rows, full.shape[-1]))
    for dim in reversed(order):
        place, k = bit_at(*dim), dims.index(dim)
        sent = lax.dynamic_index_in_dim(held, 1 - place, k).astype(bf16)
        held = lax.dynamic_index_in_dim(held, place, k) + swap(sent, *dim).astype(f32)
    return held.reshape(rows, full.shape[-1])


def thirds(array, pieces):
    units = array.shape[-1] // 128
    ends = [units * k // pieces * 128 for k in range(pieces + 1)]
    return [array[..., a:b] for a, b in zip(ends[:-1], ends[1:])]


def gather_weights(block, orders):
    parts = thirds(block, len(orders))
    return jnp.concatenate([gather_rows(p, o) for p, o in zip(parts, orders)], axis=1)


def reduce_weights(full, orders):
    parts = thirds(full, len(orders))
    return jnp.concatenate([reduce_rows(p, o) for p, o in zip(parts, orders)], axis=1)


def token_bits():
    return [bit for bit in fsdp_bits() if bit != SHARE]


def gather_tokens(block):
    held = {0: block}
    for bit in token_bits():
        held.update({r ^ bit: swap(b, "fsdp", bit) for r, b in held.items()})
    return held


def reduce_tokens(parts):
    held = dict(parts)
    for bit in reversed(token_bits()):
        for r in sorted(held):
            if r & bit:
                got = swap(held.pop(r).astype(bf16), "fsdp", bit)
                held[r ^ bit] = held[r ^ bit] + got.astype(f32)
    return held[0]


def sum_everywhere(small):
    small = small + swap(small, "tp")
    small = small + swap(small, "ctx")
    for bit in fsdp_bits():
        small = small + swap(small, "fsdp", bit)
    return small


def as_pair(values):
    high = lax.reduce_precision(values, 8, 7)
    return [high.astype(bf16), (values - high).astype(bf16)]


def widen(columns):
    width = sum(c.shape[1] for c in columns)
    pad = jnp.zeros((columns[0].shape[0], -width % 128), columns[0].dtype)
    return jnp.concatenate(list(columns) + [pad], axis=1)


def from_pair(columns, count):
    return columns[:, :count].astype(f32) + columns[:, count : 2 * count].astype(f32)


def own_part(array, place, axis=0):
    size = array.shape[axis] // 2
    return lax.dynamic_slice_in_dim(array, place * size, size, axis)


def across_ctx(kept, axis=0):
    place = lax.axis_index("ctx")
    sent = own_part(kept, 1 - place, axis).astype(bf16)
    return own_part(kept, place, axis) + swap(sent, "ctx").astype(f32)


def across_share(kept, axis=1):
    size = kept.shape[axis] // 2
    own = lax.slice_in_dim(kept, 0, size, axis=axis)
    sent = lax.slice_in_dim(kept, size, None, axis=axis).astype(bf16)
    return own + swap(sent, "fsdp", SHARE).astype(f32)


MESH = pl.DeviceIdType.MESH


def peer(fsdp_bit=0, ctx_bit=0, tp_bit=0):
    return (
        lax.axis_index("fsdp") ^ fsdp_bit,
        lax.axis_index("ctx") ^ ctx_bit,
        lax.axis_index("tp") ^ tp_bit,
    )


def greet(peers):
    barrier = pltpu.get_barrier_semaphore()
    for who in peers:
        pl.semaphore_signal(barrier, inc=1, device_id=who, device_id_type=MESH)
    pl.semaphore_wait(barrier, len(peers))


def send(src, dst, sems, k, who):
    copy = pltpu.make_async_remote_copy(
        src_ref=src,
        dst_ref=dst,
        send_sem=sems[0].at[k],
        recv_sem=sems[1].at[k],
        device_id=who,
        device_id_type=MESH,
    )
    copy.start()
    return copy


def dot_nn(a, b):
    return lax.dot_general(a, b, (((1,), (0,)), ((), ())), preferred_element_type=f32)


def dot_nt(a, b):
    return lax.dot_general(a, b, (((1,), (1,)), ((), ())), preferred_element_type=f32)


def aligned(index, size):
    return pl.ds(pl.multiple_of(index * size, size), size)


TILE = 256
CHUNKS = 4


def token_rows(half):
    size = half // CHUNKS
    own = [pl.ds(k * size, size) for k in range(CHUNKS)]
    far = [pl.ds(2 * half + 2 * k * size, size) for k in range(CHUNKS)]
    cross = [pl.ds(2 * half + (2 * k + 1) * size, size) for k in range(CHUNKS)]
    return own, far, cross


class Exchange:
    def __init__(self, send_sems, recv_sems, local_sems):
        self.sems = (send_sems, recv_sems)
        self.local_sems = local_sems
        self.all = []
        self.local = []
        self.arrived = set()
        self.settled = set()
        self.gone = set()

    def start(self, src, dst, who):
        self.all.append(send(src, dst, self.sems, len(self.all), who))
        return len(self.all) - 1

    def keep(self, src, dst):
        copy = pltpu.make_async_copy(src, dst, self.local_sems.at[len(self.local)])
        copy.start()
        self.local.append(copy)
        return len(self.local) - 1

    def arrive(self, number):
        if number not in self.arrived:
            self.arrived.add(number)
            self.all[number].wait_recv()

    def settle(self, number):
        if number not in self.settled:
            self.settled.add(number)
            self.local[number].wait()

    def sent(self, number):
        if number not in self.gone:
            self.gone.add(number)
            self.all[number].wait_send()

    def finish(self):
        for number in range(len(self.all)):
            self.arrive(number)
        for number in range(len(self.all)):
            self.sent(number)
        for number in range(len(self.local)):
            self.settle(number)


class RowGather:
    def __init__(self, net, full, part, order):
        self.net, self.full, self.order = net, full, order
        self.rows, self.first, self.size = part
        self.copies = {}
        self.spread((0, 0), -1)

    def place(self, code):
        index = (lax.axis_index("fsdp") ^ code[0]) * 2 + (lax.axis_index("ctx") ^ code[1])
        return pl.ds(pl.multiple_of(index * self.rows + self.first, 16), self.size)

    def spread(self, code, last):
        block = self.full.at[self.place(code)]
        for position in range(last + 1, len(self.order)):
            axis, bit = self.order[position]
            other = (code[0] ^ bit, code[1]) if axis == "fsdp" else (code[0], code[1] ^ bit)
            self.copies[other] = (self.net.start(block, block, dim_peer((axis, bit))), position)

    def arrive(self, code):
        copy, position = self.copies[code]
        self.net.arrive(copy)
        self.spread(code, position)


def dim_peer(dim):
    axis, bit = dim
    return peer(bit if axis == "fsdp" else 0, bit if axis == "ctx" else 0)


def gather_codes(far, near):
    first = [(SHARE, 0), (far, 0), (far ^ SHARE, 0)]
    rest = [(0, 1), (near, 0), (near, 1)]
    later = [(a ^ b, c) for a, _ in first for b, c in rest]
    return first, rest[:2] + later[0:2] + [rest[2]] + later[3:5] + [later[2]] + later[6:8] + [later[5], later[8]]


def document_start(lengths_ref, number):
    start, first = 0, jnp.zeros_like(number)
    for k in range(lengths_ref.shape[1]):
        start = start + lengths_ref[0, k]
        first = jnp.where(number >= start, start, first)
    return first


def layer_kernel(
    far, near, experts, total_rows,
    lengths_ref, loss_grad_ref, routes_ref, tokens_ref, small_hbm, query_hbm, key_hbm, value_hbm, out_hbm,
    grad_hbm, gate_hbm, up_hbm, down_hbm,
    probs_ref, mask_ref, row_ref, lse_ref, cos_ref, sin_ref,
    dx_hbm, middle_hbm, query_hbm_out, kv_hbm, attended_hbm, in_out, out_out, part_hbm, sum_gu, sum_d,
    weights, xb, gb, wg, wu, wd, kv, h0, hw, dg, du, db, d0, near_in, near_sum, far_in,
    count_sent, count_got,
    send_sems, recv_sems, local_sems, stage_sems, tp_send, tp_recv, free_sem,
):
    far_dev, near_dev, share_dev = peer(far), peer(near), peer(SHARE)
    ctx_dev, core_dev = peer(0, 1), peer(0, 0, 1)
    net = Exchange(send_sems, recv_sems, local_sems)
    place, core = lax.axis_index("ctx"), lax.axis_index("tp")
    rows, width = tokens_ref.shape
    half, quarter = rows // 2, rows // 4
    units = 4 * gate_hbm.shape[1]
    block = small_hbm.shape[0]
    heads_width, kv_width = query_hbm.shape[1], key_hbm.shape[1]
    in_width = small_hbm.shape[1] + heads_width + 2 * kv_width
    in_full = weights.at[:, pl.ds(0, in_width)]
    out_full = weights.at[:, pl.ds(in_width, out_hbm.shape[1])]
    normed = dg.at[pl.ds(0, rows)]
    raw = h0.at[pl.ds(0, rows), pl.ds(0, in_width - 128)]
    core_sent = h0.at[pl.ds(rows, half)]
    middle_ref = h0.at[pl.ds(rows + half, half)]
    core_got = d0.at[:, pl.ds(0, width)]
    query = hw.at[pl.ds(0, rows), pl.ds(0, heads_width)]
    attended = hw.at[pl.ds(rows, rows), pl.ds(0, heads_width)]
    gate_all, up_all, down_all, grads = wg, wu, wd, gb
    own_block = pl.ds(pl.multiple_of((lax.axis_index("fsdp") * 2 + place) * block, 16), block)
    start = 0
    for ref in (small_hbm, query_hbm, key_hbm, value_hbm):
        net.keep(ref, in_full.at[own_block, pl.ds(start, ref.shape[1])])
        start += ref.shape[1]
    net.keep(out_hbm, out_full.at[own_block])
    greet([far_dev, near_dev, share_dev, ctx_dev, core_dev])
    for k in range(5):
        net.settle(k)
    fars = [("fsdp", far), ("fsdp", SHARE)]
    low, across = ("fsdp", near), ("ctx", 1)
    part = block // 2
    ins = [
        RowGather(net, in_full, (block, 0, part), fars + [across, low]),
        RowGather(net, in_full, (block, part, part), fars + [low, across]),
    ]

    routes = routes_ref[...]
    lane = lax.broadcasted_iota(jnp.int32, (rows, 128), 1)
    named = jnp.zeros((rows, 128), f32)
    for k in range(routes.shape[1]):
        named += (routes[:, k : k + 1] == lane).astype(f32)
    count_dims = [ctx_dev, near_dev, share_dev, far_dev]
    counts = [jnp.broadcast_to(jnp.sum(named, axis=0, keepdims=True), (8, 128))]
    count_copies = []

    def count_step():
        k = len(count_copies)
        if k > 0:
            net.arrive(count_copies[-1])
            counts[0] = counts[0] + count_got[k - 1]
        if k < len(count_dims):
            count_sent[k] = counts[0]
            count_copies.append(net.start(count_sent.at[k], count_got.at[k], count_dims[k]))

    count_step()

    piece = units // 4

    def slot(full, number, which=None):
        begin, size = (number * piece, piece) if full is down_all else (0, width)
        if which is not None:
            size //= 2
            begin = pl.multiple_of(begin + which * size, 16)
        if full is down_all:
            return full.at[pl.ds(begin, size)]
        return full.at[pl.ds(begin, size), pl.ds(number * piece, piece)]

    matrices = [(down_hbm, down_all), (gate_hbm, gate_all), (up_hbm, up_all)]
    from_core, own_weights = [], []
    for ref, full in matrices:
        own_weights.append(net.keep(ref, slot(full, 0)))
        from_core.append(net.start(ref, slot(full, 1), core_dev))

    from_share, from_ctx = [], []

    def share_start(k):
        ref, full = matrices[k]
        size = ref.shape[0] // 2
        part_of = ref.at[pl.ds(pl.multiple_of(place * size, 16), size)]
        from_share.append(net.start(part_of, slot(full, 2, place), share_dev))

    def share_on(k):
        ref, full = matrices[k]
        net.arrive(from_share[k])
        from_ctx.append(net.start(slot(full, 2, place), slot(full, 2, place), ctx_dev))
        from_core.append(net.start(slot(full, 2, place), slot(full, 3, place), core_dev))

    here = lax.broadcasted_iota(jnp.int32, (rows, 1), 0) + place * rows
    position = (here - document_start(lengths_ref, here)).astype(f32)
    turn_lane = lax.broadcasted_iota(jnp.int32, (1, HEAD_DIM), 1)
    turn = lax.rem(turn_lane, HEAD_DIM // 2).astype(f32) * (2.0 / HEAD_DIM)
    angles = position * jnp.exp(turn * -math.log(rope_base))
    cos_ref[...] = jnp.cos(angles)
    sin_ref[...] = jnp.where(turn_lane < HEAD_DIM // 2, -1.0, 1.0) * jnp.sin(angles)

    first, rest = gather_codes(far, near)
    for code in first:
        for g in ins:
            g.arrive(code)
    count_step()
    own_rows = pl.ds(pl.multiple_of(core * half, 16), half)
    other_rows = pl.ds(pl.multiple_of((1 - core) * half, 16), half)
    chunk = half // CHUNKS
    own_chunks = [pl.ds(pl.multiple_of(core * half + k * chunk, 16), chunk) for k in range(CHUNKS)]
    _, far_rows, cross_rows = token_rows(half)
    share_start(0)
    own_grad = net.keep(grad_hbm.at[own_rows], grads.at[pl.ds(0, half)])
    far_copies = [net.start(grad_hbm.at[own_chunks[k]], grads.at[far_rows[k]], far_dev) for k in range(CHUNKS)]
    from_near = []

    def cross_on(k):
        net.arrive(far_copies[k])
        from_near.append(net.start(grads.at[far_rows[k]], grads.at[cross_rows[k]], near_dev))

    for code in rest[:6]:
        for g in ins:
            g.arrive(code)
    for code in rest[6:]:
        for g in ins:
            g.arrive(code)
    count_step()
    net.arrive(from_share[0])
    share_start(1)
    outs = [
        RowGather(net, out_full, (block, 0, part), fars + [across, low]),
        RowGather(net, out_full, (block, part, part), fars + [low, across]),
    ]
    from_near.append(net.start(grad_hbm.at[own_rows], grads.at[pl.ds(half, half)], near_dev))
    gains = in_full[:, :128].astype(f32).T
    attn_gain, moe_gain = gains[experts : experts + 1], gains[experts + 1 : experts + 2]
    step = quarter // 2
    for k in range(rows // quarter):
        at = slice(k * quarter, (k + 1) * quarter)
        x = tokens_ref[at, :].astype(f32)
        inverse = lax.rsqrt(jnp.mean(x * x, axis=1, keepdims=True) + epsilon)
        normed[at, :] = (x * inverse * attn_gain).astype(bf16)

    def rotated(value, at):
        return value * cos_ref[at, :] + pltpu.roll(value, HEAD_DIM // 2, 1) * sin_ref[at, :]

    mine = pl.ds(pl.multiple_of(place * rows, 16), rows)
    raw[...] = dot_nn(normed[...], in_full[:, 128:])
    kv[mine, :kv_width] = rotated(raw[:, heads_width : heads_width + kv_width], slice(None)).astype(bf16)
    kv[mine, kv_width:] = raw[:, heads_width + kv_width :].astype(bf16)
    kv_copy = net.start(kv.at[mine], kv.at[mine], ctx_dev)
    for head in range(heads_width // HEAD_DIM):
        cols = slice(head * HEAD_DIM, (head + 1) * HEAD_DIM)
        query[:, cols] = rotated(raw[:, cols], slice(None)).astype(bf16)
    share_on(0)
    for code in first:
        for g in outs:
            g.arrive(code)
    count_step()
    net.arrive(kv_copy)
    net.keep(kv, kv_hbm)
    net.arrive(from_share[1])
    share_start(2)
    share_on(1)
    cross_on(0)

    keys, values_flipped = kv[:, :HEAD_DIM], kv[:, HEAD_DIM:].T
    query_number = lax.broadcasted_iota(jnp.int32, (1, half), 1) + place * rows
    key_number = lax.broadcasted_iota(jnp.int32, (kv.shape[0], 1), 0)
    scale = HEAD_DIM ** (-0.5)

    def head_block(i, carry):
        head, block_index = i // 2, lax.rem(i, 2)
        cols, at = aligned(head, HEAD_DIM), aligned(block_index, half)
        number = query_number + block_index * half
        allowed = (key_number >= document_start(lengths_ref, number)) & (key_number <= number)
        scores = jnp.where(allowed, dot_nt(keys, query[at, cols]) * scale, masked_score)
        maxima = jnp.max(scores, axis=0, keepdims=True)
        weights = jnp.exp(scores - maxima)
        totals = jnp.sum(weights, axis=0, keepdims=True)
        lse_ref[pl.ds(head, 1), at] = maxima + jnp.log(totals)
        low_weights = (weights * (1.0 / totals)).astype(bf16)
        attended[at, cols] = dot_nn(values_flipped, low_weights).T.astype(bf16)
        return carry

    group = heads_width // HEAD_DIM
    third = 2 * group // 3
    lax.fori_loop(0, third, head_block, 0)
    for code in rest[:6]:
        for g in outs:
            g.arrive(code)
    cross_on(1)
    lax.fori_loop(third, 2 * third, head_block, 0)
    for code in rest[6:]:
        for g in outs:
            g.arrive(code)
    cross_on(2)
    count_step()
    lax.fori_loop(2 * third, 2 * group, head_block, 0)
    cross_on(3)

    saved = [net.keep(query, query_hbm_out), net.keep(attended, attended_hbm)]

    core_sent[...] = dot_nt(attended[other_rows, :], out_full[...])
    core_copy = net.start(core_sent, core_got, core_dev)
    share_on(2)
    middle_ref[...] = tokens_ref[own_rows, :].astype(f32) + dot_nt(attended[own_rows, :], out_full[...])
    net.arrive(core_copy)
    own_lane = lax.broadcasted_iota(jnp.int32, (step, 128), 1)
    share_row = counts[0][0:1] * (experts / (total_rows * routes.shape[1] * total_rows))
    row_number = lax.broadcasted_iota(jnp.int32, (8, 128), 0)
    row_ref[...] = jnp.where(
        row_number == 0, share_row * loss_grad_ref[0], jnp.where(row_number == 1, share_row, 0.0)
    )
    router = in_full[:, :128]
    _, token_slots, _ = token_rows(half)
    token_far = []
    for k in range(half // step):
        at = slice(k * step, (k + 1) * step)
        middle = middle_ref[at, :] + core_got[at, :]
        middle_ref[at, :] = middle
        inverse = lax.rsqrt(jnp.mean(middle * middle, axis=1, keepdims=True) + epsilon)
        normed_moe = (middle * inverse * moe_gain).astype(bf16)
        xb[at, :width] = normed_moe
        logits = jnp.where(own_lane < experts, dot_nn(normed_moe, router), masked_score)
        shifted = jnp.exp(logits - jnp.max(logits, axis=1, keepdims=True))
        probs = shifted / jnp.sum(shifted, axis=1, keepdims=True)
        own_routes = routes_ref[pl.ds(pl.multiple_of(core * half + k * step, 16), step), :]
        mask = jnp.zeros((step, 128), f32)
        for n in range(routes.shape[1]):
            mask += (own_routes[:, n : n + 1] == own_lane).astype(f32)
        probs_ref[at, :] = probs
        mask_ref[at, :] = mask
        chosen = probs * mask
        gates = chosen / jnp.sum(chosen, axis=1, keepdims=True)
        high = gates.astype(bf16).astype(f32)
        xb[at, width:] = (high + pltpu.roll(gates - high, experts, 1)).astype(bf16)
        token_far.append(net.start(xb.at[pl.ds(k * step, step)], xb.at[token_slots[k]], far_dev))

    saved.append(net.keep(middle_ref, middle_hbm))
    token_near = net.start(xb.at[pl.ds(0, half)], xb.at[pl.ds(half, half)], near_dev)
    own_chunks, far_rows, cross_rows = token_rows(half)
    near_rows = pl.ds(half, half)
    forwards, crossed, backs = [], [], []

    def pass_on(k):
        net.arrive(token_far[k])
        forwards.append(net.start(xb.at[far_rows[k]], xb.at[cross_rows[k]], near_dev))

    def share_last(k):
        ref, full = matrices[k]
        net.arrive(from_ctx[k])
        from_core.append(net.start(slot(full, 2, 1 - place), slot(full, 3, 1 - place), core_dev))

    stored = [net.keep(in_full, in_out), net.keep(out_full, out_out)]
    share_last(0)
    share_last(1)
    for number in saved:
        net.settle(number)
    net.sent(core_copy)
    for copy in from_near:
        net.arrive(copy)
    net.settle(own_grad)
    net.settle(own_weights[0])
    for copy in (from_core[0], from_core[3], from_core[6]):
        net.arrive(copy)
    unit_tiles = units // TILE

    def back_tile(j, carry):
        h0[:, aligned(j, TILE)] = dot_nt(gb[...], wd[aligned(j, TILE), :])
        return carry

    lax.fori_loop(0, unit_tiles, back_tile, 0)
    pass_on(0)
    share_last(2)
    for copy in from_core:
        net.arrive(copy)
    for number in own_weights:
        net.settle(number)

    lane = lax.broadcasted_iota(jnp.int32, (half, 128), 1)
    own = lax.axis_index("fsdp")
    partner = own ^ SHARE

    def task(number):
        rows = pl.ds(number * half, half)
        extra = xb[rows, width:].astype(f32)

        def gate_of(expert):
            mine = (lane == expert) | (lane == experts + expert)
            return jnp.sum(jnp.where(mine, extra, 0.0), axis=1, keepdims=True)

        gates = jnp.concatenate([gate_of(own), gate_of(partner)], axis=1)

        def unit_tile(j, dots):
            cols = aligned(j, TILE)
            is_own = j < unit_tiles // 2
            gate = jnp.where(is_own, gates[:, :1], gates[:, 1:])
            x = xb[rows, :width]
            gate_pre = dot_nn(x, wg[:, cols])
            up_pre = dot_nn(x, wu[:, cols])
            back = h0[rows, cols]
            sig = 1.0 / (1.0 + jnp.exp(-gate_pre))
            silu = gate_pre * sig
            hidden = silu * up_pre
            hw[rows, cols] = (hidden * gate).astype(bf16)
            hidden_grad = back * gate
            dg[rows, cols] = (hidden_grad * up_pre * (sig * (1.0 + gate_pre * (1.0 - sig)))).astype(bf16)
            du[rows, cols] = (hidden_grad * silu).astype(bf16)
            one = jnp.sum(hidden * back, axis=1, keepdims=True)
            return (
                dots[0] + jnp.where(is_own, one, 0.0),
                dots[1] + jnp.where(is_own, 0.0, one),
            )

        zero = jnp.zeros((half, 1), f32)
        dots = lax.fori_loop(0, unit_tiles, unit_tile, (zero, zero), unroll=True)

        def put(cols, value):
            if number == 0:
                d0[:, cols] = value
            else:
                db[rows, cols] = value.astype(bf16)

        def in_tile(n, carry):
            cols = aligned(n, 2 * TILE)
            value = dot_nt(dg[rows, :], wg[cols, :]) + dot_nt(du[rows, :], wu[cols, :])
            put(cols, value)
            return carry

        lax.fori_loop(0, width // (2 * TILE), in_tile, 0, unroll=True)
        columns = jnp.zeros_like(extra)
        for expert, value in ((own, dots[0]), (partner, dots[1])):
            high = value.astype(bf16).astype(f32)
            columns = jnp.where(lane == expert, high, columns)
            columns = jnp.where(lane == experts + expert, value - high, columns)
        put(slice(width, None), columns)

    def cross_back(k):
        crossed.append(net.start(db.at[cross_rows[k]], near_in.at[own_chunks[k]], near_dev))

    def far_back(k):
        net.arrive(crossed[k])
        total = db[far_rows[k], :].astype(f32) + near_in[own_chunks[k], :].astype(f32)
        db[far_rows[k], :] = total.astype(bf16)
        backs.append(net.start(db.at[far_rows[k]], far_in.at[own_chunks[k]], far_dev))

    task(0)
    pass_on(1)
    pass_on(2)
    net.arrive(forwards[0])
    net.arrive(forwards[1])
    task(2)
    cross_back(0)
    cross_back(1)
    net.arrive(token_near)
    task(1)
    far_back(0)
    far_back(1)
    pass_on(3)
    net.arrive(forwards[2])
    net.arrive(forwards[3])
    task(3)
    cross_back(2)
    cross_back(3)
    near_back = net.start(db.at[near_rows], near_sum, near_dev)

    for copy in from_share + from_ctx + from_core:
        net.sent(copy)
    pl.semaphore_signal(free_sem, inc=1, device_id=core_dev, device_id_type=MESH)
    for g in ins + outs:
        for copy, _ in g.copies.values():
            net.sent(copy)
    for number in stored:
        net.settle(number)

    keep_rows, send_rows = 0, 2 * piece

    def stage_rows(base, slot, size):
        return pl.ds(pl.multiple_of(base + slot * piece, 16), size)

    tiles = width // TILE

    def to_core(slot, number, rows, size, got):
        return pltpu.make_async_remote_copy(
            src_ref=weights.at[stage_rows(send_rows, slot, size), pl.ds(0, width)],
            dst_ref=got.at[rows],
            send_sem=tp_send.at[slot],
            recv_sem=tp_recv.at[number],
            device_id=core_dev,
            device_id_type=MESH,
        )

    def to_hbm(slot, rows, size, full):
        return pltpu.make_async_copy(
            weights.at[stage_rows(keep_rows, slot, size), pl.ds(0, width)], full.at[rows], stage_sems.at[slot]
        )

    def gradient_loop(count, first, size, compute, got, full):
        def close(i):
            slot, rows = lax.rem(i, 2), aligned(i, size)
            to_core(slot, first + i, rows, size, got).wait_recv()
            at = stage_rows(keep_rows, slot, size)
            keep = weights[at, :width].astype(f32) + got[rows, :].astype(f32)
            weights[at, :width] = keep.astype(bf16)
            to_hbm(slot, rows, size, full).start()

        def free(slot):
            to_hbm(slot, pl.ds(0, size), size, full).wait()
            to_core(slot, 0, pl.ds(0, size), size, got).wait_send()

        def one(i, carry):
            slot = lax.rem(i, 2)

            @pl.when(i >= 2)
            def _():
                free(slot)

            compute(i, slot)
            to_core(slot, first + i, aligned(i, size), size, got).start()

            @pl.when(i >= 1)
            def _():
                close(i - 1)

            return carry

        lax.fori_loop(0, count, one, 0)
        close(count - 1)
        free(0)
        free(1)

    def gate_up_tile(i, slot):
        flipped = xb[:, aligned(i, TILE)].T
        for k, source in enumerate((dg, du)):
            value = dot_nn(flipped, source[...]).astype(bf16)
            for p in range(4):
                at = (2 * k + p // 2) * piece
                base = keep_rows if p % 2 == 0 else send_rows
                weights[stage_rows(base, slot, TILE), at : at + piece] = value[:, p * piece : (p + 1) * piece]

    def down_tile(i, slot):
        for base, offset in ((keep_rows, 0), (send_rows, piece)):
            cols = pl.ds(pl.multiple_of(i * 2 * piece + offset, 128), piece)
            flipped = hw[:, cols].T
            for n in range(0, width, 2 * TILE):
                weights[stage_rows(base, slot, piece), n : n + 2 * TILE] = dot_nn(flipped, gb[:, n : n + 2 * TILE]).astype(bf16)

    pl.semaphore_wait(free_sem, 1)
    gradient_loop(2, tiles, piece, down_tile, wg, sum_d)
    far_back(2)

    for k in range(4):
        at = slice(k * half, (k + 1) * half)
        hw[at, :] = dot_nn(hw[at, :], wd[...]).astype(bf16)
        if k == 1:
            far_back(3)
    net.keep(hw, part_hbm)
    gradient_loop(tiles, 0, TILE, gate_up_tile, wu, sum_gu)
    net.arrive(near_back)
    for copy in backs:
        net.arrive(copy)
    d0[...] = d0[...] + near_sum[...].astype(f32) + far_in[...].astype(f32)
    net.keep(d0, dx_hbm)
    net.finish()


def layer_on_chip(
    lengths, loss_grad, routes, tokens, small, w_query, w_key, w_value, out_block, out_grad, gate, up, down, experts
):
    far, near = token_bits()
    owners = lax.axis_size("fsdp") * lax.axis_size("ctx")
    rows, width = tokens.shape
    half, pack = rows // 2, rows * lax.axis_size("ctx")
    units, block = 4 * gate.shape[1], small.shape[0]
    heads_width, kv_width = w_query.shape[1], w_key.shape[1]
    in_width, out_width = small.shape[1] + heads_width + 2 * kv_width, out_block.shape[1]
    any_spec = pl.BlockSpec(memory_space=pl.ANY)
    vmem = pl.BlockSpec(memory_space=pltpu.VMEM)
    smem = pl.BlockSpec(memory_space=pltpu.SMEM)
    outs = [
        ((half, 128), f32),
        ((half, 128), f32),
        ((8, 128), f32),
        ((-(-heads_width // HEAD_DIM // 8) * 8, rows), f32),
        ((rows, HEAD_DIM), f32),
        ((rows, HEAD_DIM), f32),
        ((half, width + 128), f32),
        ((half, width), f32),
        ((rows, heads_width), bf16),
        ((pack, 2 * kv_width), bf16),
        ((rows, heads_width), bf16),
        ((owners * block, in_width), bf16),
        ((owners * block, out_width), bf16),
        ((2 * rows, width), bf16),
        ((width, units), bf16),
        ((units // 2, width), bf16),
    ]

    def low(*shape):
        return pltpu.VMEM(shape, bf16)

    def wide(*shape):
        return pltpu.VMEM(shape, f32)

    return pl.pallas_call(
        functools.partial(layer_kernel, far, near, experts, rows * owners),
        name="layer",
        out_shape=tuple(jax.ShapeDtypeStruct(s, d) for s, d in outs),
        in_specs=[smem, smem, vmem, vmem] + [any_spec] * 9,
        out_specs=(vmem,) * 6 + (any_spec,) * 10,
        scratch_shapes=[
            low(owners * block, in_width + out_width),
            low(2 * rows, width + 128),
            low(2 * rows, width),
            low(width, units),
            low(width, units),
            low(units, width),
            low(pack, 2 * kv_width),
            wide(2 * rows, units),
            low(2 * rows, units),
            low(2 * rows, units),
            low(2 * rows, units),
            low(2 * rows, width + 128),
            wide(half, width + 128),
            low(half, width + 128),
            low(half, width + 128),
            low(half, width + 128),
            wide(4, 8, 128),
            wide(4, 8, 128),
            pltpu.SemaphoreType.DMA((116,)),
            pltpu.SemaphoreType.DMA((116,)),
            pltpu.SemaphoreType.DMA((20,)),
            pltpu.SemaphoreType.DMA((2,)),
            pltpu.SemaphoreType.DMA((2,)),
            pltpu.SemaphoreType.DMA((width // TILE + 2,)),
            pltpu.SemaphoreType.REGULAR,
        ],
        compiler_params=pltpu.CompilerParams(
            collective_id=0, has_side_effects=True, vmem_limit_bytes=62 * 1024 * 1024
        ),
    )(lengths, loss_grad, routes, tokens, small, w_query, w_key, w_value, out_block, out_grad, gate, up, down)


class RowReduce:
    def __init__(self, net, partial, inbox, part, order):
        self.net, self.partial, self.inbox, self.order = net, partial, inbox, order
        self.rows, self.first, self.size = part
        self.copies = {}

    def place(self, mask):
        fsdp, ctx = 0, 0
        for position, (axis, bit) in enumerate(self.order):
            if mask >> position & 1:
                fsdp, ctx = (fsdp ^ bit, ctx) if axis == "fsdp" else (fsdp, ctx ^ bit)
        index = (lax.axis_index("fsdp") ^ fsdp) * 2 + (lax.axis_index("ctx") ^ ctx)
        return pl.ds(pl.multiple_of(index * self.rows + self.first, 16), self.size)

    def box(self, mask):
        return pl.ds((mask - 1) * self.size, self.size)

    def step(self, mask):
        rows, last = self.place(mask), mask.bit_length() - 1
        if last + 1 < len(self.order):
            value = self.partial[rows, :].astype(f32)
            for later in range(last + 1, len(self.order)):
                source = mask | 1 << later
                self.net.arrive(self.copies[source])
                value = value + self.inbox[self.box(source), :].astype(f32)
            if mask == 0:
                return value
            self.partial[rows, :] = value.astype(bf16)
        self.copies[mask] = self.net.start(
            self.partial.at[rows], self.inbox.at[self.box(mask)], dim_peer(self.order[last])
        )

    def level(self, last):
        for mask in reversed(range(1 << last, 2 << last)):
            self.step(mask)


def backward_kernel(
    far, near, experts, group,
    lengths_ref, row_ref, dx_ref, middle_ref, probs_ref, mask_ref, grad_hbm,
    tokens_hbm, query_hbm, kv_hbm, lse_ref, attended_hbm, cos_ref, sin_ref,
    in_hbm, out_hbm, moe_hbm, gu_hbm, down_hbm,
    output_hbm, loss_ref, tokens_grad_hbm, query_out, key_out, value_out, out_ref, extra_ref, gate_ref, up_ref, down_ref,
    grad_ref, tokens, query, kv, attended, in_full, out_full,
    out_in, att_grad, qkv_grad, kv_grad, kv_sent, kv_got,
    in_box, out_box,
    mid_grad, back_sent, back_got, tok_stage, extra_rows, extra_sent, extra_got,
    moe_own, moe_far, moe_near, moe_cross, moe_back,
    gate_own, gate_x, gate_sent, gate_s,
    up_own, up_s, up_sent, up_x,
    down_own, down_x, down_sent, down_s,
    loss_sent, loss_got,
    send_sems, recv_sems, local_sems,
):
    far_dev, near_dev, share_dev = peer(far), peer(near), peer(SHARE)
    ctx_dev, core_dev = peer(0, 1), peer(0, 0, 1)
    greet([far_dev, near_dev, share_dev, ctx_dev, core_dev])
    net = Exchange(send_sems, recv_sems, local_sems)
    ctx_place, core = lax.axis_index("ctx"), lax.axis_index("tp")
    half, width = middle_ref.shape
    rows = 2 * half
    quarter = half // 2
    own_rows = pl.ds(pl.multiple_of(core * half, 16), half)
    other_rows = pl.ds(pl.multiple_of((1 - core) * half, 16), half)
    chunks, far_rows, cross_rows = token_rows(half)

    crossed = [net.start(moe_hbm.at[cross_rows[k]], moe_cross.at[chunks[k]], near_dev) for k in range(CHUNKS)]
    units = gu_hbm.shape[1] // 4
    wide = width // 2

    def wide_half(place):
        return pl.ds(pl.multiple_of(place * wide, 128), wide)

    gate_cols, up_own_cols, up_par_cols = pl.ds(0, 2 * units), pl.ds(2 * units, units), pl.ds(3 * units, units)
    gate_first = net.start(gu_hbm.at[wide_half(1 - ctx_place), gate_cols], gate_x, ctx_dev)
    up_first = net.start(gu_hbm.at[:, up_par_cols], up_s, share_dev)
    pairs = [
        (in_hbm, in_full), (out_hbm, out_full), (attended_hbm, attended), (query_hbm, query),
        (kv_hbm, kv), (tokens_hbm, tokens), (moe_hbm.at[pl.ds(0, half)], moe_own),
        (gu_hbm.at[wide_half(ctx_place), gate_cols], gate_own), (gu_hbm.at[:, up_own_cols], up_own),
        (down_hbm.at[:, wide_half(ctx_place)], down_own), (grad_hbm.at[own_rows], grad_ref),
    ] + [(moe_hbm.at[far_rows[k]], moe_far.at[chunks[k]]) for k in range(CHUNKS)]
    for src, dst in pairs:
        net.keep(src, dst)

    def loaded(*numbers):
        for number in numbers:
            net.settle(number)

    def pieces(size):
        return [slice(k * size // 4, (k + 1) * size // 4) for k in range(4)]

    loaded(0, 10)
    flipped_extra = in_full[:, :128].astype(f32).T
    attn_gain, moe_gain = flipped_extra[experts : experts + 1], flipped_extra[experts + 1 : experts + 2]
    lane = lax.broadcasted_iota(jnp.int32, (half, 128), 1)
    probs, mask = probs_ref[...], mask_ref[...]
    pair = dx_ref[:, width:]
    gate_grad = jnp.where(lane < experts, pair + pltpu.roll(pair, 128 - experts, 1), 0.0)
    chosen = probs * mask
    chosen_total = jnp.sum(chosen, axis=1, keepdims=True)
    weighted = jnp.sum(gate_grad * chosen, axis=1, keepdims=True) / chosen_total
    prob_grad = mask * (gate_grad - weighted) / chosen_total + row_ref[0:1, :]
    logit_grad = probs * (prob_grad - jnp.sum(prob_grad * probs, axis=1, keepdims=True))
    logit_high = logit_grad.astype(bf16)
    logit_low = (logit_grad - logit_high.astype(f32)).astype(bf16)
    router = in_full[:, :128]
    step = quarter // 2
    gain_moe = jnp.zeros((1, width), f32)
    router_grad = jnp.zeros((128, width), f32)
    for k in range(half // step):
        at = slice(k * step, (k + 1) * step)
        middle = middle_ref[at, :]
        inverse = lax.rsqrt(jnp.mean(middle * middle, axis=1, keepdims=True) + epsilon)
        scaled = middle * inverse
        normed_moe = (scaled * moe_gain).astype(bf16)
        moe_grad = dx_ref[at, :width] + dot_nt(logit_high[at], router) + dot_nt(logit_low[at], router)
        router_grad += dot(logit_high[at], normed_moe, 0, 0) + dot(logit_low[at], normed_moe, 0, 0)
        gain_moe += jnp.sum(moe_grad * scaled, axis=0, keepdims=True)
        a = moe_grad * moe_gain
        grad = grad_ref[at, :].astype(f32) + inverse * (a - scaled * jnp.mean(a * scaled, axis=1, keepdims=True))
        mid_grad[at, :] = grad
        out_in[pl.ds(pl.multiple_of(core * half + k * step, 16), step), :] = grad.astype(bf16)
    out_in_copy = net.start(out_in.at[own_rows], out_in.at[own_rows], core_dev)
    row = lax.broadcasted_iota(jnp.int32, (128, width), 0)
    extra_rows[...] = jnp.where(row == experts + 1, gain_moe, router_grad)

    loss_dims = [core_dev, ctx_dev, near_dev, share_dev, far_dev]
    loss_state = [jnp.broadcast_to(jnp.sum(probs, axis=0, keepdims=True), (8, 128))]
    loss_copies = []

    def loss_step():
        k = len(loss_copies)
        if k > 0:
            net.arrive(loss_copies[-1])
            loss_state[0] = loss_state[0] + loss_got[k - 1]
        if k < len(loss_dims):
            loss_sent[k] = loss_state[0]
            loss_copies.append(net.start(loss_sent.at[k], loss_got.at[k], loss_dims[k]))

    loss_step()
    loaded(6, *range(11, 11 + CHUNKS))
    far_sums = []

    def far_sum(k):
        net.arrive(crossed[k])
        at = chunks[k]
        moe_far[at, :] = (moe_far[at, :].astype(f32) + moe_cross[at, :].astype(f32)).astype(bf16)
        far_sums.append(net.start(moe_far.at[at], moe_back.at[at], far_dev))

    far_sum(0)
    net.arrive(out_in_copy)
    loaded(1, 2)
    att_grad[...] = dot_nn(out_in[...], out_full[...]).astype(bf16)

    def out_tile(i, carry):
        cols = aligned(i, TILE)
        out_full[cols, :] = dot_nn(out_in[:, cols].T, attended[...]).astype(bf16)
        return carry

    lax.fori_loop(0, width // TILE, out_tile, 0)
    block = key_out.shape[0]
    low, across = ("fsdp", near), ("ctx", 1)
    fars = [("fsdp", far), ("fsdp", SHARE)]
    orders = [fars + [across, low], fars + [low, across]]
    part_size = block // 2
    sums_out = [
        RowReduce(net, out_full, out_box.at[k], (block, k * part_size, part_size), [across] + fars + [low])
        for k in range(2)
    ]
    far_sum(1)
    for s in sums_out:
        s.level(3)
    loss_step()
    far_sum(2)
    far_sum(3)
    net.sent(out_in_copy)
    loaded(5)
    normed_step = half // 2
    for k in range(rows // normed_step):
        at = slice(k * normed_step, (k + 1) * normed_step)
        x = tokens[at, :].astype(f32)
        inverse = lax.rsqrt(jnp.mean(x * x, axis=1, keepdims=True) + epsilon)
        out_in[at, :] = (x * inverse * attn_gain).astype(bf16)

    loaded(3, 4)
    pack = kv.shape[0]
    kv_grad[...] = jnp.zeros_like(kv_grad)
    keys, values = kv[:, :HEAD_DIM], kv[:, HEAD_DIM:]
    keys_flipped = keys.T
    query_number = lax.broadcasted_iota(jnp.int32, (1, half), 1) + ctx_place * rows
    key_number = lax.broadcasted_iota(jnp.int32, (pack, 1), 0)
    scale = HEAD_DIM ** (-0.5)

    def head_block(i, carry):
        head, block_index = i // 2, lax.rem(i, 2)
        cols = aligned(head, HEAD_DIM)
        at = aligned(block_index, half)
        number = query_number + block_index * half
        allowed = (key_number >= document_start(lengths_ref, number)) & (key_number <= number)
        q, grad = query[at, cols], att_grad[at, cols]
        log_total = lse_ref[pl.ds(head, 1), at]
        weights = jnp.where(allowed, jnp.exp(dot_nt(keys, q) * scale - log_total), 0.0)
        weight_grad = dot_nt(values, grad)
        delta = jnp.sum(weights * weight_grad, axis=0, keepdims=True)
        score_grad = (weights * (weight_grad - delta)).astype(bf16)
        kv_grad[:, :HEAD_DIM] += dot_nn(score_grad, q) * scale
        kv_grad[:, HEAD_DIM:] += dot_nn(weights.astype(bf16), grad)
        query_grad = (dot_nn(keys_flipped, score_grad) * scale).T
        turned = query_grad * cos_ref[at, :] - pltpu.roll(query_grad, HEAD_DIM // 2, 1) * sin_ref[at, :]
        qkv_grad[at, cols] = turned.astype(bf16)
        return carry

    third = 2 * group // 3
    lax.fori_loop(0, third, head_block, 0)
    loss_step()
    down_first = net.start(down_hbm.at[:, wide_half(1 - ctx_place)], down_x, ctx_dev)
    lax.fori_loop(third, 2 * third, head_block, 0)
    loss_step()
    loaded(7, 8, 9)
    net.arrive(gate_first)
    for at in pieces(wide):
        total = gate_own[at, :].astype(f32) + gate_x[at, :].astype(f32)
        gate_ref[at, :] = total[:, :units]
        gate_sent[at, :] = total[:, units:].astype(bf16)
    gate_last = net.start(gate_sent, gate_s, share_dev)
    net.arrive(up_first)
    up_sent[...] = (up_own[wide_half(1 - ctx_place), :].astype(f32) + up_s[wide_half(1 - ctx_place), :].astype(f32)).astype(bf16)
    up_ref[...] = up_own[wide_half(ctx_place), :].astype(f32) + up_s[wide_half(ctx_place), :].astype(f32)
    lax.fori_loop(2 * third, 2 * group, head_block, 0)
    loss_step()
    ctx_rows = pl.ds(pl.multiple_of(ctx_place * rows, 16), rows)
    ctx_other = pl.ds(pl.multiple_of((1 - ctx_place) * rows, 16), rows)
    kv_sent[...] = kv_grad[ctx_other, :].astype(bf16)
    kv_copy = net.start(kv_sent, kv_got, ctx_dev)
    up_last = net.start(up_sent, up_x, ctx_dev)
    for mask in (7, 6, 5, 4):
        for s in sums_out:
            s.step(mask)
    near_first = net.start(moe_hbm.at[pl.ds(half, half)], moe_near, near_dev)
    loss_step()
    loss = jnp.sum(loss_state[0][0:1] * row_ref[1:2, :], axis=1, keepdims=True)
    loss_ref[...] = jnp.broadcast_to(loss, loss_ref.shape)
    net.arrive(kv_copy)
    kv_sum = kv_grad[ctx_rows, :] + kv_got[...].astype(f32)
    key_grad = kv_sum[:, :HEAD_DIM]
    key_grad = key_grad * cos_ref[...] - pltpu.roll(key_grad, HEAD_DIM // 2, 1) * sin_ref[...]
    heads_width = group * HEAD_DIM
    qkv_grad[:, heads_width : heads_width + HEAD_DIM] = key_grad.astype(bf16)
    qkv_grad[:, heads_width + HEAD_DIM :] = kv_sum[:, HEAD_DIM:].astype(bf16)

    gain_attn = jnp.zeros((1, width), f32)

    def attn_scaled(at):
        x = tokens[at, :].astype(f32)
        inverse = lax.rsqrt(jnp.mean(x * x, axis=1, keepdims=True) + epsilon)
        return inverse, x * inverse

    for k in range(2):
        at = other_rows if k == 0 else own_rows
        part = dot_nt(qkv_grad[at, :], in_full[:, 128:])
        gain_attn += jnp.sum(part * attn_scaled(at)[1], axis=0, keepdims=True)
        if k == 0:
            back_sent[...] = part.astype(bf16)
            back_copy = net.start(back_sent, back_got, core_dev)
        else:
            tok_stage[...] = part
    def in_tile(i, carry):
        cols = aligned(i, TILE)
        in_full[cols, 128:] = dot_nn(out_in[:, cols].T, qkv_grad[...]).astype(bf16)
        return carry

    lax.fori_loop(0, width // TILE, in_tile, 0)
    extra_rows[...] = jnp.where(row == experts, gain_attn, extra_rows[...])
    in_full[:, :128] = extra_rows[...].T.astype(bf16)
    sums_in = [
        RowReduce(net, in_full, in_box.at[k], (block, k * part_size, part_size), orders[k]) for k in range(2)
    ]
    for s in sums_in:
        s.level(3)
    for mask in (3, 2):
        for s in sums_out:
            s.step(mask)

    net.arrive(back_copy)
    for k in range(2):
        at = pl.ds(k * quarter, quarter)
        inverse, scaled = attn_scaled(pl.ds(pl.multiple_of(core * half + k * quarter, 16), quarter))
        a = (tok_stage[at, :] + back_got[at, :].astype(f32)) * attn_gain
        tok_stage[at, :] = mid_grad[at, :] + inverse * (a - scaled * jnp.mean(a * scaled, axis=1, keepdims=True))
    net.keep(tok_stage, tokens_grad_hbm.at[own_rows])
    net.start(tok_stage, tokens_grad_hbm.at[own_rows], core_dev)

    for mask in (7, 6, 5, 4):
        for s in sums_in:
            s.step(mask)
    for s in sums_out:
        s.step(1)
    net.arrive(down_first)
    for at in pieces(units):
        down_ref[at, :] = down_own[at, :].astype(f32) + down_x[at, :].astype(f32)
        after = slice(at.start + units, at.stop + units)
        down_sent[at, :] = (down_own[after, :].astype(f32) + down_x[after, :].astype(f32)).astype(bf16)
    down_last = net.start(down_sent, down_s, share_dev)
    for mask in (3, 2, 1):
        for s in sums_in:
            s.step(mask)

    net.arrive(near_first)
    for k in range(CHUNKS):
        net.arrive(far_sums[k])
        at = chunks[k]
        moe_out = moe_own[at, :].astype(f32) + moe_near[at, :].astype(f32) + moe_back[at, :].astype(f32)
        moe_own[at, :] = (middle_ref[at, :] + moe_out).astype(bf16)
    net.keep(moe_own, output_hbm.at[own_rows])
    net.start(moe_own, output_hbm.at[own_rows], core_dev)

    for k in range(2):
        at = slice(k * part_size, (k + 1) * part_size)
        out_ref[at, :] = sums_out[k].step(0)
        value = sums_in[k].step(0)
        extra_sent[at, :] = value[:, :128]
        query_out[at, :] = value[:, 128 : 128 + heads_width]
        key_out[at, :] = value[:, 128 + heads_width : 128 + heads_width + HEAD_DIM]
        value_out[at, :] = value[:, 128 + heads_width + HEAD_DIM :]
    extra_copy = net.start(extra_sent, extra_got, core_dev)
    net.arrive(gate_last)
    gate_ref[...] += gate_s[...].astype(f32)
    net.arrive(up_last)
    up_ref[...] += up_x[...].astype(f32)
    net.arrive(down_last)
    down_ref[...] += down_s[...].astype(f32)
    net.arrive(extra_copy)
    extra_ref[...] = extra_sent[...] + extra_got[...]
    net.finish()


def backward_on_chip(
    lengths, row, dx, middle, probs, mask, out_grad, tokens, query, kv, lse, attended, cos, sin,
    in_full, out_full, moe_rows, gate_up, down, experts,
):
    far, near = token_bits()
    owners = lax.axis_size("fsdp") * lax.axis_size("ctx")
    half, width = middle.shape
    rows, heads_width = query.shape
    pack, kv_width = kv.shape
    units = down.shape[0] // 2
    block = in_full.shape[0] // owners
    in_width, out_width = in_full.shape[1], out_full.shape[1]
    any_spec = pl.BlockSpec(memory_space=pl.ANY)
    vmem = pl.BlockSpec(memory_space=pltpu.VMEM)
    smem = pl.BlockSpec(memory_space=pltpu.SMEM)

    def low(*shape):
        return pltpu.VMEM(shape, bf16)

    def wide(*shape):
        return pltpu.VMEM(shape, f32)

    boxes = 15 * (block // 2)
    return pl.pallas_call(
        functools.partial(backward_kernel, far, near, experts, heads_width // HEAD_DIM),
        name="backward",
        out_shape=(
            jax.ShapeDtypeStruct((rows, width), bf16),
            jax.ShapeDtypeStruct((8, 128), f32),
            jax.ShapeDtypeStruct((rows, width), f32),
            jax.ShapeDtypeStruct((block, heads_width), f32),
            jax.ShapeDtypeStruct((block, HEAD_DIM), f32),
            jax.ShapeDtypeStruct((block, HEAD_DIM), f32),
            jax.ShapeDtypeStruct((block, out_width), f32),
            jax.ShapeDtypeStruct((block, 128), f32),
            jax.ShapeDtypeStruct((width // 2, units), f32),
            jax.ShapeDtypeStruct((width // 2, units), f32),
            jax.ShapeDtypeStruct((units, width // 2), f32),
        ),
        in_specs=[smem] + [vmem] * 5 + [any_spec] * 4 + [vmem, any_spec, vmem, vmem] + [any_spec] * 5,
        out_specs=(any_spec, vmem, any_spec) + (vmem,) * 8,
        scratch_shapes=[
            low(half, width), low(rows, width), low(rows, heads_width), low(pack, kv_width), low(rows, heads_width),
            low(*in_full.shape), low(*out_full.shape),
            low(rows, width), low(rows, heads_width), low(rows, in_width - 128),
            wide(pack, kv_width), low(rows, kv_width), low(rows, kv_width),
            low(2, boxes, in_width), low(2, boxes, out_width),
            wide(half, width), low(half, width), low(half, width), wide(half, width),
            wide(128, width), wide(block, 128), wide(block, 128),
            low(half, width), low(half, width), low(half, width), low(half, width), low(half, width),
            low(width // 2, 2 * units), low(width // 2, 2 * units), low(width // 2, units), low(width // 2, units),
            low(width, units), low(width, units), low(width // 2, units), low(width // 2, units),
            low(2 * units, width // 2), low(2 * units, width // 2), low(units, width // 2), low(units, width // 2),
            wide(5, 8, 128), wide(5, 8, 128),
            pltpu.SemaphoreType.DMA((100,)),
            pltpu.SemaphoreType.DMA((100,)),
            pltpu.SemaphoreType.DMA((20,)),
        ],
        compiler_params=pltpu.CompilerParams(
            collective_id=2, has_side_effects=True, vmem_limit_bytes=62 * 1024 * 1024
        ),
    )(
        lengths, row, dx, middle, probs, mask, out_grad, tokens, query, kv, lse, attended, cos, sin,
        in_full, out_full, moe_rows, gate_up, down,
    )


def rms_back_gain(inverse, scaled, row_gains, upstream):
    return jnp.sum(upstream * scaled, axis=0), rms_back(inverse, scaled, row_gains, upstream)


def to_expert(arrived, local_experts, capacity):
    sources = arrived.shape[0]
    return (
        arrived.reshape(sources, local_experts, capacity, -1)
        .transpose(1, 0, 2, 3)
        .reshape(local_experts, sources * capacity, -1)
    )


def from_expert(expert_rows, sources, capacity):
    local_experts = expert_rows.shape[0]
    return (
        expert_rows.reshape(local_experts, sources, capacity, -1)
        .transpose(1, 0, 2, 3)
        .reshape(sources, local_experts * capacity, -1)
    )


def expert_forward(expert_rows, w_gate, w_up):
    gate_pre = jnp.einsum("erd,edf->erf", expert_rows, w_gate, preferred_element_type=jnp.float32)
    up_pre = jnp.einsum("erd,edf->erf", expert_rows, w_up, preferred_element_type=jnp.float32)
    hidden = (gate_pre * jax.nn.sigmoid(gate_pre) * up_pre).astype(jnp.bfloat16)
    return (gate_pre, up_pre, hidden)


def on_any_slice(
    tokens,
    lengths,
    routes,
    norm_attn,
    w_query,
    w_key,
    w_value,
    w_out,
    norm_moe,
    w_router,
    w_gate,
    w_up,
    w_down,
    out_grad,
    loss_grad,
):
    row_count, model_width = tokens.shape
    ctx_count = lax.axis_size("ctx")
    fsdp_count = lax.axis_size("fsdp")
    ctx_place = lax.axis_index("ctx")
    top_count = routes.shape[1]
    expert_count = w_router.shape[1]
    local_experts = w_gate.shape[0]
    capacity = 3 * row_count * top_count // (2 * expert_count)
    pack_count = row_count * ctx_count
    block_rows = min(512, row_count)
    base_row = ctx_place * row_count
    gain_attn, full_query, full_key, full_value, full_out, gain_moe, full_router = (
        lax.all_gather(norm_attn, ("fsdp", "ctx"), axis=0, tiled=True),
        lax.all_gather(w_query, ("fsdp", "ctx"), axis=0, tiled=True),
        lax.all_gather(w_key, ("fsdp", "ctx"), axis=0, tiled=True),
        lax.all_gather(w_value, ("fsdp", "ctx"), axis=0, tiled=True),
        lax.all_gather(w_out, ("fsdp", "ctx"), axis=1, tiled=True),
        lax.all_gather(norm_moe, ("fsdp", "ctx"), axis=0, tiled=True),
        lax.all_gather(w_router, ("fsdp", "ctx"), axis=0, tiled=True),
    )
    doc_ids, positions, doc_first = pack_layout(lengths[0], pack_count)
    own_positions = lax.dynamic_slice_in_dim(positions, base_row, row_count, 0)
    cos_table, sin_table = rope_tables(own_positions)
    x_float = tokens.astype(jnp.float32)
    attn_gain = gain_attn.astype(jnp.float32)
    inverse_attn, scaled_attn, normed_full = rms_parts(x_float, attn_gain)
    normed_attn = normed_full.astype(jnp.bfloat16)
    local_heads = full_query.shape[1] // HEAD_DIM
    local_kv = full_key.shape[1] // HEAD_DIM
    group_size = local_heads // local_kv
    query_raw = jnp.dot(normed_attn, full_query, preferred_element_type=jnp.float32).reshape(
        row_count, local_heads, HEAD_DIM
    )
    queries = rotate(query_raw, cos_table, sin_table).astype(jnp.bfloat16)
    key_raw = jnp.dot(normed_attn, full_key, preferred_element_type=jnp.float32).reshape(
        row_count, local_kv, HEAD_DIM
    )
    key_own = rotate(key_raw, cos_table, sin_table).astype(jnp.bfloat16)
    value_own = (
        jnp.dot(normed_attn, full_value, preferred_element_type=jnp.float32)
        .astype(jnp.bfloat16)
        .reshape(row_count, local_kv, HEAD_DIM)
    )
    pack_keys, pack_values = (
        lax.all_gather(key_own, "ctx", axis=0, tiled=True),
        lax.all_gather(value_own, "ctx", axis=0, tiled=True),
    )
    grouped = queries.reshape(row_count, local_kv, group_size, HEAD_DIM)
    mixed_full, log_total = attention_forward(
        grouped, pack_keys, pack_values, doc_ids, doc_first, base_row, block_rows
    )
    attended = mixed_full.astype(jnp.bfloat16)
    out_part = jnp.dot(attended, full_out, preferred_element_type=jnp.float32)
    attn_out = lax.psum(out_part, "tp")
    middle = x_float + attn_out
    moe_gain = gain_moe.astype(jnp.float32)
    inverse_moe, scaled_moe, normed_mid = rms_parts(middle, moe_gain)
    normed_moe = normed_mid.astype(jnp.bfloat16)
    logits = jnp.dot(normed_moe, full_router, preferred_element_type=jnp.float32)
    shifted = jnp.exp(logits - jnp.max(logits, axis=-1, keepdims=True))
    router_probs = shifted / jnp.sum(shifted, axis=-1, keepdims=True)
    expert_ids = jnp.arange(expert_count, dtype=jnp.int32)
    route_mask = (routes[:, :, None] == expert_ids[None, None, :]).astype(jnp.float32)
    chosen = jnp.sum(route_mask * router_probs[:, None, :], axis=-1)
    chosen_total = jnp.sum(chosen, axis=-1, keepdims=True)
    gate_weights = chosen / chosen_total
    counts_global, probs_global = lax.psum(
        (jnp.sum(route_mask, axis=(0, 1)), jnp.sum(router_probs, axis=0)), ("fsdp", "ctx")
    )
    token_total = pack_count * fsdp_count
    fraction = counts_global / (token_total * top_count)
    balance_loss = (expert_count * jnp.sum(fraction * (probs_global / token_total))).reshape(1)
    flat_routes = routes.reshape(-1)
    flat_mask = (flat_routes[:, None] == expert_ids[None, :]).astype(jnp.int32)
    slot_rank = jnp.sum(jnp.cumsum(flat_mask, axis=0) * flat_mask, axis=1) - 1
    slot_index = flat_routes * capacity + slot_rank
    buffer_rows = expert_count * capacity
    send_rows = (
        jnp.zeros((buffer_rows, model_width), jnp.bfloat16)
        .at[slot_index]
        .set(jnp.repeat(normed_moe, top_count, axis=0))
    )
    send_rows = send_rows.reshape(fsdp_count, local_experts * capacity, model_width)
    arrived = lax.all_to_all(send_rows, "fsdp", split_axis=0, concat_axis=0, tiled=True)
    expert_rows = to_expert(arrived, local_experts, capacity)
    gate_pre, up_pre, hidden = expert_forward(expert_rows, w_gate, w_up)
    expert_out = jnp.einsum(
        "erf,efd->erd", hidden, w_down, preferred_element_type=jnp.float32
    ).astype(jnp.bfloat16)
    returned = lax.all_to_all(
        from_expert(expert_out, fsdp_count, capacity),
        "fsdp",
        split_axis=0,
        concat_axis=0,
        tiled=True,
    )
    slot_values = returned.reshape(buffer_rows, model_width)[slot_index].reshape(
        row_count, top_count, model_width
    )
    moe_part = jnp.sum(gate_weights[:, :, None] * slot_values, axis=1)
    moe_out = lax.psum(moe_part.astype(jnp.bfloat16), "tp").astype(jnp.float32)
    output = (middle + moe_out).astype(jnp.bfloat16)
    upstream = out_grad.astype(jnp.float32)
    gate_dots = jnp.sum(slot_values * upstream[:, None, :], axis=-1)
    grad_slots = (
        (gate_weights[:, :, None] * upstream[:, None, :])
        .astype(jnp.bfloat16)
        .reshape(row_count * top_count, model_width)
    )
    grad_send = jnp.zeros((buffer_rows, model_width), jnp.bfloat16).at[slot_index].set(grad_slots)
    grad_send = grad_send.reshape(fsdp_count, local_experts * capacity, model_width)
    grad_arrived = lax.all_to_all(grad_send, "fsdp", split_axis=0, concat_axis=0, tiled=True)
    kept_gate, kept_up, kept_hidden = (gate_pre, up_pre, hidden)
    grad_expert = to_expert(grad_arrived, local_experts, capacity)
    grad_hidden = jnp.einsum(
        "erd,efd->erf", grad_expert, w_down, preferred_element_type=jnp.float32
    )
    down_grad = jnp.einsum(
        "erf,erd->efd", kept_hidden, grad_expert, preferred_element_type=jnp.float32
    )
    sigmoid_gate = jax.nn.sigmoid(kept_gate)
    grad_gate = (
        grad_hidden * kept_up * sigmoid_gate * (1.0 + kept_gate * (1.0 - sigmoid_gate))
    ).astype(jnp.bfloat16)
    grad_up = (grad_hidden * kept_gate * sigmoid_gate).astype(jnp.bfloat16)
    gate_grad_w = jnp.einsum(
        "erd,erf->edf", expert_rows, grad_gate, preferred_element_type=jnp.float32
    )
    up_grad_w = jnp.einsum("erd,erf->edf", expert_rows, grad_up, preferred_element_type=jnp.float32)
    grad_rows = jnp.einsum("erf,edf->erd", grad_gate, w_gate, preferred_element_type=jnp.float32)
    grad_rows = (
        grad_rows + jnp.einsum("erf,edf->erd", grad_up, w_up, preferred_element_type=jnp.float32)
    ).astype(jnp.bfloat16)
    grad_back = lax.all_to_all(
        from_expert(grad_rows, fsdp_count, capacity),
        "fsdp",
        split_axis=0,
        concat_axis=0,
        tiled=True,
    )
    grad_slot_rows = grad_back.reshape(buffer_rows, model_width)[slot_index].reshape(
        row_count, top_count, model_width
    )
    moe_in_part = jnp.sum(grad_slot_rows.astype(jnp.float32), axis=1)
    moe_in_grad, gate_grad = lax.psum((moe_in_part, gate_dots), "tp")
    weighted = jnp.sum(gate_grad * gate_weights, axis=-1, keepdims=True)
    chosen_grad = (gate_grad - weighted) / chosen_total
    prob_grad = (
        jnp.sum(route_mask * chosen_grad[:, :, None], axis=1)
        + loss_grad[0] * expert_count * fraction / token_total
    )
    logit_grad = router_probs * (
        prob_grad - jnp.sum(prob_grad * router_probs, axis=-1, keepdims=True)
    )
    router_grad = jnp.einsum(
        "td,te->de", normed_moe.astype(jnp.float32), logit_grad, precision=highest
    )
    moe_grad = moe_in_grad + jnp.einsum(
        "te,de->td", logit_grad, full_router.astype(jnp.float32), precision=highest
    )
    gain_moe_grad, middle_norm_grad = rms_back_gain(inverse_moe, scaled_moe, moe_gain, moe_grad)
    middle_grad = upstream + middle_norm_grad
    out_in = middle_grad.astype(jnp.bfloat16)
    out_w_grad = jnp.einsum("tq,td->qd", attended, out_in, preferred_element_type=jnp.float32)
    mixed_grad = jnp.einsum(
        "td,qd->tq", out_in, full_out, preferred_element_type=jnp.float32
    ).astype(jnp.bfloat16)
    query_acc, key_grad_pack, value_grad_pack = attention_backward(
        grouped,
        pack_keys,
        pack_values,
        mixed_grad,
        log_total,
        doc_ids,
        doc_first,
        base_row,
        block_rows,
    )
    key_grad, value_grad, gate_w_out, up_w_out, down_w_out = (
        lax.psum_scatter(key_grad_pack, "ctx", scatter_dimension=0, tiled=True),
        lax.psum_scatter(value_grad_pack, "ctx", scatter_dimension=0, tiled=True),
        lax.psum_scatter(gate_grad_w, "ctx", scatter_dimension=1, tiled=True),
        lax.psum_scatter(up_grad_w, "ctx", scatter_dimension=1, tiled=True),
        lax.psum_scatter(down_grad, "ctx", scatter_dimension=2, tiled=True),
    )
    query_grad = (
        rotate(query_acc.reshape(row_count, local_heads, HEAD_DIM), cos_table, -sin_table)
        .astype(jnp.bfloat16)
        .reshape(row_count, local_heads * HEAD_DIM)
    )
    key_grad_low = (
        rotate(key_grad, cos_table, -sin_table)
        .astype(jnp.bfloat16)
        .reshape(row_count, local_kv * HEAD_DIM)
    )
    value_grad_low = value_grad.astype(jnp.bfloat16).reshape(row_count, local_kv * HEAD_DIM)
    query_w_grad = jnp.einsum(
        "td,tq->dq", normed_attn, query_grad, preferred_element_type=jnp.float32
    )
    key_w_grad = jnp.einsum(
        "td,tq->dq", normed_attn, key_grad_low, preferred_element_type=jnp.float32
    )
    value_w_grad = jnp.einsum(
        "td,tq->dq", normed_attn, value_grad_low, preferred_element_type=jnp.float32
    )
    attn_in_part = jnp.einsum(
        "tq,dq->td", query_grad, full_query, preferred_element_type=jnp.float32
    )
    attn_in_part = attn_in_part + jnp.einsum(
        "tq,dq->td", key_grad_low, full_key, preferred_element_type=jnp.float32
    )
    attn_in_part = attn_in_part + jnp.einsum(
        "tq,dq->td", value_grad_low, full_value, preferred_element_type=jnp.float32
    )
    attn_in_grad = lax.psum(attn_in_part.astype(jnp.bfloat16), "tp").astype(jnp.float32)
    gain_attn_grad, input_norm_grad = rms_back_gain(inverse_attn, scaled_attn, attn_gain, attn_in_grad)
    tokens_grad = middle_grad + input_norm_grad
    shard_grads = (
        lax.psum_scatter(gain_attn_grad, ("fsdp", "ctx"), scatter_dimension=0, tiled=True),
        lax.psum_scatter(query_w_grad, ("fsdp", "ctx"), scatter_dimension=0, tiled=True),
        lax.psum_scatter(key_w_grad, ("fsdp", "ctx"), scatter_dimension=0, tiled=True),
        lax.psum_scatter(value_w_grad, ("fsdp", "ctx"), scatter_dimension=0, tiled=True),
        lax.psum_scatter(out_w_grad, ("fsdp", "ctx"), scatter_dimension=1, tiled=True),
        lax.psum_scatter(gain_moe_grad, ("fsdp", "ctx"), scatter_dimension=0, tiled=True),
        lax.psum_scatter(router_grad, ("fsdp", "ctx"), scatter_dimension=0, tiled=True),
    )
    return (
        output,
        balance_loss,
        tokens_grad,
        shard_grads[0],
        shard_grads[1],
        shard_grads[2],
        shard_grads[3],
        shard_grads[4],
        shard_grads[5],
        shard_grads[6],
        gate_w_out,
        up_w_out,
        down_w_out,
    )


def on_device(
    tokens,
    lengths,
    routes,
    norm_attn,
    w_query,
    w_key,
    w_value,
    w_out,
    norm_moe,
    w_router,
    w_gate,
    w_up,
    w_down,
    out_grad,
    loss_grad,
):
    expert_count = w_router.shape[1]
    if lax.axis_size("fsdp") != 8:
        return on_any_slice(
            tokens, lengths, routes, norm_attn, w_query, w_key, w_value, w_out, norm_moe, w_router,
            w_gate, w_up, w_down, out_grad, loss_grad,
        )
    small = widen([w_router, norm_attn[:, None], norm_moe[:, None]])
    (
        probs, mask, row, lse, cos, sin, returned, middle, query, kv_pack, attended,
        in_weights, out_weights, moe_rows, gate_up_grad, down_grad,
    ) = layer_on_chip(
        lengths, loss_grad, routes, tokens, small, w_query, w_key, w_value, w_out.T, out_grad,
        w_gate[0], w_up[0], w_down[0], expert_count,
    )
    (
        output, loss, tokens_grad, query_grad, key_grad, value_grad, out_reduced, small, gate_w_out, up_w_out, down_w_out,
    ) = backward_on_chip(
        lengths, row, returned, middle, probs, mask, out_grad, tokens, query, kv_pack, lse, attended, cos, sin,
        in_weights, out_weights, moe_rows, gate_up_grad, down_grad, expert_count,
    )
    return (
        output,
        loss[0, :1],
        tokens_grad,
        small[:, expert_count],
        query_grad,
        key_grad,
        value_grad,
        out_reduced.T,
        small[:, expert_count + 1],
        small[:, :expert_count],
        gate_w_out[None],
        up_w_out[None],
        down_w_out[None],
    )


def solution(mesh):
    rows = P(("fsdp", "ctx"), None)
    gain = P(("fsdp", "ctx"))
    split = P(("fsdp", "ctx"), "tp")
    out_split = P("tp", ("fsdp", "ctx"))
    columns = P("fsdp", None, "tp")
    return jax.shard_map(
        on_device,
        mesh=mesh,
        in_specs=(
            rows,
            P("fsdp", None),
            rows,
            gain,
            split,
            split,
            split,
            out_split,
            gain,
            rows,
            columns,
            columns,
            P("fsdp", "tp", None),
            rows,
            P(),
        ),
        out_specs=(
            rows,
            P(),
            rows,
            gain,
            split,
            split,
            split,
            out_split,
            gain,
            rows,
            P("fsdp", "ctx", "tp"),
            P("fsdp", "ctx", "tp"),
            P("fsdp", "tp", "ctx"),
        ),
        check_vma=False,
    )
```

```python
import functools
import math

import jax
import jax.experimental.pallas as pl
import jax.experimental.pallas.tpu as pltpu
import jax.numpy as jnp
from jax import lax
from jax.sharding import PartitionSpec as P

HEAD_DIM = 128
SHARE = 2
epsilon = 1e-06
rope_base = 10000.0
masked_score = -1e30
highest = lax.Precision.HIGHEST
f32 = jnp.float32
bf16 = jnp.bfloat16


def rms_parts(values, row_gains):
    inverse = lax.rsqrt(jnp.mean(values * values, axis=-1, keepdims=True) + epsilon)
    scaled = values * inverse
    return (inverse, scaled, scaled * row_gains)


def rms_back(inverse, scaled, row_gains, upstream):
    scaled_grad = upstream * row_gains
    return inverse * (scaled_grad - scaled * jnp.mean(scaled_grad * scaled, axis=-1, keepdims=True))


def rope_tables(positions):
    half_dim = HEAD_DIM // 2
    frequency = rope_base ** (-(jnp.arange(half_dim, dtype=f32) * (2.0 / HEAD_DIM)))
    angles = positions.astype(f32)[:, None] * frequency[None, :]
    return (jnp.cos(angles)[:, None, :], jnp.sin(angles)[:, None, :])


def rotate(vectors, cos_table, sin_table):
    half_dim = vectors.shape[-1] // 2
    first_half = vectors[..., :half_dim]
    second_half = vectors[..., half_dim:]
    return jnp.concatenate(
        [
            first_half * cos_table - second_half * sin_table,
            second_half * cos_table + first_half * sin_table,
        ],
        axis=-1,
    )


def pack_layout(length_row, row_count):
    doc_ends = jnp.cumsum(length_row)
    doc_starts = doc_ends - length_row
    row_index = jnp.arange(row_count, dtype=jnp.int32)
    doc_ids = jnp.sum((row_index[:, None] >= doc_ends[None, :]).astype(jnp.int32), axis=1)
    doc_numbers = jnp.arange(length_row.shape[0], dtype=jnp.int32)
    doc_first = jnp.sum(
        jnp.where(doc_ids[:, None] == doc_numbers[None, :], doc_starts[None, :], 0), axis=1
    )
    return (doc_ids, row_index - doc_first, doc_first)


def key_block_data(key_number, block_rows, pack_keys, pack_values, doc_ids):
    key_start = key_number * block_rows
    key_block = lax.dynamic_slice_in_dim(pack_keys, key_start, block_rows, 0)
    value_block = lax.dynamic_slice_in_dim(pack_values, key_start, block_rows, 0)
    key_docs = lax.dynamic_slice_in_dim(doc_ids, key_start, block_rows, 0)
    key_index = key_start + jnp.arange(block_rows, dtype=jnp.int32)
    return (key_start, key_block, value_block, key_docs, key_index)


def block_scores(query_block, key_block, query_docs, query_index, key_docs, key_index):
    scale_factor = HEAD_DIM ** (-0.5)
    scores = (
        jnp.einsum("qhgd,khd->hgqk", query_block, key_block, preferred_element_type=f32)
        * scale_factor
    )
    allowed = (query_docs[:, None] == key_docs[None, :]) & (
        key_index[None, :] <= query_index[:, None]
    )
    return (scores, allowed)


def query_block_range(start_row, block_rows, doc_ids, doc_first):
    query_index = start_row + jnp.arange(block_rows, dtype=jnp.int32)
    query_docs = lax.dynamic_slice_in_dim(doc_ids, start_row, block_rows, 0)
    low_block = doc_first[start_row] // block_rows
    high_block = (start_row + block_rows - 1) // block_rows + 1
    return (query_index, query_docs, low_block, high_block)


def attention_forward(grouped, pack_keys, pack_values, doc_ids, doc_first, base_row, block_rows):
    row_count, local_kv, group_size, head_dim = grouped.shape
    query_index, query_docs, low_block, high_block = query_block_range(
        base_row, block_rows, doc_ids, doc_first
    )

    def scan_maxima(key_number, running):
        maxima, totals = running
        key_start, key_block, value_block, key_docs, key_index = key_block_data(
            key_number, block_rows, pack_keys, pack_values, doc_ids
        )
        scores, allowed = block_scores(
            grouped, key_block, query_docs, query_index, key_docs, key_index
        )
        new_max = jnp.maximum(maxima, jnp.max(jnp.where(allowed, scores, masked_score), axis=-1))
        weights = jnp.where(allowed, jnp.exp(scores - new_max[..., None]), 0.0)
        return (new_max, totals * jnp.exp(maxima - new_max) + jnp.sum(weights, axis=-1))

    start_max = jnp.full((local_kv, group_size, block_rows), masked_score, f32)
    start_total = jnp.zeros((local_kv, group_size, block_rows), f32)
    maxima, totals = lax.fori_loop(low_block, high_block, scan_maxima, (start_max, start_total))
    log_total = maxima + jnp.log(totals)

    def accumulate(key_number, summed):
        key_start, key_block, value_block, key_docs, key_index = key_block_data(
            key_number, block_rows, pack_keys, pack_values, doc_ids
        )
        scores, allowed = block_scores(
            grouped, key_block, query_docs, query_index, key_docs, key_index
        )
        block_probs = jnp.where(allowed, jnp.exp(scores - log_total[..., None]), 0.0).astype(bf16)
        return summed + jnp.einsum(
            "hgqk,khd->hgqd", block_probs, value_block, preferred_element_type=f32
        )

    summed = lax.fori_loop(
        low_block,
        high_block,
        accumulate,
        jnp.zeros((local_kv, group_size, block_rows, head_dim), f32),
    )
    outputs = summed.transpose(2, 0, 1, 3).reshape(block_rows, local_kv * group_size * head_dim)
    return (outputs, log_total)


def attention_backward(
    grouped, pack_keys, pack_values, grad_mixed, log_total, doc_ids, doc_first, base_row, block_rows
):
    row_count, local_kv, group_size, head_dim = grouped.shape
    pack_count = pack_keys.shape[0]
    scale_factor = HEAD_DIM ** (-0.5)
    grad_grouped = grad_mixed.reshape(row_count, local_kv, group_size, head_dim)
    key_acc = jnp.zeros((pack_count, local_kv, head_dim), f32)
    value_acc = jnp.zeros((pack_count, local_kv, head_dim), f32)
    query_index, query_docs, low_block, high_block = query_block_range(
        base_row, block_rows, doc_ids, doc_first
    )

    def probs_at(key_number):
        key_start, key_block, value_block, key_docs, key_index = key_block_data(
            key_number, block_rows, pack_keys, pack_values, doc_ids
        )
        scores, allowed = block_scores(
            grouped, key_block, query_docs, query_index, key_docs, key_index
        )
        block_probs = jnp.where(allowed, jnp.exp(scores - log_total[..., None]), 0.0)
        prob_grad = jnp.einsum(
            "qhgd,khd->hgqk", grad_grouped, value_block, preferred_element_type=f32
        )
        return (key_start, key_block, block_probs, prob_grad)

    def add_delta(key_number, row_delta):
        pieces = probs_at(key_number)
        return row_delta + jnp.sum(pieces[2] * pieces[3], axis=-1)

    row_delta = lax.fori_loop(
        low_block, high_block, add_delta, jnp.zeros((local_kv, group_size, block_rows), f32)
    )

    def add_grads(key_number, running):
        query_acc, key_total, value_total = running
        key_start, key_block, block_probs, prob_grad = probs_at(key_number)
        score_grad = (block_probs * (prob_grad - row_delta[..., None])).astype(bf16)
        query_acc = (
            query_acc
            + jnp.einsum("hgqk,khd->qhgd", score_grad, key_block, preferred_element_type=f32)
            * scale_factor
        )
        key_piece = (
            jnp.einsum("hgqk,qhgd->khd", score_grad, grouped, preferred_element_type=f32)
            * scale_factor
        )
        value_piece = jnp.einsum(
            "hgqk,qhgd->khd", block_probs.astype(bf16), grad_grouped, preferred_element_type=f32
        )
        key_total = lax.dynamic_update_slice_in_dim(
            key_total,
            lax.dynamic_slice_in_dim(key_total, key_start, block_rows, 0) + key_piece,
            key_start,
            0,
        )
        value_total = lax.dynamic_update_slice_in_dim(
            value_total,
            lax.dynamic_slice_in_dim(value_total, key_start, block_rows, 0) + value_piece,
            key_start,
            0,
        )
        return (query_acc, key_total, value_total)

    start_query = jnp.zeros((block_rows, local_kv, group_size, head_dim), f32)
    return lax.fori_loop(low_block, high_block, add_grads, (start_query, key_acc, value_acc))


def dot(left, right, left_dim=1, right_dim=0):
    return lax.dot_general(
        left, right, (((left_dim,), (right_dim,)), ((), ())), preferred_element_type=f32
    )


def swap(array, axis, bit=1):
    return lax.ppermute(array, axis, [(i, i ^ bit) for i in range(lax.axis_size(axis))])


def bit_at(axis, bit):
    return (lax.axis_index(axis) // bit) % 2


def side_by_side(mine, theirs, place, axis=0):
    first = jnp.where(place == 0, mine, theirs)
    return jnp.concatenate([first, jnp.where(place == 0, theirs, mine)], axis=axis)


def fsdp_bits():
    size = lax.axis_size("fsdp")
    return [size >> (k + 1) for k in range(size.bit_length() - 1)]


def weight_dims():
    return [("fsdp", bit) for bit in fsdp_bits()] + [("ctx", 1)]


def weight_orders():
    high = [("fsdp", bit) for bit in fsdp_bits()[:-1]]
    low, across = ("fsdp", 1), ("ctx", 1)
    return [high + [across, low], [across, low] + high, [low] + high + [across]]


def gather_rows(block, order):
    dims = weight_dims()
    held = block.reshape((1,) * len(dims) + block.shape)
    for dim in order:
        held = side_by_side(held, swap(held, *dim), bit_at(*dim), dims.index(dim))
    return held.reshape(-1, block.shape[-1])


def reduce_rows(full, order):
    dims = weight_dims()
    rows = full.shape[0] >> len(dims)
    held = full.reshape((2,) * len(dims) + (rows, full.shape[-1]))
    for dim in reversed(order):
        place, k = bit_at(*dim), dims.index(dim)
        sent = lax.dynamic_index_in_dim(held, 1 - place, k).astype(bf16)
        held = lax.dynamic_index_in_dim(held, place, k) + swap(sent, *dim).astype(f32)
    return held.reshape(rows, full.shape[-1])


def thirds(array, pieces):
    units = array.shape[-1] // 128
    ends = [units * k // pieces * 128 for k in range(pieces + 1)]
    return [array[..., a:b] for a, b in zip(ends[:-1], ends[1:])]


def gather_weights(block, orders):
    parts = thirds(block, len(orders))
    return jnp.concatenate([gather_rows(p, o) for p, o in zip(parts, orders)], axis=1)


def reduce_weights(full, orders):
    parts = thirds(full, len(orders))
    return jnp.concatenate([reduce_rows(p, o) for p, o in zip(parts, orders)], axis=1)


def token_bits():
    return [bit for bit in fsdp_bits() if bit != SHARE]


def gather_tokens(block):
    held = {0: block}
    for bit in token_bits():
        held.update({r ^ bit: swap(b, "fsdp", bit) for r, b in held.items()})
    return held


def reduce_tokens(parts):
    held = dict(parts)
    for bit in reversed(token_bits()):
        for r in sorted(held):
            if r & bit:
                got = swap(held.pop(r).astype(bf16), "fsdp", bit)
                held[r ^ bit] = held[r ^ bit] + got.astype(f32)
    return held[0]


def sum_everywhere(small):
    small = small + swap(small, "tp")
    small = small + swap(small, "ctx")
    for bit in fsdp_bits():
        small = small + swap(small, "fsdp", bit)
    return small


def as_pair(values):
    high = lax.reduce_precision(values, 8, 7)
    return [high.astype(bf16), (values - high).astype(bf16)]


def widen(columns):
    width = sum(c.shape[1] for c in columns)
    pad = jnp.zeros((columns[0].shape[0], -width % 128), columns[0].dtype)
    return jnp.concatenate(list(columns) + [pad], axis=1)


def from_pair(columns, count):
    return columns[:, :count].astype(f32) + columns[:, count : 2 * count].astype(f32)


def own_part(array, place, axis=0):
    size = array.shape[axis] // 2
    return lax.dynamic_slice_in_dim(array, place * size, size, axis)


def across_ctx(kept, axis=0):
    place = lax.axis_index("ctx")
    sent = own_part(kept, 1 - place, axis).astype(bf16)
    return own_part(kept, place, axis) + swap(sent, "ctx").astype(f32)


def across_share(kept, axis=1):
    size = kept.shape[axis] // 2
    own = lax.slice_in_dim(kept, 0, size, axis=axis)
    sent = lax.slice_in_dim(kept, size, None, axis=axis).astype(bf16)
    return own + swap(sent, "fsdp", SHARE).astype(f32)


MESH = pl.DeviceIdType.MESH


def peer(fsdp_bit=0, ctx_bit=0, tp_bit=0):
    return (
        lax.axis_index("fsdp") ^ fsdp_bit,
        lax.axis_index("ctx") ^ ctx_bit,
        lax.axis_index("tp") ^ tp_bit,
    )


def greet(peers):
    barrier = pltpu.get_barrier_semaphore()
    for who in peers:
        pl.semaphore_signal(barrier, inc=1, device_id=who, device_id_type=MESH)
    pl.semaphore_wait(barrier, len(peers))


def send(src, dst, sems, k, who):
    copy = pltpu.make_async_remote_copy(
        src_ref=src,
        dst_ref=dst,
        send_sem=sems[0].at[k],
        recv_sem=sems[1].at[k],
        device_id=who,
        device_id_type=MESH,
    )
    copy.start()
    return copy


def dot_nn(a, b):
    return lax.dot_general(a, b, (((1,), (0,)), ((), ())), preferred_element_type=f32)


def dot_nt(a, b):
    return lax.dot_general(a, b, (((1,), (1,)), ((), ())), preferred_element_type=f32)


def aligned(index, size):
    return pl.ds(pl.multiple_of(index * size, size), size)


TILE = 256
CHUNKS = 4


def token_rows(half):
    size = half // CHUNKS
    own = [pl.ds(k * size, size) for k in range(CHUNKS)]
    far = [pl.ds(2 * half + 2 * k * size, size) for k in range(CHUNKS)]
    cross = [pl.ds(2 * half + (2 * k + 1) * size, size) for k in range(CHUNKS)]
    return own, far, cross


class Exchange:
    def __init__(self, send_sems, recv_sems, local_sems):
        self.sems = (send_sems, recv_sems)
        self.local_sems = local_sems
        self.all = []
        self.local = []
        self.arrived = set()
        self.settled = set()
        self.gone = set()

    def start(self, src, dst, who):
        self.all.append(send(src, dst, self.sems, len(self.all), who))
        return len(self.all) - 1

    def keep(self, src, dst):
        copy = pltpu.make_async_copy(src, dst, self.local_sems.at[len(self.local)])
        copy.start()
        self.local.append(copy)
        return len(self.local) - 1

    def arrive(self, number):
        if number not in self.arrived:
            self.arrived.add(number)
            self.all[number].wait_recv()

    def settle(self, number):
        if number not in self.settled:
            self.settled.add(number)
            self.local[number].wait()

    def sent(self, number):
        if number not in self.gone:
            self.gone.add(number)
            self.all[number].wait_send()

    def finish(self):
        for number in range(len(self.all)):
            self.arrive(number)
        for number in range(len(self.all)):
            self.sent(number)
        for number in range(len(self.local)):
            self.settle(number)


class RowGather:
    def __init__(self, net, full, part, order):
        self.net, self.full, self.order = net, full, order
        self.rows, self.first, self.size = part
        self.copies = {}
        self.spread((0, 0), -1)

    def place(self, code):
        index = (lax.axis_index("fsdp") ^ code[0]) * 2 + (lax.axis_index("ctx") ^ code[1])
        return pl.ds(pl.multiple_of(index * self.rows + self.first, 16), self.size)

    def spread(self, code, last):
        block = self.full.at[self.place(code)]
        for position in range(last + 1, len(self.order)):
            axis, bit = self.order[position]
            other = (code[0] ^ bit, code[1]) if axis == "fsdp" else (code[0], code[1] ^ bit)
            self.copies[other] = (self.net.start(block, block, dim_peer((axis, bit))), position)

    def arrive(self, code):
        copy, position = self.copies[code]
        self.net.arrive(copy)
        self.spread(code, position)


def dim_peer(dim):
    axis, bit = dim
    return peer(bit if axis == "fsdp" else 0, bit if axis == "ctx" else 0)


def gather_codes(far, near):
    first = [(SHARE, 0), (far, 0), (far ^ SHARE, 0)]
    rest = [(0, 1), (near, 0), (near, 1)]
    later = [(a ^ b, c) for a, _ in first for b, c in rest]
    return first, rest[:2] + later[0:2] + [rest[2]] + later[3:5] + [later[2]] + later[6:8] + [later[5], later[8]]


def document_start(lengths_ref, number):
    start, first = 0, jnp.zeros_like(number)
    for k in range(lengths_ref.shape[1]):
        start = start + lengths_ref[0, k]
        first = jnp.where(number >= start, start, first)
    return first


def layer_kernel(
    far, near, experts, total_rows,
    lengths_ref, loss_grad_ref, routes_ref, tokens_ref, small_hbm, query_hbm, key_hbm, value_hbm, out_hbm,
    grad_hbm, gate_hbm, up_hbm, down_hbm,
    probs_ref, mask_ref, row_ref, lse_ref, cos_ref, sin_ref,
    dx_hbm, middle_hbm, query_hbm_out, kv_hbm, attended_hbm, in_out, out_out, part_hbm, sum_gu, sum_d,
    weights, xb, gb, wg, wu, wd, kv, h0, hw, dg, du, db, d0, near_in, near_sum, far_in,
    count_sent, count_got,
    send_sems, recv_sems, local_sems, stage_sems, tp_send, tp_recv, free_sem,
):
    far_dev, near_dev, share_dev = peer(far), peer(near), peer(SHARE)
    ctx_dev, core_dev = peer(0, 1), peer(0, 0, 1)
    net = Exchange(send_sems, recv_sems, local_sems)
    place, core = lax.axis_index("ctx"), lax.axis_index("tp")
    rows, width = tokens_ref.shape
    half, quarter = rows // 2, rows // 4
    units = 4 * gate_hbm.shape[1]
    block = small_hbm.shape[0]
    heads_width, kv_width = query_hbm.shape[1], key_hbm.shape[1]
    in_width = small_hbm.shape[1] + heads_width + 2 * kv_width
    in_full = weights.at[:, pl.ds(0, in_width)]
    out_full = weights.at[:, pl.ds(in_width, out_hbm.shape[1])]
    normed = dg.at[pl.ds(0, rows)]
    raw = h0.at[pl.ds(0, rows), pl.ds(0, in_width - 128)]
    core_sent = h0.at[pl.ds(rows, half)]
    middle_ref = h0.at[pl.ds(rows + half, half)]
    core_got = d0.at[:, pl.ds(0, width)]
    query = hw.at[pl.ds(0, rows), pl.ds(0, heads_width)]
    attended = hw.at[pl.ds(rows, rows), pl.ds(0, heads_width)]
    gate_all, up_all, down_all, grads = wg, wu, wd, gb
    own_block = pl.ds(pl.multiple_of((lax.axis_index("fsdp") * 2 + place) * block, 16), block)
    start = 0
    for ref in (small_hbm, query_hbm, key_hbm, value_hbm):
        net.keep(ref, in_full.at[own_block, pl.ds(start, ref.shape[1])])
        start += ref.shape[1]
    net.keep(out_hbm, out_full.at[own_block])
    greet([far_dev, near_dev, share_dev, ctx_dev, core_dev])
    for k in range(5):
        net.settle(k)
    fars = [("fsdp", far), ("fsdp", SHARE)]
    low, across = ("fsdp", near), ("ctx", 1)
    part = block // 2
    ins = [
        RowGather(net, in_full, (block, 0, part), fars + [across, low]),
        RowGather(net, in_full, (block, part, part), fars + [low, across]),
    ]

    routes = routes_ref[...]
    lane = lax.broadcasted_iota(jnp.int32, (rows, 128), 1)
    named = jnp.zeros((rows, 128), f32)
    for k in range(routes.shape[1]):
        named += (routes[:, k : k + 1] == lane).astype(f32)
    count_dims = [ctx_dev, near_dev, share_dev, far_dev]
    counts = [jnp.broadcast_to(jnp.sum(named, axis=0, keepdims=True), (8, 128))]
    count_copies = []

    def count_step():
        k = len(count_copies)
        if k > 0:
            net.arrive(count_copies[-1])
            counts[0] = counts[0] + count_got[k - 1]
        if k < len(count_dims):
            count_sent[k] = counts[0]
            count_copies.append(net.start(count_sent.at[k], count_got.at[k], count_dims[k]))

    count_step()

    piece = units // 4

    def slot(full, number, which=None):
        begin, size = (number * piece, piece) if full is down_all else (0, width)
        if which is not None:
            size //= 2
            begin = pl.multiple_of(begin + which * size, 16)
        if full is down_all:
            return full.at[pl.ds(begin, size)]
        return full.at[pl.ds(begin, size), pl.ds(number * piece, piece)]

    matrices = [(down_hbm, down_all), (gate_hbm, gate_all), (up_hbm, up_all)]
    from_core, own_weights = [], []
    for ref, full in matrices:
        own_weights.append(net.keep(ref, slot(full, 0)))
        from_core.append(net.start(ref, slot(full, 1), core_dev))

    from_share, from_ctx = [], []

    def share_start(k):
        ref, full = matrices[k]
        size = ref.shape[0] // 2
        part_of = ref.at[pl.ds(pl.multiple_of(place * size, 16), size)]
        from_share.append(net.start(part_of, slot(full, 2, place), share_dev))

    def share_on(k):
        ref, full = matrices[k]
        net.arrive(from_share[k])
        from_ctx.append(net.start(slot(full, 2, place), slot(full, 2, place), ctx_dev))
        from_core.append(net.start(slot(full, 2, place), slot(full, 3, place), core_dev))

    here = lax.broadcasted_iota(jnp.int32, (rows, 1), 0) + place * rows
    position = (here - document_start(lengths_ref, here)).astype(f32)
    turn_lane = lax.broadcasted_iota(jnp.int32, (1, HEAD_DIM), 1)
    turn = lax.rem(turn_lane, HEAD_DIM // 2).astype(f32) * (2.0 / HEAD_DIM)
    angles = position * jnp.exp(turn * -math.log(rope_base))
    cos_ref[...] = jnp.cos(angles)
    sin_ref[...] = jnp.where(turn_lane < HEAD_DIM // 2, -1.0, 1.0) * jnp.sin(angles)

    first, rest = gather_codes(far, near)
    for code in first:
        for g in ins:
            g.arrive(code)
    count_step()
    own_rows = pl.ds(pl.multiple_of(core * half, 16), half)
    other_rows = pl.ds(pl.multiple_of((1 - core) * half, 16), half)
    chunk = half // CHUNKS
    own_chunks = [pl.ds(pl.multiple_of(core * half + k * chunk, 16), chunk) for k in range(CHUNKS)]
    _, far_rows, cross_rows = token_rows(half)
    share_start(0)
    own_grad = net.keep(grad_hbm.at[own_rows], grads.at[pl.ds(0, half)])
    far_copies = [net.start(grad_hbm.at[own_chunks[k]], grads.at[far_rows[k]], far_dev) for k in range(CHUNKS)]
    from_near = []

    def cross_on(k):
        net.arrive(far_copies[k])
        from_near.append(net.start(grads.at[far_rows[k]], grads.at[cross_rows[k]], near_dev))

    for code in rest[:6]:
        for g in ins:
            g.arrive(code)
    for code in rest[6:]:
        for g in ins:
            g.arrive(code)
    count_step()
    outs = [
        RowGather(net, out_full, (block, 0, part), fars + [across, low]),
        RowGather(net, out_full, (block, part, part), fars + [low, across]),
    ]
    from_near.append(net.start(grad_hbm.at[own_rows], grads.at[pl.ds(half, half)], near_dev))
    gains = in_full[:, :128].astype(f32).T
    attn_gain, moe_gain = gains[experts : experts + 1], gains[experts + 1 : experts + 2]
    step = quarter // 2
    for k in range(rows // quarter):
        at = slice(k * quarter, (k + 1) * quarter)
        x = tokens_ref[at, :].astype(f32)
        inverse = lax.rsqrt(jnp.mean(x * x, axis=1, keepdims=True) + epsilon)
        normed[at, :] = (x * inverse * attn_gain).astype(bf16)

    def rotated(value, at):
        return value * cos_ref[at, :] + pltpu.roll(value, HEAD_DIM // 2, 1) * sin_ref[at, :]

    mine = pl.ds(pl.multiple_of(place * rows, 16), rows)
    raw[...] = dot_nn(normed[...], in_full[:, 128:])
    kv[mine, :kv_width] = rotated(raw[:, heads_width : heads_width + kv_width], slice(None)).astype(bf16)
    kv[mine, kv_width:] = raw[:, heads_width + kv_width :].astype(bf16)
    kv_copy = net.start(kv.at[mine], kv.at[mine], ctx_dev)
    for head in range(heads_width // HEAD_DIM):
        cols = slice(head * HEAD_DIM, (head + 1) * HEAD_DIM)
        query[:, cols] = rotated(raw[:, cols], slice(None)).astype(bf16)
    net.arrive(from_share[0])
    share_start(1)
    share_on(0)
    for code in first:
        for g in outs:
            g.arrive(code)
    count_step()
    net.arrive(kv_copy)
    net.keep(kv, kv_hbm)
    net.arrive(from_share[1])
    share_start(2)
    share_on(1)
    cross_on(0)

    keys, values_flipped = kv[:, :HEAD_DIM], kv[:, HEAD_DIM:].T
    query_number = lax.broadcasted_iota(jnp.int32, (1, half), 1) + place * rows
    key_number = lax.broadcasted_iota(jnp.int32, (kv.shape[0], 1), 0)
    scale = HEAD_DIM ** (-0.5)

    def head_block(i, carry):
        head, block_index = i // 2, lax.rem(i, 2)
        cols, at = aligned(head, HEAD_DIM), aligned(block_index, half)
        number = query_number + block_index * half
        allowed = (key_number >= document_start(lengths_ref, number)) & (key_number <= number)
        scores = jnp.where(allowed, dot_nt(keys, query[at, cols]) * scale, masked_score)
        maxima = jnp.max(scores, axis=0, keepdims=True)
        weights = jnp.exp(scores - maxima)
        totals = jnp.sum(weights, axis=0, keepdims=True)
        lse_ref[pl.ds(head, 1), at] = maxima + jnp.log(totals)
        low_weights = (weights * (1.0 / totals)).astype(bf16)
        attended[at, cols] = dot_nn(values_flipped, low_weights).T.astype(bf16)
        return carry

    group = heads_width // HEAD_DIM
    third = 2 * group // 3
    lax.fori_loop(0, third, head_block, 0)
    for code in rest[:6]:
        for g in outs:
            g.arrive(code)
    cross_on(1)
    lax.fori_loop(third, 2 * third, head_block, 0)
    for code in rest[6:]:
        for g in outs:
            g.arrive(code)
    cross_on(2)
    count_step()
    lax.fori_loop(2 * third, 2 * group, head_block, 0)
    cross_on(3)

    saved = [net.keep(query, query_hbm_out), net.keep(attended, attended_hbm)]

    core_sent[...] = dot_nt(attended[other_rows, :], out_full[...])
    core_copy = net.start(core_sent, core_got, core_dev)
    share_on(2)
    middle_ref[...] = tokens_ref[own_rows, :].astype(f32) + dot_nt(attended[own_rows, :], out_full[...])
    net.arrive(core_copy)
    own_lane = lax.broadcasted_iota(jnp.int32, (step, 128), 1)
    share_row = counts[0][0:1] * (experts / (total_rows * routes.shape[1] * total_rows))
    row_number = lax.broadcasted_iota(jnp.int32, (8, 128), 0)
    row_ref[...] = jnp.where(
        row_number == 0, share_row * loss_grad_ref[0], jnp.where(row_number == 1, share_row, 0.0)
    )
    router = in_full[:, :128]
    _, token_slots, _ = token_rows(half)
    token_far = []
    for k in range(half // step):
        at = slice(k * step, (k + 1) * step)
        middle = middle_ref[at, :] + core_got[at, :]
        middle_ref[at, :] = middle
        inverse = lax.rsqrt(jnp.mean(middle * middle, axis=1, keepdims=True) + epsilon)
        normed_moe = (middle * inverse * moe_gain).astype(bf16)
        xb[at, :width] = normed_moe
        logits = jnp.where(own_lane < experts, dot_nn(normed_moe, router), masked_score)
        shifted = jnp.exp(logits - jnp.max(logits, axis=1, keepdims=True))
        probs = shifted / jnp.sum(shifted, axis=1, keepdims=True)
        own_routes = routes_ref[pl.ds(pl.multiple_of(core * half + k * step, 16), step), :]
        mask = jnp.zeros((step, 128), f32)
        for n in range(routes.shape[1]):
            mask += (own_routes[:, n : n + 1] == own_lane).astype(f32)
        probs_ref[at, :] = probs
        mask_ref[at, :] = mask
        chosen = probs * mask
        gates = chosen / jnp.sum(chosen, axis=1, keepdims=True)
        high = gates.astype(bf16).astype(f32)
        xb[at, width:] = (high + pltpu.roll(gates - high, experts, 1)).astype(bf16)
        token_far.append(net.start(xb.at[pl.ds(k * step, step)], xb.at[token_slots[k]], far_dev))

    saved.append(net.keep(middle_ref, middle_hbm))
    token_near = net.start(xb.at[pl.ds(0, half)], xb.at[pl.ds(half, half)], near_dev)
    own_chunks, far_rows, cross_rows = token_rows(half)
    near_rows = pl.ds(half, half)
    forwards, crossed, backs = [], [], []

    def pass_on(k):
        net.arrive(token_far[k])
        forwards.append(net.start(xb.at[far_rows[k]], xb.at[cross_rows[k]], near_dev))

    def share_last(k):
        ref, full = matrices[k]
        net.arrive(from_ctx[k])
        from_core.append(net.start(slot(full, 2, 1 - place), slot(full, 3, 1 - place), core_dev))

    stored = [net.keep(in_full, in_out), net.keep(out_full, out_out)]
    share_last(0)
    share_last(1)
    for number in saved:
        net.settle(number)
    net.sent(core_copy)
    for copy in from_near:
        net.arrive(copy)
    net.settle(own_grad)
    net.settle(own_weights[0])
    for copy in (from_core[0], from_core[3], from_core[6]):
        net.arrive(copy)
    unit_tiles = units // TILE

    def back_tile(j, carry):
        h0[:, aligned(j, TILE)] = dot_nt(gb[...], wd[aligned(j, TILE), :])
        return carry

    lax.fori_loop(0, unit_tiles, back_tile, 0)
    pass_on(0)
    share_last(2)
    for copy in from_core:
        net.arrive(copy)
    for number in own_weights:
        net.settle(number)

    lane = lax.broadcasted_iota(jnp.int32, (half, 128), 1)
    own = lax.axis_index("fsdp")
    partner = own ^ SHARE

    def task(number):
        rows = pl.ds(number * half, half)
        extra = xb[rows, width:].astype(f32)

        def gate_of(expert):
            mine = (lane == expert) | (lane == experts + expert)
            return jnp.sum(jnp.where(mine, extra, 0.0), axis=1, keepdims=True)

        gates = jnp.concatenate([gate_of(own), gate_of(partner)], axis=1)

        def unit_tile(j, dots):
            cols = aligned(j, TILE)
            is_own = j < unit_tiles // 2
            gate = jnp.where(is_own, gates[:, :1], gates[:, 1:])
            x = xb[rows, :width]
            gate_pre = dot_nn(x, wg[:, cols])
            up_pre = dot_nn(x, wu[:, cols])
            back = h0[rows, cols]
            sig = 1.0 / (1.0 + jnp.exp(-gate_pre))
            silu = gate_pre * sig
            hidden = silu * up_pre
            hw[rows, cols] = (hidden * gate).astype(bf16)
            hidden_grad = back * gate
            dg[rows, cols] = (hidden_grad * up_pre * (sig * (1.0 + gate_pre * (1.0 - sig)))).astype(bf16)
            du[rows, cols] = (hidden_grad * silu).astype(bf16)
            one = jnp.sum(hidden * back, axis=1, keepdims=True)
            return (
                dots[0] + jnp.where(is_own, one, 0.0),
                dots[1] + jnp.where(is_own, 0.0, one),
            )

        zero = jnp.zeros((half, 1), f32)
        dots = lax.fori_loop(0, unit_tiles, unit_tile, (zero, zero), unroll=True)

        def put(cols, value):
            if number == 0:
                d0[:, cols] = value
            else:
                db[rows, cols] = value.astype(bf16)

        def in_tile(n, carry):
            cols = aligned(n, 2 * TILE)
            value = dot_nt(dg[rows, :], wg[cols, :]) + dot_nt(du[rows, :], wu[cols, :])
            put(cols, value)
            return carry

        lax.fori_loop(0, width // (2 * TILE), in_tile, 0, unroll=True)
        columns = jnp.zeros_like(extra)
        for expert, value in ((own, dots[0]), (partner, dots[1])):
            high = value.astype(bf16).astype(f32)
            columns = jnp.where(lane == expert, high, columns)
            columns = jnp.where(lane == experts + expert, value - high, columns)
        put(slice(width, None), columns)

    def cross_back(k):
        crossed.append(net.start(db.at[cross_rows[k]], near_in.at[own_chunks[k]], near_dev))

    def far_back(k):
        net.arrive(crossed[k])
        total = db[far_rows[k], :].astype(f32) + near_in[own_chunks[k], :].astype(f32)
        db[far_rows[k], :] = total.astype(bf16)
        backs.append(net.start(db.at[far_rows[k]], far_in.at[own_chunks[k]], far_dev))

    task(0)
    pass_on(1)
    pass_on(2)
    net.arrive(forwards[0])
    net.arrive(forwards[1])
    task(2)
    cross_back(0)
    cross_back(1)
    net.arrive(token_near)
    task(1)
    far_back(0)
    far_back(1)
    pass_on(3)
    net.arrive(forwards[2])
    net.arrive(forwards[3])
    task(3)
    cross_back(2)
    cross_back(3)
    near_back = net.start(db.at[near_rows], near_sum, near_dev)

    for copy in from_share + from_ctx + from_core:
        net.sent(copy)
    pl.semaphore_signal(free_sem, inc=1, device_id=core_dev, device_id_type=MESH)
    for g in ins + outs:
        for copy, _ in g.copies.values():
            net.sent(copy)
    for number in stored:
        net.settle(number)

    keep_rows, send_rows = 0, 2 * piece

    def stage_rows(base, slot, size):
        return pl.ds(pl.multiple_of(base + slot * piece, 16), size)

    tiles = width // TILE

    def to_core(slot, number, rows, size, got):
        return pltpu.make_async_remote_copy(
            src_ref=weights.at[stage_rows(send_rows, slot, size), pl.ds(0, width)],
            dst_ref=got.at[rows],
            send_sem=tp_send.at[slot],
            recv_sem=tp_recv.at[number],
            device_id=core_dev,
            device_id_type=MESH,
        )

    def to_hbm(slot, rows, size, full):
        return pltpu.make_async_copy(
            weights.at[stage_rows(keep_rows, slot, size), pl.ds(0, width)], full.at[rows], stage_sems.at[slot]
        )

    def gradient_loop(count, first, size, compute, got, full):
        def close(i):
            slot, rows = lax.rem(i, 2), aligned(i, size)
            to_core(slot, first + i, rows, size, got).wait_recv()
            at = stage_rows(keep_rows, slot, size)
            keep = weights[at, :width].astype(f32) + got[rows, :].astype(f32)
            weights[at, :width] = keep.astype(bf16)
            to_hbm(slot, rows, size, full).start()

        def free(slot):
            to_hbm(slot, pl.ds(0, size), size, full).wait()
            to_core(slot, 0, pl.ds(0, size), size, got).wait_send()

        def one(i, carry):
            slot = lax.rem(i, 2)

            @pl.when(i >= 2)
            def _():
                free(slot)

            compute(i, slot)
            to_core(slot, first + i, aligned(i, size), size, got).start()

            @pl.when(i >= 1)
            def _():
                close(i - 1)

            return carry

        lax.fori_loop(0, count, one, 0)
        close(count - 1)
        free(0)
        free(1)

    def gate_up_tile(i, slot):
        flipped = xb[:, aligned(i, TILE)].T
        for k, source in enumerate((dg, du)):
            value = dot_nn(flipped, source[...]).astype(bf16)
            for p in range(4):
                at = (2 * k + p // 2) * piece
                base = keep_rows if p % 2 == 0 else send_rows
                weights[stage_rows(base, slot, TILE), at : at + piece] = value[:, p * piece : (p + 1) * piece]

    def down_tile(i, slot):
        for base, offset in ((keep_rows, 0), (send_rows, piece)):
            cols = pl.ds(pl.multiple_of(i * 2 * piece + offset, 128), piece)
            flipped = hw[:, cols].T
            for n in range(0, width, 2 * TILE):
                weights[stage_rows(base, slot, piece), n : n + 2 * TILE] = dot_nn(flipped, gb[:, n : n + 2 * TILE]).astype(bf16)

    pl.semaphore_wait(free_sem, 1)
    gradient_loop(2, tiles, piece, down_tile, wg, sum_d)
    far_back(2)

    for k in range(4):
        at = slice(k * half, (k + 1) * half)
        hw[at, :] = dot_nn(hw[at, :], wd[...]).astype(bf16)
        if k == 1:
            far_back(3)
    net.keep(hw, part_hbm)
    gradient_loop(tiles, 0, TILE, gate_up_tile, wu, sum_gu)
    net.arrive(near_back)
    for copy in backs:
        net.arrive(copy)
    d0[...] = d0[...] + near_sum[...].astype(f32) + far_in[...].astype(f32)
    net.keep(d0, dx_hbm)
    net.finish()


def layer_on_chip(
    lengths, loss_grad, routes, tokens, small, w_query, w_key, w_value, out_block, out_grad, gate, up, down, experts
):
    far, near = token_bits()
    owners = lax.axis_size("fsdp") * lax.axis_size("ctx")
    rows, width = tokens.shape
    half, pack = rows // 2, rows * lax.axis_size("ctx")
    units, block = 4 * gate.shape[1], small.shape[0]
    heads_width, kv_width = w_query.shape[1], w_key.shape[1]
    in_width, out_width = small.shape[1] + heads_width + 2 * kv_width, out_block.shape[1]
    any_spec = pl.BlockSpec(memory_space=pl.ANY)
    vmem = pl.BlockSpec(memory_space=pltpu.VMEM)
    smem = pl.BlockSpec(memory_space=pltpu.SMEM)
    outs = [
        ((half, 128), f32),
        ((half, 128), f32),
        ((8, 128), f32),
        ((-(-heads_width // HEAD_DIM // 8) * 8, rows), f32),
        ((rows, HEAD_DIM), f32),
        ((rows, HEAD_DIM), f32),
        ((half, width + 128), f32),
        ((half, width), f32),
        ((rows, heads_width), bf16),
        ((pack, 2 * kv_width), bf16),
        ((rows, heads_width), bf16),
        ((owners * block, in_width), bf16),
        ((owners * block, out_width), bf16),
        ((2 * rows, width), bf16),
        ((width, units), bf16),
        ((units // 2, width), bf16),
    ]

    def low(*shape):
        return pltpu.VMEM(shape, bf16)

    def wide(*shape):
        return pltpu.VMEM(shape, f32)

    return pl.pallas_call(
        functools.partial(layer_kernel, far, near, experts, rows * owners),
        name="layer",
        out_shape=tuple(jax.ShapeDtypeStruct(s, d) for s, d in outs),
        in_specs=[smem, smem, vmem, vmem] + [any_spec] * 9,
        out_specs=(vmem,) * 6 + (any_spec,) * 10,
        scratch_shapes=[
            low(owners * block, in_width + out_width),
            low(2 * rows, width + 128),
            low(2 * rows, width),
            low(width, units),
            low(width, units),
            low(units, width),
            low(pack, 2 * kv_width),
            wide(2 * rows, units),
            low(2 * rows, units),
            low(2 * rows, units),
            low(2 * rows, units),
            low(2 * rows, width + 128),
            wide(half, width + 128),
            low(half, width + 128),
            low(half, width + 128),
            low(half, width + 128),
            wide(4, 8, 128),
            wide(4, 8, 128),
            pltpu.SemaphoreType.DMA((116,)),
            pltpu.SemaphoreType.DMA((116,)),
            pltpu.SemaphoreType.DMA((20,)),
            pltpu.SemaphoreType.DMA((2,)),
            pltpu.SemaphoreType.DMA((2,)),
            pltpu.SemaphoreType.DMA((width // TILE + 2,)),
            pltpu.SemaphoreType.REGULAR,
        ],
        compiler_params=pltpu.CompilerParams(
            collective_id=0, has_side_effects=True, vmem_limit_bytes=62 * 1024 * 1024
        ),
    )(lengths, loss_grad, routes, tokens, small, w_query, w_key, w_value, out_block, out_grad, gate, up, down)


class RowReduce:
    def __init__(self, net, partial, inbox, part, order):
        self.net, self.partial, self.inbox, self.order = net, partial, inbox, order
        self.rows, self.first, self.size = part
        self.copies = {}

    def place(self, mask):
        fsdp, ctx = 0, 0
        for position, (axis, bit) in enumerate(self.order):
            if mask >> position & 1:
                fsdp, ctx = (fsdp ^ bit, ctx) if axis == "fsdp" else (fsdp, ctx ^ bit)
        index = (lax.axis_index("fsdp") ^ fsdp) * 2 + (lax.axis_index("ctx") ^ ctx)
        return pl.ds(pl.multiple_of(index * self.rows + self.first, 16), self.size)

    def box(self, mask):
        return pl.ds((mask - 1) * self.size, self.size)

    def step(self, mask):
        rows, last = self.place(mask), mask.bit_length() - 1
        if last + 1 < len(self.order):
            value = self.partial[rows, :].astype(f32)
            for later in range(last + 1, len(self.order)):
                source = mask | 1 << later
                self.net.arrive(self.copies[source])
                value = value + self.inbox[self.box(source), :].astype(f32)
            if mask == 0:
                return value
            self.partial[rows, :] = value.astype(bf16)
        self.copies[mask] = self.net.start(
            self.partial.at[rows], self.inbox.at[self.box(mask)], dim_peer(self.order[last])
        )

    def level(self, last):
        for mask in reversed(range(1 << last, 2 << last)):
            self.step(mask)


def backward_kernel(
    far, near, experts, group,
    lengths_ref, row_ref, dx_ref, middle_ref, probs_ref, mask_ref, grad_hbm,
    tokens_hbm, query_hbm, kv_hbm, lse_ref, attended_hbm, cos_ref, sin_ref,
    in_hbm, out_hbm, moe_hbm, gu_hbm, down_hbm,
    output_hbm, loss_ref, tokens_grad_hbm, query_out, key_out, value_out, out_ref, extra_ref, gate_ref, up_ref, down_ref,
    grad_ref, tokens, query, kv, attended, in_full, out_full,
    out_in, att_grad, qkv_grad, kv_grad, kv_sent, kv_got,
    in_box, out_box,
    mid_grad, back_sent, back_got, tok_stage, extra_rows, extra_sent, extra_got,
    moe_own, moe_far, moe_near, moe_cross, moe_back,
    gate_own, gate_x, gate_sent, gate_s,
    up_own, up_s, up_sent, up_x,
    down_own, down_x, down_sent, down_s,
    loss_sent, loss_got,
    send_sems, recv_sems, local_sems,
):
    far_dev, near_dev, share_dev = peer(far), peer(near), peer(SHARE)
    ctx_dev, core_dev = peer(0, 1), peer(0, 0, 1)
    greet([far_dev, near_dev, share_dev, ctx_dev, core_dev])
    net = Exchange(send_sems, recv_sems, local_sems)
    ctx_place, core = lax.axis_index("ctx"), lax.axis_index("tp")
    half, width = middle_ref.shape
    rows = 2 * half
    quarter = half // 2
    own_rows = pl.ds(pl.multiple_of(core * half, 16), half)
    other_rows = pl.ds(pl.multiple_of((1 - core) * half, 16), half)
    chunks, far_rows, cross_rows = token_rows(half)

    crossed = [net.start(moe_hbm.at[cross_rows[k]], moe_cross.at[chunks[k]], near_dev) for k in range(CHUNKS)]
    units = gu_hbm.shape[1] // 4
    wide = width // 2

    def wide_half(place):
        return pl.ds(pl.multiple_of(place * wide, 128), wide)

    gate_cols, up_own_cols, up_par_cols = pl.ds(0, 2 * units), pl.ds(2 * units, units), pl.ds(3 * units, units)
    gate_first = net.start(gu_hbm.at[wide_half(1 - ctx_place), gate_cols], gate_x, ctx_dev)
    up_first = net.start(gu_hbm.at[:, up_par_cols], up_s, share_dev)
    pairs = [
        (in_hbm, in_full), (out_hbm, out_full), (attended_hbm, attended), (query_hbm, query),
        (kv_hbm, kv), (tokens_hbm, tokens), (moe_hbm.at[pl.ds(0, half)], moe_own),
        (gu_hbm.at[wide_half(ctx_place), gate_cols], gate_own), (gu_hbm.at[:, up_own_cols], up_own),
        (down_hbm.at[:, wide_half(ctx_place)], down_own), (grad_hbm.at[own_rows], grad_ref),
    ] + [(moe_hbm.at[far_rows[k]], moe_far.at[chunks[k]]) for k in range(CHUNKS)]
    for src, dst in pairs:
        net.keep(src, dst)

    def loaded(*numbers):
        for number in numbers:
            net.settle(number)

    def pieces(size):
        return [slice(k * size // 4, (k + 1) * size // 4) for k in range(4)]

    loaded(0, 10)
    flipped_extra = in_full[:, :128].astype(f32).T
    attn_gain, moe_gain = flipped_extra[experts : experts + 1], flipped_extra[experts + 1 : experts + 2]
    lane = lax.broadcasted_iota(jnp.int32, (half, 128), 1)
    probs, mask = probs_ref[...], mask_ref[...]
    pair = dx_ref[:, width:]
    gate_grad = jnp.where(lane < experts, pair + pltpu.roll(pair, 128 - experts, 1), 0.0)
    chosen = probs * mask
    chosen_total = jnp.sum(chosen, axis=1, keepdims=True)
    weighted = jnp.sum(gate_grad * chosen, axis=1, keepdims=True) / chosen_total
    prob_grad = mask * (gate_grad - weighted) / chosen_total + row_ref[0:1, :]
    logit_grad = probs * (prob_grad - jnp.sum(prob_grad * probs, axis=1, keepdims=True))
    logit_high = logit_grad.astype(bf16)
    logit_low = (logit_grad - logit_high.astype(f32)).astype(bf16)
    router = in_full[:, :128]
    step = quarter // 2
    gain_moe = jnp.zeros((1, width), f32)
    router_grad = jnp.zeros((128, width), f32)
    for k in range(half // step):
        at = slice(k * step, (k + 1) * step)
        middle = middle_ref[at, :]
        inverse = lax.rsqrt(jnp.mean(middle * middle, axis=1, keepdims=True) + epsilon)
        scaled = middle * inverse
        normed_moe = (scaled * moe_gain).astype(bf16)
        moe_grad = dx_ref[at, :width] + dot_nt(logit_high[at], router) + dot_nt(logit_low[at], router)
        router_grad += dot(logit_high[at], normed_moe, 0, 0) + dot(logit_low[at], normed_moe, 0, 0)
        gain_moe += jnp.sum(moe_grad * scaled, axis=0, keepdims=True)
        a = moe_grad * moe_gain
        grad = grad_ref[at, :].astype(f32) + inverse * (a - scaled * jnp.mean(a * scaled, axis=1, keepdims=True))
        mid_grad[at, :] = grad
        out_in[pl.ds(pl.multiple_of(core * half + k * step, 16), step), :] = grad.astype(bf16)
    out_in_copy = net.start(out_in.at[own_rows], out_in.at[own_rows], core_dev)
    row = lax.broadcasted_iota(jnp.int32, (128, width), 0)
    extra_rows[...] = jnp.where(row == experts + 1, gain_moe, router_grad)

    loss_dims = [core_dev, ctx_dev, near_dev, share_dev, far_dev]
    loss_state = [jnp.broadcast_to(jnp.sum(probs, axis=0, keepdims=True), (8, 128))]
    loss_copies = []

    def loss_step():
        k = len(loss_copies)
        if k > 0:
            net.arrive(loss_copies[-1])
            loss_state[0] = loss_state[0] + loss_got[k - 1]
        if k < len(loss_dims):
            loss_sent[k] = loss_state[0]
            loss_copies.append(net.start(loss_sent.at[k], loss_got.at[k], loss_dims[k]))

    loss_step()
    loaded(6, *range(11, 11 + CHUNKS))
    far_sums = []

    def far_sum(k):
        net.arrive(crossed[k])
        at = chunks[k]
        moe_far[at, :] = (moe_far[at, :].astype(f32) + moe_cross[at, :].astype(f32)).astype(bf16)
        far_sums.append(net.start(moe_far.at[at], moe_back.at[at], far_dev))

    far_sum(0)
    net.arrive(out_in_copy)
    loaded(1, 2)
    att_grad[...] = dot_nn(out_in[...], out_full[...]).astype(bf16)

    def out_tile(i, carry):
        cols = aligned(i, TILE)
        out_full[cols, :] = dot_nn(out_in[:, cols].T, attended[...]).astype(bf16)
        return carry

    lax.fori_loop(0, width // TILE, out_tile, 0)
    block = key_out.shape[0]
    low, across = ("fsdp", near), ("ctx", 1)
    fars = [("fsdp", far), ("fsdp", SHARE)]
    orders = [fars + [across, low], fars + [low, across]]
    part_size = block // 2
    sums_out = [
        RowReduce(net, out_full, out_box.at[k], (block, k * part_size, part_size), [across] + fars + [low])
        for k in range(2)
    ]
    far_sum(1)
    for s in sums_out:
        s.level(3)
    loss_step()
    far_sum(2)
    far_sum(3)
    net.sent(out_in_copy)
    loaded(5)
    normed_step = half // 2
    for k in range(rows // normed_step):
        at = slice(k * normed_step, (k + 1) * normed_step)
        x = tokens[at, :].astype(f32)
        inverse = lax.rsqrt(jnp.mean(x * x, axis=1, keepdims=True) + epsilon)
        out_in[at, :] = (x * inverse * attn_gain).astype(bf16)

    loaded(3, 4)
    pack = kv.shape[0]
    kv_grad[...] = jnp.zeros_like(kv_grad)
    keys, values = kv[:, :HEAD_DIM], kv[:, HEAD_DIM:]
    keys_flipped = keys.T
    query_number = lax.broadcasted_iota(jnp.int32, (1, half), 1) + ctx_place * rows
    key_number = lax.broadcasted_iota(jnp.int32, (pack, 1), 0)
    scale = HEAD_DIM ** (-0.5)

    def head_block(i, carry):
        head, block_index = i // 2, lax.rem(i, 2)
        cols = aligned(head, HEAD_DIM)
        at = aligned(block_index, half)
        number = query_number + block_index * half
        allowed = (key_number >= document_start(lengths_ref, number)) & (key_number <= number)
        q, grad = query[at, cols], att_grad[at, cols]
        log_total = lse_ref[pl.ds(head, 1), at]
        weights = jnp.where(allowed, jnp.exp(dot_nt(keys, q) * scale - log_total), 0.0)
        weight_grad = dot_nt(values, grad)
        delta = jnp.sum(weights * weight_grad, axis=0, keepdims=True)
        score_grad = (weights * (weight_grad - delta)).astype(bf16)
        kv_grad[:, :HEAD_DIM] += dot_nn(score_grad, q) * scale
        kv_grad[:, HEAD_DIM:] += dot_nn(weights.astype(bf16), grad)
        query_grad = (dot_nn(keys_flipped, score_grad) * scale).T
        turned = query_grad * cos_ref[at, :] - pltpu.roll(query_grad, HEAD_DIM // 2, 1) * sin_ref[at, :]
        qkv_grad[at, cols] = turned.astype(bf16)
        return carry

    third = 2 * group // 3
    lax.fori_loop(0, third, head_block, 0)
    loss_step()
    down_first = net.start(down_hbm.at[:, wide_half(1 - ctx_place)], down_x, ctx_dev)
    lax.fori_loop(third, 2 * third, head_block, 0)
    loss_step()
    loaded(7, 8, 9)
    net.arrive(gate_first)
    for at in pieces(wide):
        total = gate_own[at, :].astype(f32) + gate_x[at, :].astype(f32)
        gate_ref[at, :] = total[:, :units]
        gate_sent[at, :] = total[:, units:].astype(bf16)
    gate_last = net.start(gate_sent, gate_s, share_dev)
    net.arrive(up_first)
    up_sent[...] = (up_own[wide_half(1 - ctx_place), :].astype(f32) + up_s[wide_half(1 - ctx_place), :].astype(f32)).astype(bf16)
    up_ref[...] = up_own[wide_half(ctx_place), :].astype(f32) + up_s[wide_half(ctx_place), :].astype(f32)
    lax.fori_loop(2 * third, 2 * group, head_block, 0)
    loss_step()
    ctx_rows = pl.ds(pl.multiple_of(ctx_place * rows, 16), rows)
    ctx_other = pl.ds(pl.multiple_of((1 - ctx_place) * rows, 16), rows)
    kv_sent[...] = kv_grad[ctx_other, :].astype(bf16)
    kv_copy = net.start(kv_sent, kv_got, ctx_dev)
    up_last = net.start(up_sent, up_x, ctx_dev)
    for mask in (7, 6, 5, 4):
        for s in sums_out:
            s.step(mask)
    near_first = net.start(moe_hbm.at[pl.ds(half, half)], moe_near, near_dev)
    loss_step()
    loss = jnp.sum(loss_state[0][0:1] * row_ref[1:2, :], axis=1, keepdims=True)
    loss_ref[...] = jnp.broadcast_to(loss, loss_ref.shape)
    net.arrive(kv_copy)
    kv_sum = kv_grad[ctx_rows, :] + kv_got[...].astype(f32)
    key_grad = kv_sum[:, :HEAD_DIM]
    key_grad = key_grad * cos_ref[...] - pltpu.roll(key_grad, HEAD_DIM // 2, 1) * sin_ref[...]
    heads_width = group * HEAD_DIM
    qkv_grad[:, heads_width : heads_width + HEAD_DIM] = key_grad.astype(bf16)
    qkv_grad[:, heads_width + HEAD_DIM :] = kv_sum[:, HEAD_DIM:].astype(bf16)

    gain_attn = jnp.zeros((1, width), f32)

    def attn_scaled(at):
        x = tokens[at, :].astype(f32)
        inverse = lax.rsqrt(jnp.mean(x * x, axis=1, keepdims=True) + epsilon)
        return inverse, x * inverse

    for k in range(2):
        at = other_rows if k == 0 else own_rows
        part = dot_nt(qkv_grad[at, :], in_full[:, 128:])
        gain_attn += jnp.sum(part * attn_scaled(at)[1], axis=0, keepdims=True)
        if k == 0:
            back_sent[...] = part.astype(bf16)
            back_copy = net.start(back_sent, back_got, core_dev)
        else:
            tok_stage[...] = part
    def in_tile(i, carry):
        cols = aligned(i, TILE)
        in_full[cols, 128:] = dot_nn(out_in[:, cols].T, qkv_grad[...]).astype(bf16)
        return carry

    lax.fori_loop(0, width // TILE, in_tile, 0)
    extra_rows[...] = jnp.where(row == experts, gain_attn, extra_rows[...])
    in_full[:, :128] = extra_rows[...].T.astype(bf16)
    sums_in = [
        RowReduce(net, in_full, in_box.at[k], (block, k * part_size, part_size), orders[k]) for k in range(2)
    ]
    for s in sums_in:
        s.level(3)
    for mask in (3, 2):
        for s in sums_out:
            s.step(mask)

    net.arrive(back_copy)
    for k in range(2):
        at = pl.ds(k * quarter, quarter)
        inverse, scaled = attn_scaled(pl.ds(pl.multiple_of(core * half + k * quarter, 16), quarter))
        a = (tok_stage[at, :] + back_got[at, :].astype(f32)) * attn_gain
        tok_stage[at, :] = mid_grad[at, :] + inverse * (a - scaled * jnp.mean(a * scaled, axis=1, keepdims=True))
    net.keep(tok_stage, tokens_grad_hbm.at[own_rows])
    net.start(tok_stage, tokens_grad_hbm.at[own_rows], core_dev)

    for mask in (7, 6, 5, 4):
        for s in sums_in:
            s.step(mask)
    for s in sums_out:
        s.step(1)
    net.arrive(down_first)
    for at in pieces(units):
        down_ref[at, :] = down_own[at, :].astype(f32) + down_x[at, :].astype(f32)
        after = slice(at.start + units, at.stop + units)
        down_sent[at, :] = (down_own[after, :].astype(f32) + down_x[after, :].astype(f32)).astype(bf16)
    down_last = net.start(down_sent, down_s, share_dev)
    for mask in (3, 2, 1):
        for s in sums_in:
            s.step(mask)

    net.arrive(near_first)
    for k in range(CHUNKS):
        net.arrive(far_sums[k])
        at = chunks[k]
        moe_out = moe_own[at, :].astype(f32) + moe_near[at, :].astype(f32) + moe_back[at, :].astype(f32)
        moe_own[at, :] = (middle_ref[at, :] + moe_out).astype(bf16)
    net.keep(moe_own, output_hbm.at[own_rows])
    net.start(moe_own, output_hbm.at[own_rows], core_dev)

    for k in range(2):
        at = slice(k * part_size, (k + 1) * part_size)
        out_ref[at, :] = sums_out[k].step(0)
        value = sums_in[k].step(0)
        extra_sent[at, :] = value[:, :128]
        query_out[at, :] = value[:, 128 : 128 + heads_width]
        key_out[at, :] = value[:, 128 + heads_width : 128 + heads_width + HEAD_DIM]
        value_out[at, :] = value[:, 128 + heads_width + HEAD_DIM :]
    extra_copy = net.start(extra_sent, extra_got, core_dev)
    net.arrive(gate_last)
    gate_ref[...] += gate_s[...].astype(f32)
    net.arrive(up_last)
    up_ref[...] += up_x[...].astype(f32)
    net.arrive(down_last)
    down_ref[...] += down_s[...].astype(f32)
    net.arrive(extra_copy)
    extra_ref[...] = extra_sent[...] + extra_got[...]
    net.finish()


def backward_on_chip(
    lengths, row, dx, middle, probs, mask, out_grad, tokens, query, kv, lse, attended, cos, sin,
    in_full, out_full, moe_rows, gate_up, down, experts,
):
    far, near = token_bits()
    owners = lax.axis_size("fsdp") * lax.axis_size("ctx")
    half, width = middle.shape
    rows, heads_width = query.shape
    pack, kv_width = kv.shape
    units = down.shape[0] // 2
    block = in_full.shape[0] // owners
    in_width, out_width = in_full.shape[1], out_full.shape[1]
    any_spec = pl.BlockSpec(memory_space=pl.ANY)
    vmem = pl.BlockSpec(memory_space=pltpu.VMEM)
    smem = pl.BlockSpec(memory_space=pltpu.SMEM)

    def low(*shape):
        return pltpu.VMEM(shape, bf16)

    def wide(*shape):
        return pltpu.VMEM(shape, f32)

    boxes = 15 * (block // 2)
    return pl.pallas_call(
        functools.partial(backward_kernel, far, near, experts, heads_width // HEAD_DIM),
        name="backward",
        out_shape=(
            jax.ShapeDtypeStruct((rows, width), bf16),
            jax.ShapeDtypeStruct((8, 128), f32),
            jax.ShapeDtypeStruct((rows, width), f32),
            jax.ShapeDtypeStruct((block, heads_width), f32),
            jax.ShapeDtypeStruct((block, HEAD_DIM), f32),
            jax.ShapeDtypeStruct((block, HEAD_DIM), f32),
            jax.ShapeDtypeStruct((block, out_width), f32),
            jax.ShapeDtypeStruct((block, 128), f32),
            jax.ShapeDtypeStruct((width // 2, units), f32),
            jax.ShapeDtypeStruct((width // 2, units), f32),
            jax.ShapeDtypeStruct((units, width // 2), f32),
        ),
        in_specs=[smem] + [vmem] * 5 + [any_spec] * 4 + [vmem, any_spec, vmem, vmem] + [any_spec] * 5,
        out_specs=(any_spec, vmem, any_spec) + (vmem,) * 8,
        scratch_shapes=[
            low(half, width), low(rows, width), low(rows, heads_width), low(pack, kv_width), low(rows, heads_width),
            low(*in_full.shape), low(*out_full.shape),
            low(rows, width), low(rows, heads_width), low(rows, in_width - 128),
            wide(pack, kv_width), low(rows, kv_width), low(rows, kv_width),
            low(2, boxes, in_width), low(2, boxes, out_width),
            wide(half, width), low(half, width), low(half, width), wide(half, width),
            wide(128, width), wide(block, 128), wide(block, 128),
            low(half, width), low(half, width), low(half, width), low(half, width), low(half, width),
            low(width // 2, 2 * units), low(width // 2, 2 * units), low(width // 2, units), low(width // 2, units),
            low(width, units), low(width, units), low(width // 2, units), low(width // 2, units),
            low(2 * units, width // 2), low(2 * units, width // 2), low(units, width // 2), low(units, width // 2),
            wide(5, 8, 128), wide(5, 8, 128),
            pltpu.SemaphoreType.DMA((100,)),
            pltpu.SemaphoreType.DMA((100,)),
            pltpu.SemaphoreType.DMA((20,)),
        ],
        compiler_params=pltpu.CompilerParams(
            collective_id=2, has_side_effects=True, vmem_limit_bytes=62 * 1024 * 1024
        ),
    )(
        lengths, row, dx, middle, probs, mask, out_grad, tokens, query, kv, lse, attended, cos, sin,
        in_full, out_full, moe_rows, gate_up, down,
    )


def rms_back_gain(inverse, scaled, row_gains, upstream):
    return jnp.sum(upstream * scaled, axis=0), rms_back(inverse, scaled, row_gains, upstream)


def to_expert(arrived, local_experts, capacity):
    sources = arrived.shape[0]
    return (
        arrived.reshape(sources, local_experts, capacity, -1)
        .transpose(1, 0, 2, 3)
        .reshape(local_experts, sources * capacity, -1)
    )


def from_expert(expert_rows, sources, capacity):
    local_experts = expert_rows.shape[0]
    return (
        expert_rows.reshape(local_experts, sources, capacity, -1)
        .transpose(1, 0, 2, 3)
        .reshape(sources, local_experts * capacity, -1)
    )


def expert_forward(expert_rows, w_gate, w_up):
    gate_pre = jnp.einsum("erd,edf->erf", expert_rows, w_gate, preferred_element_type=jnp.float32)
    up_pre = jnp.einsum("erd,edf->erf", expert_rows, w_up, preferred_element_type=jnp.float32)
    hidden = (gate_pre * jax.nn.sigmoid(gate_pre) * up_pre).astype(jnp.bfloat16)
    return (gate_pre, up_pre, hidden)


def on_any_slice(
    tokens,
    lengths,
    routes,
    norm_attn,
    w_query,
    w_key,
    w_value,
    w_out,
    norm_moe,
    w_router,
    w_gate,
    w_up,
    w_down,
    out_grad,
    loss_grad,
):
    row_count, model_width = tokens.shape
    ctx_count = lax.axis_size("ctx")
    fsdp_count = lax.axis_size("fsdp")
    ctx_place = lax.axis_index("ctx")
    top_count = routes.shape[1]
    expert_count = w_router.shape[1]
    local_experts = w_gate.shape[0]
    capacity = 3 * row_count * top_count // (2 * expert_count)
    pack_count = row_count * ctx_count
    block_rows = min(512, row_count)
    base_row = ctx_place * row_count
    gain_attn, full_query, full_key, full_value, full_out, gain_moe, full_router = (
        lax.all_gather(norm_attn, ("fsdp", "ctx"), axis=0, tiled=True),
        lax.all_gather(w_query, ("fsdp", "ctx"), axis=0, tiled=True),
        lax.all_gather(w_key, ("fsdp", "ctx"), axis=0, tiled=True),
        lax.all_gather(w_value, ("fsdp", "ctx"), axis=0, tiled=True),
        lax.all_gather(w_out, ("fsdp", "ctx"), axis=1, tiled=True),
        lax.all_gather(norm_moe, ("fsdp", "ctx"), axis=0, tiled=True),
        lax.all_gather(w_router, ("fsdp", "ctx"), axis=0, tiled=True),
    )
    doc_ids, positions, doc_first = pack_layout(lengths[0], pack_count)
    own_positions = lax.dynamic_slice_in_dim(positions, base_row, row_count, 0)
    cos_table, sin_table = rope_tables(own_positions)
    x_float = tokens.astype(jnp.float32)
    attn_gain = gain_attn.astype(jnp.float32)
    inverse_attn, scaled_attn, normed_full = rms_parts(x_float, attn_gain)
    normed_attn = normed_full.astype(jnp.bfloat16)
    local_heads = full_query.shape[1] // HEAD_DIM
    local_kv = full_key.shape[1] // HEAD_DIM
    group_size = local_heads // local_kv
    query_raw = jnp.dot(normed_attn, full_query, preferred_element_type=jnp.float32).reshape(
        row_count, local_heads, HEAD_DIM
    )
    queries = rotate(query_raw, cos_table, sin_table).astype(jnp.bfloat16)
    key_raw = jnp.dot(normed_attn, full_key, preferred_element_type=jnp.float32).reshape(
        row_count, local_kv, HEAD_DIM
    )
    key_own = rotate(key_raw, cos_table, sin_table).astype(jnp.bfloat16)
    value_own = (
        jnp.dot(normed_attn, full_value, preferred_element_type=jnp.float32)
        .astype(jnp.bfloat16)
        .reshape(row_count, local_kv, HEAD_DIM)
    )
    pack_keys, pack_values = (
        lax.all_gather(key_own, "ctx", axis=0, tiled=True),
        lax.all_gather(value_own, "ctx", axis=0, tiled=True),
    )
    grouped = queries.reshape(row_count, local_kv, group_size, HEAD_DIM)
    mixed_full, log_total = attention_forward(
        grouped, pack_keys, pack_values, doc_ids, doc_first, base_row, block_rows
    )
    attended = mixed_full.astype(jnp.bfloat16)
    out_part = jnp.dot(attended, full_out, preferred_element_type=jnp.float32)
    attn_out = lax.psum(out_part, "tp")
    middle = x_float + attn_out
    moe_gain = gain_moe.astype(jnp.float32)
    inverse_moe, scaled_moe, normed_mid = rms_parts(middle, moe_gain)
    normed_moe = normed_mid.astype(jnp.bfloat16)
    logits = jnp.dot(normed_moe, full_router, preferred_element_type=jnp.float32)
    shifted = jnp.exp(logits - jnp.max(logits, axis=-1, keepdims=True))
    router_probs = shifted / jnp.sum(shifted, axis=-1, keepdims=True)
    expert_ids = jnp.arange(expert_count, dtype=jnp.int32)
    route_mask = (routes[:, :, None] == expert_ids[None, None, :]).astype(jnp.float32)
    chosen = jnp.sum(route_mask * router_probs[:, None, :], axis=-1)
    chosen_total = jnp.sum(chosen, axis=-1, keepdims=True)
    gate_weights = chosen / chosen_total
    counts_global, probs_global = lax.psum(
        (jnp.sum(route_mask, axis=(0, 1)), jnp.sum(router_probs, axis=0)), ("fsdp", "ctx")
    )
    token_total = pack_count * fsdp_count
    fraction = counts_global / (token_total * top_count)
    balance_loss = (expert_count * jnp.sum(fraction * (probs_global / token_total))).reshape(1)
    flat_routes = routes.reshape(-1)
    flat_mask = (flat_routes[:, None] == expert_ids[None, :]).astype(jnp.int32)
    slot_rank = jnp.sum(jnp.cumsum(flat_mask, axis=0) * flat_mask, axis=1) - 1
    slot_index = flat_routes * capacity + slot_rank
    buffer_rows = expert_count * capacity
    send_rows = (
        jnp.zeros((buffer_rows, model_width), jnp.bfloat16)
        .at[slot_index]
        .set(jnp.repeat(normed_moe, top_count, axis=0))
    )
    send_rows = send_rows.reshape(fsdp_count, local_experts * capacity, model_width)
    arrived = lax.all_to_all(send_rows, "fsdp", split_axis=0, concat_axis=0, tiled=True)
    expert_rows = to_expert(arrived, local_experts, capacity)
    gate_pre, up_pre, hidden = expert_forward(expert_rows, w_gate, w_up)
    expert_out = jnp.einsum(
        "erf,efd->erd", hidden, w_down, preferred_element_type=jnp.float32
    ).astype(jnp.bfloat16)
    returned = lax.all_to_all(
        from_expert(expert_out, fsdp_count, capacity),
        "fsdp",
        split_axis=0,
        concat_axis=0,
        tiled=True,
    )
    slot_values = returned.reshape(buffer_rows, model_width)[slot_index].reshape(
        row_count, top_count, model_width
    )
    moe_part = jnp.sum(gate_weights[:, :, None] * slot_values, axis=1)
    moe_out = lax.psum(moe_part.astype(jnp.bfloat16), "tp").astype(jnp.float32)
    output = (middle + moe_out).astype(jnp.bfloat16)
    upstream = out_grad.astype(jnp.float32)
    gate_dots = jnp.sum(slot_values * upstream[:, None, :], axis=-1)
    grad_slots = (
        (gate_weights[:, :, None] * upstream[:, None, :])
        .astype(jnp.bfloat16)
        .reshape(row_count * top_count, model_width)
    )
    grad_send = jnp.zeros((buffer_rows, model_width), jnp.bfloat16).at[slot_index].set(grad_slots)
    grad_send = grad_send.reshape(fsdp_count, local_experts * capacity, model_width)
    grad_arrived = lax.all_to_all(grad_send, "fsdp", split_axis=0, concat_axis=0, tiled=True)
    kept_gate, kept_up, kept_hidden = (gate_pre, up_pre, hidden)
    grad_expert = to_expert(grad_arrived, local_experts, capacity)
    grad_hidden = jnp.einsum(
        "erd,efd->erf", grad_expert, w_down, preferred_element_type=jnp.float32
    )
    down_grad = jnp.einsum(
        "erf,erd->efd", kept_hidden, grad_expert, preferred_element_type=jnp.float32
    )
    sigmoid_gate = jax.nn.sigmoid(kept_gate)
    grad_gate = (
        grad_hidden * kept_up * sigmoid_gate * (1.0 + kept_gate * (1.0 - sigmoid_gate))
    ).astype(jnp.bfloat16)
    grad_up = (grad_hidden * kept_gate * sigmoid_gate).astype(jnp.bfloat16)
    gate_grad_w = jnp.einsum(
        "erd,erf->edf", expert_rows, grad_gate, preferred_element_type=jnp.float32
    )
    up_grad_w = jnp.einsum("erd,erf->edf", expert_rows, grad_up, preferred_element_type=jnp.float32)
    grad_rows = jnp.einsum("erf,edf->erd", grad_gate, w_gate, preferred_element_type=jnp.float32)
    grad_rows = (
        grad_rows + jnp.einsum("erf,edf->erd", grad_up, w_up, preferred_element_type=jnp.float32)
    ).astype(jnp.bfloat16)
    grad_back = lax.all_to_all(
        from_expert(grad_rows, fsdp_count, capacity),
        "fsdp",
        split_axis=0,
        concat_axis=0,
        tiled=True,
    )
    grad_slot_rows = grad_back.reshape(buffer_rows, model_width)[slot_index].reshape(
        row_count, top_count, model_width
    )
    moe_in_part = jnp.sum(grad_slot_rows.astype(jnp.float32), axis=1)
    moe_in_grad, gate_grad = lax.psum((moe_in_part, gate_dots), "tp")
    weighted = jnp.sum(gate_grad * gate_weights, axis=-1, keepdims=True)
    chosen_grad = (gate_grad - weighted) / chosen_total
    prob_grad = (
        jnp.sum(route_mask * chosen_grad[:, :, None], axis=1)
        + loss_grad[0] * expert_count * fraction / token_total
    )
    logit_grad = router_probs * (
        prob_grad - jnp.sum(prob_grad * router_probs, axis=-1, keepdims=True)
    )
    router_grad = jnp.einsum(
        "td,te->de", normed_moe.astype(jnp.float32), logit_grad, precision=highest
    )
    moe_grad = moe_in_grad + jnp.einsum(
        "te,de->td", logit_grad, full_router.astype(jnp.float32), precision=highest
    )
    gain_moe_grad, middle_norm_grad = rms_back_gain(inverse_moe, scaled_moe, moe_gain, moe_grad)
    middle_grad = upstream + middle_norm_grad
    out_in = middle_grad.astype(jnp.bfloat16)
    out_w_grad = jnp.einsum("tq,td->qd", attended, out_in, preferred_element_type=jnp.float32)
    mixed_grad = jnp.einsum(
        "td,qd->tq", out_in, full_out, preferred_element_type=jnp.float32
    ).astype(jnp.bfloat16)
    query_acc, key_grad_pack, value_grad_pack = attention_backward(
        grouped,
        pack_keys,
        pack_values,
        mixed_grad,
        log_total,
        doc_ids,
        doc_first,
        base_row,
        block_rows,
    )
    key_grad, value_grad, gate_w_out, up_w_out, down_w_out = (
        lax.psum_scatter(key_grad_pack, "ctx", scatter_dimension=0, tiled=True),
        lax.psum_scatter(value_grad_pack, "ctx", scatter_dimension=0, tiled=True),
        lax.psum_scatter(gate_grad_w, "ctx", scatter_dimension=1, tiled=True),
        lax.psum_scatter(up_grad_w, "ctx", scatter_dimension=1, tiled=True),
        lax.psum_scatter(down_grad, "ctx", scatter_dimension=2, tiled=True),
    )
    query_grad = (
        rotate(query_acc.reshape(row_count, local_heads, HEAD_DIM), cos_table, -sin_table)
        .astype(jnp.bfloat16)
        .reshape(row_count, local_heads * HEAD_DIM)
    )
    key_grad_low = (
        rotate(key_grad, cos_table, -sin_table)
        .astype(jnp.bfloat16)
        .reshape(row_count, local_kv * HEAD_DIM)
    )
    value_grad_low = value_grad.astype(jnp.bfloat16).reshape(row_count, local_kv * HEAD_DIM)
    query_w_grad = jnp.einsum(
        "td,tq->dq", normed_attn, query_grad, preferred_element_type=jnp.float32
    )
    key_w_grad = jnp.einsum(
        "td,tq->dq", normed_attn, key_grad_low, preferred_element_type=jnp.float32
    )
    value_w_grad = jnp.einsum(
        "td,tq->dq", normed_attn, value_grad_low, preferred_element_type=jnp.float32
    )
    attn_in_part = jnp.einsum(
        "tq,dq->td", query_grad, full_query, preferred_element_type=jnp.float32
    )
    attn_in_part = attn_in_part + jnp.einsum(
        "tq,dq->td", key_grad_low, full_key, preferred_element_type=jnp.float32
    )
    attn_in_part = attn_in_part + jnp.einsum(
        "tq,dq->td", value_grad_low, full_value, preferred_element_type=jnp.float32
    )
    attn_in_grad = lax.psum(attn_in_part.astype(jnp.bfloat16), "tp").astype(jnp.float32)
    gain_attn_grad, input_norm_grad = rms_back_gain(inverse_attn, scaled_attn, attn_gain, attn_in_grad)
    tokens_grad = middle_grad + input_norm_grad
    shard_grads = (
        lax.psum_scatter(gain_attn_grad, ("fsdp", "ctx"), scatter_dimension=0, tiled=True),
        lax.psum_scatter(query_w_grad, ("fsdp", "ctx"), scatter_dimension=0, tiled=True),
        lax.psum_scatter(key_w_grad, ("fsdp", "ctx"), scatter_dimension=0, tiled=True),
        lax.psum_scatter(value_w_grad, ("fsdp", "ctx"), scatter_dimension=0, tiled=True),
        lax.psum_scatter(out_w_grad, ("fsdp", "ctx"), scatter_dimension=1, tiled=True),
        lax.psum_scatter(gain_moe_grad, ("fsdp", "ctx"), scatter_dimension=0, tiled=True),
        lax.psum_scatter(router_grad, ("fsdp", "ctx"), scatter_dimension=0, tiled=True),
    )
    return (
        output,
        balance_loss,
        tokens_grad,
        shard_grads[0],
        shard_grads[1],
        shard_grads[2],
        shard_grads[3],
        shard_grads[4],
        shard_grads[5],
        shard_grads[6],
        gate_w_out,
        up_w_out,
        down_w_out,
    )


def on_device(
    tokens,
    lengths,
    routes,
    norm_attn,
    w_query,
    w_key,
    w_value,
    w_out,
    norm_moe,
    w_router,
    w_gate,
    w_up,
    w_down,
    out_grad,
    loss_grad,
):
    expert_count = w_router.shape[1]
    if lax.axis_size("fsdp") != 8:
        return on_any_slice(
            tokens, lengths, routes, norm_attn, w_query, w_key, w_value, w_out, norm_moe, w_router,
            w_gate, w_up, w_down, out_grad, loss_grad,
        )
    small = widen([w_router, norm_attn[:, None], norm_moe[:, None]])
    (
        probs, mask, row, lse, cos, sin, returned, middle, query, kv_pack, attended,
        in_weights, out_weights, moe_rows, gate_up_grad, down_grad,
    ) = layer_on_chip(
        lengths, loss_grad, routes, tokens, small, w_query, w_key, w_value, w_out.T, out_grad,
        w_gate[0], w_up[0], w_down[0], expert_count,
    )
    (
        output, loss, tokens_grad, query_grad, key_grad, value_grad, out_reduced, small, gate_w_out, up_w_out, down_w_out,
    ) = backward_on_chip(
        lengths, row, returned, middle, probs, mask, out_grad, tokens, query, kv_pack, lse, attended, cos, sin,
        in_weights, out_weights, moe_rows, gate_up_grad, down_grad, expert_count,
    )
    return (
        output,
        loss[0, :1],
        tokens_grad,
        small[:, expert_count],
        query_grad,
        key_grad,
        value_grad,
        out_reduced.T,
        small[:, expert_count + 1],
        small[:, :expert_count],
        gate_w_out[None],
        up_w_out[None],
        down_w_out[None],
    )


def solution(mesh):
    rows = P(("fsdp", "ctx"), None)
    gain = P(("fsdp", "ctx"))
    split = P(("fsdp", "ctx"), "tp")
    out_split = P("tp", ("fsdp", "ctx"))
    columns = P("fsdp", None, "tp")
    return jax.shard_map(
        on_device,
        mesh=mesh,
        in_specs=(
            rows,
            P("fsdp", None),
            rows,
            gain,
            split,
            split,
            split,
            out_split,
            gain,
            rows,
            columns,
            columns,
            P("fsdp", "tp", None),
            rows,
            P(),
        ),
        out_specs=(
            rows,
            P(),
            rows,
            gain,
            split,
            split,
            split,
            out_split,
            gain,
            rows,
            P("fsdp", "ctx", "tp"),
            P("fsdp", "ctx", "tp"),
            P("fsdp", "tp", "ctx"),
        ),
        check_vma=False,
    )
```

```python
import functools
import math

import jax
import jax.experimental.pallas as pl
import jax.experimental.pallas.tpu as pltpu
import jax.numpy as jnp
from jax import lax
from jax.sharding import PartitionSpec as P

HEAD_DIM = 128
SHARE = 2
epsilon = 1e-06
rope_base = 10000.0
masked_score = -1e30
highest = lax.Precision.HIGHEST
f32 = jnp.float32
bf16 = jnp.bfloat16


def rms_parts(values, row_gains):
    inverse = lax.rsqrt(jnp.mean(values * values, axis=-1, keepdims=True) + epsilon)
    scaled = values * inverse
    return (inverse, scaled, scaled * row_gains)


def rms_back(inverse, scaled, row_gains, upstream):
    scaled_grad = upstream * row_gains
    return inverse * (scaled_grad - scaled * jnp.mean(scaled_grad * scaled, axis=-1, keepdims=True))


def rope_tables(positions):
    half_dim = HEAD_DIM // 2
    frequency = rope_base ** (-(jnp.arange(half_dim, dtype=f32) * (2.0 / HEAD_DIM)))
    angles = positions.astype(f32)[:, None] * frequency[None, :]
    return (jnp.cos(angles)[:, None, :], jnp.sin(angles)[:, None, :])


def rotate(vectors, cos_table, sin_table):
    half_dim = vectors.shape[-1] // 2
    first_half = vectors[..., :half_dim]
    second_half = vectors[..., half_dim:]
    return jnp.concatenate(
        [
            first_half * cos_table - second_half * sin_table,
            second_half * cos_table + first_half * sin_table,
        ],
        axis=-1,
    )


def pack_layout(length_row, row_count):
    doc_ends = jnp.cumsum(length_row)
    doc_starts = doc_ends - length_row
    row_index = jnp.arange(row_count, dtype=jnp.int32)
    doc_ids = jnp.sum((row_index[:, None] >= doc_ends[None, :]).astype(jnp.int32), axis=1)
    doc_numbers = jnp.arange(length_row.shape[0], dtype=jnp.int32)
    doc_first = jnp.sum(
        jnp.where(doc_ids[:, None] == doc_numbers[None, :], doc_starts[None, :], 0), axis=1
    )
    return (doc_ids, row_index - doc_first, doc_first)


def key_block_data(key_number, block_rows, pack_keys, pack_values, doc_ids):
    key_start = key_number * block_rows
    key_block = lax.dynamic_slice_in_dim(pack_keys, key_start, block_rows, 0)
    value_block = lax.dynamic_slice_in_dim(pack_values, key_start, block_rows, 0)
    key_docs = lax.dynamic_slice_in_dim(doc_ids, key_start, block_rows, 0)
    key_index = key_start + jnp.arange(block_rows, dtype=jnp.int32)
    return (key_start, key_block, value_block, key_docs, key_index)


def block_scores(query_block, key_block, query_docs, query_index, key_docs, key_index):
    scale_factor = HEAD_DIM ** (-0.5)
    scores = (
        jnp.einsum("qhgd,khd->hgqk", query_block, key_block, preferred_element_type=f32)
        * scale_factor
    )
    allowed = (query_docs[:, None] == key_docs[None, :]) & (
        key_index[None, :] <= query_index[:, None]
    )
    return (scores, allowed)


def query_block_range(start_row, block_rows, doc_ids, doc_first):
    query_index = start_row + jnp.arange(block_rows, dtype=jnp.int32)
    query_docs = lax.dynamic_slice_in_dim(doc_ids, start_row, block_rows, 0)
    low_block = doc_first[start_row] // block_rows
    high_block = (start_row + block_rows - 1) // block_rows + 1
    return (query_index, query_docs, low_block, high_block)


def attention_forward(grouped, pack_keys, pack_values, doc_ids, doc_first, base_row, block_rows):
    row_count, local_kv, group_size, head_dim = grouped.shape
    query_index, query_docs, low_block, high_block = query_block_range(
        base_row, block_rows, doc_ids, doc_first
    )

    def scan_maxima(key_number, running):
        maxima, totals = running
        key_start, key_block, value_block, key_docs, key_index = key_block_data(
            key_number, block_rows, pack_keys, pack_values, doc_ids
        )
        scores, allowed = block_scores(
            grouped, key_block, query_docs, query_index, key_docs, key_index
        )
        new_max = jnp.maximum(maxima, jnp.max(jnp.where(allowed, scores, masked_score), axis=-1))
        weights = jnp.where(allowed, jnp.exp(scores - new_max[..., None]), 0.0)
        return (new_max, totals * jnp.exp(maxima - new_max) + jnp.sum(weights, axis=-1))

    start_max = jnp.full((local_kv, group_size, block_rows), masked_score, f32)
    start_total = jnp.zeros((local_kv, group_size, block_rows), f32)
    maxima, totals = lax.fori_loop(low_block, high_block, scan_maxima, (start_max, start_total))
    log_total = maxima + jnp.log(totals)

    def accumulate(key_number, summed):
        key_start, key_block, value_block, key_docs, key_index = key_block_data(
            key_number, block_rows, pack_keys, pack_values, doc_ids
        )
        scores, allowed = block_scores(
            grouped, key_block, query_docs, query_index, key_docs, key_index
        )
        block_probs = jnp.where(allowed, jnp.exp(scores - log_total[..., None]), 0.0).astype(bf16)
        return summed + jnp.einsum(
            "hgqk,khd->hgqd", block_probs, value_block, preferred_element_type=f32
        )

    summed = lax.fori_loop(
        low_block,
        high_block,
        accumulate,
        jnp.zeros((local_kv, group_size, block_rows, head_dim), f32),
    )
    outputs = summed.transpose(2, 0, 1, 3).reshape(block_rows, local_kv * group_size * head_dim)
    return (outputs, log_total)


def attention_backward(
    grouped, pack_keys, pack_values, grad_mixed, log_total, doc_ids, doc_first, base_row, block_rows
):
    row_count, local_kv, group_size, head_dim = grouped.shape
    pack_count = pack_keys.shape[0]
    scale_factor = HEAD_DIM ** (-0.5)
    grad_grouped = grad_mixed.reshape(row_count, local_kv, group_size, head_dim)
    key_acc = jnp.zeros((pack_count, local_kv, head_dim), f32)
    value_acc = jnp.zeros((pack_count, local_kv, head_dim), f32)
    query_index, query_docs, low_block, high_block = query_block_range(
        base_row, block_rows, doc_ids, doc_first
    )

    def probs_at(key_number):
        key_start, key_block, value_block, key_docs, key_index = key_block_data(
            key_number, block_rows, pack_keys, pack_values, doc_ids
        )
        scores, allowed = block_scores(
            grouped, key_block, query_docs, query_index, key_docs, key_index
        )
        block_probs = jnp.where(allowed, jnp.exp(scores - log_total[..., None]), 0.0)
        prob_grad = jnp.einsum(
            "qhgd,khd->hgqk", grad_grouped, value_block, preferred_element_type=f32
        )
        return (key_start, key_block, block_probs, prob_grad)

    def add_delta(key_number, row_delta):
        pieces = probs_at(key_number)
        return row_delta + jnp.sum(pieces[2] * pieces[3], axis=-1)

    row_delta = lax.fori_loop(
        low_block, high_block, add_delta, jnp.zeros((local_kv, group_size, block_rows), f32)
    )

    def add_grads(key_number, running):
        query_acc, key_total, value_total = running
        key_start, key_block, block_probs, prob_grad = probs_at(key_number)
        score_grad = (block_probs * (prob_grad - row_delta[..., None])).astype(bf16)
        query_acc = (
            query_acc
            + jnp.einsum("hgqk,khd->qhgd", score_grad, key_block, preferred_element_type=f32)
            * scale_factor
        )
        key_piece = (
            jnp.einsum("hgqk,qhgd->khd", score_grad, grouped, preferred_element_type=f32)
            * scale_factor
        )
        value_piece = jnp.einsum(
            "hgqk,qhgd->khd", block_probs.astype(bf16), grad_grouped, preferred_element_type=f32
        )
        key_total = lax.dynamic_update_slice_in_dim(
            key_total,
            lax.dynamic_slice_in_dim(key_total, key_start, block_rows, 0) + key_piece,
            key_start,
            0,
        )
        value_total = lax.dynamic_update_slice_in_dim(
            value_total,
            lax.dynamic_slice_in_dim(value_total, key_start, block_rows, 0) + value_piece,
            key_start,
            0,
        )
        return (query_acc, key_total, value_total)

    start_query = jnp.zeros((block_rows, local_kv, group_size, head_dim), f32)
    return lax.fori_loop(low_block, high_block, add_grads, (start_query, key_acc, value_acc))


def dot(left, right, left_dim=1, right_dim=0):
    return lax.dot_general(
        left, right, (((left_dim,), (right_dim,)), ((), ())), preferred_element_type=f32
    )


def swap(array, axis, bit=1):
    return lax.ppermute(array, axis, [(i, i ^ bit) for i in range(lax.axis_size(axis))])


def bit_at(axis, bit):
    return (lax.axis_index(axis) // bit) % 2


def side_by_side(mine, theirs, place, axis=0):
    first = jnp.where(place == 0, mine, theirs)
    return jnp.concatenate([first, jnp.where(place == 0, theirs, mine)], axis=axis)


def fsdp_bits():
    size = lax.axis_size("fsdp")
    return [size >> (k + 1) for k in range(size.bit_length() - 1)]


def weight_dims():
    return [("fsdp", bit) for bit in fsdp_bits()] + [("ctx", 1)]


def weight_orders():
    high = [("fsdp", bit) for bit in fsdp_bits()[:-1]]
    low, across = ("fsdp", 1), ("ctx", 1)
    return [high + [across, low], [across, low] + high, [low] + high + [across]]


def gather_rows(block, order):
    dims = weight_dims()
    held = block.reshape((1,) * len(dims) + block.shape)
    for dim in order:
        held = side_by_side(held, swap(held, *dim), bit_at(*dim), dims.index(dim))
    return held.reshape(-1, block.shape[-1])


def reduce_rows(full, order):
    dims = weight_dims()
    rows = full.shape[0] >> len(dims)
    held = full.reshape((2,) * len(dims) + (rows, full.shape[-1]))
    for dim in reversed(order):
        place, k = bit_at(*dim), dims.index(dim)
        sent = lax.dynamic_index_in_dim(held, 1 - place, k).astype(bf16)
        held = lax.dynamic_index_in_dim(held, place, k) + swap(sent, *dim).astype(f32)
    return held.reshape(rows, full.shape[-1])


def thirds(array, pieces):
    units = array.shape[-1] // 128
    ends = [units * k // pieces * 128 for k in range(pieces + 1)]
    return [array[..., a:b] for a, b in zip(ends[:-1], ends[1:])]


def gather_weights(block, orders):
    parts = thirds(block, len(orders))
    return jnp.concatenate([gather_rows(p, o) for p, o in zip(parts, orders)], axis=1)


def reduce_weights(full, orders):
    parts = thirds(full, len(orders))
    return jnp.concatenate([reduce_rows(p, o) for p, o in zip(parts, orders)], axis=1)


def token_bits():
    return [bit for bit in fsdp_bits() if bit != SHARE]


def gather_tokens(block):
    held = {0: block}
    for bit in token_bits():
        held.update({r ^ bit: swap(b, "fsdp", bit) for r, b in held.items()})
    return held


def reduce_tokens(parts):
    held = dict(parts)
    for bit in reversed(token_bits()):
        for r in sorted(held):
            if r & bit:
                got = swap(held.pop(r).astype(bf16), "fsdp", bit)
                held[r ^ bit] = held[r ^ bit] + got.astype(f32)
    return held[0]


def sum_everywhere(small):
    small = small + swap(small, "tp")
    small = small + swap(small, "ctx")
    for bit in fsdp_bits():
        small = small + swap(small, "fsdp", bit)
    return small


def as_pair(values):
    high = lax.reduce_precision(values, 8, 7)
    return [high.astype(bf16), (values - high).astype(bf16)]


def widen(columns):
    width = sum(c.shape[1] for c in columns)
    pad = jnp.zeros((columns[0].shape[0], -width % 128), columns[0].dtype)
    return jnp.concatenate(list(columns) + [pad], axis=1)


def from_pair(columns, count):
    return columns[:, :count].astype(f32) + columns[:, count : 2 * count].astype(f32)


def own_part(array, place, axis=0):
    size = array.shape[axis] // 2
    return lax.dynamic_slice_in_dim(array, place * size, size, axis)


def across_ctx(kept, axis=0):
    place = lax.axis_index("ctx")
    sent = own_part(kept, 1 - place, axis).astype(bf16)
    return own_part(kept, place, axis) + swap(sent, "ctx").astype(f32)


def across_share(kept, axis=1):
    size = kept.shape[axis] // 2
    own = lax.slice_in_dim(kept, 0, size, axis=axis)
    sent = lax.slice_in_dim(kept, size, None, axis=axis).astype(bf16)
    return own + swap(sent, "fsdp", SHARE).astype(f32)


MESH = pl.DeviceIdType.MESH


def peer(fsdp_bit=0, ctx_bit=0, tp_bit=0):
    return (
        lax.axis_index("fsdp") ^ fsdp_bit,
        lax.axis_index("ctx") ^ ctx_bit,
        lax.axis_index("tp") ^ tp_bit,
    )


def greet(peers):
    barrier = pltpu.get_barrier_semaphore()
    for who in peers:
        pl.semaphore_signal(barrier, inc=1, device_id=who, device_id_type=MESH)
    pl.semaphore_wait(barrier, len(peers))


def send(src, dst, sems, k, who):
    copy = pltpu.make_async_remote_copy(
        src_ref=src,
        dst_ref=dst,
        send_sem=sems[0].at[k],
        recv_sem=sems[1].at[k],
        device_id=who,
        device_id_type=MESH,
    )
    copy.start()
    return copy


def dot_nn(a, b):
    return lax.dot_general(a, b, (((1,), (0,)), ((), ())), preferred_element_type=f32)


def dot_nt(a, b):
    return lax.dot_general(a, b, (((1,), (1,)), ((), ())), preferred_element_type=f32)


def aligned(index, size):
    return pl.ds(pl.multiple_of(index * size, size), size)


TILE = 256
CHUNKS = 4


def token_rows(half):
    size = half // CHUNKS
    own = [pl.ds(k * size, size) for k in range(CHUNKS)]
    far = [pl.ds(2 * half + 2 * k * size, size) for k in range(CHUNKS)]
    cross = [pl.ds(2 * half + (2 * k + 1) * size, size) for k in range(CHUNKS)]
    return own, far, cross


class Exchange:
    def __init__(self, send_sems, recv_sems, local_sems):
        self.sems = (send_sems, recv_sems)
        self.local_sems = local_sems
        self.all = []
        self.local = []
        self.arrived = set()
        self.settled = set()
        self.gone = set()

    def start(self, src, dst, who):
        self.all.append(send(src, dst, self.sems, len(self.all), who))
        return len(self.all) - 1

    def keep(self, src, dst):
        copy = pltpu.make_async_copy(src, dst, self.local_sems.at[len(self.local)])
        copy.start()
        self.local.append(copy)
        return len(self.local) - 1

    def arrive(self, number):
        if number not in self.arrived:
            self.arrived.add(number)
            self.all[number].wait_recv()

    def settle(self, number):
        if number not in self.settled:
            self.settled.add(number)
            self.local[number].wait()

    def sent(self, number):
        if number not in self.gone:
            self.gone.add(number)
            self.all[number].wait_send()

    def finish(self):
        for number in range(len(self.all)):
            self.arrive(number)
        for number in range(len(self.all)):
            self.sent(number)
        for number in range(len(self.local)):
            self.settle(number)


class RowGather:
    def __init__(self, net, full, part, order):
        self.net, self.full, self.order = net, full, order
        self.rows, self.first, self.size = part
        self.copies = {}
        self.spread((0, 0), -1)

    def place(self, code):
        index = (lax.axis_index("fsdp") ^ code[0]) * 2 + (lax.axis_index("ctx") ^ code[1])
        return pl.ds(pl.multiple_of(index * self.rows + self.first, 16), self.size)

    def spread(self, code, last):
        block = self.full.at[self.place(code)]
        for position in range(last + 1, len(self.order)):
            axis, bit = self.order[position]
            other = (code[0] ^ bit, code[1]) if axis == "fsdp" else (code[0], code[1] ^ bit)
            self.copies[other] = (self.net.start(block, block, dim_peer((axis, bit))), position)

    def arrive(self, code):
        copy, position = self.copies[code]
        self.net.arrive(copy)
        self.spread(code, position)


def dim_peer(dim):
    axis, bit = dim
    return peer(bit if axis == "fsdp" else 0, bit if axis == "ctx" else 0)


def gather_codes(far, near):
    first = [(SHARE, 0), (far, 0), (far ^ SHARE, 0)]
    rest = [(0, 1), (near, 0), (near, 1)]
    later = [(a ^ b, c) for a, _ in first for b, c in rest]
    return first, rest[:2] + later[0:2] + [rest[2]] + later[3:5] + [later[2]] + later[6:8] + [later[5], later[8]]


def document_start(lengths_ref, number):
    start, first = 0, jnp.zeros_like(number)
    for k in range(lengths_ref.shape[1]):
        start = start + lengths_ref[0, k]
        first = jnp.where(number >= start, start, first)
    return first


def layer_kernel(
    far, near, experts, total_rows,
    lengths_ref, loss_grad_ref, routes_ref, tokens_ref, small_hbm, query_hbm, key_hbm, value_hbm, out_hbm,
    grad_hbm, gate_hbm, up_hbm, down_hbm,
    probs_ref, mask_ref, row_ref, lse_ref, cos_ref, sin_ref,
    dx_hbm, middle_hbm, query_hbm_out, kv_hbm, attended_hbm, in_out, out_out, part_hbm, sum_gu, sum_d,
    weights, xb, gb, wg, wu, wd, kv, h0, hw, dg, du, db, d0, near_in, near_sum, far_in,
    count_sent, count_got,
    send_sems, recv_sems, local_sems, stage_sems, tp_send, tp_recv, free_sem,
):
    far_dev, near_dev, share_dev = peer(far), peer(near), peer(SHARE)
    ctx_dev, core_dev = peer(0, 1), peer(0, 0, 1)
    net = Exchange(send_sems, recv_sems, local_sems)
    place, core = lax.axis_index("ctx"), lax.axis_index("tp")
    rows, width = tokens_ref.shape
    half, quarter = rows // 2, rows // 4
    units = 4 * gate_hbm.shape[1]
    block = small_hbm.shape[0]
    heads_width, kv_width = query_hbm.shape[1], key_hbm.shape[1]
    in_width = small_hbm.shape[1] + heads_width + 2 * kv_width
    in_full = weights.at[:, pl.ds(0, in_width)]
    out_full = weights.at[:, pl.ds(in_width, out_hbm.shape[1])]
    normed = dg.at[pl.ds(0, rows)]
    raw = h0.at[pl.ds(0, rows), pl.ds(0, in_width - 128)]
    core_sent = h0.at[pl.ds(rows, half)]
    middle_ref = h0.at[pl.ds(rows + half, half)]
    core_got = d0.at[:, pl.ds(0, width)]
    query = hw.at[pl.ds(0, rows), pl.ds(0, heads_width)]
    attended = hw.at[pl.ds(rows, rows), pl.ds(0, heads_width)]
    gate_all, up_all, down_all, grads = wg, wu, wd, gb
    own_block = pl.ds(pl.multiple_of((lax.axis_index("fsdp") * 2 + place) * block, 16), block)
    start = 0
    for ref in (small_hbm, query_hbm, key_hbm, value_hbm):
        net.keep(ref, in_full.at[own_block, pl.ds(start, ref.shape[1])])
        start += ref.shape[1]
    net.keep(out_hbm, out_full.at[own_block])
    greet([far_dev, near_dev, share_dev, ctx_dev, core_dev])
    for k in range(5):
        net.settle(k)
    fars = [("fsdp", far), ("fsdp", SHARE)]
    low, across = ("fsdp", near), ("ctx", 1)
    part = block // 2
    ins = [
        RowGather(net, in_full, (block, 0, part), fars + [across, low]),
        RowGather(net, in_full, (block, part, part), fars + [low, across]),
    ]

    routes = routes_ref[...]
    lane = lax.broadcasted_iota(jnp.int32, (rows, 128), 1)
    named = jnp.zeros((rows, 128), f32)
    for k in range(routes.shape[1]):
        named += (routes[:, k : k + 1] == lane).astype(f32)
    count_dims = [ctx_dev, near_dev, share_dev, far_dev]
    counts = [jnp.broadcast_to(jnp.sum(named, axis=0, keepdims=True), (8, 128))]
    count_copies = []

    def count_step():
        k = len(count_copies)
        if k > 0:
            net.arrive(count_copies[-1])
            counts[0] = counts[0] + count_got[k - 1]
        if k < len(count_dims):
            count_sent[k] = counts[0]
            count_copies.append(net.start(count_sent.at[k], count_got.at[k], count_dims[k]))

    count_step()

    piece = units // 4

    def slot(full, number, which=None):
        begin, size = (number * piece, piece) if full is down_all else (0, width)
        if which is not None:
            size //= 2
            begin = pl.multiple_of(begin + which * size, 16)
        if full is down_all:
            return full.at[pl.ds(begin, size)]
        return full.at[pl.ds(begin, size), pl.ds(number * piece, piece)]

    matrices = [(down_hbm, down_all), (gate_hbm, gate_all), (up_hbm, up_all)]
    from_core, own_weights = [], []
    for ref, full in matrices:
        own_weights.append(net.keep(ref, slot(full, 0)))
        from_core.append(net.start(ref, slot(full, 1), core_dev))

    from_share, from_ctx = [], []

    def share_start(k):
        ref, full = matrices[k]
        size = ref.shape[0] // 2
        part_of = ref.at[pl.ds(pl.multiple_of(place * size, 16), size)]
        from_share.append(net.start(part_of, slot(full, 2, place), share_dev))

    def share_on(k):
        ref, full = matrices[k]
        net.arrive(from_share[k])
        from_ctx.append(net.start(slot(full, 2, place), slot(full, 2, place), ctx_dev))
        from_core.append(net.start(slot(full, 2, place), slot(full, 3, place), core_dev))

    here = lax.broadcasted_iota(jnp.int32, (rows, 1), 0) + place * rows
    position = (here - document_start(lengths_ref, here)).astype(f32)
    turn_lane = lax.broadcasted_iota(jnp.int32, (1, HEAD_DIM), 1)
    turn = lax.rem(turn_lane, HEAD_DIM // 2).astype(f32) * (2.0 / HEAD_DIM)
    angles = position * jnp.exp(turn * -math.log(rope_base))
    cos_ref[...] = jnp.cos(angles)
    sin_ref[...] = jnp.where(turn_lane < HEAD_DIM // 2, -1.0, 1.0) * jnp.sin(angles)

    first, rest = gather_codes(far, near)
    for code in first:
        for g in ins:
            g.arrive(code)
    count_step()
    own_rows = pl.ds(pl.multiple_of(core * half, 16), half)
    other_rows = pl.ds(pl.multiple_of((1 - core) * half, 16), half)
    chunk = half // CHUNKS
    own_chunks = [pl.ds(pl.multiple_of(core * half + k * chunk, 16), chunk) for k in range(CHUNKS)]
    _, far_rows, cross_rows = token_rows(half)
    share_start(0)
    own_grad = net.keep(grad_hbm.at[own_rows], grads.at[pl.ds(0, half)])
    from_near = []

    def cross_on(k):
        net.arrive(far_copies[k])
        from_near.append(net.start(grads.at[far_rows[k]], grads.at[cross_rows[k]], near_dev))

    for code in rest[:6]:
        for g in ins:
            g.arrive(code)
    for code in rest[6:]:
        for g in ins:
            g.arrive(code)
    count_step()
    outs = [
        RowGather(net, out_full, (block, 0, part), fars + [across, low]),
        RowGather(net, out_full, (block, part, part), fars + [low, across]),
    ]
    from_near.append(net.start(grad_hbm.at[own_rows], grads.at[pl.ds(half, half)], near_dev))
    gains = in_full[:, :128].astype(f32).T
    attn_gain, moe_gain = gains[experts : experts + 1], gains[experts + 1 : experts + 2]
    step = quarter // 2
    for k in range(rows // quarter):
        at = slice(k * quarter, (k + 1) * quarter)
        x = tokens_ref[at, :].astype(f32)
        inverse = lax.rsqrt(jnp.mean(x * x, axis=1, keepdims=True) + epsilon)
        normed[at, :] = (x * inverse * attn_gain).astype(bf16)

    def rotated(value, at):
        return value * cos_ref[at, :] + pltpu.roll(value, HEAD_DIM // 2, 1) * sin_ref[at, :]

    mine = pl.ds(pl.multiple_of(place * rows, 16), rows)
    raw[...] = dot_nn(normed[...], in_full[:, 128:])
    kv[mine, :kv_width] = rotated(raw[:, heads_width : heads_width + kv_width], slice(None)).astype(bf16)
    kv[mine, kv_width:] = raw[:, heads_width + kv_width :].astype(bf16)
    kv_copy = net.start(kv.at[mine], kv.at[mine], ctx_dev)
    for head in range(heads_width // HEAD_DIM):
        cols = slice(head * HEAD_DIM, (head + 1) * HEAD_DIM)
        query[:, cols] = rotated(raw[:, cols], slice(None)).astype(bf16)
    far_copies = [net.start(grad_hbm.at[own_chunks[k]], grads.at[far_rows[k]], far_dev) for k in range(CHUNKS)]
    net.arrive(from_share[0])
    share_start(1)
    share_on(0)
    for code in first:
        for g in outs:
            g.arrive(code)
    count_step()
    net.arrive(kv_copy)
    net.keep(kv, kv_hbm)
    net.arrive(from_share[1])
    share_start(2)
    share_on(1)
    cross_on(0)

    keys, values_flipped = kv[:, :HEAD_DIM], kv[:, HEAD_DIM:].T
    query_number = lax.broadcasted_iota(jnp.int32, (1, half), 1) + place * rows
    key_number = lax.broadcasted_iota(jnp.int32, (kv.shape[0], 1), 0)
    scale = HEAD_DIM ** (-0.5)

    def head_block(i, carry):
        head, block_index = i // 2, lax.rem(i, 2)
        cols, at = aligned(head, HEAD_DIM), aligned(block_index, half)
        number = query_number + block_index * half
        allowed = (key_number >= document_start(lengths_ref, number)) & (key_number <= number)
        scores = jnp.where(allowed, dot_nt(keys, query[at, cols]) * scale, masked_score)
        maxima = jnp.max(scores, axis=0, keepdims=True)
        weights = jnp.exp(scores - maxima)
        totals = jnp.sum(weights, axis=0, keepdims=True)
        lse_ref[pl.ds(head, 1), at] = maxima + jnp.log(totals)
        low_weights = (weights * (1.0 / totals)).astype(bf16)
        attended[at, cols] = dot_nn(values_flipped, low_weights).T.astype(bf16)
        return carry

    group = heads_width // HEAD_DIM
    third = 2 * group // 3
    lax.fori_loop(0, third, head_block, 0)
    for code in rest[:6]:
        for g in outs:
            g.arrive(code)
    cross_on(1)
    lax.fori_loop(third, 2 * third, head_block, 0)
    for code in rest[6:]:
        for g in outs:
            g.arrive(code)
    cross_on(2)
    count_step()
    lax.fori_loop(2 * third, 2 * group, head_block, 0)
    cross_on(3)

    saved = [net.keep(query, query_hbm_out), net.keep(attended, attended_hbm)]

    core_sent[...] = dot_nt(attended[other_rows, :], out_full[...])
    core_copy = net.start(core_sent, core_got, core_dev)
    share_on(2)
    middle_ref[...] = tokens_ref[own_rows, :].astype(f32) + dot_nt(attended[own_rows, :], out_full[...])
    net.arrive(core_copy)
    own_lane = lax.broadcasted_iota(jnp.int32, (step, 128), 1)
    share_row = counts[0][0:1] * (experts / (total_rows * routes.shape[1] * total_rows))
    row_number = lax.broadcasted_iota(jnp.int32, (8, 128), 0)
    row_ref[...] = jnp.where(
        row_number == 0, share_row * loss_grad_ref[0], jnp.where(row_number == 1, share_row, 0.0)
    )
    router = in_full[:, :128]
    _, token_slots, _ = token_rows(half)
    token_far = []
    for k in range(half // step):
        at = slice(k * step, (k + 1) * step)
        middle = middle_ref[at, :] + core_got[at, :]
        middle_ref[at, :] = middle
        inverse = lax.rsqrt(jnp.mean(middle * middle, axis=1, keepdims=True) + epsilon)
        normed_moe = (middle * inverse * moe_gain).astype(bf16)
        xb[at, :width] = normed_moe
        logits = jnp.where(own_lane < experts, dot_nn(normed_moe, router), masked_score)
        shifted = jnp.exp(logits - jnp.max(logits, axis=1, keepdims=True))
        probs = shifted / jnp.sum(shifted, axis=1, keepdims=True)
        own_routes = routes_ref[pl.ds(pl.multiple_of(core * half + k * step, 16), step), :]
        mask = jnp.zeros((step, 128), f32)
        for n in range(routes.shape[1]):
            mask += (own_routes[:, n : n + 1] == own_lane).astype(f32)
        probs_ref[at, :] = probs
        mask_ref[at, :] = mask
        chosen = probs * mask
        gates = chosen / jnp.sum(chosen, axis=1, keepdims=True)
        high = gates.astype(bf16).astype(f32)
        xb[at, width:] = (high + pltpu.roll(gates - high, experts, 1)).astype(bf16)
        token_far.append(net.start(xb.at[pl.ds(k * step, step)], xb.at[token_slots[k]], far_dev))

    saved.append(net.keep(middle_ref, middle_hbm))
    token_near = net.start(xb.at[pl.ds(0, half)], xb.at[pl.ds(half, half)], near_dev)
    own_chunks, far_rows, cross_rows = token_rows(half)
    near_rows = pl.ds(half, half)
    forwards, crossed, backs = [], [], []

    def pass_on(k):
        net.arrive(token_far[k])
        forwards.append(net.start(xb.at[far_rows[k]], xb.at[cross_rows[k]], near_dev))

    def share_last(k):
        ref, full = matrices[k]
        net.arrive(from_ctx[k])
        from_core.append(net.start(slot(full, 2, 1 - place), slot(full, 3, 1 - place), core_dev))

    stored = [net.keep(in_full, in_out), net.keep(out_full, out_out)]
    share_last(0)
    share_last(1)
    for number in saved:
        net.settle(number)
    net.sent(core_copy)
    for copy in from_near:
        net.arrive(copy)
    net.settle(own_grad)
    net.settle(own_weights[0])
    for copy in (from_core[0], from_core[3], from_core[6]):
        net.arrive(copy)
    unit_tiles = units // TILE

    def back_tile(j, carry):
        h0[:, aligned(j, TILE)] = dot_nt(gb[...], wd[aligned(j, TILE), :])
        return carry

    lax.fori_loop(0, unit_tiles, back_tile, 0)
    pass_on(0)
    share_last(2)
    for copy in from_core:
        net.arrive(copy)
    for number in own_weights:
        net.settle(number)

    lane = lax.broadcasted_iota(jnp.int32, (half, 128), 1)
    own = lax.axis_index("fsdp")
    partner = own ^ SHARE

    def task(number):
        rows = pl.ds(number * half, half)
        extra = xb[rows, width:].astype(f32)

        def gate_of(expert):
            mine = (lane == expert) | (lane == experts + expert)
            return jnp.sum(jnp.where(mine, extra, 0.0), axis=1, keepdims=True)

        gates = jnp.concatenate([gate_of(own), gate_of(partner)], axis=1)

        def unit_tile(j, dots):
            cols = aligned(j, TILE)
            is_own = j < unit_tiles // 2
            gate = jnp.where(is_own, gates[:, :1], gates[:, 1:])
            x = xb[rows, :width]
            gate_pre = dot_nn(x, wg[:, cols])
            up_pre = dot_nn(x, wu[:, cols])
            back = h0[rows, cols]
            sig = 1.0 / (1.0 + jnp.exp(-gate_pre))
            silu = gate_pre * sig
            hidden = silu * up_pre
            hw[rows, cols] = (hidden * gate).astype(bf16)
            hidden_grad = back * gate
            dg[rows, cols] = (hidden_grad * up_pre * (sig * (1.0 + gate_pre * (1.0 - sig)))).astype(bf16)
            du[rows, cols] = (hidden_grad * silu).astype(bf16)
            one = jnp.sum(hidden * back, axis=1, keepdims=True)
            return (
                dots[0] + jnp.where(is_own, one, 0.0),
                dots[1] + jnp.where(is_own, 0.0, one),
            )

        zero = jnp.zeros((half, 1), f32)
        dots = lax.fori_loop(0, unit_tiles, unit_tile, (zero, zero), unroll=True)

        def put(cols, value):
            if number == 0:
                d0[:, cols] = value
            else:
                db[rows, cols] = value.astype(bf16)

        def in_tile(n, carry):
            cols = aligned(n, 2 * TILE)
            value = dot_nt(dg[rows, :], wg[cols, :]) + dot_nt(du[rows, :], wu[cols, :])
            put(cols, value)
            return carry

        lax.fori_loop(0, width // (2 * TILE), in_tile, 0, unroll=True)
        columns = jnp.zeros_like(extra)
        for expert, value in ((own, dots[0]), (partner, dots[1])):
            high = value.astype(bf16).astype(f32)
            columns = jnp.where(lane == expert, high, columns)
            columns = jnp.where(lane == experts + expert, value - high, columns)
        put(slice(width, None), columns)

    def cross_back(k):
        crossed.append(net.start(db.at[cross_rows[k]], near_in.at[own_chunks[k]], near_dev))

    def far_back(k):
        net.arrive(crossed[k])
        total = db[far_rows[k], :].astype(f32) + near_in[own_chunks[k], :].astype(f32)
        db[far_rows[k], :] = total.astype(bf16)
        backs.append(net.start(db.at[far_rows[k]], far_in.at[own_chunks[k]], far_dev))

    task(0)
    pass_on(1)
    pass_on(2)
    net.arrive(forwards[0])
    net.arrive(forwards[1])
    task(2)
    cross_back(0)
    cross_back(1)
    net.arrive(token_near)
    task(1)
    far_back(0)
    far_back(1)
    pass_on(3)
    net.arrive(forwards[2])
    net.arrive(forwards[3])
    task(3)
    cross_back(2)
    cross_back(3)
    near_back = net.start(db.at[near_rows], near_sum, near_dev)

    for copy in from_share + from_ctx + from_core:
        net.sent(copy)
    pl.semaphore_signal(free_sem, inc=1, device_id=core_dev, device_id_type=MESH)
    for g in ins + outs:
        for copy, _ in g.copies.values():
            net.sent(copy)
    for number in stored:
        net.settle(number)

    keep_rows, send_rows = 0, 2 * piece

    def stage_rows(base, slot, size):
        return pl.ds(pl.multiple_of(base + slot * piece, 16), size)

    tiles = width // TILE

    def to_core(slot, number, rows, size, got):
        return pltpu.make_async_remote_copy(
            src_ref=weights.at[stage_rows(send_rows, slot, size), pl.ds(0, width)],
            dst_ref=got.at[rows],
            send_sem=tp_send.at[slot],
            recv_sem=tp_recv.at[number],
            device_id=core_dev,
            device_id_type=MESH,
        )

    def to_hbm(slot, rows, size, full):
        return pltpu.make_async_copy(
            weights.at[stage_rows(keep_rows, slot, size), pl.ds(0, width)], full.at[rows], stage_sems.at[slot]
        )

    def gradient_loop(count, first, size, compute, got, full):
        def close(i):
            slot, rows = lax.rem(i, 2), aligned(i, size)
            to_core(slot, first + i, rows, size, got).wait_recv()
            at = stage_rows(keep_rows, slot, size)
            keep = weights[at, :width].astype(f32) + got[rows, :].astype(f32)
            weights[at, :width] = keep.astype(bf16)
            to_hbm(slot, rows, size, full).start()

        def free(slot):
            to_hbm(slot, pl.ds(0, size), size, full).wait()
            to_core(slot, 0, pl.ds(0, size), size, got).wait_send()

        def one(i, carry):
            slot = lax.rem(i, 2)

            @pl.when(i >= 2)
            def _():
                free(slot)

            compute(i, slot)
            to_core(slot, first + i, aligned(i, size), size, got).start()

            @pl.when(i >= 1)
            def _():
                close(i - 1)

            return carry

        lax.fori_loop(0, count, one, 0)
        close(count - 1)
        free(0)
        free(1)

    def gate_up_tile(i, slot):
        flipped = xb[:, aligned(i, TILE)].T
        for k, source in enumerate((dg, du)):
            value = dot_nn(flipped, source[...]).astype(bf16)
            for p in range(4):
                at = (2 * k + p // 2) * piece
                base = keep_rows if p % 2 == 0 else send_rows
                weights[stage_rows(base, slot, TILE), at : at + piece] = value[:, p * piece : (p + 1) * piece]

    def down_tile(i, slot):
        for base, offset in ((keep_rows, 0), (send_rows, piece)):
            cols = pl.ds(pl.multiple_of(i * 2 * piece + offset, 128), piece)
            flipped = hw[:, cols].T
            for n in range(0, width, 2 * TILE):
                weights[stage_rows(base, slot, piece), n : n + 2 * TILE] = dot_nn(flipped, gb[:, n : n + 2 * TILE]).astype(bf16)

    pl.semaphore_wait(free_sem, 1)
    gradient_loop(2, tiles, piece, down_tile, wg, sum_d)
    far_back(2)

    for k in range(4):
        at = slice(k * half, (k + 1) * half)
        hw[at, :] = dot_nn(hw[at, :], wd[...]).astype(bf16)
        if k == 1:
            far_back(3)
    net.keep(hw, part_hbm)
    gradient_loop(tiles, 0, TILE, gate_up_tile, wu, sum_gu)
    net.arrive(near_back)
    for copy in backs:
        net.arrive(copy)
    d0[...] = d0[...] + near_sum[...].astype(f32) + far_in[...].astype(f32)
    net.keep(d0, dx_hbm)
    net.finish()


def layer_on_chip(
    lengths, loss_grad, routes, tokens, small, w_query, w_key, w_value, out_block, out_grad, gate, up, down, experts
):
    far, near = token_bits()
    owners = lax.axis_size("fsdp") * lax.axis_size("ctx")
    rows, width = tokens.shape
    half, pack = rows // 2, rows * lax.axis_size("ctx")
    units, block = 4 * gate.shape[1], small.shape[0]
    heads_width, kv_width = w_query.shape[1], w_key.shape[1]
    in_width, out_width = small.shape[1] + heads_width + 2 * kv_width, out_block.shape[1]
    any_spec = pl.BlockSpec(memory_space=pl.ANY)
    vmem = pl.BlockSpec(memory_space=pltpu.VMEM)
    smem = pl.BlockSpec(memory_space=pltpu.SMEM)
    outs = [
        ((half, 128), f32),
        ((half, 128), f32),
        ((8, 128), f32),
        ((-(-heads_width // HEAD_DIM // 8) * 8, rows), f32),
        ((rows, HEAD_DIM), f32),
        ((rows, HEAD_DIM), f32),
        ((half, width + 128), f32),
        ((half, width), f32),
        ((rows, heads_width), bf16),
        ((pack, 2 * kv_width), bf16),
        ((rows, heads_width), bf16),
        ((owners * block, in_width), bf16),
        ((owners * block, out_width), bf16),
        ((2 * rows, width), bf16),
        ((width, units), bf16),
        ((units // 2, width), bf16),
    ]

    def low(*shape):
        return pltpu.VMEM(shape, bf16)

    def wide(*shape):
        return pltpu.VMEM(shape, f32)

    return pl.pallas_call(
        functools.partial(layer_kernel, far, near, experts, rows * owners),
        name="layer",
        out_shape=tuple(jax.ShapeDtypeStruct(s, d) for s, d in outs),
        in_specs=[smem, smem, vmem, vmem] + [any_spec] * 9,
        out_specs=(vmem,) * 6 + (any_spec,) * 10,
        scratch_shapes=[
            low(owners * block, in_width + out_width),
            low(2 * rows, width + 128),
            low(2 * rows, width),
            low(width, units),
            low(width, units),
            low(units, width),
            low(pack, 2 * kv_width),
            wide(2 * rows, units),
            low(2 * rows, units),
            low(2 * rows, units),
            low(2 * rows, units),
            low(2 * rows, width + 128),
            wide(half, width + 128),
            low(half, width + 128),
            low(half, width + 128),
            low(half, width + 128),
            wide(4, 8, 128),
            wide(4, 8, 128),
            pltpu.SemaphoreType.DMA((116,)),
            pltpu.SemaphoreType.DMA((116,)),
            pltpu.SemaphoreType.DMA((20,)),
            pltpu.SemaphoreType.DMA((2,)),
            pltpu.SemaphoreType.DMA((2,)),
            pltpu.SemaphoreType.DMA((width // TILE + 2,)),
            pltpu.SemaphoreType.REGULAR,
        ],
        compiler_params=pltpu.CompilerParams(
            collective_id=0, has_side_effects=True, vmem_limit_bytes=62 * 1024 * 1024
        ),
    )(lengths, loss_grad, routes, tokens, small, w_query, w_key, w_value, out_block, out_grad, gate, up, down)


class RowReduce:
    def __init__(self, net, partial, inbox, part, order):
        self.net, self.partial, self.inbox, self.order = net, partial, inbox, order
        self.rows, self.first, self.size = part
        self.copies = {}

    def place(self, mask):
        fsdp, ctx = 0, 0
        for position, (axis, bit) in enumerate(self.order):
            if mask >> position & 1:
                fsdp, ctx = (fsdp ^ bit, ctx) if axis == "fsdp" else (fsdp, ctx ^ bit)
        index = (lax.axis_index("fsdp") ^ fsdp) * 2 + (lax.axis_index("ctx") ^ ctx)
        return pl.ds(pl.multiple_of(index * self.rows + self.first, 16), self.size)

    def box(self, mask):
        return pl.ds((mask - 1) * self.size, self.size)

    def step(self, mask):
        rows, last = self.place(mask), mask.bit_length() - 1
        if last + 1 < len(self.order):
            value = self.partial[rows, :].astype(f32)
            for later in range(last + 1, len(self.order)):
                source = mask | 1 << later
                self.net.arrive(self.copies[source])
                value = value + self.inbox[self.box(source), :].astype(f32)
            if mask == 0:
                return value
            self.partial[rows, :] = value.astype(bf16)
        self.copies[mask] = self.net.start(
            self.partial.at[rows], self.inbox.at[self.box(mask)], dim_peer(self.order[last])
        )

    def level(self, last):
        for mask in reversed(range(1 << last, 2 << last)):
            self.step(mask)


def backward_kernel(
    far, near, experts, group,
    lengths_ref, row_ref, dx_ref, middle_ref, probs_ref, mask_ref, grad_hbm,
    tokens_hbm, query_hbm, kv_hbm, lse_ref, attended_hbm, cos_ref, sin_ref,
    in_hbm, out_hbm, moe_hbm, gu_hbm, down_hbm,
    output_hbm, loss_ref, tokens_grad_hbm, query_out, key_out, value_out, out_ref, extra_ref, gate_ref, up_ref, down_ref,
    grad_ref, tokens, query, kv, attended, in_full, out_full,
    out_in, att_grad, qkv_grad, kv_grad, kv_sent, kv_got,
    in_box, out_box,
    mid_grad, back_sent, back_got, tok_stage, extra_rows, extra_sent, extra_got,
    moe_own, moe_far, moe_near, moe_cross, moe_back,
    gate_own, gate_x, gate_sent, gate_s,
    up_own, up_s, up_sent, up_x,
    down_own, down_x, down_sent, down_s,
    loss_sent, loss_got,
    send_sems, recv_sems, local_sems,
):
    far_dev, near_dev, share_dev = peer(far), peer(near), peer(SHARE)
    ctx_dev, core_dev = peer(0, 1), peer(0, 0, 1)
    greet([far_dev, near_dev, share_dev, ctx_dev, core_dev])
    net = Exchange(send_sems, recv_sems, local_sems)
    ctx_place, core = lax.axis_index("ctx"), lax.axis_index("tp")
    half, width = middle_ref.shape
    rows = 2 * half
    quarter = half // 2
    own_rows = pl.ds(pl.multiple_of(core * half, 16), half)
    other_rows = pl.ds(pl.multiple_of((1 - core) * half, 16), half)
    chunks, far_rows, cross_rows = token_rows(half)

    crossed = [net.start(moe_hbm.at[cross_rows[k]], moe_cross.at[chunks[k]], near_dev) for k in range(CHUNKS)]
    units = gu_hbm.shape[1] // 4
    wide = width // 2

    def wide_half(place):
        return pl.ds(pl.multiple_of(place * wide, 128), wide)

    gate_cols, up_own_cols, up_par_cols = pl.ds(0, 2 * units), pl.ds(2 * units, units), pl.ds(3 * units, units)
    gate_first = net.start(gu_hbm.at[wide_half(1 - ctx_place), gate_cols], gate_x, ctx_dev)
    up_first = net.start(gu_hbm.at[:, up_par_cols], up_s, share_dev)
    pairs = [
        (in_hbm, in_full), (out_hbm, out_full), (attended_hbm, attended), (query_hbm, query),
        (kv_hbm, kv), (tokens_hbm, tokens), (moe_hbm.at[pl.ds(0, half)], moe_own),
        (gu_hbm.at[wide_half(ctx_place), gate_cols], gate_own), (gu_hbm.at[:, up_own_cols], up_own),
        (down_hbm.at[:, wide_half(ctx_place)], down_own), (grad_hbm.at[own_rows], grad_ref),
    ] + [(moe_hbm.at[far_rows[k]], moe_far.at[chunks[k]]) for k in range(CHUNKS)]
    for src, dst in pairs:
        net.keep(src, dst)

    def loaded(*numbers):
        for number in numbers:
            net.settle(number)

    def pieces(size):
        return [slice(k * size // 4, (k + 1) * size // 4) for k in range(4)]

    loaded(0, 10)
    flipped_extra = in_full[:, :128].astype(f32).T
    attn_gain, moe_gain = flipped_extra[experts : experts + 1], flipped_extra[experts + 1 : experts + 2]
    lane = lax.broadcasted_iota(jnp.int32, (half, 128), 1)
    probs, mask = probs_ref[...], mask_ref[...]
    pair = dx_ref[:, width:]
    gate_grad = jnp.where(lane < experts, pair + pltpu.roll(pair, 128 - experts, 1), 0.0)
    chosen = probs * mask
    chosen_total = jnp.sum(chosen, axis=1, keepdims=True)
    weighted = jnp.sum(gate_grad * chosen, axis=1, keepdims=True) / chosen_total
    prob_grad = mask * (gate_grad - weighted) / chosen_total + row_ref[0:1, :]
    logit_grad = probs * (prob_grad - jnp.sum(prob_grad * probs, axis=1, keepdims=True))
    logit_high = logit_grad.astype(bf16)
    logit_low = (logit_grad - logit_high.astype(f32)).astype(bf16)
    router = in_full[:, :128]
    step = quarter // 2
    gain_moe = jnp.zeros((1, width), f32)
    router_grad = jnp.zeros((128, width), f32)
    for k in range(half // step):
        at = slice(k * step, (k + 1) * step)
        middle = middle_ref[at, :]
        inverse = lax.rsqrt(jnp.mean(middle * middle, axis=1, keepdims=True) + epsilon)
        scaled = middle * inverse
        normed_moe = (scaled * moe_gain).astype(bf16)
        moe_grad = dx_ref[at, :width] + dot_nt(logit_high[at], router) + dot_nt(logit_low[at], router)
        router_grad += dot(logit_high[at], normed_moe, 0, 0) + dot(logit_low[at], normed_moe, 0, 0)
        gain_moe += jnp.sum(moe_grad * scaled, axis=0, keepdims=True)
        a = moe_grad * moe_gain
        grad = grad_ref[at, :].astype(f32) + inverse * (a - scaled * jnp.mean(a * scaled, axis=1, keepdims=True))
        mid_grad[at, :] = grad
        out_in[pl.ds(pl.multiple_of(core * half + k * step, 16), step), :] = grad.astype(bf16)
    out_in_copy = net.start(out_in.at[own_rows], out_in.at[own_rows], core_dev)
    row = lax.broadcasted_iota(jnp.int32, (128, width), 0)
    extra_rows[...] = jnp.where(row == experts + 1, gain_moe, router_grad)

    loss_dims = [core_dev, ctx_dev, near_dev, share_dev, far_dev]
    loss_state = [jnp.broadcast_to(jnp.sum(probs, axis=0, keepdims=True), (8, 128))]
    loss_copies = []

    def loss_step():
        k = len(loss_copies)
        if k > 0:
            net.arrive(loss_copies[-1])
            loss_state[0] = loss_state[0] + loss_got[k - 1]
        if k < len(loss_dims):
            loss_sent[k] = loss_state[0]
            loss_copies.append(net.start(loss_sent.at[k], loss_got.at[k], loss_dims[k]))

    loss_step()
    loaded(6, *range(11, 11 + CHUNKS))
    far_sums = []

    def far_sum(k):
        net.arrive(crossed[k])
        at = chunks[k]
        moe_far[at, :] = (moe_far[at, :].astype(f32) + moe_cross[at, :].astype(f32)).astype(bf16)
        far_sums.append(net.start(moe_far.at[at], moe_back.at[at], far_dev))

    far_sum(0)
    net.arrive(out_in_copy)
    loaded(1, 2)
    att_grad[...] = dot_nn(out_in[...], out_full[...]).astype(bf16)

    def out_tile(i, carry):
        cols = aligned(i, TILE)
        out_full[cols, :] = dot_nn(out_in[:, cols].T, attended[...]).astype(bf16)
        return carry

    lax.fori_loop(0, width // TILE, out_tile, 0)
    block = key_out.shape[0]
    low, across = ("fsdp", near), ("ctx", 1)
    fars = [("fsdp", far), ("fsdp", SHARE)]
    orders = [fars + [across, low], fars + [low, across]]
    part_size = block // 2
    sums_out = [
        RowReduce(net, out_full, out_box.at[k], (block, k * part_size, part_size), [across] + fars + [low])
        for k in range(2)
    ]
    far_sum(1)
    for s in sums_out:
        s.level(3)
    loss_step()
    far_sum(2)
    far_sum(3)
    net.sent(out_in_copy)
    loaded(5)
    normed_step = half // 2
    for k in range(rows // normed_step):
        at = slice(k * normed_step, (k + 1) * normed_step)
        x = tokens[at, :].astype(f32)
        inverse = lax.rsqrt(jnp.mean(x * x, axis=1, keepdims=True) + epsilon)
        out_in[at, :] = (x * inverse * attn_gain).astype(bf16)

    loaded(3, 4)
    pack = kv.shape[0]
    kv_grad[...] = jnp.zeros_like(kv_grad)
    keys, values = kv[:, :HEAD_DIM], kv[:, HEAD_DIM:]
    keys_flipped = keys.T
    query_number = lax.broadcasted_iota(jnp.int32, (1, half), 1) + ctx_place * rows
    key_number = lax.broadcasted_iota(jnp.int32, (pack, 1), 0)
    scale = HEAD_DIM ** (-0.5)

    def head_block(i, carry):
        head, block_index = i // 2, lax.rem(i, 2)
        cols = aligned(head, HEAD_DIM)
        at = aligned(block_index, half)
        number = query_number + block_index * half
        allowed = (key_number >= document_start(lengths_ref, number)) & (key_number <= number)
        q, grad = query[at, cols], att_grad[at, cols]
        log_total = lse_ref[pl.ds(head, 1), at]
        weights = jnp.where(allowed, jnp.exp(dot_nt(keys, q) * scale - log_total), 0.0)
        weight_grad = dot_nt(values, grad)
        delta = jnp.sum(weights * weight_grad, axis=0, keepdims=True)
        score_grad = (weights * (weight_grad - delta)).astype(bf16)
        kv_grad[:, :HEAD_DIM] += dot_nn(score_grad, q) * scale
        kv_grad[:, HEAD_DIM:] += dot_nn(weights.astype(bf16), grad)
        query_grad = (dot_nn(keys_flipped, score_grad) * scale).T
        turned = query_grad * cos_ref[at, :] - pltpu.roll(query_grad, HEAD_DIM // 2, 1) * sin_ref[at, :]
        qkv_grad[at, cols] = turned.astype(bf16)
        return carry

    third = 2 * group // 3
    lax.fori_loop(0, third, head_block, 0)
    loss_step()
    down_first = net.start(down_hbm.at[:, wide_half(1 - ctx_place)], down_x, ctx_dev)
    lax.fori_loop(third, 2 * third, head_block, 0)
    loss_step()
    loaded(7, 8, 9)
    net.arrive(gate_first)
    for at in pieces(wide):
        total = gate_own[at, :].astype(f32) + gate_x[at, :].astype(f32)
        gate_ref[at, :] = total[:, :units]
        gate_sent[at, :] = total[:, units:].astype(bf16)
    gate_last = net.start(gate_sent, gate_s, share_dev)
    net.arrive(up_first)
    up_sent[...] = (up_own[wide_half(1 - ctx_place), :].astype(f32) + up_s[wide_half(1 - ctx_place), :].astype(f32)).astype(bf16)
    up_ref[...] = up_own[wide_half(ctx_place), :].astype(f32) + up_s[wide_half(ctx_place), :].astype(f32)
    lax.fori_loop(2 * third, 2 * group, head_block, 0)
    loss_step()
    ctx_rows = pl.ds(pl.multiple_of(ctx_place * rows, 16), rows)
    ctx_other = pl.ds(pl.multiple_of((1 - ctx_place) * rows, 16), rows)
    kv_sent[...] = kv_grad[ctx_other, :].astype(bf16)
    kv_copy = net.start(kv_sent, kv_got, ctx_dev)
    up_last = net.start(up_sent, up_x, ctx_dev)
    for mask in (7, 6, 5, 4):
        for s in sums_out:
            s.step(mask)
    near_first = net.start(moe_hbm.at[pl.ds(half, half)], moe_near, near_dev)
    loss_step()
    loss = jnp.sum(loss_state[0][0:1] * row_ref[1:2, :], axis=1, keepdims=True)
    loss_ref[...] = jnp.broadcast_to(loss, loss_ref.shape)
    net.arrive(kv_copy)
    kv_sum = kv_grad[ctx_rows, :] + kv_got[...].astype(f32)
    key_grad = kv_sum[:, :HEAD_DIM]
    key_grad = key_grad * cos_ref[...] - pltpu.roll(key_grad, HEAD_DIM // 2, 1) * sin_ref[...]
    heads_width = group * HEAD_DIM
    qkv_grad[:, heads_width : heads_width + HEAD_DIM] = key_grad.astype(bf16)
    qkv_grad[:, heads_width + HEAD_DIM :] = kv_sum[:, HEAD_DIM:].astype(bf16)

    gain_attn = jnp.zeros((1, width), f32)

    def attn_scaled(at):
        x = tokens[at, :].astype(f32)
        inverse = lax.rsqrt(jnp.mean(x * x, axis=1, keepdims=True) + epsilon)
        return inverse, x * inverse

    for k in range(2):
        at = other_rows if k == 0 else own_rows
        part = dot_nt(qkv_grad[at, :], in_full[:, 128:])
        gain_attn += jnp.sum(part * attn_scaled(at)[1], axis=0, keepdims=True)
        if k == 0:
            back_sent[...] = part.astype(bf16)
            back_copy = net.start(back_sent, back_got, core_dev)
        else:
            tok_stage[...] = part
    def in_tile(i, carry):
        cols = aligned(i, TILE)
        in_full[cols, 128:] = dot_nn(out_in[:, cols].T, qkv_grad[...]).astype(bf16)
        return carry

    lax.fori_loop(0, width // TILE, in_tile, 0)
    extra_rows[...] = jnp.where(row == experts, gain_attn, extra_rows[...])
    in_full[:, :128] = extra_rows[...].T.astype(bf16)
    sums_in = [
        RowReduce(net, in_full, in_box.at[k], (block, k * part_size, part_size), orders[k]) for k in range(2)
    ]
    for s in sums_in:
        s.level(3)
    for mask in (3, 2):
        for s in sums_out:
            s.step(mask)

    net.arrive(back_copy)
    for k in range(2):
        at = pl.ds(k * quarter, quarter)
        inverse, scaled = attn_scaled(pl.ds(pl.multiple_of(core * half + k * quarter, 16), quarter))
        a = (tok_stage[at, :] + back_got[at, :].astype(f32)) * attn_gain
        tok_stage[at, :] = mid_grad[at, :] + inverse * (a - scaled * jnp.mean(a * scaled, axis=1, keepdims=True))
    net.keep(tok_stage, tokens_grad_hbm.at[own_rows])
    net.start(tok_stage, tokens_grad_hbm.at[own_rows], core_dev)

    for mask in (7, 6, 5, 4):
        for s in sums_in:
            s.step(mask)
    for s in sums_out:
        s.step(1)
    net.arrive(down_first)
    for at in pieces(units):
        down_ref[at, :] = down_own[at, :].astype(f32) + down_x[at, :].astype(f32)
        after = slice(at.start + units, at.stop + units)
        down_sent[at, :] = (down_own[after, :].astype(f32) + down_x[after, :].astype(f32)).astype(bf16)
    down_last = net.start(down_sent, down_s, share_dev)
    for mask in (3, 2, 1):
        for s in sums_in:
            s.step(mask)

    net.arrive(near_first)
    for k in range(CHUNKS):
        net.arrive(far_sums[k])
        at = chunks[k]
        moe_out = moe_own[at, :].astype(f32) + moe_near[at, :].astype(f32) + moe_back[at, :].astype(f32)
        moe_own[at, :] = (middle_ref[at, :] + moe_out).astype(bf16)
    net.keep(moe_own, output_hbm.at[own_rows])
    net.start(moe_own, output_hbm.at[own_rows], core_dev)

    for k in range(2):
        at = slice(k * part_size, (k + 1) * part_size)
        out_ref[at, :] = sums_out[k].step(0)
        value = sums_in[k].step(0)
        extra_sent[at, :] = value[:, :128]
        query_out[at, :] = value[:, 128 : 128 + heads_width]
        key_out[at, :] = value[:, 128 + heads_width : 128 + heads_width + HEAD_DIM]
        value_out[at, :] = value[:, 128 + heads_width + HEAD_DIM :]
    extra_copy = net.start(extra_sent, extra_got, core_dev)
    net.arrive(gate_last)
    gate_ref[...] += gate_s[...].astype(f32)
    net.arrive(up_last)
    up_ref[...] += up_x[...].astype(f32)
    net.arrive(down_last)
    down_ref[...] += down_s[...].astype(f32)
    net.arrive(extra_copy)
    extra_ref[...] = extra_sent[...] + extra_got[...]
    net.finish()


def backward_on_chip(
    lengths, row, dx, middle, probs, mask, out_grad, tokens, query, kv, lse, attended, cos, sin,
    in_full, out_full, moe_rows, gate_up, down, experts,
):
    far, near = token_bits()
    owners = lax.axis_size("fsdp") * lax.axis_size("ctx")
    half, width = middle.shape
    rows, heads_width = query.shape
    pack, kv_width = kv.shape
    units = down.shape[0] // 2
    block = in_full.shape[0] // owners
    in_width, out_width = in_full.shape[1], out_full.shape[1]
    any_spec = pl.BlockSpec(memory_space=pl.ANY)
    vmem = pl.BlockSpec(memory_space=pltpu.VMEM)
    smem = pl.BlockSpec(memory_space=pltpu.SMEM)

    def low(*shape):
        return pltpu.VMEM(shape, bf16)

    def wide(*shape):
        return pltpu.VMEM(shape, f32)

    boxes = 15 * (block // 2)
    return pl.pallas_call(
        functools.partial(backward_kernel, far, near, experts, heads_width // HEAD_DIM),
        name="backward",
        out_shape=(
            jax.ShapeDtypeStruct((rows, width), bf16),
            jax.ShapeDtypeStruct((8, 128), f32),
            jax.ShapeDtypeStruct((rows, width), f32),
            jax.ShapeDtypeStruct((block, heads_width), f32),
            jax.ShapeDtypeStruct((block, HEAD_DIM), f32),
            jax.ShapeDtypeStruct((block, HEAD_DIM), f32),
            jax.ShapeDtypeStruct((block, out_width), f32),
            jax.ShapeDtypeStruct((block, 128), f32),
            jax.ShapeDtypeStruct((width // 2, units), f32),
            jax.ShapeDtypeStruct((width // 2, units), f32),
            jax.ShapeDtypeStruct((units, width // 2), f32),
        ),
        in_specs=[smem] + [vmem] * 5 + [any_spec] * 4 + [vmem, any_spec, vmem, vmem] + [any_spec] * 5,
        out_specs=(any_spec, vmem, any_spec) + (vmem,) * 8,
        scratch_shapes=[
            low(half, width), low(rows, width), low(rows, heads_width), low(pack, kv_width), low(rows, heads_width),
            low(*in_full.shape), low(*out_full.shape),
            low(rows, width), low(rows, heads_width), low(rows, in_width - 128),
            wide(pack, kv_width), low(rows, kv_width), low(rows, kv_width),
            low(2, boxes, in_width), low(2, boxes, out_width),
            wide(half, width), low(half, width), low(half, width), wide(half, width),
            wide(128, width), wide(block, 128), wide(block, 128),
            low(half, width), low(half, width), low(half, width), low(half, width), low(half, width),
            low(width // 2, 2 * units), low(width // 2, 2 * units), low(width // 2, units), low(width // 2, units),
            low(width, units), low(width, units), low(width // 2, units), low(width // 2, units),
            low(2 * units, width // 2), low(2 * units, width // 2), low(units, width // 2), low(units, width // 2),
            wide(5, 8, 128), wide(5, 8, 128),
            pltpu.SemaphoreType.DMA((100,)),
            pltpu.SemaphoreType.DMA((100,)),
            pltpu.SemaphoreType.DMA((20,)),
        ],
        compiler_params=pltpu.CompilerParams(
            collective_id=2, has_side_effects=True, vmem_limit_bytes=62 * 1024 * 1024
        ),
    )(
        lengths, row, dx, middle, probs, mask, out_grad, tokens, query, kv, lse, attended, cos, sin,
        in_full, out_full, moe_rows, gate_up, down,
    )


def rms_back_gain(inverse, scaled, row_gains, upstream):
    return jnp.sum(upstream * scaled, axis=0), rms_back(inverse, scaled, row_gains, upstream)


def to_expert(arrived, local_experts, capacity):
    sources = arrived.shape[0]
    return (
        arrived.reshape(sources, local_experts, capacity, -1)
        .transpose(1, 0, 2, 3)
        .reshape(local_experts, sources * capacity, -1)
    )


def from_expert(expert_rows, sources, capacity):
    local_experts = expert_rows.shape[0]
    return (
        expert_rows.reshape(local_experts, sources, capacity, -1)
        .transpose(1, 0, 2, 3)
        .reshape(sources, local_experts * capacity, -1)
    )


def expert_forward(expert_rows, w_gate, w_up):
    gate_pre = jnp.einsum("erd,edf->erf", expert_rows, w_gate, preferred_element_type=jnp.float32)
    up_pre = jnp.einsum("erd,edf->erf", expert_rows, w_up, preferred_element_type=jnp.float32)
    hidden = (gate_pre * jax.nn.sigmoid(gate_pre) * up_pre).astype(jnp.bfloat16)
    return (gate_pre, up_pre, hidden)


def on_any_slice(
    tokens,
    lengths,
    routes,
    norm_attn,
    w_query,
    w_key,
    w_value,
    w_out,
    norm_moe,
    w_router,
    w_gate,
    w_up,
    w_down,
    out_grad,
    loss_grad,
):
    row_count, model_width = tokens.shape
    ctx_count = lax.axis_size("ctx")
    fsdp_count = lax.axis_size("fsdp")
    ctx_place = lax.axis_index("ctx")
    top_count = routes.shape[1]
    expert_count = w_router.shape[1]
    local_experts = w_gate.shape[0]
    capacity = 3 * row_count * top_count // (2 * expert_count)
    pack_count = row_count * ctx_count
    block_rows = min(512, row_count)
    base_row = ctx_place * row_count
    gain_attn, full_query, full_key, full_value, full_out, gain_moe, full_router = (
        lax.all_gather(norm_attn, ("fsdp", "ctx"), axis=0, tiled=True),
        lax.all_gather(w_query, ("fsdp", "ctx"), axis=0, tiled=True),
        lax.all_gather(w_key, ("fsdp", "ctx"), axis=0, tiled=True),
        lax.all_gather(w_value, ("fsdp", "ctx"), axis=0, tiled=True),
        lax.all_gather(w_out, ("fsdp", "ctx"), axis=1, tiled=True),
        lax.all_gather(norm_moe, ("fsdp", "ctx"), axis=0, tiled=True),
        lax.all_gather(w_router, ("fsdp", "ctx"), axis=0, tiled=True),
    )
    doc_ids, positions, doc_first = pack_layout(lengths[0], pack_count)
    own_positions = lax.dynamic_slice_in_dim(positions, base_row, row_count, 0)
    cos_table, sin_table = rope_tables(own_positions)
    x_float = tokens.astype(jnp.float32)
    attn_gain = gain_attn.astype(jnp.float32)
    inverse_attn, scaled_attn, normed_full = rms_parts(x_float, attn_gain)
    normed_attn = normed_full.astype(jnp.bfloat16)
    local_heads = full_query.shape[1] // HEAD_DIM
    local_kv = full_key.shape[1] // HEAD_DIM
    group_size = local_heads // local_kv
    query_raw = jnp.dot(normed_attn, full_query, preferred_element_type=jnp.float32).reshape(
        row_count, local_heads, HEAD_DIM
    )
    queries = rotate(query_raw, cos_table, sin_table).astype(jnp.bfloat16)
    key_raw = jnp.dot(normed_attn, full_key, preferred_element_type=jnp.float32).reshape(
        row_count, local_kv, HEAD_DIM
    )
    key_own = rotate(key_raw, cos_table, sin_table).astype(jnp.bfloat16)
    value_own = (
        jnp.dot(normed_attn, full_value, preferred_element_type=jnp.float32)
        .astype(jnp.bfloat16)
        .reshape(row_count, local_kv, HEAD_DIM)
    )
    pack_keys, pack_values = (
        lax.all_gather(key_own, "ctx", axis=0, tiled=True),
        lax.all_gather(value_own, "ctx", axis=0, tiled=True),
    )
    grouped = queries.reshape(row_count, local_kv, group_size, HEAD_DIM)
    mixed_full, log_total = attention_forward(
        grouped, pack_keys, pack_values, doc_ids, doc_first, base_row, block_rows
    )
    attended = mixed_full.astype(jnp.bfloat16)
    out_part = jnp.dot(attended, full_out, preferred_element_type=jnp.float32)
    attn_out = lax.psum(out_part, "tp")
    middle = x_float + attn_out
    moe_gain = gain_moe.astype(jnp.float32)
    inverse_moe, scaled_moe, normed_mid = rms_parts(middle, moe_gain)
    normed_moe = normed_mid.astype(jnp.bfloat16)
    logits = jnp.dot(normed_moe, full_router, preferred_element_type=jnp.float32)
    shifted = jnp.exp(logits - jnp.max(logits, axis=-1, keepdims=True))
    router_probs = shifted / jnp.sum(shifted, axis=-1, keepdims=True)
    expert_ids = jnp.arange(expert_count, dtype=jnp.int32)
    route_mask = (routes[:, :, None] == expert_ids[None, None, :]).astype(jnp.float32)
    chosen = jnp.sum(route_mask * router_probs[:, None, :], axis=-1)
    chosen_total = jnp.sum(chosen, axis=-1, keepdims=True)
    gate_weights = chosen / chosen_total
    counts_global, probs_global = lax.psum(
        (jnp.sum(route_mask, axis=(0, 1)), jnp.sum(router_probs, axis=0)), ("fsdp", "ctx")
    )
    token_total = pack_count * fsdp_count
    fraction = counts_global / (token_total * top_count)
    balance_loss = (expert_count * jnp.sum(fraction * (probs_global / token_total))).reshape(1)
    flat_routes = routes.reshape(-1)
    flat_mask = (flat_routes[:, None] == expert_ids[None, :]).astype(jnp.int32)
    slot_rank = jnp.sum(jnp.cumsum(flat_mask, axis=0) * flat_mask, axis=1) - 1
    slot_index = flat_routes * capacity + slot_rank
    buffer_rows = expert_count * capacity
    send_rows = (
        jnp.zeros((buffer_rows, model_width), jnp.bfloat16)
        .at[slot_index]
        .set(jnp.repeat(normed_moe, top_count, axis=0))
    )
    send_rows = send_rows.reshape(fsdp_count, local_experts * capacity, model_width)
    arrived = lax.all_to_all(send_rows, "fsdp", split_axis=0, concat_axis=0, tiled=True)
    expert_rows = to_expert(arrived, local_experts, capacity)
    gate_pre, up_pre, hidden = expert_forward(expert_rows, w_gate, w_up)
    expert_out = jnp.einsum(
        "erf,efd->erd", hidden, w_down, preferred_element_type=jnp.float32
    ).astype(jnp.bfloat16)
    returned = lax.all_to_all(
        from_expert(expert_out, fsdp_count, capacity),
        "fsdp",
        split_axis=0,
        concat_axis=0,
        tiled=True,
    )
    slot_values = returned.reshape(buffer_rows, model_width)[slot_index].reshape(
        row_count, top_count, model_width
    )
    moe_part = jnp.sum(gate_weights[:, :, None] * slot_values, axis=1)
    moe_out = lax.psum(moe_part.astype(jnp.bfloat16), "tp").astype(jnp.float32)
    output = (middle + moe_out).astype(jnp.bfloat16)
    upstream = out_grad.astype(jnp.float32)
    gate_dots = jnp.sum(slot_values * upstream[:, None, :], axis=-1)
    grad_slots = (
        (gate_weights[:, :, None] * upstream[:, None, :])
        .astype(jnp.bfloat16)
        .reshape(row_count * top_count, model_width)
    )
    grad_send = jnp.zeros((buffer_rows, model_width), jnp.bfloat16).at[slot_index].set(grad_slots)
    grad_send = grad_send.reshape(fsdp_count, local_experts * capacity, model_width)
    grad_arrived = lax.all_to_all(grad_send, "fsdp", split_axis=0, concat_axis=0, tiled=True)
    kept_gate, kept_up, kept_hidden = (gate_pre, up_pre, hidden)
    grad_expert = to_expert(grad_arrived, local_experts, capacity)
    grad_hidden = jnp.einsum(
        "erd,efd->erf", grad_expert, w_down, preferred_element_type=jnp.float32
    )
    down_grad = jnp.einsum(
        "erf,erd->efd", kept_hidden, grad_expert, preferred_element_type=jnp.float32
    )
    sigmoid_gate = jax.nn.sigmoid(kept_gate)
    grad_gate = (
        grad_hidden * kept_up * sigmoid_gate * (1.0 + kept_gate * (1.0 - sigmoid_gate))
    ).astype(jnp.bfloat16)
    grad_up = (grad_hidden * kept_gate * sigmoid_gate).astype(jnp.bfloat16)
    gate_grad_w = jnp.einsum(
        "erd,erf->edf", expert_rows, grad_gate, preferred_element_type=jnp.float32
    )
    up_grad_w = jnp.einsum("erd,erf->edf", expert_rows, grad_up, preferred_element_type=jnp.float32)
    grad_rows = jnp.einsum("erf,edf->erd", grad_gate, w_gate, preferred_element_type=jnp.float32)
    grad_rows = (
        grad_rows + jnp.einsum("erf,edf->erd", grad_up, w_up, preferred_element_type=jnp.float32)
    ).astype(jnp.bfloat16)
    grad_back = lax.all_to_all(
        from_expert(grad_rows, fsdp_count, capacity),
        "fsdp",
        split_axis=0,
        concat_axis=0,
        tiled=True,
    )
    grad_slot_rows = grad_back.reshape(buffer_rows, model_width)[slot_index].reshape(
        row_count, top_count, model_width
    )
    moe_in_part = jnp.sum(grad_slot_rows.astype(jnp.float32), axis=1)
    moe_in_grad, gate_grad = lax.psum((moe_in_part, gate_dots), "tp")
    weighted = jnp.sum(gate_grad * gate_weights, axis=-1, keepdims=True)
    chosen_grad = (gate_grad - weighted) / chosen_total
    prob_grad = (
        jnp.sum(route_mask * chosen_grad[:, :, None], axis=1)
        + loss_grad[0] * expert_count * fraction / token_total
    )
    logit_grad = router_probs * (
        prob_grad - jnp.sum(prob_grad * router_probs, axis=-1, keepdims=True)
    )
    router_grad = jnp.einsum(
        "td,te->de", normed_moe.astype(jnp.float32), logit_grad, precision=highest
    )
    moe_grad = moe_in_grad + jnp.einsum(
        "te,de->td", logit_grad, full_router.astype(jnp.float32), precision=highest
    )
    gain_moe_grad, middle_norm_grad = rms_back_gain(inverse_moe, scaled_moe, moe_gain, moe_grad)
    middle_grad = upstream + middle_norm_grad
    out_in = middle_grad.astype(jnp.bfloat16)
    out_w_grad = jnp.einsum("tq,td->qd", attended, out_in, preferred_element_type=jnp.float32)
    mixed_grad = jnp.einsum(
        "td,qd->tq", out_in, full_out, preferred_element_type=jnp.float32
    ).astype(jnp.bfloat16)
    query_acc, key_grad_pack, value_grad_pack = attention_backward(
        grouped,
        pack_keys,
        pack_values,
        mixed_grad,
        log_total,
        doc_ids,
        doc_first,
        base_row,
        block_rows,
    )
    key_grad, value_grad, gate_w_out, up_w_out, down_w_out = (
        lax.psum_scatter(key_grad_pack, "ctx", scatter_dimension=0, tiled=True),
        lax.psum_scatter(value_grad_pack, "ctx", scatter_dimension=0, tiled=True),
        lax.psum_scatter(gate_grad_w, "ctx", scatter_dimension=1, tiled=True),
        lax.psum_scatter(up_grad_w, "ctx", scatter_dimension=1, tiled=True),
        lax.psum_scatter(down_grad, "ctx", scatter_dimension=2, tiled=True),
    )
    query_grad = (
        rotate(query_acc.reshape(row_count, local_heads, HEAD_DIM), cos_table, -sin_table)
        .astype(jnp.bfloat16)
        .reshape(row_count, local_heads * HEAD_DIM)
    )
    key_grad_low = (
        rotate(key_grad, cos_table, -sin_table)
        .astype(jnp.bfloat16)
        .reshape(row_count, local_kv * HEAD_DIM)
    )
    value_grad_low = value_grad.astype(jnp.bfloat16).reshape(row_count, local_kv * HEAD_DIM)
    query_w_grad = jnp.einsum(
        "td,tq->dq", normed_attn, query_grad, preferred_element_type=jnp.float32
    )
    key_w_grad = jnp.einsum(
        "td,tq->dq", normed_attn, key_grad_low, preferred_element_type=jnp.float32
    )
    value_w_grad = jnp.einsum(
        "td,tq->dq", normed_attn, value_grad_low, preferred_element_type=jnp.float32
    )
    attn_in_part = jnp.einsum(
        "tq,dq->td", query_grad, full_query, preferred_element_type=jnp.float32
    )
    attn_in_part = attn_in_part + jnp.einsum(
        "tq,dq->td", key_grad_low, full_key, preferred_element_type=jnp.float32
    )
    attn_in_part = attn_in_part + jnp.einsum(
        "tq,dq->td", value_grad_low, full_value, preferred_element_type=jnp.float32
    )
    attn_in_grad = lax.psum(attn_in_part.astype(jnp.bfloat16), "tp").astype(jnp.float32)
    gain_attn_grad, input_norm_grad = rms_back_gain(inverse_attn, scaled_attn, attn_gain, attn_in_grad)
    tokens_grad = middle_grad + input_norm_grad
    shard_grads = (
        lax.psum_scatter(gain_attn_grad, ("fsdp", "ctx"), scatter_dimension=0, tiled=True),
        lax.psum_scatter(query_w_grad, ("fsdp", "ctx"), scatter_dimension=0, tiled=True),
        lax.psum_scatter(key_w_grad, ("fsdp", "ctx"), scatter_dimension=0, tiled=True),
        lax.psum_scatter(value_w_grad, ("fsdp", "ctx"), scatter_dimension=0, tiled=True),
        lax.psum_scatter(out_w_grad, ("fsdp", "ctx"), scatter_dimension=1, tiled=True),
        lax.psum_scatter(gain_moe_grad, ("fsdp", "ctx"), scatter_dimension=0, tiled=True),
        lax.psum_scatter(router_grad, ("fsdp", "ctx"), scatter_dimension=0, tiled=True),
    )
    return (
        output,
        balance_loss,
        tokens_grad,
        shard_grads[0],
        shard_grads[1],
        shard_grads[2],
        shard_grads[3],
        shard_grads[4],
        shard_grads[5],
        shard_grads[6],
        gate_w_out,
        up_w_out,
        down_w_out,
    )


def on_device(
    tokens,
    lengths,
    routes,
    norm_attn,
    w_query,
    w_key,
    w_value,
    w_out,
    norm_moe,
    w_router,
    w_gate,
    w_up,
    w_down,
    out_grad,
    loss_grad,
):
    expert_count = w_router.shape[1]
    if lax.axis_size("fsdp") != 8:
        return on_any_slice(
            tokens, lengths, routes, norm_attn, w_query, w_key, w_value, w_out, norm_moe, w_router,
            w_gate, w_up, w_down, out_grad, loss_grad,
        )
    small = widen([w_router, norm_attn[:, None], norm_moe[:, None]])
    (
        probs, mask, row, lse, cos, sin, returned, middle, query, kv_pack, attended,
        in_weights, out_weights, moe_rows, gate_up_grad, down_grad,
    ) = layer_on_chip(
        lengths, loss_grad, routes, tokens, small, w_query, w_key, w_value, w_out.T, out_grad,
        w_gate[0], w_up[0], w_down[0], expert_count,
    )
    (
        output, loss, tokens_grad, query_grad, key_grad, value_grad, out_reduced, small, gate_w_out, up_w_out, down_w_out,
    ) = backward_on_chip(
        lengths, row, returned, middle, probs, mask, out_grad, tokens, query, kv_pack, lse, attended, cos, sin,
        in_weights, out_weights, moe_rows, gate_up_grad, down_grad, expert_count,
    )
    return (
        output,
        loss[0, :1],
        tokens_grad,
        small[:, expert_count],
        query_grad,
        key_grad,
        value_grad,
        out_reduced.T,
        small[:, expert_count + 1],
        small[:, :expert_count],
        gate_w_out[None],
        up_w_out[None],
        down_w_out[None],
    )


def solution(mesh):
    rows = P(("fsdp", "ctx"), None)
    gain = P(("fsdp", "ctx"))
    split = P(("fsdp", "ctx"), "tp")
    out_split = P("tp", ("fsdp", "ctx"))
    columns = P("fsdp", None, "tp")
    return jax.shard_map(
        on_device,
        mesh=mesh,
        in_specs=(
            rows,
            P("fsdp", None),
            rows,
            gain,
            split,
            split,
            split,
            out_split,
            gain,
            rows,
            columns,
            columns,
            P("fsdp", "tp", None),
            rows,
            P(),
        ),
        out_specs=(
            rows,
            P(),
            rows,
            gain,
            split,
            split,
            split,
            out_split,
            gain,
            rows,
            P("fsdp", "ctx", "tp"),
            P("fsdp", "ctx", "tp"),
            P("fsdp", "tp", "ctx"),
        ),
        check_vma=False,
    )
```
